32 devices in a mesh: gx: 2 (over x), gy: 4 (over y, core), gz: 4 (over z).
Axes of the slice: x: 2, y: 2, z: 4, core: 2. Of those that a mesh axis runs over, the one named last changes fastest.
Arguments:
- initial: float32 [32, 64, 512], P('gx', 'gy', 'gz'), may hold values from -6 to 6
- right_side: float32 [32, 64, 512], P('gx', 'gy', 'gz'), may hold values from -8 to 8
- alpha: float32 [32, 64, 512], P('gx', 'gy', 'gz'), may hold values from 0.5 to 2
- beta_x: float32 [32, 64, 512], P('gx', 'gy', 'gz'), may hold values from 0.25 to 4
- beta_y: float32 [32, 64, 512], P('gx', 'gy', 'gz'), may hold values from 0.25 to 4
- beta_z: float32 [32, 64, 512], P('gx', 'gy', 'gz'), may hold values from 0.25 to 4
Outputs:
- solution: float32 [32, 64, 512], P('gx', 'gy', 'gz')
The draws below stay inside these ranges and needn't reach their ends.
All inputs are finite; a program needn't handle non-finite values.
Results may differ from the reference program's by a relative error of at most 0.000098.
Values sent between devices are 32-bit elements; how exact they have to be, the bound alone decides.
No kernel may reach another device: no remote copies, remote signals or barrier semaphores. Data moves between devices by JAX's collectives and lax.ppermute only.
A program may use at most 128 MiB of HBM per device.

```python
import math
import jax
import jax.numpy as jnp

LEVELS = 6
SWEEPS = 2
BOTTOM = 8
NX = 32
NY = 64
NZ = 512


def levels(key, dims, shards, least, high):
    gain = 1.0
    for axis_at, shards_of in shards:
        steps = jax.random.uniform(jax.random.fold_in(jax.random.fold_in(key, 6), axis_at), (shards_of,), jnp.float32, least / len(shards), high / len(shards))
        gain = gain * jnp.repeat(jnp.exp(steps), dims[axis_at] // shards_of).reshape((-1,) + (1,) * (len(dims) - 1 - axis_at))
    return gain


def normal_values(rng, extent, deviation, limit, split=(), kind=jnp.bfloat16):
    loudness = levels(rng, extent, split, -0.22, 0.18) if split else 1.0
    drawn = jax.random.normal(rng, extent, jnp.float32) * deviation * loudness
    return jnp.minimum(jnp.maximum(drawn, -limit), limit).astype(kind)


def setup_inputs(seed: int = 0) -> dict:
    keys = jax.random.split(jax.random.key(seed), 7)
    initial = normal_values(keys[0], (NX, NY, NZ), 1.0, 6.0, ((0, 2), (1, 4), (2, 4)), jnp.float32)
    right_side = normal_values(keys[1], (NX, NY, NZ), 1.0, 8.0, ((0, 2), (1, 4), (2, 4)), jnp.float32)
    alpha = jnp.clip(jnp.exp(math.log(2.0) - 1.3862944 * jax.random.uniform(keys[2], (NX, NY, NZ), jnp.float32) ** levels(keys[2], (NX, NY, NZ), ((0, 2), (1, 4), (2, 4)), -0.2, 0.2)), 0.5, 2.0)
    beta_x = jnp.clip(jnp.exp(math.log(4.0) - 2.7725887 * jax.random.uniform(keys[3], (NX, NY, NZ), jnp.float32) ** levels(keys[3], (NX, NY, NZ), ((0, 2), (1, 4), (2, 4)), -0.2, 0.2)), 0.25, 4.0)
    beta_y = jnp.clip(jnp.exp(math.log(4.0) - 2.7725887 * jax.random.uniform(keys[4], (NX, NY, NZ), jnp.float32) ** levels(keys[4], (NX, NY, NZ), ((0, 2), (1, 4), (2, 4)), -0.2, 0.2)), 0.25, 4.0)
    beta_z = jnp.clip(jnp.exp(math.log(4.0) - 2.7725887 * jax.random.uniform(keys[5], (NX, NY, NZ), jnp.float32) ** levels(keys[5], (NX, NY, NZ), ((0, 2), (1, 4), (2, 4)), -0.2, 0.2)), 0.25, 4.0)
    return {"initial": initial, "right_side": right_side, "alpha": alpha, "beta_x": beta_x, "beta_y": beta_y, "beta_z": beta_z}


relax = 2.0 / 3.0


def lower_faces(values, axis):
    widths = [(0, 0), (0, 0), (0, 0)]
    widths[axis] = (1, 0)
    padded = jnp.pad(values, widths)
    sizes = values.shape
    return padded[:sizes[0], :sizes[1], :sizes[2]]


def coarsen_cells(values):
    sx, sy, sz = values.shape
    blocks = values.reshape(sx // 2, 2, sy // 2, 2, sz // 2, 2)
    total = blocks[:, 0, :, 0, :, 0]
    for first in range(2):
        for second in range(2):
            for third in range(2):
                if first + second + third > 0:
                    total = total + blocks[:, first, :, second, :, third]
    return 0.125 * total


def coarsen_faces(values, axis):
    sx, sy, sz = values.shape
    blocks = values.reshape(sx // 2, 2, sy // 2, 2, sz // 2, 2)
    others = [other for other in range(3) if other != axis]
    total = None
    for first in range(2):
        for second in range(2):
            index = [slice(None)] * 6
            index[2 * axis + 1] = 1
            index[2 * others[0] + 1] = first
            index[2 * others[1] + 1] = second
            term = blocks[tuple(index)]
            total = term if total is None else total + term
    return 0.25 * total


def coarsen_all(base):
    alpha, beta_x, beta_y, beta_z = base
    return (coarsen_cells(alpha), coarsen_faces(beta_x, 0), coarsen_faces(beta_y, 1), coarsen_faces(beta_z, 2))


def prolong(values):
    return jnp.repeat(jnp.repeat(jnp.repeat(values, 2, 0), 2, 1), 2, 2)


def full_coeffs(base):
    alpha, beta_x, beta_y, beta_z = base
    weight = 0.25 ** (LEVELS - 1)
    return (weight * alpha, beta_x, beta_y, beta_z, lower_faces(beta_x, 0), lower_faces(beta_y, 1), lower_faces(beta_z, 2))


def apply_op(padded, coeffs, scale):
    alpha, beta_x, beta_y, beta_z, low_x, low_y, low_z = coeffs
    centre = padded[1:-1, 1:-1, 1:-1]
    flux = beta_x * (centre - padded[2:, 1:-1, 1:-1]) + low_x * (centre - padded[:-2, 1:-1, 1:-1])
    flux = flux + beta_y * (centre - padded[1:-1, 2:, 1:-1]) + low_y * (centre - padded[1:-1, :-2, 1:-1])
    flux = flux + beta_z * (centre - padded[1:-1, 1:-1, 2:]) + low_z * (centre - padded[1:-1, 1:-1, :-2])
    return alpha * centre + scale * flux


def diagonal_of(coeffs, scale):
    alpha, beta_x, beta_y, beta_z, low_x, low_y, low_z = coeffs
    return alpha + scale * (beta_x + low_x + beta_y + low_y + beta_z + low_z)


def zero_pad(values):
    return jnp.pad(values, 1)


def smooth(field, rhs, coeffs, scale, count, pad_fn):
    diag = diagonal_of(coeffs, scale)
    for sweep in range(count):
        field = field + relax * (rhs - apply_op(pad_fn(field), coeffs, scale)) / diag
    return field


def full_cycle(level, rhs, base):
    coeffs = full_coeffs(base)
    scale = 0.25 ** level
    field = jnp.zeros(rhs.shape, jnp.float32)
    if level == LEVELS - 1:
        return smooth(field, rhs, coeffs, scale, BOTTOM, zero_pad)
    field = smooth(field, rhs, coeffs, scale, SWEEPS, zero_pad)
    remain = rhs - apply_op(zero_pad(field), coeffs, scale)
    correction = full_cycle(level + 1, coarsen_cells(remain), coarsen_all(base))
    field = field + prolong(correction)
    return smooth(field, rhs, coeffs, scale, SWEEPS, zero_pad)


def reference(initial, right_side, alpha, beta_x, beta_y, beta_z):
    base = (alpha, beta_x, beta_y, beta_z)
    coeffs = full_coeffs(base)
    field = smooth(initial, right_side, coeffs, 1.0, SWEEPS, zero_pad)
    remain = right_side - apply_op(zero_pad(field), coeffs, 1.0)
    correction = full_cycle(1, coarsen_cells(remain), coarsen_all(base))
    field = field + prolong(correction)
    return smooth(field, right_side, coeffs, 1.0, SWEEPS, zero_pad)
```

```python
import jax
import jax.numpy as jnp
from jax import lax
from jax.sharding import PartitionSpec as P

LEVELS = 6
SWEEPS = 2
BOTTOM = 8


relax = 2.0 / 3.0


def from_behind(block, axis, distance):
    devices = range(lax.axis_size(axis))
    route = [(i - distance, i) for i in devices if i - distance in devices]
    return lax.ppermute(block, axis, route)


def with_halo(cells, sides, width):
    for axis, dim in sides:
        count = lax.axis_size(axis)
        odd = lax.axis_index(axis) % 2 == 1
        head = lax.slice_in_dim(cells, 0, width, axis=dim)
        tail = lax.slice_in_dim(cells, cells.shape[dim] - width, cells.shape[dim], axis=dim)
        first = [(i, i ^ 1) for i in range(count) if i ^ 1 < count]
        second = [(i, ((i + 1) ^ 1) - 1) for i in range(1, count) if ((i + 1) ^ 1) - 1 < count]
        one = lax.ppermute(jnp.where(odd, head, tail), axis, first)
        if second:
            two = lax.ppermute(jnp.where(odd, tail, head), axis, second)
        else:
            two = jnp.zeros_like(one)
        below = jnp.where(odd, one, two)
        above = jnp.where(odd, two, one)
        cells = jnp.concatenate([below, cells, above], axis=dim)
    return cells


def pair_table(count):
    rows = lax.broadcasted_iota(jnp.int32, (count, count // 2), 0)
    cols = lax.broadcasted_iota(jnp.int32, (count, count // 2), 1)
    return (rows // 2 == cols).astype(jnp.float32)


def odd_table(count):
    rows = lax.broadcasted_iota(jnp.int32, (count, count // 2), 0)
    cols = lax.broadcasted_iota(jnp.int32, (count, count // 2), 1)
    return (rows == 2 * cols + 1).astype(jnp.float32)


def along_second(values, table):
    return jnp.einsum(
        "ayc,yb->abc",
        values,
        table,
        precision=lax.Precision.HIGHEST,
        preferred_element_type=jnp.float32,
    )


def along_third(values, table):
    return jnp.einsum(
        "abz,zc->abc",
        values,
        table,
        precision=lax.Precision.HIGHEST,
        preferred_element_type=jnp.float32,
    )


def reduce_first(values, pick_odd):
    sx, sy, sz = values.shape
    blocks = values.reshape(sx // 2, 2, sy, sz)
    if pick_odd:
        return blocks[:, 1]
    return blocks[:, 0] + blocks[:, 1]


def reduce_dims(values, odd_axis):
    sx, sy, sz = values.shape
    values = reduce_first(values, odd_axis == 0)
    second = odd_table(sy) if odd_axis == 1 else pair_table(sy)
    values = along_second(values, second)
    third = odd_table(sz) if odd_axis == 2 else pair_table(sz)
    return along_third(values, third)


def coarsen_cells(values):
    return 0.125 * reduce_dims(values, -1)


def coarsen_faces(values, axis):
    return 0.25 * reduce_dims(values, axis)


def coarsen_all(base):
    alpha, beta_x, beta_y, beta_z = base
    return (
        coarsen_cells(alpha),
        coarsen_faces(beta_x, 0),
        coarsen_faces(beta_y, 1),
        coarsen_faces(beta_z, 2),
    )


def prolong(values):
    sx, sy, sz = values.shape
    spread = along_third(values, jnp.transpose(pair_table(2 * sz)))
    spread = along_second(spread, jnp.transpose(pair_table(2 * sy)))
    return jnp.repeat(spread, 2, 0)


def lower_faces(values, axis):
    widths = [(0, 0), (0, 0), (0, 0)]
    widths[axis] = (1, 0)
    padded = jnp.pad(values, widths)
    sizes = values.shape
    return padded[: sizes[0], : sizes[1], : sizes[2]]


def full_coeffs(base):
    alpha, beta_x, beta_y, beta_z = base
    weight = 0.25 ** (LEVELS - 1)
    return (
        weight * alpha,
        beta_x,
        beta_y,
        beta_z,
        lower_faces(beta_x, 0),
        lower_faces(beta_y, 1),
        lower_faces(beta_z, 2),
    )


def local_coeffs(base):
    alpha, beta_x, beta_y, beta_z = base
    weight = 0.25 ** (LEVELS - 1)
    edge_x = from_behind(beta_x[-1:, :, :], "gx", 1)
    edge_y = from_behind(beta_y[:, -1:, :], "gy", 1)
    edge_z = from_behind(beta_z[:, :, -1:], "gz", 1)
    low_x = jnp.concatenate([edge_x, beta_x[:-1, :, :]], axis=0)
    low_y = jnp.concatenate([edge_y, beta_y[:, :-1, :]], axis=1)
    low_z = jnp.concatenate([edge_z, beta_z[:, :, :-1]], axis=2)
    return (weight * alpha, beta_x, beta_y, beta_z, low_x, low_y, low_z)


def apply_op(padded, coeffs, scale):
    alpha, beta_x, beta_y, beta_z, low_x, low_y, low_z = coeffs
    centre = padded[1:-1, 1:-1, 1:-1]
    flux = beta_x * (centre - padded[2:, 1:-1, 1:-1]) + low_x * (centre - padded[:-2, 1:-1, 1:-1])
    flux = (
        flux
        + beta_y * (centre - padded[1:-1, 2:, 1:-1])
        + low_y * (centre - padded[1:-1, :-2, 1:-1])
    )
    flux = (
        flux
        + beta_z * (centre - padded[1:-1, 1:-1, 2:])
        + low_z * (centre - padded[1:-1, 1:-1, :-2])
    )
    return alpha * centre + scale * flux


def diagonal_of(coeffs, scale):
    alpha, beta_x, beta_y, beta_z, low_x, low_y, low_z = coeffs
    return alpha + scale * (beta_x + low_x + beta_y + low_y + beta_z + low_z)


def zero_pad(values):
    return jnp.pad(values, 1)


def halo_pad(values):
    return with_halo(values, (("gx", 0), ("gy", 1), ("gz", 2)), 1)


def smooth(field, rhs, coeffs, scale, count, pad_fn):
    diag = diagonal_of(coeffs, scale)
    for sweep in range(count):
        field = field + relax * (rhs - apply_op(pad_fn(field), coeffs, scale)) / diag
    return field


def full_cycle(level, rhs, base):
    coeffs = full_coeffs(base)
    scale = 0.25**level
    field = jnp.zeros(rhs.shape, jnp.float32)
    if level == LEVELS - 1:
        return smooth(field, rhs, coeffs, scale, BOTTOM, zero_pad)
    field = smooth(field, rhs, coeffs, scale, SWEEPS, zero_pad)
    remain = rhs - apply_op(zero_pad(field), coeffs, scale)
    correction = full_cycle(level + 1, coarsen_cells(remain), coarsen_all(base))
    field = field + prolong(correction)
    return smooth(field, rhs, coeffs, scale, SWEEPS, zero_pad)


def local(initial, right_side, alpha, beta_x, beta_y, beta_z):
    gather_level = 2
    base = (alpha, beta_x, beta_y, beta_z)
    field = initial
    rhs = right_side
    saved = []
    for level in range(gather_level):
        scale = 0.25**level
        coeffs = local_coeffs(base)
        if level > 0:
            field = jnp.zeros(rhs.shape, jnp.float32)
        field = smooth(field, rhs, coeffs, scale, SWEEPS, halo_pad)
        remain = rhs - apply_op(halo_pad(field), coeffs, scale)
        saved.append((field, rhs, coeffs, scale))
        rhs = coarsen_cells(remain)
        base = coarsen_all(base)
    block_x, block_y, block_z = rhs.shape
    packed = jnp.stack([rhs, base[0], base[1], base[2], base[3]])[None]
    devices = lax.axis_size("gx") * lax.axis_size("gy") * lax.axis_size("gz")
    copies = jnp.broadcast_to(packed, (devices,) + packed.shape[1:])
    gathered = lax.all_to_all(copies, ("gx", "gy", "gz"), 0, 0, tiled=True)
    count_x = lax.axis_size("gx")
    count_y = lax.axis_size("gy")
    count_z = lax.axis_size("gz")
    whole = gathered.reshape(count_x, count_y, count_z, 5, block_x, block_y, block_z)
    whole = whole.transpose(3, 0, 4, 1, 5, 2, 6).reshape(
        5, count_x * block_x, count_y * block_y, count_z * block_z
    )
    correction_full = full_cycle(gather_level, whole[0], (whole[1], whole[2], whole[3], whole[4]))
    start_x = lax.axis_index("gx") * block_x
    start_y = lax.axis_index("gy") * block_y
    start_z = lax.axis_index("gz") * block_z
    correction = lax.dynamic_slice(
        correction_full, (start_x, start_y, start_z), (block_x, block_y, block_z)
    )
    for level in reversed(range(gather_level)):
        field, rhs, coeffs, scale = saved[level]
        field = field + prolong(correction)
        correction = smooth(field, rhs, coeffs, scale, SWEEPS, halo_pad)
    return correction


def solution(mesh):
    in_specs = (
        P("gx", "gy", "gz"),
        P("gx", "gy", "gz"),
        P("gx", "gy", "gz"),
        P("gx", "gy", "gz"),
        P("gx", "gy", "gz"),
        P("gx", "gy", "gz"),
    )
    out_specs = P("gx", "gy", "gz")
    return jax.shard_map(local, mesh=mesh, in_specs=in_specs, out_specs=out_specs, check_vma=False)
```

```python
import functools

import jax
import jax.numpy as jnp
from jax import lax
from jax.experimental import pallas as pl
from jax.experimental.pallas import tpu as pltpu
from jax.sharding import PartitionSpec as P

LEVELS = 6
SWEEPS = 2
BOTTOM = 8
WEIGHT = 0.25 ** (LEVELS - 1)
RELAX = 2.0 / 3.0
KEEP = 1.0 / 3.0

WIDE = 7
SIDE = 8
NEAR = 4
LANES = 128

VM = pl.BlockSpec(memory_space=pltpu.VMEM)
SM = pl.BlockSpec(memory_space=pltpu.SMEM)
F32 = jnp.float32


def lane_of(shape):
    return lax.broadcasted_iota(jnp.int32, shape, len(shape) - 1)


def pick(flag, yes, no):
    return jnp.where(jnp.full(yes.shape, flag, jnp.int32) == 1, yes, no)


def neighbours(axis_size, odd, one, two):
    if axis_size == 2:
        two = jnp.zeros_like(one)
    return pick(odd, one, two), pick(odd, two, one)


def turn(values, shift, axis):
    return pltpu.roll(values, shift % values.shape[axis], axis)


def parts_of(values):
    high = values.astype(jnp.bfloat16)
    rest = values - high.astype(F32)
    middle = rest.astype(jnp.bfloat16)
    low = (rest - middle.astype(F32)).astype(jnp.bfloat16)
    return high, middle, low


def times_table(values, table):
    table = table.astype(jnp.bfloat16)
    total = None
    for part in reversed(parts_of(values)):
        term = jnp.dot(part, table, preferred_element_type=F32)
        total = term if total is None else total + term
    return total


def table_times(table, values):
    table = table.astype(jnp.bfloat16)
    total = None
    for part in reversed(parts_of(values)):
        term = jnp.dot(table, part, preferred_element_type=F32)
        total = term if total is None else total + term
    return total


def iota2(shape, axis):
    return lax.broadcasted_iota(jnp.int32, shape, axis)


def pair_table(rows, cols, odd):
    row = iota2((rows, cols), 0)
    col = iota2((rows, cols), 1)
    hit = (row == 2 * col + 1) if odd else (row // 2 == col)
    return hit.astype(F32)


def below_x(values):
    if values.shape[0] == 1:
        return jnp.zeros_like(values)
    return jnp.concatenate([jnp.zeros_like(values[:1]), values[:-1]], axis=0)


def above_x(values):
    if values.shape[0] == 1:
        return jnp.zeros_like(values)
    return jnp.concatenate([values[1:], jnp.zeros_like(values[:1])], axis=0)


def pull(values, faces):
    bx, by, bz = faces
    total = bx * above_x(values) + below_x(bx * values)
    total = total + (by * turn(values, -1, 1) + turn(by * values, 1, 1))
    return total + (bz * turn(values, -1, 2) + turn(bz * values, 1, 2))


def diagonal(mass, faces, coupled):
    bx, by, bz = faces
    _, cy, cz = coupled
    return mass + bx + below_x(bx) + by + turn(cy, 1, 1) + bz + turn(cz, 1, 2)


def relaxer(mass, diag):
    inside = mass > 0.0
    return jnp.where(inside, RELAX / jnp.where(inside, diag, 1.0), 0.0)


def sweep(values, rhs, weight, faces):
    return KEEP * values + weight * (rhs + pull(values, faces))


def pack_z_kernel(where_ref, *refs):
    ins, (first, second) = refs[:6], refs[6:]
    odd = where_ref[2] % 2
    sx, sy, sz = ins[0].shape
    half = sx // 2
    lane = lane_of((half, sy, LANES))
    head = jnp.zeros((half, sy, LANES), F32)
    tail = head
    for a, ref in enumerate(ins):
        for g in range(2):
            block = ref[g * half:(g + 1) * half]
            at = 64 * g + SIDE * a
            mask = (lane >= at) & (lane < at + SIDE)
            head = jnp.where(mask, turn(block, at, 2), head)
            tail = jnp.where(mask, turn(block, at + SIDE, 2), tail)
    first[...] = pick(odd, head, tail)
    second[...] = pick(odd, tail, head)


def face_x_kernel(counts, where_ref, *refs):
    ins, one_ref, two_ref = refs[:6], refs[6], refs[7]
    zpack, sends = refs[8], refs[9:]
    sx, sy, sz = ins[0].shape
    half = sx // 2
    below, above = neighbours(counts[2], where_ref[2] % 2, one_ref[...], two_ref[...])
    lane = lane_of(below.shape)
    zpack[:half] = jnp.where(lane < 64, above, turn(below, 64, 2))
    zpack[half:] = jnp.where(lane < 64, turn(above, 64, 2), below)
    odd = where_ref[0] % 2
    for k, send in enumerate(sends):
        start = (1 - odd if k == 0 else odd) * (sx - WIDE)
        for a, ref in enumerate(tuple(ins) + (zpack,)):
            send[a] = ref[pl.ds(start, WIDE)]


def face_y_kernel(counts, where_ref, *refs):
    ins, halos, sends = refs[:7], refs[7:-2], refs[-2:]
    sx, sy, sz = ins[0].shape
    odd_x = where_ref[0] % 2
    odd = where_ref[1] % 2
    for k, send in enumerate(sends):
        start = pl.multiple_of((1 - odd if k == 0 else odd) * (sy - SIDE), SIDE)
        rows = pl.ds(start, SIDE)
        for a, ref in enumerate(ins):
            one = halos[0][a, :, rows, :]
            two = halos[-1][a, :, rows, :]
            below, above = neighbours(counts[0], odd_x, one, two)
            send[a, :WIDE] = below
            send[a, WIDE:WIDE + sx] = ref[:, rows, :]
            send[a, WIDE + sx:] = above


def ring_up(main, halo, lane):
    main_up, halo_up = turn(main, -1, 1), turn(halo, -1, 1)
    last = lane == LANES - 1
    return jnp.where(last, halo_up, main_up), jnp.where(last, main_up, halo_up)


def ring_down(main, halo, lane):
    main_down, halo_down = turn(main, 1, 1), turn(halo, 1, 1)
    zero = lane == 0
    return jnp.where(zero, halo_down, main_down), jnp.where(zero, main_down, halo_down)


def pull_slab(field, bx, by, bz, x, lane):
    centre = [half[x] for half in field]
    out = []
    for k in range(2):
        c, face = centre[k], by[k][x]
        t = bx[k][x] * field[k][x + 1] + bx[k][x - 1] * field[k][x - 1]
        out.append(t + (face * turn(c, -1, 0) + turn(face * c, 1, 0)))
    faces = [half[x] for half in bz]
    ups = ring_up(centre[0], centre[1], lane)
    downs = ring_down(faces[0] * centre[0], faces[1] * centre[1], lane)
    return centre, [out[k] + (faces[k] * ups[k] + downs[k]) for k in range(2)]


def down_kernel(counts, devices, where_ref, *refs):
    ins = refs[:7]
    n_x = 1 if counts[0] == 2 else 2
    halos_x = refs[7:7 + n_x]
    one_y, two_y = refs[7 + n_x:9 + n_x]
    outs = refs[9 + n_x:16 + n_x]
    copies, own1, first1, second1, kept, weight_out, faces_out = outs
    grid, other, scales, summed, left = refs[16 + n_x:]
    sx, sy, sz = ins[0].shape
    ex, ey = sx + 2 * WIDE, sy + 2 * SIDE
    odd_x, odd_y, odd_z = where_ref[0] % 2, where_ref[1] % 2, where_ref[2] % 2

    mid_x = slice(WIDE, WIDE + sx)
    mid_y = slice(SIDE, SIDE + sy)
    for a in range(7):
        to = grid.at[a, 0]
        below, above = neighbours(counts[0], odd_x, halos_x[0][a], halos_x[-1][a])
        to[:WIDE, mid_y, :] = below
        to[mid_x, mid_y, :] = ins[a][...]
        to[WIDE + sx:, mid_y, :] = above
        below, above = neighbours(counts[1], odd_y, one_y[a], two_y[a])
        to[:, :SIDE, :] = below
        to[:, SIDE + sy:, :] = above
    lane = lane_of((ey, LANES))

    def unpack(x, carry):
        packed = grid[6, 0, x]
        for a in range(6):
            right = turn(packed, -SIDE * a, 1)
            other_side = turn(packed, 56 - SIDE * a, 1)
            grid[a, 1, x] = jnp.where(
                lane < SIDE, right, jnp.where(lane >= LANES - SIDE, other_side, 0.0)
            )
        return carry

    lax.fori_loop(0, ex, unpack, 0)

    field = [grid.at[0, k] for k in range(2)]
    rhs = [grid.at[1, k] for k in range(2)]
    alpha = [grid.at[2, k] for k in range(2)]
    bx = [grid.at[3, k] for k in range(2)]
    by = [grid.at[4, k] for k in range(2)]
    bz = [grid.at[5, k] for k in range(2)]
    diag = [scales.at[0, k] for k in range(2)]
    weight = [scales.at[1, k] for k in range(2)]
    halfway = [other.at[k] for k in range(2)]

    def first_sweep(x, carry):
        faces = [half[x] for half in bz]
        downs = ring_down(faces[0], faces[1], lane)
        centre, near = pull_slab(field, bx, by, bz, x, lane)
        for k in range(2):
            face = by[k][x]
            mass = WEIGHT * alpha[k][x]
            d = mass + bx[k][x] + bx[k][x - 1] + face + turn(face, 1, 0) + faces[k] + downs[k]
            w = relaxer(mass, d)
            diag[k][x] = d
            weight[k][x] = w
            halfway[k][x] = KEEP * centre[k] + w * (rhs[k][x] + near[k])
        return carry

    lax.fori_loop(1, ex - 1, first_sweep, 0)

    def second_sweep(x, carry):
        centre, near = pull_slab(halfway, bx, by, bz, x, lane)
        for k in range(2):
            field[k][x] = KEEP * centre[k] + weight[k][x] * (rhs[k][x] + near[k])
        return carry

    lax.fori_loop(2, ex - 2, second_sweep, 0)

    def residual(x, carry):
        centre, near = pull_slab(field, bx, by, bz, x, lane)
        for k in range(2):
            halfway[k][x] = rhs[k][x] - diag[k][x] * centre[k] + near[k]
        return carry

    lax.fori_loop(3, ex - 3, residual, 0)

    for k in range(2):
        kept[k] = grid[0, k, WIDE - 2:WIDE + sx + 2]
        weight_out[k] = scales[1, k, WIDE - 2:WIDE + sx + 2]
        for n, a in enumerate((1, 3, 4, 5)):
            faces_out[n, k] = grid[a, k, WIDE - 2:WIDE + sx + 2]

    x1, y1 = sx // 2 + 6, ey // 2
    blocks = ((alpha, False, False), (bx, True, False), (by, False, True), (bz, False, False))
    for n, (source, odd_first, odd_second) in enumerate(blocks):
        for k in range(2):

            def add_up(i, carry, n=n, source=source, k=k, odd_first=odd_first, odd_second=odd_second):
                total = None
                for p in (1,) if odd_first else (0, 1):
                    for q in (1,) if odd_second else (0, 1):
                        term = source[k][2 * i + 1 + p, pl.ds(q, y1, stride=2), :]
                        total = term if total is None else total + term
                summed[n, i, :, k * LANES:(k + 1) * LANES] = total
                return carry

            lax.fori_loop(0, x1, add_up, 0)
    for k in range(2):

        def add_rhs(i, carry, k=k):
            total = None
            for p in range(2):
                for q in range(2):
                    term = halfway[k][2 * i + 1 + p, pl.ds(q, y1, stride=2), :]
                    total = term if total is None else total + term
            summed[4, i, :, k * LANES:(k + 1) * LANES] = total
            return carry

        lax.fori_loop(1, x1 - 1, add_rhs, 0)
    summed[4, 0] = jnp.zeros((y1, 2 * LANES), F32)
    summed[4, x1 - 1] = jnp.zeros((y1, 2 * LANES), F32)

    pairs = pair_table(2 * LANES, LANES, False)
    odds = pair_table(2 * LANES, LANES, True)

    def coarse(n, table, factor):
        flat = summed[n].reshape(x1 * y1, 2 * LANES)
        return factor * times_table(flat, table).reshape(x1, y1, LANES)

    mass1 = coarse(0, pairs, 0.125 * WEIGHT)
    faces1 = (coarse(1, pairs, 0.0625), coarse(2, pairs, 0.0625), coarse(3, odds, 0.0625))
    rhs1 = coarse(4, pairs, 0.125)
    diag1 = diagonal(mass1, faces1, faces1)
    weight1 = relaxer(mass1, diag1)
    field1 = weight1 * rhs1
    field1 = sweep(field1, rhs1, weight1, faces1)
    remain1 = rhs1 - diag1 * field1 + pull(field1, faces1)

    bx1, by1, bz1 = sx // 2, sy // 2, sz // 2
    mine = slice(3, 3 + bx1)
    rows = slice(NEAR, NEAR + by1)
    lane1 = lane_of((bx1, by1, LANES))
    head = jnp.zeros((bx1, by1, LANES), F32)
    tail = head
    for n, values in enumerate((rhs1, weight1) + faces1):
        block = jnp.where(lane1 < bz1, values[mine, rows, :], 0.0)
        own1[n] = block
        at = NEAR * n
        mask = (lane1 >= at) & (lane1 < at + NEAR)
        head = jnp.where(mask, turn(block, at, 2), head)
        tail = jnp.where(mask, turn(block, at + NEAR - bz1, 2), tail)
    first1[...] = pick(odd_z, head, tail)
    second1[...] = pick(odd_z, tail, head)

    x2, y2, z2 = bx1 // 2, by1 // 2, bz1 // 2
    parts = (
        (remain1, False, False, False, 0.125),
        (mass1, False, False, False, 0.125),
        (faces1[0], True, False, False, 0.0625),
        (faces1[1], False, True, False, 0.0625),
        (faces1[2], False, False, True, 0.0625),
    )
    pairs2 = pair_table(LANES, LANES, False)
    odds2 = pair_table(LANES, LANES, True)
    lane2 = lane_of((y2, LANES))
    for n, (values, odd_first, odd_second, odd_third, factor) in enumerate(parts):
        left[n] = values[mine]
        rows2 = []
        for i in range(x2):
            total = None
            for p in (1,) if odd_first else (0, 1):
                for q in (1,) if odd_second else (0, 1):
                    term = left[n, 2 * i + p, pl.ds(NEAR + q, y2, stride=2), :]
                    total = term if total is None else total + term
            rows2.append(total)
        flat = jnp.concatenate(rows2, axis=0)
        flat = factor * times_table(flat, odds2 if odd_third else pairs2)
        packed = jnp.zeros((y2, LANES), F32)
        for i in range(x2):
            block = flat[i * y2:(i + 1) * y2]
            mask = (lane2 >= i * z2) & (lane2 < (i + 1) * z2)
            packed = jnp.where(mask, turn(block, i * z2, 1), packed)
        for d in range(devices):
            copies[d, n] = packed


def near_x_kernel(counts, where_ref, own_ref, one_ref, two_ref, ring, *sends):
    n, bx, by, _ = own_ref.shape
    below, above = neighbours(counts[2], where_ref[2] % 2, one_ref[...], two_ref[...])
    lane = lane_of(below.shape)
    for a in range(n):
        right = turn(above, LANES // 2 - NEAR * a, 2)
        left = turn(below, LANES - NEAR - NEAR * a, 2)
        block = jnp.where(lane < LANES // 2, own_ref[a], 0.0)
        block = jnp.where((lane >= LANES // 2) & (lane < LANES // 2 + NEAR), right, block)
        ring[a] = jnp.where(lane >= LANES - NEAR, left, block)
    odd = where_ref[0] % 2
    for k, send in enumerate(sends):
        start = (1 - odd if k == 0 else odd) * (bx - NEAR)
        for a in range(n):
            send[a] = ring[a, pl.ds(start, NEAR)]


def near_y_kernel(counts, where_ref, ring, *refs):
    halos, sends = refs[:-2], refs[-2:]
    n, bx, by, _ = ring.shape
    odd_x, odd = where_ref[0] % 2, where_ref[1] % 2
    for a in range(n):
        below, above = neighbours(counts[0], odd_x, halos[0][a], halos[-1][a])
        block = jnp.concatenate([below, ring[a], above], axis=0)
        head, tail = block[:, :NEAR], block[:, by - NEAR:]
        sends[0][a] = pick(odd, head, tail)
        sends[1][a] = pick(odd, tail, head)


def halve(values, factor, odd_axis):
    x, y, z = values.shape
    if odd_axis == 0:
        values = jnp.concatenate([values[2 * i + 1:2 * i + 2] for i in range(x // 2)], axis=0)
    else:
        values = jnp.concatenate(
            [values[2 * i:2 * i + 1] + values[2 * i + 1:2 * i + 2] for i in range(x // 2)], axis=0
        )
    to_y = max(8, y // 2)
    to_z = max(LANES, z // 2)
    flat = values.reshape(x // 2 * y, z)
    flat = times_table(flat, pair_table(z, to_z, odd_axis == 2))
    row = iota2((to_y, y), 0)
    col = iota2((to_y, y), 1)
    table = (col == 2 * row + 1) if odd_axis == 1 else (col // 2 == row)
    table = table.astype(F32)
    blocks = [table_times(table, flat[i * y:(i + 1) * y])[None] for i in range(x // 2)]
    return factor * jnp.concatenate(blocks, axis=0)


def double(values, shape):
    x, y, z = values.shape
    to_x, to_y, to_z = shape
    row = iota2((to_y, y), 0)
    col = iota2((to_y, y), 1)
    table_y = (row // 2 == col).astype(F32)
    row = iota2((z, to_z), 0)
    col = iota2((z, to_z), 1)
    table_z = (col // 2 == row).astype(F32)
    blocks = [table_times(table_y, values[i])[None] for i in range(x)]
    flat = jnp.concatenate(blocks, axis=0).reshape(x * to_y, z)
    flat = times_table(flat, table_z).reshape(x, to_y, to_z)
    return jnp.concatenate([flat[i // 2:i // 2 + 1] for i in range(to_x)], axis=0)


def coupled_faces(faces, y, z):
    bx, by, bz = faces
    row = lax.broadcasted_iota(jnp.int32, by.shape, 1)
    return bx, jnp.where(row == y - 1, 0.0, by), jnp.where(lane_of(bz.shape) == z - 1, 0.0, bz)


def coarse_cycle(level, rhs, mass, faces, y, z):
    coupled = coupled_faces(faces, y, z)
    diag = diagonal(mass, faces, coupled)
    weight = relaxer(mass, diag)
    field = weight * rhs
    if level == LEVELS - 1:
        for _ in range(BOTTOM - 1):
            field = sweep(field, rhs, weight, coupled)
        return field
    for _ in range(SWEEPS - 1):
        field = sweep(field, rhs, weight, coupled)
    remain = rhs - diag * field + pull(field, coupled)
    correction = coarse_cycle(
        level + 1,
        halve(remain, 0.125, -1),
        halve(mass, 0.125, -1),
        tuple(halve(face, 0.0625, axis) for axis, face in enumerate(faces)),
        y // 2,
        z // 2,
    )
    field = field + double(correction, field.shape)
    for _ in range(SWEEPS):
        field = sweep(field, rhs, weight, coupled)
    return field


def up_kernel(counts, where_ref, gathered, ring, *refs):
    n_x = 1 if counts[0] == 2 else 2
    halos_x = refs[:n_x]
    one_y, two_y, kept, weight_ref, faces_ref = refs[n_x:n_x + 5]
    out = refs[n_x + 5]
    whole, second, field, halfway, spread = refs[n_x + 6:]
    odd_x, odd_y = where_ref[0] % 2, where_ref[1] % 2
    gx, gy, gz = counts
    n, bx1, by1, _ = ring.shape
    x2, y2, z2 = bx1 // 2, by1 // 2, LANES // 4
    columns = max(LANES, gz * z2)
    lane = lane_of((y2, LANES))

    for a in range(n):
        for i in range(gx):
            for j in range(gy):
                for x in range(x2):
                    for part in range(columns // LANES):
                        total = jnp.zeros((y2, LANES), F32)
                        for k in range(LANES // z2):
                            column = part * (LANES // z2) + k
                            if column < gz:
                                block = gathered[(i * gy + j) * gz + column, a]
                                mask = (lane >= k * z2) & (lane < (k + 1) * z2)
                                total = jnp.where(mask, turn(block, (k - x) * z2, 1), total)
                        whole[
                            a, i * x2 + x, j * y2:(j + 1) * y2, part * LANES:(part + 1) * LANES
                        ] = total
    correction = coarse_cycle(
        2, whole[0], whole[1], (whole[2], whole[3], whole[4]), gy * y2, gz * z2
    )

    wide = gx * x2
    half = NEAR // 2
    ex1, ey1 = bx1 + 2 * NEAR, by1 + 2 * NEAR
    second[:half] = jnp.zeros((half,) + correction.shape[1:], F32)
    second[half:half + wide] = correction
    second[half + wide:] = jnp.zeros((half,) + correction.shape[1:], F32)
    window = second[pl.ds(where_ref[0] * x2, x2 + NEAR)]
    rows = correction.shape[1]
    row = iota2((ey1, rows), 0)
    col = iota2((ey1, rows), 1)
    table_y = (col == where_ref[1] * y2 + (row // 2 - half)).astype(F32)
    row = iota2((columns, LANES), 0)
    col = iota2((columns, LANES), 1)
    place = jnp.where(col < LANES * 3 // 4, col, col - LANES)
    table_z = (row == where_ref[2] * z2 + lax.shift_right_arithmetic(place, 1)).astype(F32)
    flat = times_table(window.reshape((x2 + NEAR) * rows, columns), table_z)
    blocks = [table_times(table_y, flat[i * rows:(i + 1) * rows])[None] for i in range(x2 + NEAR)]
    lifted = jnp.concatenate([blocks[i // 2] for i in range(ex1)], axis=0)

    level1 = []
    for a in range(n):
        below, above = neighbours(gx, odd_x, halos_x[0][a], halos_x[-1][a])
        block = jnp.concatenate([below, ring[a], above], axis=0)
        below, above = neighbours(gy, odd_y, one_y[a], two_y[a])
        level1.append(jnp.concatenate([below, block, above], axis=1))
    rhs1, weight1 = level1[:2]
    faces1 = tuple(level1[2:])
    field1 = weight1 * rhs1
    field1 = sweep(field1, rhs1, weight1, faces1)
    field1 = field1 + jnp.where(weight1 > 0.0, lifted, 0.0)
    for _ in range(SWEEPS):
        field1 = sweep(field1, rhs1, weight1, faces1)

    sx, sy, sz = out.shape
    ex, ey = sx + 4, sy + 2 * SIDE
    near = field1[NEAR - 1:NEAR + bx1 + 1].reshape((bx1 + 2) * ey1, LANES)
    row = iota2((LANES, 2 * LANES), 0)
    col = iota2((LANES, 2 * LANES), 1)
    lifted = times_table(near, (col // 2 == row).astype(F32))
    for k in range(2):
        block = lifted[:, k * LANES:(k + 1) * LANES].reshape(bx1 + 2, ey1, LANES)
        for i in range(bx1 + 2):
            for q in range(2):
                spread[k, i, pl.ds(q, ey1, stride=2), :] = block[i]
    for x in range(ex):
        for k in range(2):
            field[k, x] = kept[k, x] + spread[k, x // 2]

    lane = lane_of((ey, LANES))
    rhs, bx, by, bz = ([faces_ref.at[a, k] for k in range(2)] for a in range(4))
    before = [field.at[k] for k in range(2)]
    after = [halfway.at[k] for k in range(2)]

    def sweep_out(x, carry):
        centre, around = pull_slab(before, bx, by, bz, x, lane)
        for k in range(2):
            after[k][x] = KEEP * centre[k] + weight_ref[k, x] * (rhs[k][x] + around[k])
        return carry

    lax.fori_loop(1, ex - 1, sweep_out, 0)

    def sweep_own(x, carry):
        centre, around = pull_slab(after, bx, by, bz, x, lane)
        value = KEEP * centre[0] + weight_ref[0, x] * (rhs[0][x] + around[0])
        out[x - 2] = value[SIDE:SIDE + sy]
        return carry

    lax.fori_loop(2, ex - 2, sweep_own, 0)


def run(kernel, outs, where, arrays, scratch=()):
    return pl.pallas_call(
        kernel,
        out_shape=tuple(jax.ShapeDtypeStruct(shape, F32) for shape in outs),
        in_specs=[SM] + [VM] * len(arrays),
        out_specs=tuple(VM for _ in outs),
        scratch_shapes=[pltpu.VMEM(shape, F32) for shape in scratch],
        compiler_params=pltpu.CompilerParams(vmem_limit_bytes=56 * 1024 * 1024),
    )(where, *arrays)


def swaps(axis, sends):
    count = lax.axis_size(axis)
    got = []
    for k, block in enumerate(sends):
        pairs = [(i, i + 1) for i in range(k, count - 1, 2)]
        pairs = [pair for low, high in pairs for pair in ((low, high), (high, low))]
        got.append(lax.ppermute(block, axis, pairs))
    return got


def local(initial, right_side, alpha, beta_x, beta_y, beta_z):
    axes = ("gx", "gy", "gz")
    counts = tuple(lax.axis_size(axis) for axis in axes)
    devices = counts[0] * counts[1] * counts[2]
    where = jnp.stack([lax.axis_index(axis) for axis in axes]).astype(jnp.int32)
    ins = (initial, right_side, alpha, beta_x, beta_y, beta_z)
    sx, sy, sz = initial.shape
    n_x = 1 if counts[0] == 2 else 2
    ex, ey = sx + 2 * WIDE, sy + 2 * SIDE
    sends = run(pack_z_kernel, [(sx // 2, sy, LANES)] * 2, where, ins)
    got = swaps("gz", sends)
    zpack, *sends = run(
        functools.partial(face_x_kernel, counts),
        [(sx, sy, LANES)] + [(7, WIDE, sy, LANES)] * n_x,
        where,
        ins + tuple(got),
    )
    ins = ins + (zpack,)
    got_x = swaps("gx", sends)
    sends = run(
        functools.partial(face_y_kernel, counts),
        [(7, ex, SIDE, LANES)] * 2,
        where,
        ins + tuple(got_x),
    )
    got_y = swaps("gy", sends)
    x1, y1 = sx // 2, sy // 2
    copies, own1, first1, second1, kept, weight, faces = run(
        functools.partial(down_kernel, counts, devices),
        [
            (devices, 5, y1 // 2, LANES),
            (5, x1, y1, LANES),
            (x1, y1, LANES),
            (x1, y1, LANES),
            (2, sx + 4, ey, LANES),
            (2, sx + 4, ey, LANES),
            (4, 2, sx + 4, ey, LANES),
        ],
        where,
        ins + tuple(got_x) + tuple(got_y),
        [
            (7, 2, ex, ey, LANES),
            (2, ex, ey, LANES),
            (2, 2, ex, ey, LANES),
            (5, x1 + 6, ey // 2, 2 * LANES),
            (5, x1, ey // 2, LANES),
        ],
    )
    gathered = lax.all_to_all(copies, axes, 0, 0, tiled=True)
    got = swaps("gz", (first1, second1))
    ring, *sends = run(
        functools.partial(near_x_kernel, counts),
        [(5, x1, y1, LANES)] + [(5, NEAR, y1, LANES)] * n_x,
        where,
        (own1,) + tuple(got),
    )
    near_x = swaps("gx", sends)
    sends = run(
        functools.partial(near_y_kernel, counts),
        [(5, x1 + 2 * NEAR, NEAR, LANES)] * 2,
        where,
        (ring,) + tuple(near_x),
    )
    near_y = swaps("gy", sends)
    wide, rows = counts[0] * x1 // 2, counts[1] * y1 // 2
    columns = max(LANES, counts[2] * sz // 4)
    (result,) = run(
        functools.partial(up_kernel, counts),
        [(sx, sy, sz)],
        where,
        (gathered, ring) + tuple(near_x) + tuple(near_y) + (kept, weight, faces),
        [
            (5, wide, rows, columns),
            (wide + NEAR, rows, columns),
            (2, sx + 4, ey, LANES),
            (2, sx + 4, ey, LANES),
            (2, x1 + 2, ey, LANES),
        ],
    )
    return result


def solution(mesh):
    spec = P("gx", "gy", "gz")
    return jax.shard_map(
        local, mesh=mesh, in_specs=(spec,) * 6, out_specs=spec, check_vma=False
    )
```

```python
import functools

import jax
import jax.numpy as jnp
from jax import lax
from jax.experimental import pallas as pl
from jax.experimental.pallas import tpu as pltpu
from jax.sharding import PartitionSpec as P

LEVELS = 6
SWEEPS = 2
BOTTOM = 8
WEIGHT = 0.25 ** (LEVELS - 1)
RELAX = 2.0 / 3.0
KEEP = 1.0 / 3.0

HALO = 4
NEAR = 4
LANES = 128

VM = pl.BlockSpec(memory_space=pltpu.VMEM)
SM = pl.BlockSpec(memory_space=pltpu.SMEM)
F32 = jnp.float32


def lane_of(shape):
    return lax.broadcasted_iota(jnp.int32, shape, len(shape) - 1)


def pick(flag, yes, no):
    return jnp.where(jnp.full(yes.shape, flag, jnp.int32) == 1, yes, no)


def neighbours(axis_size, odd, one, two):
    if axis_size == 2:
        two = jnp.zeros_like(one)
    return pick(odd, one, two), pick(odd, two, one)


def turn(values, shift, axis):
    return pltpu.roll(values, shift % values.shape[axis], axis)


def parts_of(values):
    high = values.astype(jnp.bfloat16)
    rest = values - high.astype(F32)
    middle = rest.astype(jnp.bfloat16)
    low = (rest - middle.astype(F32)).astype(jnp.bfloat16)
    return high, middle, low


def times_table(values, table):
    table = table.astype(jnp.bfloat16)
    total = None
    for part in reversed(parts_of(values)):
        term = jnp.dot(part, table, preferred_element_type=F32)
        total = term if total is None else total + term
    return total


def table_times(table, values):
    table = table.astype(jnp.bfloat16)
    total = None
    for part in reversed(parts_of(values)):
        term = jnp.dot(table, part, preferred_element_type=F32)
        total = term if total is None else total + term
    return total


def iota2(shape, axis):
    return lax.broadcasted_iota(jnp.int32, shape, axis)


def pair_table(rows, cols, odd):
    row = iota2((rows, cols), 0)
    col = iota2((rows, cols), 1)
    hit = (row == 2 * col + 1) if odd else (row // 2 == col)
    return hit.astype(F32)


def below_x(values):
    if values.shape[0] == 1:
        return jnp.zeros_like(values)
    return jnp.concatenate([jnp.zeros_like(values[:1]), values[:-1]], axis=0)


def above_x(values):
    if values.shape[0] == 1:
        return jnp.zeros_like(values)
    return jnp.concatenate([values[1:], jnp.zeros_like(values[:1])], axis=0)


def pull(values, faces):
    bx, by, bz = faces
    total = bx * above_x(values) + below_x(bx * values)
    total = total + (by * turn(values, -1, 1) + turn(by * values, 1, 1))
    return total + (bz * turn(values, -1, 2) + turn(bz * values, 1, 2))


def diagonal(mass, faces, coupled):
    bx, by, bz = faces
    _, cy, cz = coupled
    return mass + bx + below_x(bx) + by + turn(cy, 1, 1) + bz + turn(cz, 1, 2)


def relaxer(mass, diag):
    inside = mass > 0.0
    return jnp.where(inside, RELAX / jnp.where(inside, diag, 1.0), 0.0)


def sweep(values, rhs, weight, faces):
    return KEEP * values + weight * (rhs + pull(values, faces))


def pack_z_kernel(where_ref, *refs):
    ins, (first, second) = refs[:6], refs[6:]
    odd = where_ref[2] % 2
    sx, sy, sz = ins[0].shape
    half = sx // 2
    lane = lane_of((half, sy, LANES))
    head = jnp.zeros((half, sy, LANES), F32)
    tail = head
    for a, ref in enumerate(ins):
        for g in range(2):
            block = ref[g * half:(g + 1) * half]
            at = 64 * g + HALO * a
            mask = (lane >= at) & (lane < at + HALO)
            head = jnp.where(mask, turn(block, at, 2), head)
            tail = jnp.where(mask, turn(block, at + HALO, 2), tail)
    first[...] = pick(odd, head, tail)
    second[...] = pick(odd, tail, head)


def face_x_kernel(counts, where_ref, *refs):
    ins, one_ref, two_ref = refs[:6], refs[6], refs[7]
    zpack, sends = refs[8], refs[9:]
    sx, sy, sz = ins[0].shape
    half = sx // 2
    below, above = neighbours(counts[2], where_ref[2] % 2, one_ref[...], two_ref[...])
    lane = lane_of(below.shape)
    zpack[:half] = jnp.where(lane < 64, above, turn(below, 64, 2))
    zpack[half:] = jnp.where(lane < 64, turn(above, 64, 2), below)
    odd = where_ref[0] % 2
    for k, send in enumerate(sends):
        start = (1 - odd if k == 0 else odd) * (sx - HALO)
        for a, ref in enumerate(tuple(ins) + (zpack,)):
            send[a] = ref[pl.ds(start, HALO)]


def face_y_kernel(counts, where_ref, *refs):
    ins, halos, sends = refs[:7], refs[7:-2], refs[-2:]
    sx, sy, sz = ins[0].shape
    odd_x = where_ref[0] % 2
    odd = where_ref[1] % 2
    for a, ref in enumerate(ins):
        below, above = neighbours(counts[0], odd_x, halos[0][a], halos[-1][a])
        for at, block in ((0, below), (HALO, ref[...]), (HALO + sx, above)):
            head, tail = block[:, :HALO], block[:, sy - HALO:]
            span = slice(at, at + block.shape[0])
            sends[0][a, span] = pick(odd, head, tail)
            sends[1][a, span] = pick(odd, tail, head)


def each(first, last, step, body):
    rounds = (last - first) // step

    def go(i, carry):
        for j in range(step):
            body(first + i * step + j)
        return carry

    if rounds:
        lax.fori_loop(0, rounds, go, 0)
    for x in range(first + rounds * step, last):
        body(x)


def ring_up(main, halo, lane):
    main_up, halo_up = turn(main, -1, 1), turn(halo, -1, 1)
    last = lane == LANES - 1
    return jnp.where(last, halo_up, main_up), jnp.where(last, main_up, halo_up)


def ring_down(main, halo, lane):
    main_down, halo_down = turn(main, 1, 1), turn(halo, 1, 1)
    zero = lane == 0
    return jnp.where(zero, halo_down, main_down), jnp.where(zero, main_down, halo_down)


def pull_slab(field, bx, by, bz, x, lane):
    centre = [half[x] for half in field]
    out = []
    for k in range(2):
        c, face = centre[k], by[k][x]
        t = bx[k][x] * field[k][x + 1] + bx[k][x - 1] * field[k][x - 1]
        out.append(t + (face * turn(c, -1, 0) + turn(face * c, 1, 0)))
    faces = [half[x] for half in bz]
    ups = ring_up(centre[0], centre[1], lane)
    downs = ring_down(faces[0] * centre[0], faces[1] * centre[1], lane)
    return centre, [out[k] + (faces[k] * ups[k] + downs[k]) for k in range(2)]


def down_kernel(counts, where_ref, *refs):
    ins = refs[:7]
    n_x = 1 if counts[0] == 2 else 2
    halos_x = refs[7:7 + n_x]
    one_y, two_y = refs[7 + n_x:9 + n_x]
    own1, first1, second1, coarse2, kept_m, kept_h, weight_m, weight_h = refs[9 + n_x:17 + n_x]
    faces_out, scratch = refs[17 + n_x:25 + n_x], refs[25 + n_x:]
    mains, halves = scratch[:7], scratch[7:13]
    half_m, half_h, diag, sums, left = scratch[13:]
    sx, sy, sz = ins[0].shape
    ex, ey = sx + 2 * HALO, sy + 2 * HALO
    odd_x, odd_y, odd_z = where_ref[0] % 2, where_ref[1] % 2, where_ref[2] % 2

    for a in range(7):
        to = mains[a]
        below, above = neighbours(counts[0], odd_x, halos_x[0][a], halos_x[-1][a])
        to[:HALO, :sy] = below
        to[HALO:HALO + sx, :sy] = ins[a][...]
        to[HALO + sx:, :sy] = above
        below, above = neighbours(counts[1], odd_y, one_y[a], two_y[a])
        to[:, sy:] = jnp.concatenate([above, below], axis=1)
    lane = lane_of((ey, LANES))

    def unpack(x):
        packed = mains[6][x]
        for a in range(6):
            right = turn(packed, -HALO * a, 1)
            other_side = turn(packed, 64 - HALO - HALO * a, 1)
            halves[a][x] = jnp.where(
                lane < HALO, right, jnp.where(lane >= LANES - HALO, other_side, 0.0)
            )

    each(0, ex, 4, unpack)
    field, rhs, alpha, bx, by, bz = zip(mains[:6], halves)
    halfway, weight, kept = (half_m, half_h), (weight_m, weight_h), (kept_m, kept_h)

    def first_sweep(x):
        faces = [half[x] for half in bz]
        downs = ring_down(faces[0], faces[1], lane)
        centre, near = pull_slab(field, bx, by, bz, x, lane)
        for k in range(2):
            face = by[k][x]
            mass = WEIGHT * alpha[k][x]
            d = mass + bx[k][x] + bx[k][x - 1] + face + turn(face, 1, 0) + faces[k] + downs[k]
            w = relaxer(mass, d)
            if k == 0:
                diag[x] = d
            weight[k][x] = w
            halfway[k][x] = KEEP * centre[k] + w * (rhs[k][x] + near[k])

    each(1, ex - 1, 4, first_sweep)

    def second_sweep(x):
        centre, near = pull_slab(halfway, bx, by, bz, x, lane)
        for k in range(2):
            kept[k][x] = KEEP * centre[k] + weight[k][x] * (rhs[k][x] + near[k])

    each(2, ex - 2, 4, second_sweep)

    def residual(x):
        centre, near = pull_slab(kept, bx, by, bz, x, lane)
        half_m[x] = rhs[0][x] - diag[x] * centre[0] + near[0]

    each(HALO, ex - HALO, 4, residual)
    for n, source in enumerate((rhs, bx, by, bz)):
        for k in range(2):
            faces_out[2 * n + k][...] = source[k][...]

    x1, y1, z1 = sx // 2, sy // 2, sz // 2

    def rows_of(source, x, firsts, seconds):
        total = None
        for p in firsts:
            for q in seconds:
                term = source[x + p, pl.ds(q, y1, stride=2), :]
                total = term if total is None else total + term
        return total

    both, last = (0, 1), (1,)
    for i in range(x1):
        x = HALO + 2 * i
        sums[0, i] = rows_of(half_m, x, both, both)
        sums[1, i] = rows_of(alpha[0], x, both, both)
        sums[2, i] = rows_of(bx[0], x, last, both)
        sums[3, i] = rows_of(by[0], x, both, last)
        left[...] = turn(by[0][x] + by[0][x + 1], 1, 0)
        sums[4, i] = left[pl.ds(0, y1, stride=2), :]
        sums[5, i] = rows_of(bz[0], x, both, both)
    sums[6, 0] = rows_of(bx[0], HALO - 2, last, both)
    edge_z = [rows_of(bz[1], HALO + 2 * i, both, both)[None] for i in range(x1)]
    edge_z = 0.0625 * jnp.concatenate(edge_z, axis=0)
    pairs = pair_table(LANES, LANES, False)
    odds = pair_table(LANES, LANES, True)

    def to_level1(first, count, table, factor):
        flat = sums[first:first + count].reshape(count * x1 * y1, LANES)
        return factor * times_table(flat, table).reshape(count, x1, y1, LANES)

    paired = to_level1(0, 5, pairs, 0.0625)
    rhs1, mass1 = 2.0 * paired[0], (2.0 * WEIGHT) * paired[1]
    faces1 = (paired[2], paired[3], to_level1(5, 1, odds, 0.0625)[0])
    edge_x = 0.0625 * times_table(sums[6, 0], pairs)[None]
    lane1 = lane_of((x1, y1, LANES))
    diag1 = mass1 + faces1[0] + jnp.concatenate([edge_x, faces1[0][:-1]], axis=0)
    diag1 = diag1 + faces1[1] + paired[4]
    diag1 = diag1 + faces1[2] + jnp.where(lane1 == 0, turn(edge_z, 1, 2), turn(faces1[2], 1, 2))
    inside = lane1 < z1
    weight1 = jnp.where(inside, RELAX / jnp.where(inside, diag1, 1.0), 0.0)

    head = jnp.zeros((x1, y1, LANES), F32)
    tail = head
    for n, values in enumerate((rhs1, weight1) + faces1):
        block = jnp.where(inside, values, 0.0)
        own1[n] = block
        at = NEAR * n
        mask = (lane1 >= at) & (lane1 < at + NEAR)
        head = jnp.where(mask, turn(block, at, 2), head)
        tail = jnp.where(mask, turn(block, at + NEAR - z1, 2), tail)
    first1[...] = pick(odd_z, head, tail)
    second1[...] = pick(odd_z, tail, head)

    parts = (
        (mass1, False, False, False, 0.125),
        (faces1[0], True, False, False, 0.0625),
        (faces1[1], False, True, False, 0.0625),
        (faces1[2], False, False, True, 0.0625),
    )
    for n, (values, *odd_axes, factor) in enumerate(parts):
        sums[n] = values
        coarse2[n] = level2_rows(sums.at[n], odd_axes, factor, x1 // 2, y1 // 2, z1 // 2)


def level2_rows(source, odd_axes, factor, x2, y2, z2):
    rows = []
    for i in range(x2):
        total = None
        for p in (1,) if odd_axes[0] else (0, 1):
            for q in (1,) if odd_axes[1] else (0, 1):
                term = source[2 * i + p, pl.ds(q, y2, stride=2), :]
                total = term if total is None else total + term
        rows.append(total)
    flat = jnp.concatenate(rows, axis=0)
    flat = factor * times_table(flat, pair_table(LANES, LANES, odd_axes[2]))
    lane = lane_of((y2, LANES))
    packed = jnp.zeros((y2, LANES), F32)
    for i in range(x2):
        mask = (lane >= i * z2) & (lane < (i + 1) * z2)
        packed = jnp.where(mask, turn(flat[i * y2:(i + 1) * y2], i * z2, 1), packed)
    return packed


def near_x_kernel(counts, where_ref, own_ref, one_ref, two_ref, ring, *sends):
    n, bx, by, _ = own_ref.shape
    below, above = neighbours(counts[2], where_ref[2] % 2, one_ref[...], two_ref[...])
    lane = lane_of(below.shape)
    for a in range(n):
        right = turn(above, LANES // 2 - NEAR * a, 2)
        left = turn(below, LANES - NEAR - NEAR * a, 2)
        block = jnp.where(lane < LANES // 2, own_ref[a], 0.0)
        block = jnp.where((lane >= LANES // 2) & (lane < LANES // 2 + NEAR), right, block)
        ring[a] = jnp.where(lane >= LANES - NEAR, left, block)
    odd = where_ref[0] % 2
    for k, send in enumerate(sends):
        start = (1 - odd if k == 0 else odd) * (bx - NEAR)
        for a in range(n):
            send[a] = ring[a, pl.ds(start, NEAR)]


def near_y_kernel(counts, where_ref, ring, *refs):
    halos, sends = refs[:-2], refs[-2:]
    n, bx, by, _ = ring.shape
    odd_x, odd = where_ref[0] % 2, where_ref[1] % 2
    for a in range(n):
        below, above = neighbours(counts[0], odd_x, halos[0][a], halos[-1][a])
        block = jnp.concatenate([below, ring[a], above], axis=0)
        head, tail = block[:, :NEAR], block[:, by - NEAR:]
        sends[0][a] = pick(odd, head, tail)
        sends[1][a] = pick(odd, tail, head)


def near_kernel(counts, devices, where_ref, ring, *refs):
    n_x = 1 if counts[0] == 2 else 2
    halos_x = refs[:n_x]
    one_y, two_y, coarse2, copies, level1, left = refs[n_x:]
    n, bx1, by1, _ = ring.shape
    odd_x, odd_y = where_ref[0] % 2, where_ref[1] % 2
    whole = []
    for a in range(n):
        below, above = neighbours(counts[0], odd_x, halos_x[0][a], halos_x[-1][a])
        block = jnp.concatenate([below, ring[a], above], axis=0)
        below, above = neighbours(counts[1], odd_y, one_y[a], two_y[a])
        whole.append(jnp.concatenate([block, above, below], axis=1))
    rhs1, weight1 = whole[:2]
    faces1 = tuple(whole[2:])
    field1 = weight1 * rhs1
    field1 = sweep(field1, rhs1, weight1, faces1)
    for a, values in enumerate([field1] + whole):
        level1[a] = values
    mine = slice(NEAR, NEAR + bx1)
    inner = weight1[mine]
    diag1 = RELAX / jnp.where(inner > 0.0, inner, 1.0)
    remain = rhs1[mine] - diag1 * field1[mine] + pull(field1, faces1)[mine]
    left[...] = remain
    packed = level2_rows(left, (False,) * 3, 0.125, bx1 // 2, by1 // 2, LANES // 4)
    for d in range(devices):
        copies[d, 0] = packed
        for a in range(n - 1):
            copies[d, a + 1] = coarse2[a]


def halve(values, factor, odd_axis):
    x, y, z = values.shape
    if odd_axis == 0:
        values = jnp.concatenate([values[2 * i + 1:2 * i + 2] for i in range(x // 2)], axis=0)
    else:
        values = jnp.concatenate(
            [values[2 * i:2 * i + 1] + values[2 * i + 1:2 * i + 2] for i in range(x // 2)], axis=0
        )
    to_y = max(8, y // 2)
    to_z = max(LANES, z // 2)
    flat = values.reshape(x // 2 * y, z)
    flat = times_table(flat, pair_table(z, to_z, odd_axis == 2))
    row = iota2((to_y, y), 0)
    col = iota2((to_y, y), 1)
    table = (col == 2 * row + 1) if odd_axis == 1 else (col // 2 == row)
    table = table.astype(F32)
    blocks = [table_times(table, flat[i * y:(i + 1) * y])[None] for i in range(x // 2)]
    return factor * jnp.concatenate(blocks, axis=0)


def double(values, shape):
    x, y, z = values.shape
    to_x, to_y, to_z = shape
    row = iota2((to_y, y), 0)
    col = iota2((to_y, y), 1)
    table_y = (row // 2 == col).astype(F32)
    row = iota2((z, to_z), 0)
    col = iota2((z, to_z), 1)
    table_z = (col // 2 == row).astype(F32)
    blocks = [table_times(table_y, values[i])[None] for i in range(x)]
    flat = jnp.concatenate(blocks, axis=0).reshape(x * to_y, z)
    flat = times_table(flat, table_z).reshape(x, to_y, to_z)
    return jnp.concatenate([flat[i // 2:i // 2 + 1] for i in range(to_x)], axis=0)


def coupled_faces(faces, y, z):
    bx, by, bz = faces
    row = lax.broadcasted_iota(jnp.int32, by.shape, 1)
    return bx, jnp.where(row == y - 1, 0.0, by), jnp.where(lane_of(bz.shape) == z - 1, 0.0, bz)


def coarse_cycle(level, rhs, mass, faces, y, z):
    coupled = coupled_faces(faces, y, z)
    diag = diagonal(mass, faces, coupled)
    weight = relaxer(mass, diag)
    field = weight * rhs
    if level == LEVELS - 1:
        for _ in range(BOTTOM - 1):
            field = sweep(field, rhs, weight, coupled)
        return field
    for _ in range(SWEEPS - 1):
        field = sweep(field, rhs, weight, coupled)
    remain = rhs - diag * field + pull(field, coupled)
    correction = coarse_cycle(
        level + 1,
        halve(remain, 0.125, -1),
        halve(mass, 0.125, -1),
        tuple(halve(face, 0.0625, axis) for axis, face in enumerate(faces)),
        y // 2,
        z // 2,
    )
    field = field + double(correction, field.shape)
    for _ in range(SWEEPS):
        field = sweep(field, rhs, weight, coupled)
    return field


def up_kernel(counts, where_ref, gathered, level1, *refs):
    kept, weight, rhs, bx, by, bz = zip(refs[0:12:2], refs[1:12:2])
    out, whole, second, spread_m, spread_h, field_m, field_h, half_m, half_h = refs[12:]
    gx, gy, gz = counts
    sx, sy, sz = out.shape
    x1, y1 = sx // 2, sy // 2
    x2, y2, z2 = x1 // 2, y1 // 2, sz // 4
    columns = max(LANES, gz * z2)
    lane = lane_of((y2, LANES))

    for a in range(5):
        for i in range(gx):
            for j in range(gy):
                for x in range(x2):
                    for part in range(columns // LANES):
                        total = jnp.zeros((y2, LANES), F32)
                        for k in range(LANES // z2):
                            column = part * (LANES // z2) + k
                            if column < gz:
                                block = gathered[(i * gy + j) * gz + column, a]
                                mask = (lane >= k * z2) & (lane < (k + 1) * z2)
                                total = jnp.where(mask, turn(block, (k - x) * z2, 1), total)
                        whole[
                            a, i * x2 + x, j * y2:(j + 1) * y2, part * LANES:(part + 1) * LANES
                        ] = total
    correction = coarse_cycle(
        2, whole[0], whole[1], (whole[2], whole[3], whole[4]), gy * y2, gz * z2
    )

    wide = gx * x2
    half = NEAR // 2
    ex1, ey1 = x1 + 2 * NEAR, y1 + 2 * NEAR
    second[:half] = jnp.zeros((half,) + correction.shape[1:], F32)
    second[half:half + wide] = correction
    second[half + wide:] = jnp.zeros((half,) + correction.shape[1:], F32)
    window = second[pl.ds(where_ref[0] * x2, x2 + NEAR)]
    rows = correction.shape[1]
    row = iota2((ey1, rows), 0)
    col = iota2((ey1, rows), 1)
    place = jnp.where(row < y1 + NEAR, row, row - ey1)
    table_y = (col == where_ref[1] * y2 + lax.shift_right_arithmetic(place, 1)).astype(F32)
    row = iota2((columns, LANES), 0)
    col = iota2((columns, LANES), 1)
    place = jnp.where(col < LANES * 3 // 4, col, col - LANES)
    table_z = (row == where_ref[2] * z2 + lax.shift_right_arithmetic(place, 1)).astype(F32)
    flat = times_table(window.reshape((x2 + NEAR) * rows, columns), table_z)
    blocks = [table_times(table_y, flat[i * rows:(i + 1) * rows])[None] for i in range(x2 + NEAR)]
    lifted = jnp.concatenate([blocks[i // 2] for i in range(ex1)], axis=0)
    field1, rhs1, weight1 = level1[0], level1[1], level1[2]
    faces1 = (level1[3], level1[4], level1[5])
    field1 = field1 + jnp.where(weight1 > 0.0, lifted, 0.0)
    for _ in range(SWEEPS):
        field1 = sweep(field1, rhs1, weight1, faces1)

    ex, ey = sx + 2 * HALO, sy + 2 * HALO
    near = field1[NEAR - 1:NEAR + x1 + 1].reshape((x1 + 2) * ey1, LANES)
    row = iota2((LANES, 2 * LANES), 0)
    col = iota2((LANES, 2 * LANES), 1)
    lifted = times_table(near, (col // 2 == row).astype(F32))
    quarter = NEAR // 2
    for k, spread in enumerate((spread_m, spread_h)):
        block = lifted[:, k * LANES:(k + 1) * LANES].reshape(x1 + 2, ey1, LANES)
        for i in range(x1 + 2):
            for q in range(2):
                spread[i, pl.ds(q, y1, stride=2), :] = block[i, :y1]
                spread[i, pl.ds(sy + q, quarter, stride=2), :] = block[i, y1:y1 + quarter]
                spread[i, pl.ds(sy + HALO + q, quarter, stride=2), :] = block[i, ey1 - quarter:]
    before, after = (field_m, field_h), (half_m, half_h)
    first = HALO - 2
    for x in range(first, ex - first):
        for k, spread in enumerate((spread_m, spread_h)):
            before[k][x] = kept[k][x] + spread[(x - first) // 2]

    lane = lane_of((ey, LANES))

    def sweep_out(x):
        centre, around = pull_slab(before, bx, by, bz, x, lane)
        for k in range(2):
            after[k][x] = KEEP * centre[k] + weight[k][x] * (rhs[k][x] + around[k])

    each(first + 1, ex - first - 1, 4, sweep_out)

    def sweep_own(x):
        centre, around = pull_slab(after, bx, by, bz, x, lane)
        value = KEEP * centre[0] + weight[0][x] * (rhs[0][x] + around[0])
        out[x - HALO] = value[:sy]

    each(HALO, ex - HALO, 4, sweep_own)


def run(kernel, outs, where, arrays, scratch=(), grant=16):
    return pl.pallas_call(
        kernel,
        out_shape=tuple(jax.ShapeDtypeStruct(shape, F32) for shape in outs),
        in_specs=[SM] + [VM] * len(arrays),
        out_specs=tuple(VM for _ in outs),
        scratch_shapes=[pltpu.VMEM(shape, F32) for shape in scratch],
        compiler_params=pltpu.CompilerParams(vmem_limit_bytes=grant * 1024 * 1024),
    )(where, *arrays)


def swaps(axis, sends):
    count = lax.axis_size(axis)
    got = []
    for k, block in enumerate(sends):
        pairs = [(i, i + 1) for i in range(k, count - 1, 2)]
        pairs = [pair for low, high in pairs for pair in ((low, high), (high, low))]
        got.append(lax.ppermute(block, axis, pairs))
    return got


def local(initial, right_side, alpha, beta_x, beta_y, beta_z):
    axes = ("gx", "gy", "gz")
    counts = tuple(lax.axis_size(axis) for axis in axes)
    devices = counts[0] * counts[1] * counts[2]
    where = jnp.stack([lax.axis_index(axis) for axis in axes]).astype(jnp.int32)
    ins = (initial, right_side, alpha, beta_x, beta_y, beta_z)
    sx, sy, sz = initial.shape
    n_x = 1 if counts[0] == 2 else 2
    ex, ey = sx + 2 * HALO, sy + 2 * HALO
    fine = (ex, ey, LANES)

    sends = run(pack_z_kernel, [(sx // 2, sy, LANES)] * 2, where, ins)
    got = swaps("gz", sends)
    zpack, *sends = run(
        functools.partial(face_x_kernel, counts),
        [(sx, sy, LANES)] + [(7, HALO, sy, LANES)] * n_x,
        where,
        ins + tuple(got),
    )
    ins = ins + (zpack,)
    got_x = swaps("gx", sends)
    sends = run(
        functools.partial(face_y_kernel, counts),
        [(7, ex, HALO, LANES)] * 2,
        where,
        ins + tuple(got_x),
    )
    got_y = swaps("gy", sends)
    x1, y1 = sx // 2, sy // 2
    own1, first1, second1, coarse2, *fine_arrays = run(
        functools.partial(down_kernel, counts),
        [(5, x1, y1, LANES), (x1, y1, LANES), (x1, y1, LANES), (4, y1 // 2, LANES)] + [fine] * 12,
        where,
        ins + tuple(got_x) + tuple(got_y),
        [fine] * 16 + [(7, x1, y1, LANES), (ey, LANES)],
        24,
    )

    got = swaps("gz", (first1, second1))
    ring, *sends = run(
        functools.partial(near_x_kernel, counts),
        [(5, x1, y1, LANES)] + [(5, NEAR, y1, LANES)] * n_x,
        where,
        (own1,) + tuple(got),
    )
    near_x = swaps("gx", sends)
    sends = run(
        functools.partial(near_y_kernel, counts),
        [(5, x1 + 2 * NEAR, NEAR, LANES)] * 2,
        where,
        (ring,) + tuple(near_x),
    )
    near_y = swaps("gy", sends)
    copies, level1 = run(
        functools.partial(near_kernel, counts, devices),
        [(devices, 5, y1 // 2, LANES), (6, x1 + 2 * NEAR, y1 + 2 * NEAR, LANES)],
        where,
        (ring,) + tuple(near_x) + tuple(near_y) + (coarse2,),
        [(x1, y1 + 2 * NEAR, LANES)],
    )

    gathered = lax.all_to_all(copies, axes, 0, 0, tiled=True)
    wide, rows = counts[0] * x1 // 2, counts[1] * y1 // 2
    columns = max(LANES, counts[2] * sz // 4)
    (result,) = run(
        functools.partial(up_kernel, counts),
        [(sx, sy, sz)],
        where,
        (gathered, level1) + tuple(fine_arrays),
        [(5, wide, rows, columns), (wide + NEAR, rows, columns)]
        + [(x1 + 2, ey, LANES)] * 2
        + [fine] * 4,
        24,
    )
    return result


def solution(mesh):
    spec = P("gx", "gy", "gz")
    return jax.shard_map(
        local, mesh=mesh, in_specs=(spec,) * 6, out_specs=spec, check_vma=False
    )
```

```python
import functools

import jax
import jax.numpy as jnp
from jax import lax
from jax.experimental import pallas as pl
from jax.experimental.pallas import tpu as pltpu
from jax.sharding import PartitionSpec as P

LEVELS = 6
SWEEPS = 2
BOTTOM = 8
WEIGHT = 0.25 ** (LEVELS - 1)
RELAX = 2.0 / 3.0
KEEP = 1.0 / 3.0

HALO = 4
NEAR = 4
LANES = 128
PLACE = (0, 11, 21, 31, 41, 51)
DEPTH = (11, 10, 10, 10, 10, 11)
SIDE = LANES // 2

VM = pl.BlockSpec(memory_space=pltpu.VMEM)
SM = pl.BlockSpec(memory_space=pltpu.SMEM)
F32 = jnp.float32


def lane_of(shape):
    return lax.broadcasted_iota(jnp.int32, shape, len(shape) - 1)


def pick(flag, yes, no):
    return jnp.where(jnp.full(yes.shape, flag, jnp.int32) == 1, yes, no)


def neighbours(axis_size, odd, one, two):
    if axis_size == 2:
        two = jnp.zeros_like(one)
    return pick(odd, one, two), pick(odd, two, one)


def turn(values, shift, axis):
    return pltpu.roll(values, shift % values.shape[axis], axis)


def parts_of(values):
    high = values.astype(jnp.bfloat16)
    rest = values - high.astype(F32)
    middle = rest.astype(jnp.bfloat16)
    low = (rest - middle.astype(F32)).astype(jnp.bfloat16)
    return high, middle, low


def times_table(values, table):
    table = table.astype(jnp.bfloat16)
    total = None
    for part in reversed(parts_of(values)):
        term = jnp.dot(part, table, preferred_element_type=F32)
        total = term if total is None else total + term
    return total


def table_times(table, values):
    table = table.astype(jnp.bfloat16)
    total = None
    for part in reversed(parts_of(values)):
        term = jnp.dot(table, part, preferred_element_type=F32)
        total = term if total is None else total + term
    return total


def iota2(shape, axis):
    return lax.broadcasted_iota(jnp.int32, shape, axis)


def pair_table(rows, cols, odd):
    row = iota2((rows, cols), 0)
    col = iota2((rows, cols), 1)
    hit = (row == 2 * col + 1) if odd else (row // 2 == col)
    return hit.astype(F32)


def below_x(values):
    if values.shape[0] == 1:
        return jnp.zeros_like(values)
    return jnp.concatenate([jnp.zeros_like(values[:1]), values[:-1]], axis=0)


def above_x(values):
    if values.shape[0] == 1:
        return jnp.zeros_like(values)
    return jnp.concatenate([values[1:], jnp.zeros_like(values[:1])], axis=0)


def pull(values, faces):
    bx, by, bz = faces
    total = bx * above_x(values) + below_x(bx * values)
    total = total + (by * turn(values, -1, 1) + turn(by * values, 1, 1))
    return total + (bz * turn(values, -1, 2) + turn(bz * values, 1, 2))


def diagonal(mass, faces, coupled):
    bx, by, bz = faces
    _, cy, cz = coupled
    return mass + bx + below_x(bx) + by + turn(cy, 1, 1) + bz + turn(cz, 1, 2)


def relaxer(mass, diag):
    inside = mass > 0.0
    return jnp.where(inside, RELAX / jnp.where(inside, diag, 1.0), 0.0)


def sweep(values, rhs, weight, faces):
    return KEEP * values + weight * (rhs + pull(values, faces))


def pack_z_kernel(where_ref, *refs):
    ins, (first, second) = refs[:6], refs[6:]
    odd = where_ref[2] % 2
    sx, sy, sz = ins[0].shape
    half = sx // 2
    lane = lane_of((half, sy, LANES))
    head = jnp.zeros((half, sy, LANES), F32)
    tail = head
    for a, ref in enumerate(ins):
        for g in range(2):
            values = ref[g * half:(g + 1) * half]
            at = SIDE * g + PLACE[a]
            mask = (lane >= at) & (lane < at + DEPTH[a])
            head = jnp.where(mask, turn(values, at, 2), head)
            tail = jnp.where(mask, turn(values, at + DEPTH[a], 2), tail)
    first[...] = pick(odd, head, tail)
    second[...] = pick(odd, tail, head)


def face_x_kernel(counts, where_ref, *refs):
    ins, one_ref, two_ref = refs[:6], refs[6], refs[7]
    zpack, sends = refs[8], refs[9:]
    sx, sy, sz = ins[0].shape
    half = sx // 2
    below, above = neighbours(counts[2], where_ref[2] % 2, one_ref[...], two_ref[...])
    lane = lane_of(below.shape)
    zpack[:half] = jnp.where(lane < SIDE, above, turn(below, SIDE, 2))
    zpack[half:] = jnp.where(lane < SIDE, turn(above, SIDE, 2), below)
    odd = where_ref[0] % 2
    for k, send in enumerate(sends):
        start = (1 - odd if k == 0 else odd) * (sx - HALO)
        for a, ref in enumerate(tuple(ins) + (zpack,)):
            send[a] = ref[pl.ds(start, HALO)]


def face_y_kernel(counts, where_ref, *refs):
    ins, halos, sends = refs[:7], refs[7:-2], refs[-2:]
    sx, sy, sz = ins[0].shape
    odd_x = where_ref[0] % 2
    odd = where_ref[1] % 2
    for a, ref in enumerate(ins):
        below, above = neighbours(counts[0], odd_x, halos[0][a], halos[-1][a])
        for at, block in ((0, below), (HALO, ref[...]), (HALO + sx, above)):
            head, tail = block[:, :HALO], block[:, sy - HALO:]
            span = slice(at, at + block.shape[0])
            sends[0][a, span] = pick(odd, head, tail)
            sends[1][a, span] = pick(odd, tail, head)


def each(first, last, step, body):
    rounds = (last - first) // step

    def go(i, carry):
        for j in range(step):
            body(first + i * step + j)
        return carry

    if rounds:
        lax.fori_loop(0, rounds, go, 0)
    for x in range(first + rounds * step, last):
        body(x)


def ring_up(main, halo, lane):
    main_up, halo_up = turn(main, -1, 1), turn(halo, -1, 1)
    last = lane == LANES - 1
    return jnp.where(last, halo_up, main_up), jnp.where(last, main_up, halo_up)


def ring_down(main, halo, lane):
    main_down, halo_down = turn(main, 1, 1), turn(halo, 1, 1)
    zero = lane == 0
    return jnp.where(zero, halo_down, main_down), jnp.where(zero, main_down, halo_down)


def pull_slab(field, bx, by, bz, x, lane):
    centre = [half[x] for half in field]
    out = []
    for k in range(2):
        c, face = centre[k], by[k][x]
        t = bx[k][x] * field[k][x + 1] + bx[k][x - 1] * field[k][x - 1]
        out.append(t + (face * turn(c, -1, 0) + turn(face * c, 1, 0)))
    faces = [half[x] for half in bz]
    ups = ring_up(centre[0], centre[1], lane)
    downs = ring_down(faces[0] * centre[0], faces[1] * centre[1], lane)
    return centre, [out[k] + (faces[k] * ups[k] + downs[k]) for k in range(2)]


def down_kernel(counts, where_ref, *refs):
    ins, refs = refs[:7], refs[7:]
    n_x = 1 if counts[0] == 2 else 2
    halos_x = refs[:n_x]
    one_y, two_y, own1, coarse2 = refs[n_x:4 + n_x]
    sends, refs = refs[4 + n_x:4 + 2 * n_x], refs[4 + 2 * n_x:]
    kept_m, kept_h, weight_m, weight_h = refs[:4]
    faces_out, scratch = refs[4:12], refs[12:]
    mains, halves = scratch[:7], scratch[7:13]
    half_m, half_h, diag_m, diag_h, sums, left, pairing = scratch[13:]
    sx, sy, sz = ins[0].shape
    ex, ey = sx + 2 * HALO, sy + 2 * HALO
    odd_x, odd_y = where_ref[0] % 2, where_ref[1] % 2

    for a in range(7):
        to = mains[a]
        below, above = neighbours(counts[0], odd_x, halos_x[0][a], halos_x[-1][a])
        to[:HALO, :sy] = below
        to[HALO:HALO + sx, :sy] = ins[a][...]
        to[HALO + sx:, :sy] = above
        below, above = neighbours(counts[1], odd_y, one_y[a], two_y[a])
        to[:, sy:] = jnp.concatenate([above, below], axis=1)
    lane = lane_of((ey, LANES))

    def unpack(x):
        packed = mains[6][x]
        for a in range(6):
            at, depth = PLACE[a], DEPTH[a]
            right = turn(packed, -at, 1)
            other_side = turn(packed, SIDE - depth - at, 1)
            halves[a][x] = jnp.where(
                lane < depth, right, jnp.where(lane >= LANES - depth, other_side, 0.0)
            )

    each(0, ex, 4, unpack)
    field, rhs, alpha, bx, by, bz = zip(mains[:6], halves)
    halfway, weight, kept = (half_m, half_h), (weight_m, weight_h), (kept_m, kept_h)
    diag = (diag_m, diag_h)

    def first_sweep(x):
        faces = [half[x] for half in bz]
        downs = ring_down(faces[0], faces[1], lane)
        centre, near = pull_slab(field, bx, by, bz, x, lane)
        for k in range(2):
            face = by[k][x]
            mass = WEIGHT * alpha[k][x]
            d = mass + bx[k][x] + bx[k][x - 1] + face + turn(face, 1, 0) + faces[k] + downs[k]
            w = relaxer(mass, d)
            diag[k][x] = d
            weight[k][x] = w
            halfway[k][x] = KEEP * centre[k] + w * (rhs[k][x] + near[k])

    each(1, ex - 1, 4, first_sweep)

    def second_sweep(x):
        centre, near = pull_slab(halfway, bx, by, bz, x, lane)
        for k in range(2):
            kept[k][x] = KEEP * centre[k] + weight[k][x] * (rhs[k][x] + near[k])

    each(2, ex - 2, 4, second_sweep)

    def residual(x):
        centre, near = pull_slab(kept, bx, by, bz, x, lane)
        for k in range(2):
            halfway[k][x] = rhs[k][x] - diag[k][x] * centre[k] + near[k]

    each(HALO, ex - HALO, 4, residual)
    for n, source in enumerate((rhs, bx, by, bz)):
        for k in range(2):
            faces_out[2 * n + k][...] = source[k][...]

    x1, y1 = sx // 2, sy // 2

    def rows_of(source, x, firsts, seconds):
        total = None
        for p in firsts:
            for q in seconds:
                term = source[x + p, pl.ds(q, y1, stride=2), :]
                total = term if total is None else total + term
        return total

    both, last = (0, 1), (1,)
    for k in range(2):
        lanes = slice(k * LANES, (k + 1) * LANES)
        for i in range(x1):
            x = HALO + 2 * i
            sums[0, i, :, lanes] = rows_of(halfway[k], x, both, both)
            sums[1, i, :, lanes] = rows_of(alpha[k], x, both, both)
            sums[2, i, :, lanes] = rows_of(bx[k], x, last, both)
            sums[3, i, :, lanes] = rows_of(by[k], x, both, last)
            left[...] = turn(by[k][x] + by[k][x + 1], 1, 0)
            sums[4, i, :, lanes] = left[pl.ds(0, y1, stride=2), :]
            sums[5, i, :, lanes] = rows_of(bz[k], x, both, both)
        sums[6, 0, :, lanes] = rows_of(bx[k], HALO - 2, last, both)
    pairs = pair_table(2 * LANES, LANES, False)
    odds = pair_table(2 * LANES, LANES, True)

    def to_level1(first, count, table, factor):
        flat = sums[first:first + count].reshape(count * x1 * y1, 2 * LANES)
        return factor * times_table(flat, table).reshape(count, x1, y1, LANES)

    paired = to_level1(0, 5, pairs, 0.0625)
    rhs1, mass1 = 2.0 * paired[0], (2.0 * WEIGHT) * paired[1]
    faces1 = (paired[2], paired[3], to_level1(5, 1, odds, 0.0625)[0])
    edge_x = 0.0625 * times_table(sums[6, 0], pairs)[None]
    diag1 = mass1 + faces1[0] + jnp.concatenate([edge_x, faces1[0][:-1]], axis=0)
    diag1 = diag1 + faces1[1] + paired[4] + faces1[2] + turn(faces1[2], 1, 2)
    weight1 = relaxer(mass1, diag1)
    for n, values in enumerate((rhs1, weight1) + faces1):
        own1[n] = values
        head, tail = values[:NEAR], values[x1 - NEAR:]
        for k, send in enumerate(sends):
            send[n] = pick(odd_x, head, tail) if k == 0 else pick(odd_x, tail, head)

    parts = (
        (mass1, False, False, False, 0.125),
        (faces1[0], True, False, False, 0.0625),
        (faces1[1], False, True, False, 0.0625),
        (faces1[2], False, False, True, 0.0625),
    )
    for n, (values, *odd_axes, factor) in enumerate(parts):
        pairing[n] = values
        coarse2[n] = level2_rows(pairing.at[n], odd_axes, factor, x1 // 2, y1 // 2, sz // 4)


def level2_rows(source, odd_axes, factor, x2, y2, z2):
    rows = []
    for i in range(x2):
        total = None
        for p in (1,) if odd_axes[0] else (0, 1):
            for q in (1,) if odd_axes[1] else (0, 1):
                term = source[2 * i + p, pl.ds(q, y2, stride=2), :]
                total = term if total is None else total + term
        rows.append(total)
    flat = jnp.concatenate(rows, axis=0)
    flat = factor * times_table(flat, pair_table(LANES, LANES, odd_axes[2]))
    lane = lane_of((y2, LANES))
    packed = jnp.zeros((y2, LANES), F32)
    for i in range(x2):
        mask = (lane >= i * z2) & (lane < (i + 1) * z2)
        packed = jnp.where(mask, turn(flat[i * y2:(i + 1) * y2], i * z2, 1), packed)
    return packed


def near_y_kernel(counts, where_ref, ring, *refs):
    halos, sends = refs[:-2], refs[-2:]
    n, bx, by, _ = ring.shape
    odd_x, odd = where_ref[0] % 2, where_ref[1] % 2
    for a in range(n):
        below, above = neighbours(counts[0], odd_x, halos[0][a], halos[-1][a])
        block = jnp.concatenate([below, ring[a], above], axis=0)
        head, tail = block[:, :NEAR], block[:, by - NEAR:]
        sends[0][a] = pick(odd, head, tail)
        sends[1][a] = pick(odd, tail, head)


def near_kernel(counts, devices, where_ref, ring, *refs):
    n_x = 1 if counts[0] == 2 else 2
    halos_x = refs[:n_x]
    one_y, two_y, coarse2, copies, level1, left = refs[n_x:]
    n, bx1, by1, _ = ring.shape
    odd_x, odd_y = where_ref[0] % 2, where_ref[1] % 2
    whole = []
    for a in range(n):
        below, above = neighbours(counts[0], odd_x, halos_x[0][a], halos_x[-1][a])
        block = jnp.concatenate([below, ring[a], above], axis=0)
        below, above = neighbours(counts[1], odd_y, one_y[a], two_y[a])
        whole.append(jnp.concatenate([block, above, below], axis=1))
    rhs1, weight1 = whole[:2]
    faces1 = tuple(whole[2:])
    field1 = weight1 * rhs1
    field1 = sweep(field1, rhs1, weight1, faces1)
    for a, values in enumerate([field1] + whole):
        level1[a] = values
    mine = slice(NEAR, NEAR + bx1)
    inner = weight1[mine]
    diag1 = RELAX / jnp.where(inner > 0.0, inner, 1.0)
    remain = rhs1[mine] - diag1 * field1[mine] + pull(field1, faces1)[mine]
    left[...] = remain
    packed = level2_rows(left, (False,) * 3, 0.125, bx1 // 2, by1 // 2, LANES // 4)
    for d in range(devices):
        copies[d, 0] = packed
        for a in range(n - 1):
            copies[d, a + 1] = coarse2[a]


def halve(values, factor, odd_axis):
    x, y, z = values.shape
    if odd_axis == 0:
        values = jnp.concatenate([values[2 * i + 1:2 * i + 2] for i in range(x // 2)], axis=0)
    else:
        values = jnp.concatenate(
            [values[2 * i:2 * i + 1] + values[2 * i + 1:2 * i + 2] for i in range(x // 2)], axis=0
        )
    to_y = max(8, y // 2)
    to_z = max(LANES, z // 2)
    flat = values.reshape(x // 2 * y, z)
    flat = times_table(flat, pair_table(z, to_z, odd_axis == 2))
    row = iota2((to_y, y), 0)
    col = iota2((to_y, y), 1)
    table = (col == 2 * row + 1) if odd_axis == 1 else (col // 2 == row)
    table = table.astype(F32)
    blocks = [table_times(table, flat[i * y:(i + 1) * y])[None] for i in range(x // 2)]
    return factor * jnp.concatenate(blocks, axis=0)


def double(values, shape):
    x, y, z = values.shape
    to_x, to_y, to_z = shape
    row = iota2((to_y, y), 0)
    col = iota2((to_y, y), 1)
    table_y = (row // 2 == col).astype(F32)
    row = iota2((z, to_z), 0)
    col = iota2((z, to_z), 1)
    table_z = (col // 2 == row).astype(F32)
    blocks = [table_times(table_y, values[i])[None] for i in range(x)]
    flat = jnp.concatenate(blocks, axis=0).reshape(x * to_y, z)
    flat = times_table(flat, table_z).reshape(x, to_y, to_z)
    return jnp.concatenate([flat[i // 2:i // 2 + 1] for i in range(to_x)], axis=0)


def coupled_faces(faces, y, z):
    bx, by, bz = faces
    row = lax.broadcasted_iota(jnp.int32, by.shape, 1)
    return bx, jnp.where(row == y - 1, 0.0, by), jnp.where(lane_of(bz.shape) == z - 1, 0.0, bz)


def coarse_cycle(level, rhs, mass, faces, y, z):
    coupled = coupled_faces(faces, y, z)
    diag = diagonal(mass, faces, coupled)
    weight = relaxer(mass, diag)
    field = weight * rhs
    if level == LEVELS - 1:
        for _ in range(BOTTOM - 1):
            field = sweep(field, rhs, weight, coupled)
        return field
    for _ in range(SWEEPS - 1):
        field = sweep(field, rhs, weight, coupled)
    remain = rhs - diag * field + pull(field, coupled)
    correction = coarse_cycle(
        level + 1,
        halve(remain, 0.125, -1),
        halve(mass, 0.125, -1),
        tuple(halve(face, 0.0625, axis) for axis, face in enumerate(faces)),
        y // 2,
        z // 2,
    )
    field = field + double(correction, field.shape)
    for _ in range(SWEEPS):
        field = sweep(field, rhs, weight, coupled)
    return field


def up_kernel(counts, where_ref, gathered, level1, *refs):
    kept, weight, rhs, bx, by, bz = zip(refs[0:12:2], refs[1:12:2])
    out, whole, second, spread_m, spread_h, field_m, field_h, half_m, half_h = refs[12:]
    gx, gy, gz = counts
    sx, sy, sz = out.shape
    x1, y1 = sx // 2, sy // 2
    x2, y2, z2 = x1 // 2, y1 // 2, sz // 4
    columns = max(LANES, gz * z2)
    lane = lane_of((y2, LANES))

    for a in range(5):
        for i in range(gx):
            for j in range(gy):
                for x in range(x2):
                    for part in range(columns // LANES):
                        total = jnp.zeros((y2, LANES), F32)
                        for k in range(LANES // z2):
                            column = part * (LANES // z2) + k
                            if column < gz:
                                block = gathered[(i * gy + j) * gz + column, a]
                                mask = (lane >= k * z2) & (lane < (k + 1) * z2)
                                total = jnp.where(mask, turn(block, (k - x) * z2, 1), total)
                        whole[
                            a, i * x2 + x, j * y2:(j + 1) * y2, part * LANES:(part + 1) * LANES
                        ] = total
    correction = coarse_cycle(
        2, whole[0], whole[1], (whole[2], whole[3], whole[4]), gy * y2, gz * z2
    )

    wide = gx * x2
    half = NEAR // 2
    ex1, ey1 = x1 + 2 * NEAR, y1 + 2 * NEAR
    second[:half] = jnp.zeros((half,) + correction.shape[1:], F32)
    second[half:half + wide] = correction
    second[half + wide:] = jnp.zeros((half,) + correction.shape[1:], F32)
    window = second[pl.ds(where_ref[0] * x2, x2 + NEAR)]
    rows = correction.shape[1]
    row = iota2((ey1, rows), 0)
    col = iota2((ey1, rows), 1)
    place = jnp.where(row < y1 + NEAR, row, row - ey1)
    table_y = (col == where_ref[1] * y2 + lax.shift_right_arithmetic(place, 1)).astype(F32)
    row = iota2((columns, LANES), 0)
    col = iota2((columns, LANES), 1)
    place = jnp.where(col < LANES * 3 // 4, col, col - LANES)
    table_z = (row == where_ref[2] * z2 + lax.shift_right_arithmetic(place, 1)).astype(F32)
    flat = times_table(window.reshape((x2 + NEAR) * rows, columns), table_z)
    blocks = [table_times(table_y, flat[i * rows:(i + 1) * rows])[None] for i in range(x2 + NEAR)]
    lifted = jnp.concatenate([blocks[i // 2] for i in range(ex1)], axis=0)
    field1, rhs1, weight1 = level1[0], level1[1], level1[2]
    faces1 = (level1[3], level1[4], level1[5])
    field1 = field1 + jnp.where(weight1 > 0.0, lifted, 0.0)
    for _ in range(SWEEPS):
        field1 = sweep(field1, rhs1, weight1, faces1)

    ex, ey = sx + 2 * HALO, sy + 2 * HALO
    near = field1[NEAR - 1:NEAR + x1 + 1].reshape((x1 + 2) * ey1, LANES)
    row = iota2((LANES, 2 * LANES), 0)
    col = iota2((LANES, 2 * LANES), 1)
    lifted = times_table(near, (col // 2 == row).astype(F32))
    quarter = NEAR // 2
    for k, spread in enumerate((spread_m, spread_h)):
        block = lifted[:, k * LANES:(k + 1) * LANES].reshape(x1 + 2, ey1, LANES)
        for i in range(x1 + 2):
            for q in range(2):
                spread[i, pl.ds(q, y1, stride=2), :] = block[i, :y1]
                spread[i, pl.ds(sy + q, quarter, stride=2), :] = block[i, y1:y1 + quarter]
                spread[i, pl.ds(sy + HALO + q, quarter, stride=2), :] = block[i, ey1 - quarter:]
    before, after = (field_m, field_h), (half_m, half_h)
    first = HALO - 2
    for x in range(first, ex - first):
        for k, spread in enumerate((spread_m, spread_h)):
            before[k][x] = kept[k][x] + spread[(x - first) // 2]

    lane = lane_of((ey, LANES))

    def sweep_out(x):
        centre, around = pull_slab(before, bx, by, bz, x, lane)
        for k in range(2):
            after[k][x] = KEEP * centre[k] + weight[k][x] * (rhs[k][x] + around[k])

    each(first + 1, ex - first - 1, 4, sweep_out)

    def sweep_own(x):
        centre, around = pull_slab(after, bx, by, bz, x, lane)
        value = KEEP * centre[0] + weight[0][x] * (rhs[0][x] + around[0])
        out[x - HALO] = value[:sy]

    each(HALO, ex - HALO, 4, sweep_own)


def run(kernel, outs, where, arrays, scratch=(), grant=16):
    return pl.pallas_call(
        kernel,
        out_shape=tuple(jax.ShapeDtypeStruct(shape, F32) for shape in outs),
        in_specs=[SM] + [VM] * len(arrays),
        out_specs=tuple(VM for _ in outs),
        scratch_shapes=[pltpu.VMEM(shape, F32) for shape in scratch],
        compiler_params=pltpu.CompilerParams(vmem_limit_bytes=grant * 1024 * 1024),
    )(where, *arrays)


def swaps(axis, sends):
    count = lax.axis_size(axis)
    got = []
    for k, block in reversed(list(enumerate(sends))):
        pairs = [(i, i + 1) for i in range(k, count - 1, 2)]
        pairs = [pair for low, high in pairs for pair in ((low, high), (high, low))]
        got.append(lax.ppermute(block, axis, pairs))
    return got[::-1]


def local(initial, right_side, alpha, beta_x, beta_y, beta_z):
    axes = ("gx", "gy", "gz")
    counts = tuple(lax.axis_size(axis) for axis in axes)
    devices = counts[0] * counts[1] * counts[2]
    where = jnp.stack([lax.axis_index(axis) for axis in axes]).astype(jnp.int32)
    ins = (initial, right_side, alpha, beta_x, beta_y, beta_z)
    sx, sy, sz = initial.shape
    n_x = 1 if counts[0] == 2 else 2
    ex, ey = sx + 2 * HALO, sy + 2 * HALO
    fine = (ex, ey, LANES)

    sends = run(pack_z_kernel, [(sx // 2, sy, LANES)] * 2, where, ins, grant=60)
    got = swaps("gz", sends)
    zpack, *sends = run(
        functools.partial(face_x_kernel, counts),
        [(sx, sy, LANES)] + [(7, HALO, sy, LANES)] * n_x,
        where,
        ins + tuple(got),
    )
    ins = ins + (zpack,)
    got_x = swaps("gx", sends)
    sends = run(
        functools.partial(face_y_kernel, counts),
        [(7, ex, HALO, LANES)] * 2,
        where,
        ins + tuple(got_x),
    )
    got_y = swaps("gy", sends)
    x1, y1 = sx // 2, sy // 2
    ring, coarse2, *outs = run(
        functools.partial(down_kernel, counts),
        [(5, x1, y1, LANES), (4, y1 // 2, LANES)] + [(5, NEAR, y1, LANES)] * n_x + [fine] * 12,
        where,
        ins + tuple(got_x) + tuple(got_y),
        [fine] * 17 + [(7, x1, y1, 2 * LANES), (ey, LANES), (4, x1, y1, LANES)],
        24,
    )
    sends, fine_arrays = outs[:n_x], outs[n_x:]

    near_x = swaps("gx", sends)
    sends = run(
        functools.partial(near_y_kernel, counts),
        [(5, x1 + 2 * NEAR, NEAR, LANES)] * 2,
        where,
        (ring,) + tuple(near_x),
    )
    near_y = swaps("gy", sends)
    copies, level1 = run(
        functools.partial(near_kernel, counts, devices),
        [(devices, 5, y1 // 2, LANES), (6, x1 + 2 * NEAR, y1 + 2 * NEAR, LANES)],
        where,
        (ring,) + tuple(near_x) + tuple(near_y) + (coarse2,),
        [(x1, y1 + 2 * NEAR, LANES)],
    )

    gathered = lax.all_to_all(copies, axes, 0, 0, tiled=True)
    wide, rows = counts[0] * x1 // 2, counts[1] * y1 // 2
    columns = max(LANES, counts[2] * sz // 4)
    (result,) = run(
        functools.partial(up_kernel, counts),
        [(sx, sy, sz)],
        where,
        (gathered, level1) + tuple(fine_arrays),
        [(5, wide, rows, columns), (wide + NEAR, rows, columns)]
        + [(x1 + 2, ey, LANES)] * 2
        + [fine] * 4,
        24,
    )
    return result


def solution(mesh):
    spec = P("gx", "gy", "gz")
    return jax.shard_map(
        local, mesh=mesh, in_specs=(spec,) * 6, out_specs=spec, check_vma=False
    )
```

```python
import functools

import jax
import jax.numpy as jnp
from jax import lax
from jax.experimental import pallas as pl
from jax.experimental.pallas import tpu as pltpu
from jax.sharding import PartitionSpec as P

LEVELS = 6
SWEEPS = 2
BOTTOM = 8
WEIGHT = 0.25 ** (LEVELS - 1)
RELAX = 2.0 / 3.0
KEEP = 1.0 / 3.0

HALO = 4
NEAR = 4
LANES = 128
PLACE = (0, 11, 21, 31, 41, 51)
DEPTH = (11, 10, 10, 10, 10, 11)
SIDE = LANES // 2
STRIDE = 256

VM = pl.BlockSpec(memory_space=pltpu.VMEM)
SM = pl.BlockSpec(memory_space=pltpu.SMEM)
F32 = jnp.float32


def position(where_ref):
    code = where_ref[0]
    return code // (STRIDE * STRIDE), code // STRIDE % STRIDE, code % STRIDE


def lane_of(shape):
    return lax.broadcasted_iota(jnp.int32, shape, len(shape) - 1)


def pick(flag, yes, no):
    return jnp.where(jnp.full(yes.shape, flag, jnp.int32) == 1, yes, no)


def neighbours(axis_size, odd, one, two):
    if axis_size == 2:
        two = jnp.zeros_like(one)
    return pick(odd, one, two), pick(odd, two, one)


def turn(values, shift, axis):
    return pltpu.roll(values, shift % values.shape[axis], axis)


def parts_of(values):
    high = values.astype(jnp.bfloat16)
    rest = values - high.astype(F32)
    middle = rest.astype(jnp.bfloat16)
    low = (rest - middle.astype(F32)).astype(jnp.bfloat16)
    return high, middle, low


def times_table(values, table):
    table = table.astype(jnp.bfloat16)
    total = None
    for part in reversed(parts_of(values)):
        term = jnp.dot(part, table, preferred_element_type=F32)
        total = term if total is None else total + term
    return total


def table_times(table, values):
    table = table.astype(jnp.bfloat16)
    total = None
    for part in reversed(parts_of(values)):
        term = jnp.dot(table, part, preferred_element_type=F32)
        total = term if total is None else total + term
    return total


def iota2(shape, axis):
    return lax.broadcasted_iota(jnp.int32, shape, axis)


def pair_table(rows, cols, odd):
    row = iota2((rows, cols), 0)
    col = iota2((rows, cols), 1)
    hit = (row == 2 * col + 1) if odd else (row // 2 == col)
    return hit.astype(F32)


def below_x(values):
    if values.shape[0] == 1:
        return jnp.zeros_like(values)
    return jnp.concatenate([jnp.zeros_like(values[:1]), values[:-1]], axis=0)


def above_x(values):
    if values.shape[0] == 1:
        return jnp.zeros_like(values)
    return jnp.concatenate([values[1:], jnp.zeros_like(values[:1])], axis=0)


def pull(values, faces, step=1):
    bx, by, bz = faces
    total = bx * above_x(values) + below_x(bx * values)
    total = total + (by * turn(values, -step, 1) + turn(by * values, step, 1))
    return total + (bz * turn(values, -step, 2) + turn(bz * values, step, 2))


def diagonal(mass, faces, coupled, step=1):
    bx, by, bz = faces
    _, cy, cz = coupled
    return mass + bx + below_x(bx) + by + turn(cy, step, 1) + bz + turn(cz, step, 2)


def relaxer(mass, diag):
    inside = mass > 0.0
    return jnp.where(inside, RELAX / jnp.where(inside, diag, 1.0), 0.0)


def sweep(values, rhs, weight, faces, step=1):
    return KEEP * values + weight * (rhs + pull(values, faces, step))


def pack_z_kernel(where_ref, *refs):
    ins, (first, second) = refs[:6], refs[6:]
    odd = position(where_ref)[2] % 2
    sx, sy, sz = ins[0].shape
    half = sx // 2
    lane = lane_of((half, sy, LANES))
    head = jnp.zeros((half, sy, LANES), F32)
    tail = head
    for a, ref in enumerate(ins):
        for g in range(2):
            values = ref[g * half:(g + 1) * half]
            at = SIDE * g + PLACE[a]
            mask = (lane >= at) & (lane < at + DEPTH[a])
            head = jnp.where(mask, turn(values, at, 2), head)
            tail = jnp.where(mask, turn(values, at + DEPTH[a], 2), tail)
    first[...] = pick(odd, head, tail)
    second[...] = pick(odd, tail, head)


def face_x_kernel(counts, where_ref, *refs):
    ins, one_ref, two_ref = refs[:6], refs[6], refs[7]
    zpack, sends = refs[8], refs[9:]
    sx, sy, sz = ins[0].shape
    half = sx // 2
    below, above = neighbours(counts[2], position(where_ref)[2] % 2, one_ref[...], two_ref[...])
    lane = lane_of(below.shape)
    zpack[:half] = jnp.where(lane < SIDE, above, turn(below, SIDE, 2))
    zpack[half:] = jnp.where(lane < SIDE, turn(above, SIDE, 2), below)
    odd = position(where_ref)[0] % 2
    for k, send in enumerate(sends):
        start = (1 - odd if k == 0 else odd) * (sx - HALO)
        for a, ref in enumerate(tuple(ins) + (zpack,)):
            send[a] = ref[pl.ds(start, HALO)]


def face_y_kernel(counts, where_ref, *refs):
    ins, halos, sends = refs[:7], refs[7:-2], refs[:-3:-1]
    sx, sy, sz = ins[0].shape
    odd_x, odd = (place % 2 for place in position(where_ref)[:2])
    for a, ref in enumerate(ins):
        below, above = neighbours(counts[0], odd_x, halos[0][a], halos[-1][a])
        for at, block in ((0, below), (HALO, ref[...]), (HALO + sx, above)):
            head, tail = block[:, :HALO], block[:, sy - HALO:]
            span = slice(at, at + block.shape[0])
            sends[0][a, span] = pick(odd, head, tail)
            sends[1][a, span] = pick(odd, tail, head)


def each(first, last, step, body):
    rounds = (last - first) // step

    def go(i, carry):
        for j in range(step):
            body(first + i * step + j)
        return carry

    if rounds:
        lax.fori_loop(0, rounds, go, 0)
    for x in range(first + rounds * step, last):
        body(x)


def ring_up(main, halo, lane):
    main_up, halo_up = turn(main, -1, 1), turn(halo, -1, 1)
    last = lane == LANES - 1
    return jnp.where(last, halo_up, main_up), jnp.where(last, main_up, halo_up)


def ring_down(main, halo, lane):
    main_down, halo_down = turn(main, 1, 1), turn(halo, 1, 1)
    zero = lane == 0
    return jnp.where(zero, halo_down, main_down), jnp.where(zero, main_down, halo_down)


def pull_slab(field, bx, by, bz, x, lane):
    centre = [half[x] for half in field]
    out = []
    for k in range(2):
        c, face = centre[k], by[k][x]
        t = bx[k][x] * field[k][x + 1] + bx[k][x - 1] * field[k][x - 1]
        out.append(t + (face * turn(c, -1, 0) + turn(face * c, 1, 0)))
    faces = [half[x] for half in bz]
    ups = ring_up(centre[0], centre[1], lane)
    downs = ring_down(faces[0] * centre[0], faces[1] * centre[1], lane)
    return centre, [out[k] + (faces[k] * ups[k] + downs[k]) for k in range(2)]


def down_kernel(counts, where_ref, *refs):
    ins, refs = refs[:7], refs[7:]
    n_x = 1 if counts[0] == 2 else 2
    halos_x = refs[:n_x]
    two_y, one_y, own1, coarse2 = refs[n_x:4 + n_x]
    sends, refs = refs[4 + n_x:4 + 2 * n_x], refs[4 + 2 * n_x:]
    kept_m, kept_h, weight_m, weight_h = refs[:4]
    faces_out, scratch = refs[4:12], refs[12:]
    rhs, bx, by, bz = zip(faces_out[::2], faces_out[1::2])
    field, alpha = scratch[:2], scratch[2:4]
    packs, half_m, half_h, diag_m, diag_h, sums, left, pairing = scratch[4:]
    arrays = (field, rhs, alpha, bx, by, bz)
    sx, sy, sz = ins[0].shape
    ex, ey = sx + 2 * HALO, sy + 2 * HALO
    odd_x, odd_y = (place % 2 for place in position(where_ref)[:2])

    for a in range(7):
        to = packs if a == 6 else arrays[a][0]
        below, above = neighbours(counts[0], odd_x, halos_x[0][a], halos_x[-1][a])
        to[:HALO, :sy] = below
        to[HALO:HALO + sx, :sy] = ins[a][...]
        to[HALO + sx:, :sy] = above
        below, above = neighbours(counts[1], odd_y, one_y[a], two_y[a])
        to[:, sy:] = jnp.concatenate([above, below], axis=1)
    lane = lane_of((ey, LANES))

    def unpack(x):
        packed = packs[x]
        for a in range(6):
            at, depth = PLACE[a], DEPTH[a]
            right = turn(packed, -at, 1)
            other_side = turn(packed, SIDE - depth - at, 1)
            arrays[a][1][x] = jnp.where(
                lane < depth, right, jnp.where(lane >= LANES - depth, other_side, 0.0)
            )

    each(0, ex, 4, unpack)
    halfway, weight, kept = (half_m, half_h), (weight_m, weight_h), (kept_m, kept_h)
    diag = (diag_m, diag_h)

    def first_sweep(x):
        faces = [half[x] for half in bz]
        downs = ring_down(faces[0], faces[1], lane)
        centre, near = pull_slab(field, bx, by, bz, x, lane)
        for k in range(2):
            face = by[k][x]
            mass = WEIGHT * alpha[k][x]
            d = mass + bx[k][x] + bx[k][x - 1] + face + turn(face, 1, 0) + faces[k] + downs[k]
            w = relaxer(mass, d)
            diag[k][x] = d
            weight[k][x] = w
            halfway[k][x] = KEEP * centre[k] + w * (rhs[k][x] + near[k])

    each(1, ex - 1, 4, first_sweep)

    def second_sweep(x):
        centre, near = pull_slab(halfway, bx, by, bz, x, lane)
        for k in range(2):
            kept[k][x] = KEEP * centre[k] + weight[k][x] * (rhs[k][x] + near[k])

    each(2, ex - 2, 4, second_sweep)

    def residual(x):
        centre, near = pull_slab(kept, bx, by, bz, x, lane)
        for k in range(2):
            halfway[k][x] = rhs[k][x] - diag[k][x] * centre[k] + near[k]

    each(HALO, ex - HALO, 4, residual)

    x1, y1 = sx // 2, sy // 2

    def rows_of(source, x, firsts, seconds):
        total = None
        for p in firsts:
            for q in seconds:
                term = source[x + p, pl.ds(q, y1, stride=2), :]
                total = term if total is None else total + term
        return total

    both, last = (0, 1), (1,)
    for k in range(2):
        lanes = slice(k * LANES, (k + 1) * LANES)
        for i in range(x1):
            x = HALO + 2 * i
            sums[0, i, :, lanes] = rows_of(halfway[k], x, both, both)
            sums[1, i, :, lanes] = rows_of(alpha[k], x, both, both)
            sums[2, i, :, lanes] = rows_of(bx[k], x, last, both)
            sums[3, i, :, lanes] = rows_of(by[k], x, both, last)
            left[...] = turn(by[k][x] + by[k][x + 1], 1, 0)
            sums[4, i, :, lanes] = left[pl.ds(0, y1, stride=2), :]
            sums[5, i, :, lanes] = rows_of(bz[k], x, both, both)
        sums[6, 0, :, lanes] = rows_of(bx[k], HALO - 2, last, both)
    pairs = pair_table(2 * LANES, LANES, False)
    odds = pair_table(2 * LANES, LANES, True)

    def to_level1(first, count, table, factor):
        flat = sums[first:first + count].reshape(count * x1 * y1, 2 * LANES)
        return factor * times_table(flat, table).reshape(count, x1, y1, LANES)

    paired = to_level1(0, 5, pairs, 0.0625)
    rhs1, mass1 = 2.0 * paired[0], (2.0 * WEIGHT) * paired[1]
    faces1 = (paired[2], paired[3], to_level1(5, 1, odds, 0.0625)[0])
    edge_x = 0.0625 * times_table(sums[6, 0], pairs)[None]
    diag1 = mass1 + faces1[0] + jnp.concatenate([edge_x, faces1[0][:-1]], axis=0)
    diag1 = diag1 + faces1[1] + paired[4] + faces1[2] + turn(faces1[2], 1, 2)
    weight1 = relaxer(mass1, diag1)
    for n, values in enumerate((rhs1, weight1) + faces1):
        own1[n] = values
        head, tail = values[:NEAR], values[x1 - NEAR:]
        for k, send in enumerate(sends):
            send[n] = pick(odd_x, head, tail) if k == 0 else pick(odd_x, tail, head)

    parts = (
        (mass1, False, False, False, 0.125),
        (faces1[0], True, False, False, 0.0625),
        (faces1[1], False, True, False, 0.0625),
        (faces1[2], False, False, True, 0.0625),
    )
    for n, (values, *odd_axes, factor) in enumerate(parts):
        pairing[n] = values
        coarse2[n] = level2_rows(pairing.at[n], odd_axes, factor, x1 // 2, y1 // 2, sz // 4)


def level2_rows(source, odd_axes, factor, x2, y2, z2):
    rows = []
    for i in range(x2):
        total = None
        for p in (1,) if odd_axes[0] else (0, 1):
            for q in (1,) if odd_axes[1] else (0, 1):
                term = source[2 * i + p, pl.ds(q, y2, stride=2), :]
                total = term if total is None else total + term
        rows.append(total)
    flat = jnp.concatenate(rows, axis=0)
    flat = factor * times_table(flat, pair_table(LANES, LANES, odd_axes[2]))
    lane = lane_of((y2, LANES))
    packed = jnp.zeros((y2, LANES), F32)
    for i in range(x2):
        mask = (lane >= i * z2) & (lane < (i + 1) * z2)
        packed = jnp.where(mask, turn(flat[i * y2:(i + 1) * y2], i * z2, 1), packed)
    return packed


def near_y_kernel(counts, where_ref, ring, *refs):
    halos, sends = refs[:-2], refs[:-3:-1]
    n, bx, by, _ = ring.shape
    odd_x, odd = (place % 2 for place in position(where_ref)[:2])
    for a in range(n):
        below, above = neighbours(counts[0], odd_x, halos[0][a], halos[-1][a])
        block = jnp.concatenate([below, ring[a], above], axis=0)
        head, tail = block[:, :NEAR], block[:, by - NEAR:]
        sends[0][a] = pick(odd, head, tail)
        sends[1][a] = pick(odd, tail, head)


def near_kernel(counts, devices, where_ref, ring, *refs):
    n_x = 1 if counts[0] == 2 else 2
    halos_x = refs[:n_x]
    two_y, one_y, coarse2, copies, level1, left = refs[n_x:]
    n, bx1, by1, _ = ring.shape
    odd_x, odd_y = (place % 2 for place in position(where_ref)[:2])
    whole = []
    for a in range(n):
        below, above = neighbours(counts[0], odd_x, halos_x[0][a], halos_x[-1][a])
        block = jnp.concatenate([below, ring[a], above], axis=0)
        below, above = neighbours(counts[1], odd_y, one_y[a], two_y[a])
        whole.append(jnp.concatenate([block, above, below], axis=1))
    rhs1, weight1 = whole[:2]
    faces1 = tuple(whole[2:])
    field1 = weight1 * rhs1
    field1 = sweep(field1, rhs1, weight1, faces1)
    for a, values in enumerate([field1] + whole):
        level1[a] = values
    mine = slice(NEAR, NEAR + bx1)
    inner = weight1[mine]
    diag1 = RELAX / jnp.where(inner > 0.0, inner, 1.0)
    remain = rhs1[mine] - diag1 * field1[mine] + pull(field1, faces1)[mine]
    left[...] = remain
    packed = level2_rows(left, (False,) * 3, 0.125, bx1 // 2, by1 // 2, LANES // 4)
    for d in range(devices):
        copies[d, 0] = packed
        for a in range(n - 1):
            copies[d, a + 1] = coarse2[a]


def halve(values, odd_axis, step):
    half = values.shape[0] // 2
    even = [values[2 * i:2 * i + 1] for i in range(half)]
    odd = [values[2 * i + 1:2 * i + 2] for i in range(half)]
    if odd_axis != 0:
        odd = [a + b for a, b in zip(even, odd)]
    values = jnp.concatenate(odd, axis=0)
    for axis in (1, 2):
        next_one = turn(values, -step, axis)
        values = next_one if odd_axis == axis else values + next_one
    return values


def double(values, step):
    values = values + turn(values, step, 1)
    values = values + turn(values, step, 2)
    return jnp.concatenate([values[i // 2:i // 2 + 1] for i in range(2 * values.shape[0])], axis=0)


def coarse_levels(mass, faces, y, z):
    levels = []
    for level in range(2, LEVELS):
        step = 2 ** (level - 2)
        bx, by, bz = faces
        row = lax.broadcasted_iota(jnp.int32, by.shape, 1)
        lane = lane_of(bz.shape)
        coupled = (
            bx,
            jnp.where(row == (y - 1) * step, 0.0, by),
            jnp.where(lane == (z - 1) * step, 0.0, bz),
        )
        mass = jnp.where((row % step == 0) & (lane % step == 0), mass, 0.0)
        diag = diagonal(mass, faces, coupled, step)
        levels.append((diag, relaxer(mass, diag), coupled))
        if level < LEVELS - 1:
            faces = tuple(0.0625 * halve(face, axis, step) for axis, face in enumerate(faces))
            mass = 0.125 * halve(mass, -1, step)
            y, z = y // 2, z // 2
    return levels


def coarse_cycle(level, rhs, levels):
    step = 2 ** (level - 2)
    diag, weight, faces = levels[level - 2]
    field = weight * rhs
    if level == LEVELS - 1:
        for _ in range(BOTTOM - 1):
            field = sweep(field, rhs, weight, faces, step)
        return field
    for _ in range(SWEEPS - 1):
        field = sweep(field, rhs, weight, faces, step)
    remain = rhs - diag * field + pull(field, faces, step)
    correction = coarse_cycle(level + 1, 0.125 * halve(remain, -1, step), levels)
    field = field + double(correction, step)
    for _ in range(SWEEPS):
        field = sweep(field, rhs, weight, faces, step)
    return field


def up_kernel(counts, where_ref, gathered, level1, *refs):
    kept, weight, rhs, bx, by, bz = zip(refs[0:12:2], refs[1:12:2])
    out, whole, second, spread_m, spread_h, field_m, field_h, half_m, half_h = refs[12:]
    gx, gy, gz = counts
    at_x, at_y, at_z = position(where_ref)
    sx, sy, sz = out.shape
    x1, y1 = sx // 2, sy // 2
    x2, y2, z2 = x1 // 2, y1 // 2, sz // 4
    columns = max(LANES, gz * z2)
    lane = lane_of((y2, LANES))

    for a in range(5):
        for i in range(gx):
            for j in range(gy):
                for x in range(x2):
                    for part in range(columns // LANES):
                        total = jnp.zeros((y2, LANES), F32)
                        for k in range(LANES // z2):
                            column = part * (LANES // z2) + k
                            if column < gz:
                                block = gathered[(i * gy + j) * gz + column, a]
                                mask = (lane >= k * z2) & (lane < (k + 1) * z2)
                                total = jnp.where(mask, turn(block, (k - x) * z2, 1), total)
                        whole[
                            a, i * x2 + x, j * y2:(j + 1) * y2, part * LANES:(part + 1) * LANES
                        ] = total
    levels = coarse_levels(whole[1], (whole[2], whole[3], whole[4]), gy * y2, gz * z2)
    correction = coarse_cycle(2, whole[0], levels)

    wide = gx * x2
    half = NEAR // 2
    ex1, ey1 = x1 + 2 * NEAR, y1 + 2 * NEAR
    second[:half] = jnp.zeros((half,) + correction.shape[1:], F32)
    second[half:half + wide] = correction
    second[half + wide:] = jnp.zeros((half,) + correction.shape[1:], F32)
    window = second[pl.ds(at_x * x2, x2 + NEAR)]
    rows = correction.shape[1]
    row = iota2((ey1, rows), 0)
    col = iota2((ey1, rows), 1)
    place = jnp.where(row < y1 + NEAR, row, row - ey1)
    table_y = (col == at_y * y2 + lax.shift_right_arithmetic(place, 1)).astype(F32)
    row = iota2((columns, LANES), 0)
    col = iota2((columns, LANES), 1)
    place = jnp.where(col < LANES * 3 // 4, col, col - LANES)
    table_z = (row == at_z * z2 + lax.shift_right_arithmetic(place, 1)).astype(F32)
    flat = times_table(window.reshape((x2 + NEAR) * rows, columns), table_z)
    blocks = [table_times(table_y, flat[i * rows:(i + 1) * rows])[None] for i in range(x2 + NEAR)]
    lifted = jnp.concatenate([blocks[i // 2] for i in range(ex1)], axis=0)
    field1, rhs1, weight1 = level1[0], level1[1], level1[2]
    faces1 = (level1[3], level1[4], level1[5])
    field1 = field1 + jnp.where(weight1 > 0.0, lifted, 0.0)
    for _ in range(SWEEPS):
        field1 = sweep(field1, rhs1, weight1, faces1)

    ex, ey = sx + 2 * HALO, sy + 2 * HALO
    near = field1[NEAR - 1:NEAR + x1 + 1].reshape((x1 + 2) * ey1, LANES)
    row = iota2((LANES, 2 * LANES), 0)
    col = iota2((LANES, 2 * LANES), 1)
    lifted = times_table(near, (col // 2 == row).astype(F32))
    quarter = NEAR // 2
    for k, spread in enumerate((spread_m, spread_h)):
        block = lifted[:, k * LANES:(k + 1) * LANES].reshape(x1 + 2, ey1, LANES)
        for i in range(x1 + 2):
            for q in range(2):
                spread[i, pl.ds(q, y1, stride=2), :] = block[i, :y1]
                spread[i, pl.ds(sy + q, quarter, stride=2), :] = block[i, y1:y1 + quarter]
                spread[i, pl.ds(sy + HALO + q, quarter, stride=2), :] = block[i, ey1 - quarter:]
    before, after = (field_m, field_h), (half_m, half_h)
    first = HALO - 2
    for x in range(first, ex - first):
        for k, spread in enumerate((spread_m, spread_h)):
            before[k][x] = kept[k][x] + spread[(x - first) // 2]

    lane = lane_of((ey, LANES))

    def sweep_out(x):
        centre, around = pull_slab(before, bx, by, bz, x, lane)
        for k in range(2):
            after[k][x] = KEEP * centre[k] + weight[k][x] * (rhs[k][x] + around[k])

    each(first + 1, ex - first - 1, 4, sweep_out)

    def sweep_own(x):
        centre, around = pull_slab(after, bx, by, bz, x, lane)
        value = KEEP * centre[0] + weight[0][x] * (rhs[0][x] + around[0])
        out[x - HALO] = value[:sy]

    each(HALO, ex - HALO, 4, sweep_own)


def run(kernel, outs, where, arrays, scratch=(), grant=16):
    return pl.pallas_call(
        kernel,
        out_shape=tuple(jax.ShapeDtypeStruct(shape, F32) for shape in outs),
        in_specs=[SM] + [VM] * len(arrays),
        out_specs=tuple(VM for _ in outs),
        scratch_shapes=[pltpu.VMEM(shape, F32) for shape in scratch],
        compiler_params=pltpu.CompilerParams(vmem_limit_bytes=grant * 1024 * 1024),
    )(where, *arrays)


def swaps(axis, sends):
    count = lax.axis_size(axis)
    got = []
    for k, block in reversed(list(enumerate(sends))):
        pairs = [(i, i + 1) for i in range(k, count - 1, 2)]
        pairs = [pair for low, high in pairs for pair in ((low, high), (high, low))]
        got.append(lax.ppermute(block, axis, pairs))
    return got[::-1]


def local(initial, right_side, alpha, beta_x, beta_y, beta_z):
    axes = ("gx", "gy", "gz")
    counts = tuple(lax.axis_size(axis) for axis in axes)
    devices = counts[0] * counts[1] * counts[2]
    where = (lax.axis_index("gx") * STRIDE + lax.axis_index("gy")) * STRIDE + lax.axis_index("gz")
    where = where.astype(jnp.int32).reshape(1)
    ins = (initial, right_side, alpha, beta_x, beta_y, beta_z)
    sx, sy, sz = initial.shape
    n_x = 1 if counts[0] == 2 else 2
    ex, ey = sx + 2 * HALO, sy + 2 * HALO
    fine = (ex, ey, LANES)

    sends = run(pack_z_kernel, [(sx // 2, sy, LANES)] * 2, where, ins, grant=60)
    got = swaps("gz", sends)
    zpack, *sends = run(
        functools.partial(face_x_kernel, counts),
        [(sx, sy, LANES)] + [(7, HALO, sy, LANES)] * n_x,
        where,
        ins + tuple(got),
    )
    ins = ins + (zpack,)
    got_x = swaps("gx", sends)
    sends = run(
        functools.partial(face_y_kernel, counts),
        [(7, ex, HALO, LANES)] * 2,
        where,
        ins + tuple(got_x),
    )
    two_y, one_y = swaps("gy", sends[::-1])[::-1]
    x1, y1 = sx // 2, sy // 2
    ring, coarse2, *outs = run(
        functools.partial(down_kernel, counts),
        [(5, x1, y1, LANES), (4, y1 // 2, LANES)] + [(5, NEAR, y1, LANES)] * n_x + [fine] * 12,
        where,
        ins + tuple(got_x) + (two_y, one_y),
        [fine] * 9 + [(7, x1, y1, 2 * LANES), (ey, LANES), (4, x1, y1, LANES)],
        24,
    )
    sends, fine_arrays = outs[:n_x], outs[n_x:]

    near_x = swaps("gx", sends)
    sends = run(
        functools.partial(near_y_kernel, counts),
        [(5, x1 + 2 * NEAR, NEAR, LANES)] * 2,
        where,
        (ring,) + tuple(near_x),
    )
    near_y = swaps("gy", sends[::-1])[::-1]
    copies, level1 = run(
        functools.partial(near_kernel, counts, devices),
        [(devices, 5, y1 // 2, LANES), (6, x1 + 2 * NEAR, y1 + 2 * NEAR, LANES)],
        where,
        (ring,) + tuple(near_x) + tuple(near_y) + (coarse2,),
        [(x1, y1 + 2 * NEAR, LANES)],
    )

    gathered = lax.all_to_all(copies, axes, 0, 0, tiled=True)
    wide, rows = counts[0] * x1 // 2, counts[1] * y1 // 2
    columns = max(LANES, counts[2] * sz // 4)
    (result,) = run(
        functools.partial(up_kernel, counts),
        [(sx, sy, sz)],
        where,
        (gathered, level1) + tuple(fine_arrays),
        [(5, wide, rows, columns), (wide + NEAR, rows, columns)]
        + [(x1 + 2, ey, LANES)] * 2
        + [fine] * 4,
        24,
    )
    return result


def solution(mesh):
    spec = P("gx", "gy", "gz")
    return jax.shard_map(
        local, mesh=mesh, in_specs=(spec,) * 6, out_specs=spec, check_vma=False
    )
```

```python
import functools

import jax
import jax.numpy as jnp
from jax import lax
from jax.experimental import pallas as pl
from jax.experimental.pallas import tpu as pltpu
from jax.sharding import PartitionSpec as P

LEVELS = 6
SWEEPS = 2
BOTTOM = 8
WEIGHT = 0.25 ** (LEVELS - 1)
RELAX = 2.0 / 3.0
KEEP = 1.0 / 3.0

HALO = 4
NEAR = 4
LANES = 128
PLACE = (0, 11, 21, 31, 41, 51)
DEPTH = (11, 10, 10, 10, 10, 11)
SIDE = LANES // 2
STRIDE = 256

VM = pl.BlockSpec(memory_space=pltpu.VMEM)
SM = pl.BlockSpec(memory_space=pltpu.SMEM)
F32 = jnp.float32


def position(where_ref):
    code = where_ref[0]
    return code // (STRIDE * STRIDE), code // STRIDE % STRIDE, code % STRIDE


def lane_of(shape):
    return lax.broadcasted_iota(jnp.int32, shape, len(shape) - 1)


def pick(flag, yes, no):
    return jnp.where(jnp.full(yes.shape, flag, jnp.int32) == 1, yes, no)


def neighbours(axis_size, odd, one, two):
    if axis_size == 2:
        two = jnp.zeros_like(one)
    return pick(odd, one, two), pick(odd, two, one)


def turn(values, shift, axis):
    return pltpu.roll(values, shift % values.shape[axis], axis)


def parts_of(values):
    high = values.astype(jnp.bfloat16)
    rest = values - high.astype(F32)
    middle = rest.astype(jnp.bfloat16)
    low = (rest - middle.astype(F32)).astype(jnp.bfloat16)
    return high, middle, low


def times_table(values, table):
    table = table.astype(jnp.bfloat16)
    total = None
    for part in reversed(parts_of(values)):
        term = jnp.dot(part, table, preferred_element_type=F32)
        total = term if total is None else total + term
    return total


def table_times(table, values):
    table = table.astype(jnp.bfloat16)
    total = None
    for part in reversed(parts_of(values)):
        term = jnp.dot(table, part, preferred_element_type=F32)
        total = term if total is None else total + term
    return total


def iota2(shape, axis):
    return lax.broadcasted_iota(jnp.int32, shape, axis)


def pair_table(rows, cols, odd):
    row = iota2((rows, cols), 0)
    col = iota2((rows, cols), 1)
    hit = (row == 2 * col + 1) if odd else (row // 2 == col)
    return hit.astype(F32)


def below_x(values):
    if values.shape[0] == 1:
        return jnp.zeros_like(values)
    return jnp.concatenate([jnp.zeros_like(values[:1]), values[:-1]], axis=0)


def above_x(values):
    if values.shape[0] == 1:
        return jnp.zeros_like(values)
    return jnp.concatenate([values[1:], jnp.zeros_like(values[:1])], axis=0)


def pull(values, faces, step=1):
    bx, by, bz = faces
    total = bx * above_x(values) + below_x(bx * values)
    total = total + (by * turn(values, -step, 1) + turn(by * values, step, 1))
    return total + (bz * turn(values, -step, 2) + turn(bz * values, step, 2))


def diagonal(mass, faces, coupled, step=1):
    bx, by, bz = faces
    _, cy, cz = coupled
    return mass + bx + below_x(bx) + by + turn(cy, step, 1) + bz + turn(cz, step, 2)


def relaxer(mass, diag):
    inside = mass > 0.0
    return jnp.where(inside, RELAX / jnp.where(inside, diag, 1.0), 0.0)


def sweep(values, rhs, weight, faces, step=1):
    return KEEP * values + weight * (rhs + pull(values, faces, step))


def pack_z_kernel(where_ref, *refs):
    ins, (first, second) = refs[:6], refs[6:]
    odd = position(where_ref)[2] % 2
    sx, sy, sz = ins[0].shape
    half = sx // 2
    lane = lane_of((half, sy, LANES))
    head = jnp.zeros((half, sy, LANES), F32)
    tail = head
    for a, ref in enumerate(ins):
        for g in range(2):
            values = ref[g * half:(g + 1) * half]
            at = SIDE * g + PLACE[a]
            mask = (lane >= at) & (lane < at + DEPTH[a])
            head = jnp.where(mask, turn(values, at, 2), head)
            tail = jnp.where(mask, turn(values, at + DEPTH[a], 2), tail)
    first[...] = pick(odd, head, tail)
    second[...] = pick(odd, tail, head)


def face_x_kernel(counts, where_ref, *refs):
    ins, one_ref, two_ref = refs[:6], refs[6], refs[7]
    zpack, sends = refs[8], refs[9:]
    sx, sy, sz = ins[0].shape
    half = sx // 2
    below, above = neighbours(counts[2], position(where_ref)[2] % 2, one_ref[...], two_ref[...])
    lane = lane_of(below.shape)
    zpack[:half] = jnp.where(lane < SIDE, above, turn(below, SIDE, 2))
    zpack[half:] = jnp.where(lane < SIDE, turn(above, SIDE, 2), below)
    odd = position(where_ref)[0] % 2
    for k, send in enumerate(sends):
        start = (1 - odd if k == 0 else odd) * (sx - HALO)
        for a, ref in enumerate(tuple(ins) + (zpack,)):
            send[a] = ref[pl.ds(start, HALO)]


def face_y_kernel(counts, where_ref, *refs):
    ins, halos, sends = refs[:7], refs[7:-2], refs[:-3:-1]
    sx, sy, sz = ins[0].shape
    odd_x, odd = (place % 2 for place in position(where_ref)[:2])
    for a, ref in enumerate(ins):
        below, above = neighbours(counts[0], odd_x, halos[0][a], halos[-1][a])
        for at, block in ((0, below), (HALO, ref[...]), (HALO + sx, above)):
            head, tail = block[:, :HALO], block[:, sy - HALO:]
            span = slice(at, at + block.shape[0])
            sends[0][a, span] = pick(odd, head, tail)
            sends[1][a, span] = pick(odd, tail, head)


def each(first, last, step, body):
    rounds = (last - first) // step

    def go(i, carry):
        for j in range(step):
            body(first + i * step + j)
        return carry

    if rounds:
        lax.fori_loop(0, rounds, go, 0)
    for x in range(first + rounds * step, last):
        body(x)


def ring_up(main, halo, lane):
    main_up, halo_up = turn(main, -1, 1), turn(halo, -1, 1)
    last = lane == LANES - 1
    return jnp.where(last, halo_up, main_up), jnp.where(last, main_up, halo_up)


def ring_down(main, halo, lane):
    main_down, halo_down = turn(main, 1, 1), turn(halo, 1, 1)
    zero = lane == 0
    return jnp.where(zero, halo_down, main_down), jnp.where(zero, main_down, halo_down)


def pull_slab(field, bx, by, bz, x, lane):
    centre = [half[x] for half in field]
    out = []
    for k in range(2):
        c, face = centre[k], by[k][x]
        t = bx[k][x] * field[k][x + 1] + bx[k][x - 1] * field[k][x - 1]
        out.append(t + (face * turn(c, -1, 0) + turn(face * c, 1, 0)))
    faces = [half[x] for half in bz]
    ups = ring_up(centre[0], centre[1], lane)
    downs = ring_down(faces[0] * centre[0], faces[1] * centre[1], lane)
    return centre, [out[k] + (faces[k] * ups[k] + downs[k]) for k in range(2)]


def unpacked(packed, a, lane):
    at, depth = PLACE[a], DEPTH[a]
    axis = packed.ndim - 1
    right, left = turn(packed, -at, axis), turn(packed, SIDE - depth - at, axis)
    return jnp.where(lane < depth, right, jnp.where(lane >= LANES - depth, left, 0.0))


def rows_of(source, x, firsts, seconds):
    total = None
    for p in firsts:
        for q in seconds:
            term = source[x + p, pl.ds(q, source.shape[1] // 2, stride=2), :]
            total = term if total is None else total + term
    return total


BOTH, ODD = (0, 1), (1,)


def to_level1(sums, first, count, table, factor):
    _, x1, y1, _ = sums.shape
    flat = sums[first:first + count].reshape(count * x1 * y1, 2 * LANES)
    return factor * times_table(flat, table).reshape(count, x1, y1, LANES)


def coefficient_kernel(counts, devices, where_ref, *refs):
    ins, refs = refs[2:7], refs[7:]
    n_x = 1 if counts[0] == 2 else 2
    halos_x, (copies, coeffs1, halo, sums, pairing) = refs[:n_x], refs[n_x:]
    sx, sy, sz = ins[0].shape
    odd_x = position(where_ref)[0] % 2
    x1, y1 = sx // 2, sy // 2
    lane = lane_of((sx, sy, LANES))
    lanes = [slice(k * LANES, (k + 1) * LANES) for k in range(2)]
    edge_lane = lane_of((1, sy, LANES))
    below, _ = neighbours(counts[0], odd_x, halos_x[0][3, HALO - 1:], halos_x[-1][3, HALO - 1:])
    packed, _ = neighbours(counts[0], odd_x, halos_x[0][6, HALO - 1:], halos_x[-1][6, HALO - 1:])
    for k, edge in enumerate((below, unpacked(packed, 3, edge_lane))):
        halo[k, 0:1] = edge
        sums[4, 0, :, lanes[k]] = rows_of(halo.at[k], 0, (0,), BOTH)
    for n, (firsts, seconds) in enumerate(((BOTH, BOTH), (ODD, BOTH), (BOTH, ODD), (BOTH, BOTH))):
        halo[0] = unpacked(ins[4][...], n + 2, lane)
        for i in range(x1):
            sums[n, i, :, lanes[0]] = rows_of(ins[n], 2 * i, firsts, seconds)
            sums[n, i, :, lanes[1]] = rows_of(halo.at[0], 2 * i, firsts, seconds)
    pairs = pair_table(2 * LANES, LANES, False)
    odds = pair_table(2 * LANES, LANES, True)
    paired = to_level1(sums, 0, 3, pairs, 0.0625)
    mass1 = (2.0 * WEIGHT) * paired[0]
    faces1 = (paired[1], paired[2], to_level1(sums, 3, 1, odds, 0.0625)[0])
    edge = 0.0625 * times_table(sums[4, 0], pairs)[None]
    diag1 = mass1 + faces1[0] + jnp.concatenate([edge, faces1[0][:-1]], axis=0)
    diag1 = diag1 + faces1[1] + faces1[2] + turn(faces1[2], 1, 2)
    for n, values in enumerate((mass1, diag1) + faces1):
        coeffs1[n] = values
    parts = (
        (mass1, False, False, False, 0.125),
        (faces1[0], True, False, False, 0.0625),
        (faces1[1], False, True, False, 0.0625),
        (faces1[2], False, False, True, 0.0625),
    )
    for n, (values, *odd_axes, factor) in enumerate(parts):
        pairing[n] = values
        packed = level2_rows(pairing.at[n], odd_axes, factor, x1 // 2, y1 // 2, sz // 4)
        for d in range(devices):
            copies[d, n] = packed


def down_kernel(counts, where_ref, *refs):
    ins, refs = refs[:7], refs[7:]
    n_x = 1 if counts[0] == 2 else 2
    halos_x = refs[:n_x]
    two_y, one_y, coeffs1, own1 = refs[n_x:4 + n_x]
    sends, refs = refs[4 + n_x:4 + 2 * n_x], refs[4 + 2 * n_x:]
    kept_m, kept_h, weight_m, weight_h = refs[:4]
    faces_out, scratch = refs[4:12], refs[12:]
    rhs, bx, by, bz = zip(faces_out[::2], faces_out[1::2])
    field, alpha = scratch[:2], scratch[2:4]
    packs, half_m, half_h, diag_m, diag_h, sums, left = scratch[4:]
    arrays = (field, rhs, alpha, bx, by, bz)
    sx, sy, sz = ins[0].shape
    ex, ey = sx + 2 * HALO, sy + 2 * HALO
    odd_x, odd_y = (place % 2 for place in position(where_ref)[:2])

    for a in range(7):
        to = packs if a == 6 else arrays[a][0]
        below, above = neighbours(counts[0], odd_x, halos_x[0][a], halos_x[-1][a])
        to[:HALO, :sy] = below
        to[HALO:HALO + sx, :sy] = ins[a][...]
        to[HALO + sx:, :sy] = above
        below, above = neighbours(counts[1], odd_y, one_y[a], two_y[a])
        to[:, sy:] = jnp.concatenate([above, below], axis=1)
    lane = lane_of((ey, LANES))

    def unpack(x):
        packed = packs[x]
        for a in range(6):
            arrays[a][1][x] = unpacked(packed, a, lane)

    each(0, ex, 4, unpack)
    halfway, weight, kept = (half_m, half_h), (weight_m, weight_h), (kept_m, kept_h)
    diag = (diag_m, diag_h)

    def first_sweep(x):
        faces = [half[x] for half in bz]
        downs = ring_down(faces[0], faces[1], lane)
        centre, near = pull_slab(field, bx, by, bz, x, lane)
        for k in range(2):
            face = by[k][x]
            mass = WEIGHT * alpha[k][x]
            d = mass + bx[k][x] + bx[k][x - 1] + face + turn(face, 1, 0) + faces[k] + downs[k]
            w = relaxer(mass, d)
            diag[k][x] = d
            weight[k][x] = w
            halfway[k][x] = KEEP * centre[k] + w * (rhs[k][x] + near[k])

    each(1, ex - 1, 4, first_sweep)

    def second_sweep(x):
        centre, near = pull_slab(halfway, bx, by, bz, x, lane)
        for k in range(2):
            kept[k][x] = KEEP * centre[k] + weight[k][x] * (rhs[k][x] + near[k])

    each(2, ex - 2, 4, second_sweep)

    def residual(x):
        centre, near = pull_slab(kept, bx, by, bz, x, lane)
        for k in range(2):
            halfway[k][x] = rhs[k][x] - diag[k][x] * centre[k] + near[k]

    each(HALO, ex - HALO, 4, residual)

    x1, y1 = sx // 2, sy // 2
    for k in range(2):
        lanes = slice(k * LANES, (k + 1) * LANES)
        for i in range(x1):
            x = HALO + 2 * i
            total = None
            for p in BOTH:
                for q in BOTH:
                    term = halfway[k][x + p, pl.ds(q, y1, stride=2), :]
                    total = term if total is None else total + term
            sums[0, i, :, lanes] = total
            left[...] = turn(by[k][x] + by[k][x + 1], 1, 0)
            sums[1, i, :, lanes] = left[pl.ds(0, y1, stride=2), :]
    rhs1, low_y = to_level1(sums, 0, 2, pair_table(2 * LANES, LANES, False), 0.0625)
    weight1 = relaxer(coeffs1[0], coeffs1[1] + low_y)
    for n, values in enumerate((2.0 * rhs1, weight1, coeffs1[2], coeffs1[3], coeffs1[4])):
        own1[n] = values
        head, tail = values[:NEAR], values[x1 - NEAR:]
        for k, send in enumerate(sends):
            send[n] = pick(odd_x, head, tail) if k == 0 else pick(odd_x, tail, head)


def level2_rows(source, odd_axes, factor, x2, y2, z2):
    rows = []
    for i in range(x2):
        total = None
        for p in (1,) if odd_axes[0] else (0, 1):
            for q in (1,) if odd_axes[1] else (0, 1):
                term = source[2 * i + p, pl.ds(q, y2, stride=2), :]
                total = term if total is None else total + term
        rows.append(total)
    flat = jnp.concatenate(rows, axis=0)
    flat = factor * times_table(flat, pair_table(LANES, LANES, odd_axes[2]))
    lane = lane_of((y2, LANES))
    packed = jnp.zeros((y2, LANES), F32)
    for i in range(x2):
        mask = (lane >= i * z2) & (lane < (i + 1) * z2)
        packed = jnp.where(mask, turn(flat[i * y2:(i + 1) * y2], i * z2, 1), packed)
    return packed


def near_y_kernel(counts, where_ref, ring, *refs):
    refs = refs[:-3] + refs[-2:]
    halos, sends = refs[:-2], refs[:-3:-1]
    n, bx, by, _ = ring.shape
    odd_x, odd = (place % 2 for place in position(where_ref)[:2])
    for a in range(n):
        below, above = neighbours(counts[0], odd_x, halos[0][a], halos[-1][a])
        block = jnp.concatenate([below, ring[a], above], axis=0)
        head, tail = block[:, :NEAR], block[:, by - NEAR:]
        sends[0][a] = pick(odd, head, tail)
        sends[1][a] = pick(odd, tail, head)


def near_kernel(counts, devices, where_ref, ring, *refs):
    n_x = 1 if counts[0] == 2 else 2
    halos_x = refs[:n_x]
    two_y, one_y, copies, level1, left = refs[n_x:]
    n, bx1, by1, _ = ring.shape
    odd_x, odd_y = (place % 2 for place in position(where_ref)[:2])
    whole = []
    for a in range(n):
        below, above = neighbours(counts[0], odd_x, halos_x[0][a], halos_x[-1][a])
        block = jnp.concatenate([below, ring[a], above], axis=0)
        below, above = neighbours(counts[1], odd_y, one_y[a], two_y[a])
        whole.append(jnp.concatenate([block, above, below], axis=1))
    rhs1, weight1 = whole[:2]
    faces1 = tuple(whole[2:])
    field1 = weight1 * rhs1
    field1 = sweep(field1, rhs1, weight1, faces1)
    for a, values in enumerate([field1] + whole):
        level1[a] = values
    mine = slice(NEAR, NEAR + bx1)
    inner = weight1[mine]
    diag1 = RELAX / jnp.where(inner > 0.0, inner, 1.0)
    remain = rhs1[mine] - diag1 * field1[mine] + pull(field1, faces1)[mine]
    left[...] = remain
    packed = level2_rows(left, (False,) * 3, 0.125, bx1 // 2, by1 // 2, LANES // 4)
    for d in range(devices):
        copies[d] = packed


def halve(values, odd_axis, step):
    half = values.shape[0] // 2
    even = [values[2 * i:2 * i + 1] for i in range(half)]
    odd = [values[2 * i + 1:2 * i + 2] for i in range(half)]
    if odd_axis != 0:
        odd = [a + b for a, b in zip(even, odd)]
    values = jnp.concatenate(odd, axis=0)
    for axis in (1, 2):
        next_one = turn(values, -step, axis)
        values = next_one if odd_axis == axis else values + next_one
    return values


def double(values, step):
    values = values + turn(values, step, 1)
    values = values + turn(values, step, 2)
    return jnp.concatenate([values[i // 2:i // 2 + 1] for i in range(2 * values.shape[0])], axis=0)


def coarse_levels(mass, faces, y, z):
    levels = []
    for level in range(2, LEVELS):
        step = 2 ** (level - 2)
        bx, by, bz = faces
        row = lax.broadcasted_iota(jnp.int32, by.shape, 1)
        lane = lane_of(bz.shape)
        coupled = (
            bx,
            jnp.where(row == (y - 1) * step, 0.0, by),
            jnp.where(lane == (z - 1) * step, 0.0, bz),
        )
        mass = jnp.where((row % step == 0) & (lane % step == 0), mass, 0.0)
        diag = diagonal(mass, faces, coupled, step)
        levels.append((diag, relaxer(mass, diag), coupled))
        if level < LEVELS - 1:
            faces = tuple(0.0625 * halve(face, axis, step) for axis, face in enumerate(faces))
            mass = 0.125 * halve(mass, -1, step)
            y, z = y // 2, z // 2
    return levels


def coarse_cycle(level, rhs, levels):
    step = 2 ** (level - 2)
    diag, weight, faces = levels[level - 2]
    field = weight * rhs
    if level == LEVELS - 1:
        for _ in range(BOTTOM - 1):
            field = sweep(field, rhs, weight, faces, step)
        return field
    for _ in range(SWEEPS - 1):
        field = sweep(field, rhs, weight, faces, step)
    remain = rhs - diag * field + pull(field, faces, step)
    correction = coarse_cycle(level + 1, 0.125 * halve(remain, -1, step), levels)
    field = field + double(correction, step)
    for _ in range(SWEEPS):
        field = sweep(field, rhs, weight, faces, step)
    return field


def spread_out(counts, slots, whole):
    gx, gy, gz = counts
    y2 = slots.shape[-2]
    x2 = whole.shape[0] // gx
    z2 = LANES // x2
    lane = lane_of((y2, LANES))
    for i in range(gx):
        for j in range(gy):
            for x in range(x2):
                for part in range(whole.shape[2] // LANES):
                    total = jnp.zeros((y2, LANES), F32)
                    for k in range(LANES // z2):
                        column = part * (LANES // z2) + k
                        if column < gz:
                            block = slots[(i * gy + j) * gz + column]
                            mask = (lane >= k * z2) & (lane < (k + 1) * z2)
                            total = jnp.where(mask, turn(block, (k - x) * z2, 1), total)
                    lanes = slice(part * LANES, (part + 1) * LANES)
                    whole[i * x2 + x, j * y2:(j + 1) * y2, lanes] = total


def coarse_kernel(counts, gathered, *refs):
    outs, whole = refs[:-1], refs[-1]
    y2 = gathered.shape[2]
    z2 = LANES * counts[0] // whole.shape[1]
    for a in range(4):
        spread_out(counts, gathered.at[:, a], whole.at[a])
    faces = (whole[1], whole[2], whole[3])
    levels = coarse_levels(whole[0], faces, counts[1] * y2, counts[2] * z2)
    for out, (diag, weight, coupled) in zip(outs, levels):
        for n, values in enumerate((diag, weight) + coupled):
            out[n] = values


def up_kernel(counts, where_ref, gathered, level1, *refs):
    kept, weight, rhs, bx, by, bz = zip(refs[0:12:2], refs[1:12:2])
    depth = LEVELS - 2
    coarse, refs = refs[12:12 + depth], refs[12 + depth:]
    out, whole, second, spread_m, spread_h, field_m, field_h, half_m, half_h = refs
    gx, gy, gz = counts
    at_x, at_y, at_z = position(where_ref)
    sx, sy, sz = out.shape
    x1, y1 = sx // 2, sy // 2
    x2, y2, z2 = x1 // 2, y1 // 2, sz // 4
    columns = max(LANES, gz * z2)
    spread_out(counts, gathered, whole)
    levels = [(ref[0], ref[1], (ref[2], ref[3], ref[4])) for ref in coarse]
    correction = coarse_cycle(2, whole[...], levels)

    wide = gx * x2
    half = NEAR // 2
    ex1, ey1 = x1 + 2 * NEAR, y1 + 2 * NEAR
    second[:half] = jnp.zeros((half,) + correction.shape[1:], F32)
    second[half:half + wide] = correction
    second[half + wide:] = jnp.zeros((half,) + correction.shape[1:], F32)
    window = second[pl.ds(at_x * x2, x2 + NEAR)]
    rows = correction.shape[1]
    row = iota2((ey1, rows), 0)
    col = iota2((ey1, rows), 1)
    place = jnp.where(row < y1 + NEAR, row, row - ey1)
    table_y = (col == at_y * y2 + lax.shift_right_arithmetic(place, 1)).astype(F32)
    row = iota2((columns, LANES), 0)
    col = iota2((columns, LANES), 1)
    place = jnp.where(col < LANES * 3 // 4, col, col - LANES)
    table_z = (row == at_z * z2 + lax.shift_right_arithmetic(place, 1)).astype(F32)
    flat = times_table(window.reshape((x2 + NEAR) * rows, columns), table_z)
    blocks = [table_times(table_y, flat[i * rows:(i + 1) * rows])[None] for i in range(x2 + NEAR)]
    lifted = jnp.concatenate([blocks[i // 2] for i in range(ex1)], axis=0)
    field1, rhs1, weight1 = level1[0], level1[1], level1[2]
    faces1 = (level1[3], level1[4], level1[5])
    field1 = field1 + jnp.where(weight1 > 0.0, lifted, 0.0)
    for _ in range(SWEEPS):
        field1 = sweep(field1, rhs1, weight1, faces1)

    ex, ey = sx + 2 * HALO, sy + 2 * HALO
    near = field1[NEAR - 1:NEAR + x1 + 1].reshape((x1 + 2) * ey1, LANES)
    row = iota2((LANES, 2 * LANES), 0)
    col = iota2((LANES, 2 * LANES), 1)
    lifted = times_table(near, (col // 2 == row).astype(F32))
    quarter = NEAR // 2
    for k, spread in enumerate((spread_m, spread_h)):
        block = lifted[:, k * LANES:(k + 1) * LANES].reshape(x1 + 2, ey1, LANES)
        for i in range(x1 + 2):
            for q in range(2):
                spread[i, pl.ds(q, y1, stride=2), :] = block[i, :y1]
                spread[i, pl.ds(sy + q, quarter, stride=2), :] = block[i, y1:y1 + quarter]
                spread[i, pl.ds(sy + HALO + q, quarter, stride=2), :] = block[i, ey1 - quarter:]
    before, after = (field_m, field_h), (half_m, half_h)
    first = HALO - 2
    for x in range(first, ex - first):
        for k, spread in enumerate((spread_m, spread_h)):
            before[k][x] = kept[k][x] + spread[(x - first) // 2]

    lane = lane_of((ey, LANES))

    def sweep_out(x):
        centre, around = pull_slab(before, bx, by, bz, x, lane)
        for k in range(2):
            after[k][x] = KEEP * centre[k] + weight[k][x] * (rhs[k][x] + around[k])

    each(first + 1, ex - first - 1, 4, sweep_out)

    def sweep_own(x):
        centre, around = pull_slab(after, bx, by, bz, x, lane)
        value = KEEP * centre[0] + weight[0][x] * (rhs[0][x] + around[0])
        out[x - HALO] = value[:sy]

    each(HALO, ex - HALO, 4, sweep_own)


def run(kernel, outs, where, arrays, scratch=(), grant=16, micros=1):
    return pl.pallas_call(
        kernel,
        out_shape=tuple(jax.ShapeDtypeStruct(shape, F32) for shape in outs),
        in_specs=[SM] * len(where) + [VM] * len(arrays),
        out_specs=tuple(VM for _ in outs),
        scratch_shapes=[pltpu.VMEM(shape, F32) for shape in scratch],
        compiler_params=pltpu.CompilerParams(vmem_limit_bytes=grant * 1024 * 1024),
        cost_estimate=pl.CostEstimate(
            flops=0, bytes_accessed=int(micros * 3.6e6), transcendentals=0
        ),
    )(*where, *arrays)


def swaps(axis, sends):
    count = lax.axis_size(axis)
    got = []
    for k, block in reversed(list(enumerate(sends))):
        pairs = [(i, i + 1) for i in range(k, count - 1, 2)]
        pairs = [pair for low, high in pairs for pair in ((low, high), (high, low))]
        got.append(lax.ppermute(block, axis, pairs))
    return got[::-1]


def local(initial, right_side, alpha, beta_x, beta_y, beta_z):
    axes = ("gx", "gy", "gz")
    counts = tuple(lax.axis_size(axis) for axis in axes)
    devices = counts[0] * counts[1] * counts[2]
    where = (lax.axis_index("gx") * STRIDE + lax.axis_index("gy")) * STRIDE + lax.axis_index("gz")
    where = (where.astype(jnp.int32).reshape(1),)
    ins = (initial, right_side, alpha, beta_x, beta_y, beta_z)
    sx, sy, sz = initial.shape
    n_x = 1 if counts[0] == 2 else 2
    ex, ey = sx + 2 * HALO, sy + 2 * HALO
    fine = (ex, ey, LANES)

    sends = run(pack_z_kernel, [(sx // 2, sy, LANES)] * 2, where, ins, grant=60)
    got = swaps("gz", sends)
    zpack, *sends = run(
        functools.partial(face_x_kernel, counts),
        [(sx, sy, LANES)] + [(7, HALO, sy, LANES)] * n_x,
        where,
        ins + tuple(got),
    )
    ins = ins + (zpack,)
    got_x = swaps("gx", sends)
    sends = run(
        functools.partial(face_y_kernel, counts),
        [(7, ex, HALO, LANES)] * 2,
        where,
        ins + tuple(got_x),
    )
    two_y, one_y = swaps("gy", sends[::-1])[::-1]
    x1, y1 = sx // 2, sy // 2
    copies, coeffs1 = run(
        functools.partial(coefficient_kernel, counts, devices),
        [(devices, 4, y1 // 2, LANES), (5, x1, y1, LANES)],
        where,
        ins + tuple(got_x),
        [(2, sx, sy, LANES), (5, x1, y1, 2 * LANES), (4, x1, y1, LANES)],
        micros=2,
    )
    gathered = lax.all_to_all(copies, axes, 0, 0, tiled=True)
    ring, *outs = run(
        functools.partial(down_kernel, counts),
        [(5, x1, y1, LANES)] + [(5, NEAR, y1, LANES)] * n_x + [fine] * 12,
        where,
        ins + tuple(got_x) + (two_y, one_y, coeffs1),
        [fine] * 9 + [(2, x1, y1, 2 * LANES), (ey, LANES)],
        24,
        micros=4,
    )
    sends, fine_arrays = outs[:n_x], outs[n_x:]

    near_x = swaps("gx", sends)
    sends = run(
        functools.partial(near_y_kernel, counts),
        [(5, x1 + 2 * NEAR, NEAR, LANES)] * 2,
        where,
        (ring,) + tuple(near_x) + (gathered,),
    )
    near_y = swaps("gy", sends[::-1])[::-1]
    copies, level1 = run(
        functools.partial(near_kernel, counts, devices),
        [(devices, y1 // 2, LANES), (6, x1 + 2 * NEAR, y1 + 2 * NEAR, LANES)],
        where,
        (ring,) + tuple(near_x) + tuple(near_y),
        [(x1, y1 + 2 * NEAR, LANES)],
    )

    wide, rows = counts[0] * x1 // 2, counts[1] * y1 // 2
    columns = max(LANES, counts[2] * sz // 4)
    levels = run(
        functools.partial(coarse_kernel, counts),
        [(5, wide >> n, rows, columns) for n in range(LEVELS - 2)],
        (),
        (gathered,),
        [(4, wide, rows, columns)],
        micros=2,
    )
    gathered = lax.all_to_all(copies, axes, 0, 0, tiled=True)
    (result,) = run(
        functools.partial(up_kernel, counts),
        [(sx, sy, sz)],
        where,
        (gathered, level1) + tuple(fine_arrays) + tuple(levels),
        [(wide, rows, columns), (wide + NEAR, rows, columns)]
        + [(x1 + 2, ey, LANES)] * 2
        + [fine] * 4,
        24,
        micros=4,
    )
    return result


def solution(mesh):
    spec = P("gx", "gy", "gz")
    return jax.shard_map(
        local, mesh=mesh, in_specs=(spec,) * 6, out_specs=spec, check_vma=False
    )
```

```python
import functools

import jax
import jax.numpy as jnp
from jax import lax
from jax.experimental import pallas as pl
from jax.experimental.pallas import tpu as pltpu
from jax.sharding import PartitionSpec as P

LEVELS = 6
SWEEPS = 2
BOTTOM = 8
WEIGHT = 0.25 ** (LEVELS - 1)
RELAX = 2.0 / 3.0
KEEP = 1.0 / 3.0

HALO = 4
NEAR = 4
LANES = 128
PLACE = (0, 11, 21, 31, 41, 51)
DEPTH = (11, 10, 10, 10, 10, 11)
SIDE = LANES // 2
STRIDE = 256

VM = pl.BlockSpec(memory_space=pltpu.VMEM)
SM = pl.BlockSpec(memory_space=pltpu.SMEM)
F32 = jnp.float32


def position(where_ref):
    code = where_ref[0]
    return code // (STRIDE * STRIDE), code // STRIDE % STRIDE, code % STRIDE


def lane_of(shape):
    return lax.broadcasted_iota(jnp.int32, shape, len(shape) - 1)


def pick(flag, yes, no):
    return jnp.where(jnp.full(yes.shape, flag, jnp.int32) == 1, yes, no)


def neighbours(axis_size, odd, one, two):
    if axis_size == 2:
        two = jnp.zeros_like(one)
    return pick(odd, one, two), pick(odd, two, one)


def turn(values, shift, axis):
    return pltpu.roll(values, shift % values.shape[axis], axis)


def parts_of(values):
    high = values.astype(jnp.bfloat16)
    rest = values - high.astype(F32)
    middle = rest.astype(jnp.bfloat16)
    low = (rest - middle.astype(F32)).astype(jnp.bfloat16)
    return high, middle, low


def times_table(values, table):
    table = table.astype(jnp.bfloat16)
    total = None
    for part in reversed(parts_of(values)):
        term = jnp.dot(part, table, preferred_element_type=F32)
        total = term if total is None else total + term
    return total


def table_times(table, values):
    table = table.astype(jnp.bfloat16)
    total = None
    for part in reversed(parts_of(values)):
        term = jnp.dot(table, part, preferred_element_type=F32)
        total = term if total is None else total + term
    return total


def iota2(shape, axis):
    return lax.broadcasted_iota(jnp.int32, shape, axis)


def pair_table(rows, cols, odd):
    row = iota2((rows, cols), 0)
    col = iota2((rows, cols), 1)
    hit = (row == 2 * col + 1) if odd else (row // 2 == col)
    return hit.astype(F32)


def below_x(values):
    if values.shape[0] == 1:
        return jnp.zeros_like(values)
    return jnp.concatenate([jnp.zeros_like(values[:1]), values[:-1]], axis=0)


def above_x(values):
    if values.shape[0] == 1:
        return jnp.zeros_like(values)
    return jnp.concatenate([values[1:], jnp.zeros_like(values[:1])], axis=0)


def pull(values, faces, step=1):
    bx, by, bz = faces
    total = bx * above_x(values) + below_x(bx * values)
    total = total + (by * turn(values, -step, 1) + turn(by * values, step, 1))
    return total + (bz * turn(values, -step, 2) + turn(bz * values, step, 2))


def diagonal(mass, faces, coupled, step=1):
    bx, by, bz = faces
    _, cy, cz = coupled
    return mass + bx + below_x(bx) + by + turn(cy, step, 1) + bz + turn(cz, step, 2)


def relaxer(mass, diag):
    inside = mass > 0.0
    return jnp.where(inside, RELAX / jnp.where(inside, diag, 1.0), 0.0)


def sweep(values, rhs, weight, faces, step=1):
    return KEEP * values + weight * (rhs + pull(values, faces, step))


def faces_x(values, odd, n_x, width):
    head, tail = values[:, :width], values[:, values.shape[1] - width:]
    return [pick(odd, head, tail), pick(odd, tail, head)][:n_x]


def faces_y(values, odd, width):
    head, tail = values[:, :width], values[:, values.shape[1] - width:]
    return pick(odd, head, tail), pick(odd, tail, head)


def corner_sends(below, above, odd, corners):
    packs = []
    for rows, sign in ((slice(0, 8), 1), (slice(below.shape[1] - 8, below.shape[1]), -1)):
        low = [below[3 - i, rows] for i in range(4)]
        high = [above[i, rows] for i in range(4)]
        pack = []
        if corners:
            pack = [low[0], high[0]]
            low, high = low[1:], high[1:]
        row = iota2(low[0].shape, 0)
        row = row if sign == 1 else 7 - row
        pack += [
            jnp.where(row < 3, low[0], turn(low[2], 3 * sign, 0)),
            jnp.where(row < 2, low[1], turn(high[1], 2 * sign, 0)),
            jnp.where(row < 3, high[0], turn(high[2], 3 * sign, 0)),
        ]
        packs.append([p[:4] if sign == 1 else p[4:] for p in pack])
    return [(pick(odd, h, t), pick(odd, t, h)) for h, t in zip(*packs)]


def corner_tiles(tiles):
    first, second, third = tiles[-3:]
    upper = iota2(first.shape, 0) < 4

    def inner(tile, by):
        return jnp.where(upper, turn(tile, -by, 0), turn(tile, by, 0))

    low = [first, second, inner(first, 3)]
    high = [third, inner(second, 2), inner(third, 3)]
    if len(tiles) == 5:
        low, high = tiles[:1] + low, tiles[1:2] + high
    else:
        zero = jnp.zeros_like(first)
        low, high = low + [zero], high + [zero]
    return low[::-1], high


def faces_kernel(counts, where_ref, *refs):
    ins, refs = refs[:6], refs[6:]
    n_x = 1 if counts[0] == 2 else 2
    sends_x, (two_y, one_y, first, second) = refs[:n_x], refs[n_x:]
    odd_x, odd_y, odd = (place % 2 for place in position(where_ref))
    sx, sy, sz = ins[0].shape
    half = sx // 2
    lane = lane_of((half, sy, LANES))
    head = jnp.zeros((half, sy, LANES), F32)
    tail = head
    for a, ref in enumerate(ins):
        for send, face in zip(sends_x, faces_x(ref[...][None], odd_x, n_x, HALO)):
            send[a] = face[0]
        one_y[a], two_y[a] = faces_y(ref[...], odd_y, HALO)
        for g in range(2):
            values = ref[g * half:(g + 1) * half]
            at = SIDE * g + PLACE[a]
            mask = (lane >= at) & (lane < at + DEPTH[a])
            head = jnp.where(mask, turn(values, at, 2), head)
            tail = jnp.where(mask, turn(values, at + DEPTH[a], 2), tail)
    first[...] = pick(odd, head, tail)
    second[...] = pick(odd, tail, head)


def halo_z_kernel(counts, where_ref, one_ref, two_ref, zpack, *sends):
    odd_x, _, odd = (place % 2 for place in position(where_ref))
    half = one_ref.shape[0]
    below, above = neighbours(counts[2], odd, one_ref[...], two_ref[...])
    lane = lane_of(below.shape)
    zpack[:half] = jnp.where(lane < SIDE, above, turn(below, SIDE, 2))
    zpack[half:] = jnp.where(lane < SIDE, turn(above, SIDE, 2), below)
    for send, face in zip(sends, faces_x(zpack[...][None], odd_x, len(sends), HALO)):
        send[...] = face[0]


def corners_kernel(counts, where_ref, zpack, *refs):
    n_x = 1 if counts[0] == 2 else 2
    main_x, halos_x, (two_y, one_y) = refs[:n_x], refs[n_x:2 * n_x], refs[2 * n_x:]
    odd_x, odd = (place % 2 for place in position(where_ref)[:2])
    for a in range(7):
        if a < 6:
            below, above = neighbours(counts[0], odd_x, main_x[0][a], main_x[-1][a])
        else:
            below, above = neighbours(counts[0], odd_x, halos_x[0][...], halos_x[-1][...])
        for n, pair in enumerate(corner_sends(below, above, odd, False)):
            one_y[3 * a + n], two_y[3 * a + n] = pair
    one_y[21:], two_y[21:] = faces_y(zpack[...], odd, HALO)


def each(first, last, step, body):
    rounds = (last - first) // step

    def go(i, carry):
        for j in range(step):
            body(first + i * step + j)
        return carry

    if rounds:
        lax.fori_loop(0, rounds, go, 0)
    for x in range(first + rounds * step, last):
        body(x)


def ring_up(main, halo, lane):
    main_up, halo_up = turn(main, -1, 1), turn(halo, -1, 1)
    last = lane == LANES - 1
    return jnp.where(last, halo_up, main_up), jnp.where(last, main_up, halo_up)


def ring_down(main, halo, lane):
    main_down, halo_down = turn(main, 1, 1), turn(halo, 1, 1)
    zero = lane == 0
    return jnp.where(zero, halo_down, main_down), jnp.where(zero, main_down, halo_down)


def pull_slab(field, bx, by, bz, x, lane):
    centre = [half[x] for half in field]
    out = []
    for k in range(2):
        c, face = centre[k], by[k][x]
        t = bx[k][x] * field[k][x + 1] + bx[k][x - 1] * field[k][x - 1]
        out.append(t + (face * turn(c, -1, 0) + turn(face * c, 1, 0)))
    faces = [half[x] for half in bz]
    ups = ring_up(centre[0], centre[1], lane)
    downs = ring_down(faces[0] * centre[0], faces[1] * centre[1], lane)
    return centre, [out[k] + (faces[k] * ups[k] + downs[k]) for k in range(2)]


def unpacked(packed, a, lane):
    at, depth = PLACE[a], DEPTH[a]
    axis = packed.ndim - 1
    right, left = turn(packed, -at, axis), turn(packed, SIDE - depth - at, axis)
    return jnp.where(lane < depth, right, jnp.where(lane >= LANES - depth, left, 0.0))


def rows_of(source, x, firsts, seconds):
    total = None
    for p in firsts:
        for q in seconds:
            term = source[x + p, pl.ds(q, source.shape[1] // 2, stride=2), :]
            total = term if total is None else total + term
    return total


BOTH, ODD = (0, 1), (1,)


def to_level1(sums, first, count, table, factor):
    _, x1, y1, _ = sums.shape
    flat = sums[first:first + count].reshape(count * x1 * y1, 2 * LANES)
    return factor * times_table(flat, table).reshape(count, x1, y1, LANES)


def coefficient_kernel(counts, where_ref, *refs):
    ins, refs = refs[2:7], refs[7:]
    n_x = 1 if counts[0] == 2 else 2
    main_x, halos_x = refs[:n_x], refs[n_x:2 * n_x]
    coarse2, coeffs1, halo, sums, pairing = refs[2 * n_x:]
    sx, sy, sz = ins[0].shape
    odd_x = position(where_ref)[0] % 2
    x1, y1 = sx // 2, sy // 2
    lane = lane_of((sx, sy, LANES))
    lanes = [slice(k * LANES, (k + 1) * LANES) for k in range(2)]
    edge_lane = lane_of((1, sy, LANES))
    last = slice(HALO - 1, HALO)
    below, _ = neighbours(counts[0], odd_x, main_x[0][3, last], main_x[-1][3, last])
    packed, _ = neighbours(counts[0], odd_x, halos_x[0][last], halos_x[-1][last])
    for k, edge in enumerate((below, unpacked(packed, 3, edge_lane))):
        halo[k, 0:1] = edge
        sums[4, 0, :, lanes[k]] = rows_of(halo.at[k], 0, (0,), BOTH)
    for n, (firsts, seconds) in enumerate(((BOTH, BOTH), (ODD, BOTH), (BOTH, ODD), (BOTH, BOTH))):
        halo[0] = unpacked(ins[4][...], n + 2, lane)
        for i in range(x1):
            sums[n, i, :, lanes[0]] = rows_of(ins[n], 2 * i, firsts, seconds)
            sums[n, i, :, lanes[1]] = rows_of(halo.at[0], 2 * i, firsts, seconds)
    pairs = pair_table(2 * LANES, LANES, False)
    odds = pair_table(2 * LANES, LANES, True)
    paired = to_level1(sums, 0, 3, pairs, 0.0625)
    mass1 = (2.0 * WEIGHT) * paired[0]
    faces1 = (paired[1], paired[2], to_level1(sums, 3, 1, odds, 0.0625)[0])
    edge = 0.0625 * times_table(sums[4, 0], pairs)[None]
    diag1 = mass1 + faces1[0] + jnp.concatenate([edge, faces1[0][:-1]], axis=0)
    diag1 = diag1 + faces1[1] + faces1[2] + turn(faces1[2], 1, 2)
    for n, values in enumerate((mass1, diag1) + faces1):
        coeffs1[n] = values
    parts = (
        (mass1, False, False, False, 0.125),
        (faces1[0], True, False, False, 0.0625),
        (faces1[1], False, True, False, 0.0625),
        (faces1[2], False, False, True, 0.0625),
    )
    for n, (values, *odd_axes, factor) in enumerate(parts):
        pairing[n] = values
        coarse2[n] = level2_rows(pairing.at[n], odd_axes, factor, x1 // 2, y1 // 2, sz // 4)


def down_kernel(counts, where_ref, *refs):
    ins, refs = refs[:7], refs[7:]
    n_x = 1 if counts[0] == 2 else 2
    main_x, halos_x = refs[:n_x], refs[n_x:2 * n_x]
    main_two, main_one, rest_two, rest_one, coeffs1, own1 = refs[2 * n_x:6 + 2 * n_x]
    refs = refs[6 + 2 * n_x:]
    sends, near_two, near_one, refs = refs[:n_x], refs[n_x], refs[n_x + 1], refs[n_x + 2:]
    kept_m, kept_h, weight_m, weight_h = refs[:4]
    faces_out, scratch = refs[4:12], refs[12:]
    rhs, bx, by, bz = zip(faces_out[::2], faces_out[1::2])
    field, alpha = scratch[:2], scratch[2:4]
    packs, half_m, half_h, diag_m, diag_h, sums, left = scratch[4:]
    arrays = (field, rhs, alpha, bx, by, bz)
    sx, sy, sz = ins[0].shape
    ex, ey = sx + 2 * HALO, sy + 2 * HALO
    odd_x, odd_y = (place % 2 for place in position(where_ref)[:2])

    rest = neighbours(counts[1], odd_y, rest_one[...], rest_two[...])
    rest = jnp.concatenate(rest[::-1], axis=1)
    for a in range(7):
        if a < 6:
            to = arrays[a][0]
            below, above = neighbours(counts[0], odd_x, main_x[0][a], main_x[-1][a])
            rows = neighbours(counts[1], odd_y, main_one[a], main_two[a])
            rows = jnp.concatenate(rows[::-1], axis=1)
        else:
            to = packs
            below, above = neighbours(counts[0], odd_x, halos_x[0][...], halos_x[-1][...])
            rows = rest[21:]
        to[:HALO, :sy] = below
        to[HALO:HALO + sx, :sy] = ins[a][...]
        to[HALO + sx:, :sy] = above
        to[HALO:HALO + sx, sy:] = rows
        low, high = corner_tiles([rest[3 * a + n] for n in range(3)])
        for n in range(HALO):
            to[n, sy:] = low[n]
            to[HALO + sx + n, sy:] = high[n]
    lane = lane_of((ey, LANES))

    def unpack(x):
        packed = packs[x]
        for a in range(6):
            arrays[a][1][x] = unpacked(packed, a, lane)

    each(0, ex, 4, unpack)
    halfway, weight, kept = (half_m, half_h), (weight_m, weight_h), (kept_m, kept_h)
    diag = (diag_m, diag_h)

    def first_sweep(x):
        faces = [half[x] for half in bz]
        downs = ring_down(faces[0], faces[1], lane)
        centre, near = pull_slab(field, bx, by, bz, x, lane)
        for k in range(2):
            face = by[k][x]
            mass = WEIGHT * alpha[k][x]
            d = mass + bx[k][x] + bx[k][x - 1] + face + turn(face, 1, 0) + faces[k] + downs[k]
            w = relaxer(mass, d)
            diag[k][x] = d
            weight[k][x] = w
            halfway[k][x] = KEEP * centre[k] + w * (rhs[k][x] + near[k])

    each(1, ex - 1, 4, first_sweep)

    def second_sweep(x):
        centre, near = pull_slab(halfway, bx, by, bz, x, lane)
        for k in range(2):
            kept[k][x] = KEEP * centre[k] + weight[k][x] * (rhs[k][x] + near[k])

    each(2, ex - 2, 4, second_sweep)

    def residual(x):
        centre, near = pull_slab(kept, bx, by, bz, x, lane)
        for k in range(2):
            halfway[k][x] = rhs[k][x] - diag[k][x] * centre[k] + near[k]

    each(HALO, ex - HALO, 4, residual)

    x1, y1 = sx // 2, sy // 2
    for k in range(2):
        lanes = slice(k * LANES, (k + 1) * LANES)
        for i in range(x1):
            x = HALO + 2 * i
            total = None
            for p in BOTH:
                for q in BOTH:
                    term = halfway[k][x + p, pl.ds(q, y1, stride=2), :]
                    total = term if total is None else total + term
            sums[0, i, :, lanes] = total
            left[...] = turn(by[k][x] + by[k][x + 1], 1, 0)
            sums[1, i, :, lanes] = left[pl.ds(0, y1, stride=2), :]
    rhs1, low_y = to_level1(sums, 0, 2, pair_table(2 * LANES, LANES, False), 0.0625)
    weight1 = relaxer(coeffs1[0], coeffs1[1] + low_y)
    for n, values in enumerate((2.0 * rhs1, weight1, coeffs1[2], coeffs1[3], coeffs1[4])):
        own1[n] = values
        for send, face in zip(sends, faces_x(values[None], odd_x, n_x, NEAR)):
            send[n] = face[0]
        near_one[n], near_two[n] = faces_y(values, odd_y, NEAR)


def level2_rows(source, odd_axes, factor, x2, y2, z2):
    rows = []
    for i in range(x2):
        total = None
        for p in (1,) if odd_axes[0] else (0, 1):
            for q in (1,) if odd_axes[1] else (0, 1):
                term = source[2 * i + p, pl.ds(q, y2, stride=2), :]
                total = term if total is None else total + term
        rows.append(total)
    flat = jnp.concatenate(rows, axis=0)
    flat = factor * times_table(flat, pair_table(LANES, LANES, odd_axes[2]))
    lane = lane_of((y2, LANES))
    packed = jnp.zeros((y2, LANES), F32)
    for i in range(x2):
        mask = (lane >= i * z2) & (lane < (i + 1) * z2)
        packed = jnp.where(mask, turn(flat[i * y2:(i + 1) * y2], i * z2, 1), packed)
    return packed


def near_corners_kernel(counts, where_ref, *refs):
    halos_x, (two_y, one_y) = refs[:-2], refs[-2:]
    odd_x, odd = (place % 2 for place in position(where_ref)[:2])
    for a in range(halos_x[0].shape[0]):
        below, above = neighbours(counts[0], odd_x, halos_x[0][a], halos_x[-1][a])
        for n, pair in enumerate(corner_sends(below, above, odd, True)):
            one_y[5 * a + n], two_y[5 * a + n] = pair


def near_kernel(counts, devices, where_ref, ring, *refs):
    n_x = 1 if counts[0] == 2 else 2
    halos_x = refs[:n_x]
    main_two, main_one, rest_two, rest_one, coarse2, copies, level1, left = refs[n_x:]
    n, bx1, by1, _ = ring.shape
    odd_x, odd_y = (place % 2 for place in position(where_ref)[:2])
    rest = neighbours(counts[1], odd_y, rest_one[...], rest_two[...])
    rest = jnp.concatenate(rest[::-1], axis=1)
    whole = []
    for a in range(n):
        below, above = neighbours(counts[0], odd_x, halos_x[0][a], halos_x[-1][a])
        rows = neighbours(counts[1], odd_y, main_one[a], main_two[a])
        rows = jnp.concatenate(rows[::-1], axis=1)
        low, high = corner_tiles([rest[5 * a + k] for k in range(5)])
        rows = jnp.concatenate(
            [tile[None] for tile in low] + [rows] + [tile[None] for tile in high], axis=0
        )
        block = jnp.concatenate([below, ring[a], above], axis=0)
        whole.append(jnp.concatenate([block, rows], axis=1))
    rhs1, weight1 = whole[:2]
    faces1 = tuple(whole[2:])
    field1 = weight1 * rhs1
    field1 = sweep(field1, rhs1, weight1, faces1)
    for a, values in enumerate([field1] + whole):
        level1[a] = values
    mine = slice(NEAR, NEAR + bx1)
    inner = weight1[mine]
    diag1 = RELAX / jnp.where(inner > 0.0, inner, 1.0)
    remain = rhs1[mine] - diag1 * field1[mine] + pull(field1, faces1)[mine]
    left[...] = remain
    packed = level2_rows(left, (False,) * 3, 0.125, bx1 // 2, by1 // 2, LANES // 4)
    for d in range(devices):
        copies[d, 0] = packed
        for a in range(n - 1):
            copies[d, a + 1] = coarse2[a]


def halve(values, odd_axis, step):
    half = values.shape[0] // 2
    even = [values[2 * i:2 * i + 1] for i in range(half)]
    odd = [values[2 * i + 1:2 * i + 2] for i in range(half)]
    if odd_axis != 0:
        odd = [a + b for a, b in zip(even, odd)]
    values = jnp.concatenate(odd, axis=0)
    for axis in (1, 2):
        next_one = turn(values, -step, axis)
        values = next_one if odd_axis == axis else values + next_one
    return values


def double(values, step):
    values = values + turn(values, step, 1)
    values = values + turn(values, step, 2)
    return jnp.concatenate([values[i // 2:i // 2 + 1] for i in range(2 * values.shape[0])], axis=0)


def coarse_levels(mass, faces, y, z):
    levels = []
    for level in range(2, LEVELS):
        step = 2 ** (level - 2)
        bx, by, bz = faces
        row = lax.broadcasted_iota(jnp.int32, by.shape, 1)
        lane = lane_of(bz.shape)
        coupled = (
            bx,
            jnp.where(row == (y - 1) * step, 0.0, by),
            jnp.where(lane == (z - 1) * step, 0.0, bz),
        )
        mass = jnp.where((row % step == 0) & (lane % step == 0), mass, 0.0)
        diag = diagonal(mass, faces, coupled, step)
        levels.append((diag, relaxer(mass, diag), coupled))
        if level < LEVELS - 1:
            faces = tuple(0.0625 * halve(face, axis, step) for axis, face in enumerate(faces))
            mass = 0.125 * halve(mass, -1, step)
            y, z = y // 2, z // 2
    return levels


def coarse_cycle(level, rhs, levels):
    step = 2 ** (level - 2)
    diag, weight, faces = levels[level - 2]
    field = weight * rhs
    if level == LEVELS - 1:
        for _ in range(BOTTOM - 1):
            field = sweep(field, rhs, weight, faces, step)
        return field
    for _ in range(SWEEPS - 1):
        field = sweep(field, rhs, weight, faces, step)
    remain = rhs - diag * field + pull(field, faces, step)
    correction = coarse_cycle(level + 1, 0.125 * halve(remain, -1, step), levels)
    field = field + double(correction, step)
    for _ in range(SWEEPS):
        field = sweep(field, rhs, weight, faces, step)
    return field


def spread_out(counts, slots, whole):
    gx, gy, gz = counts
    y2 = slots.shape[-2]
    x2 = whole.shape[0] // gx
    z2 = LANES // x2
    lane = lane_of((y2, LANES))
    for i in range(gx):
        for j in range(gy):
            for x in range(x2):
                for part in range(whole.shape[2] // LANES):
                    total = jnp.zeros((y2, LANES), F32)
                    for k in range(LANES // z2):
                        column = part * (LANES // z2) + k
                        if column < gz:
                            block = slots[(i * gy + j) * gz + column]
                            mask = (lane >= k * z2) & (lane < (k + 1) * z2)
                            total = jnp.where(mask, turn(block, (k - x) * z2, 1), total)
                    lanes = slice(part * LANES, (part + 1) * LANES)
                    whole[i * x2 + x, j * y2:(j + 1) * y2, lanes] = total


def up_kernel(counts, where_ref, gathered, level1, *refs):
    kept, weight, rhs, bx, by, bz = zip(refs[0:12:2], refs[1:12:2])
    out, whole, second, spread_m, spread_h, field_m, field_h, half_m, half_h = refs[12:]
    gx, gy, gz = counts
    at_x, at_y, at_z = position(where_ref)
    sx, sy, sz = out.shape
    x1, y1 = sx // 2, sy // 2
    x2, y2, z2 = x1 // 2, y1 // 2, sz // 4
    columns = max(LANES, gz * z2)
    for a in range(5):
        spread_out(counts, gathered.at[:, a], whole.at[a])
    levels = coarse_levels(whole[1], (whole[2], whole[3], whole[4]), gy * y2, gz * z2)
    correction = coarse_cycle(2, whole[0], levels)

    wide = gx * x2
    half = NEAR // 2
    ex1, ey1 = x1 + 2 * NEAR, y1 + 2 * NEAR
    second[:half] = jnp.zeros((half,) + correction.shape[1:], F32)
    second[half:half + wide] = correction
    second[half + wide:] = jnp.zeros((half,) + correction.shape[1:], F32)
    window = second[pl.ds(at_x * x2, x2 + NEAR)]
    rows = correction.shape[1]
    row = iota2((ey1, rows), 0)
    col = iota2((ey1, rows), 1)
    place = jnp.where(row < y1 + NEAR, row, row - ey1)
    table_y = (col == at_y * y2 + lax.shift_right_arithmetic(place, 1)).astype(F32)
    row = iota2((columns, LANES), 0)
    col = iota2((columns, LANES), 1)
    place = jnp.where(col < LANES * 3 // 4, col, col - LANES)
    table_z = (row == at_z * z2 + lax.shift_right_arithmetic(place, 1)).astype(F32)
    flat = times_table(window.reshape((x2 + NEAR) * rows, columns), table_z)
    blocks = [table_times(table_y, flat[i * rows:(i + 1) * rows])[None] for i in range(x2 + NEAR)]
    lifted = jnp.concatenate([blocks[i // 2] for i in range(ex1)], axis=0)
    field1, rhs1, weight1 = level1[0], level1[1], level1[2]
    faces1 = (level1[3], level1[4], level1[5])
    field1 = field1 + jnp.where(weight1 > 0.0, lifted, 0.0)
    for _ in range(SWEEPS):
        field1 = sweep(field1, rhs1, weight1, faces1)

    ex, ey = sx + 2 * HALO, sy + 2 * HALO
    near = field1[NEAR - 1:NEAR + x1 + 1].reshape((x1 + 2) * ey1, LANES)
    row = iota2((LANES, 2 * LANES), 0)
    col = iota2((LANES, 2 * LANES), 1)
    lifted = times_table(near, (col // 2 == row).astype(F32))
    quarter = NEAR // 2
    for k, spread in enumerate((spread_m, spread_h)):
        block = lifted[:, k * LANES:(k + 1) * LANES].reshape(x1 + 2, ey1, LANES)
        for i in range(x1 + 2):
            for q in range(2):
                spread[i, pl.ds(q, y1, stride=2), :] = block[i, :y1]
                spread[i, pl.ds(sy + q, quarter, stride=2), :] = block[i, y1:y1 + quarter]
                spread[i, pl.ds(sy + HALO + q, quarter, stride=2), :] = block[i, ey1 - quarter:]
    before, after = (field_m, field_h), (half_m, half_h)
    first = HALO - 2
    for x in range(first, ex - first):
        for k, spread in enumerate((spread_m, spread_h)):
            before[k][x] = kept[k][x] + spread[(x - first) // 2]

    lane = lane_of((ey, LANES))

    def sweep_out(x):
        centre, around = pull_slab(before, bx, by, bz, x, lane)
        for k in range(2):
            after[k][x] = KEEP * centre[k] + weight[k][x] * (rhs[k][x] + around[k])

    each(first + 1, ex - first - 1, 4, sweep_out)

    def sweep_own(x):
        centre, around = pull_slab(after, bx, by, bz, x, lane)
        value = KEEP * centre[0] + weight[0][x] * (rhs[0][x] + around[0])
        out[x - HALO] = value[:sy]

    each(HALO, ex - HALO, 4, sweep_own)


def run(kernel, outs, where, arrays, scratch=(), grant=16, micros=1):
    return pl.pallas_call(
        kernel,
        out_shape=tuple(jax.ShapeDtypeStruct(shape, F32) for shape in outs),
        in_specs=[SM] * len(where) + [VM] * len(arrays),
        out_specs=tuple(VM for _ in outs),
        scratch_shapes=[pltpu.VMEM(shape, F32) for shape in scratch],
        compiler_params=pltpu.CompilerParams(vmem_limit_bytes=grant * 1024 * 1024),
        cost_estimate=pl.CostEstimate(
            flops=0, bytes_accessed=int(micros * 3.6e6), transcendentals=0
        ),
    )(*where, *arrays)


def swaps(axis, sends):
    count = lax.axis_size(axis)
    got = []
    for k, block in reversed(list(enumerate(sends))):
        pairs = [(i, i + 1) for i in range(k, count - 1, 2)]
        pairs = [pair for low, high in pairs for pair in ((low, high), (high, low))]
        got.append(lax.ppermute(block, axis, pairs))
    return got[::-1]


def local(initial, right_side, alpha, beta_x, beta_y, beta_z):
    axes = ("gx", "gy", "gz")
    counts = tuple(lax.axis_size(axis) for axis in axes)
    devices = counts[0] * counts[1] * counts[2]
    where = (lax.axis_index("gx") * STRIDE + lax.axis_index("gy")) * STRIDE + lax.axis_index("gz")
    where = (where.astype(jnp.int32).reshape(1),)
    ins = (initial, right_side, alpha, beta_x, beta_y, beta_z)
    sx, sy, sz = initial.shape
    n_x = 1 if counts[0] == 2 else 2
    ex, ey = sx + 2 * HALO, sy + 2 * HALO
    fine = (ex, ey, LANES)

    *sends_x, two_y, one_y, first, second = run(
        functools.partial(faces_kernel, counts),
        [(6, HALO, sy, LANES)] * n_x
        + [(6, sx, HALO, LANES)] * 2
        + [(sx // 2, sy, LANES)] * 2,
        where,
        ins,
        grant=60,
    )
    main_x = tuple(swaps("gx", sends_x))
    main_y = tuple(swaps("gy", (one_y, two_y))[::-1])
    got = swaps("gz", (first, second))
    zpack, *sends = run(
        functools.partial(halo_z_kernel, counts),
        [(sx, sy, LANES)] + [(HALO, sy, LANES)] * n_x,
        where,
        tuple(got),
    )
    halos_x = tuple(swaps("gx", sends))
    two_y, one_y = run(
        functools.partial(corners_kernel, counts),
        [(21 + sx, HALO, LANES)] * 2,
        where,
        (zpack,) + main_x + halos_x,
    )
    rest_y = tuple(swaps("gy", (one_y, two_y))[::-1])
    x1, y1 = sx // 2, sy // 2
    ins = ins + (zpack,)
    coarse2, coeffs1 = run(
        functools.partial(coefficient_kernel, counts),
        [(4, y1 // 2, LANES), (5, x1, y1, LANES)],
        where,
        ins + main_x + halos_x,
        [(2, sx, sy, LANES), (5, x1, y1, 2 * LANES), (4, x1, y1, LANES)],
        micros=2,
    )
    own1, *outs = run(
        functools.partial(down_kernel, counts),
        [(5, x1, y1, LANES)]
        + [(5, NEAR, y1, LANES)] * n_x
        + [(5, x1, NEAR, LANES)] * 2
        + [fine] * 12,
        where,
        ins + main_x + halos_x + main_y + rest_y + (coeffs1,),
        [fine] * 9 + [(2, x1, y1, 2 * LANES), (ey, LANES)],
        24,
        micros=4,
    )
    sends_x, (two_y, one_y), fine_arrays = outs[:n_x], outs[n_x:n_x + 2], outs[n_x + 2:]

    near_x = tuple(swaps("gx", sends_x))
    near_y = tuple(swaps("gy", (one_y, two_y))[::-1])
    two_y, one_y = run(
        functools.partial(near_corners_kernel, counts), [(25, NEAR, LANES)] * 2, where, near_x
    )
    rest_y = tuple(swaps("gy", (one_y, two_y))[::-1])
    copies, level1 = run(
        functools.partial(near_kernel, counts, devices),
        [(devices, 5, y1 // 2, LANES), (6, x1 + 2 * NEAR, y1 + 2 * NEAR, LANES)],
        where,
        (own1,) + near_x + near_y + rest_y + (coarse2,),
        [(x1, y1 + 2 * NEAR, LANES)],
    )

    gathered = lax.all_to_all(copies, axes, 0, 0, tiled=True)
    wide, rows = counts[0] * x1 // 2, counts[1] * y1 // 2
    columns = max(LANES, counts[2] * sz // 4)
    (result,) = run(
        functools.partial(up_kernel, counts),
        [(sx, sy, sz)],
        where,
        (gathered, level1) + tuple(fine_arrays),
        [(5, wide, rows, columns), (wide + NEAR, rows, columns)]
        + [(x1 + 2, ey, LANES)] * 2
        + [fine] * 4,
        24,
        micros=4,
    )
    return result


def solution(mesh):
    spec = P("gx", "gy", "gz")
    return jax.shard_map(
        local, mesh=mesh, in_specs=(spec,) * 6, out_specs=spec, check_vma=False
    )
```

```python
import functools

import jax
import jax.numpy as jnp
from jax import lax
from jax.experimental import pallas as pl
from jax.experimental.pallas import tpu as pltpu
from jax.sharding import PartitionSpec as P

LEVELS = 6
SWEEPS = 2
BOTTOM = 8
WEIGHT = 0.25 ** (LEVELS - 1)
RELAX = 2.0 / 3.0
KEEP = 1.0 / 3.0

HALO = 4
NEAR = 4
LANES = 128
PLACE = (0, 11, 21, 31, 41, 51)
DEPTH = (11, 10, 10, 10, 10, 11)
SIDE = LANES // 2
STRIDE = 256

VM = pl.BlockSpec(memory_space=pltpu.VMEM)
SM = pl.BlockSpec(memory_space=pltpu.SMEM)
F32 = jnp.float32


def position(where_ref):
    code = where_ref[0]
    return code // (STRIDE * STRIDE), code // STRIDE % STRIDE, code % STRIDE


def lane_of(shape):
    return lax.broadcasted_iota(jnp.int32, shape, len(shape) - 1)


def pick(flag, yes, no):
    return jnp.where(jnp.full(yes.shape, flag, jnp.int32) == 1, yes, no)


def neighbours(count, place, one, two):
    if count == 2:
        two = jnp.zeros_like(one)
    else:
        ends = jnp.full(two.shape, place, jnp.int32)
        two = jnp.where((ends == 0) | (ends == count - 1), 0.0, two)
    return pick(place % 2, one, two), pick(place % 2, two, one)


def turn(values, shift, axis):
    return pltpu.roll(values, shift % values.shape[axis], axis)


def parts_of(values):
    high = values.astype(jnp.bfloat16)
    rest = values - high.astype(F32)
    middle = rest.astype(jnp.bfloat16)
    low = (rest - middle.astype(F32)).astype(jnp.bfloat16)
    return high, middle, low


def times_table(values, table):
    table = table.astype(jnp.bfloat16)
    total = None
    for part in reversed(parts_of(values)):
        term = jnp.dot(part, table, preferred_element_type=F32)
        total = term if total is None else total + term
    return total


def table_times(table, values):
    table = table.astype(jnp.bfloat16)
    total = None
    for part in reversed(parts_of(values)):
        term = jnp.dot(table, part, preferred_element_type=F32)
        total = term if total is None else total + term
    return total


def iota2(shape, axis):
    return lax.broadcasted_iota(jnp.int32, shape, axis)


def pair_table(rows, cols, odd):
    row = iota2((rows, cols), 0)
    col = iota2((rows, cols), 1)
    hit = (row == 2 * col + 1) if odd else (row // 2 == col)
    return hit.astype(F32)


def below_x(values):
    if values.shape[0] == 1:
        return jnp.zeros_like(values)
    return jnp.concatenate([jnp.zeros_like(values[:1]), values[:-1]], axis=0)


def above_x(values):
    if values.shape[0] == 1:
        return jnp.zeros_like(values)
    return jnp.concatenate([values[1:], jnp.zeros_like(values[:1])], axis=0)


def pull(values, faces, step=1):
    bx, by, bz = faces
    total = bx * above_x(values) + below_x(bx * values)
    total = total + (by * turn(values, -step, 1) + turn(by * values, step, 1))
    return total + (bz * turn(values, -step, 2) + turn(bz * values, step, 2))


def diagonal(mass, faces, coupled, step=1):
    bx, by, bz = faces
    _, cy, cz = coupled
    return mass + bx + below_x(bx) + by + turn(cy, step, 1) + bz + turn(cz, step, 2)


def relaxer(mass, diag):
    inside = mass > 0.0
    return jnp.where(inside, RELAX / jnp.where(inside, diag, 1.0), 0.0)


def sweep(values, rhs, weight, faces, step=1):
    return KEEP * values + weight * (rhs + pull(values, faces, step))


def faces_x(values, odd, n_x, width):
    head, tail = values[:, :width], values[:, values.shape[1] - width:]
    return [pick(odd, head, tail), pick(odd, tail, head)][:n_x]


def faces_y(values, odd, width):
    head, tail = values[:, :width], values[:, values.shape[1] - width:]
    return pick(odd, head, tail), pick(odd, tail, head)


def corner_sends(below, above, odd, corners):
    packs = []
    for rows, sign in ((slice(0, 8), 1), (slice(below.shape[1] - 8, below.shape[1]), -1)):
        low = [below[3 - i, rows] for i in range(4)]
        high = [above[i, rows] for i in range(4)]
        pack = []
        if corners:
            pack = [low[0], high[0]]
            low, high = low[1:], high[1:]
        row = iota2(low[0].shape, 0)
        row = row if sign == 1 else 7 - row
        pack += [
            jnp.where(row < 3, low[0], turn(low[2], 3 * sign, 0)),
            jnp.where(row < 2, low[1], turn(high[1], 2 * sign, 0)),
            jnp.where(row < 3, high[0], turn(high[2], 3 * sign, 0)),
        ]
        packs.append([p[:4] if sign == 1 else p[4:] for p in pack])
    return [(pick(odd, h, t), pick(odd, t, h)) for h, t in zip(*packs)]


def corner_tiles(tiles):
    first, second, third = tiles[-3:]
    upper = iota2(first.shape, 0) < 4

    def inner(tile, by):
        return jnp.where(upper, turn(tile, -by, 0), turn(tile, by, 0))

    low = [first, second, inner(first, 3)]
    high = [third, inner(second, 2), inner(third, 3)]
    if len(tiles) == 5:
        low, high = tiles[:1] + low, tiles[1:2] + high
    else:
        zero = jnp.zeros_like(first)
        low, high = low + [zero], high + [zero]
    return low[::-1], high


def faces_kernel(counts, where_ref, *refs):
    ins, refs = refs[:6], refs[6:]
    n_x = 1 if counts[0] == 2 else 2
    sends_x, (two_y, one_y, first, second) = refs[:n_x], refs[n_x:]
    odd_x, odd_y, odd = (place % 2 for place in position(where_ref))
    sx, sy, sz = ins[0].shape
    half = sx // 2
    lane = lane_of((half, sy, LANES))
    head = jnp.zeros((half, sy, LANES), F32)
    tail = head
    for a, ref in enumerate(ins):
        for send, face in zip(sends_x, faces_x(ref[...][None], odd_x, n_x, HALO)):
            send[a] = face[0]
        one_y[a], two_y[a] = faces_y(ref[...], odd_y, HALO)
        for g in range(2):
            values = ref[g * half:(g + 1) * half]
            at = SIDE * g + PLACE[a]
            mask = (lane >= at) & (lane < at + DEPTH[a])
            head = jnp.where(mask, turn(values, at, 2), head)
            tail = jnp.where(mask, turn(values, at + DEPTH[a], 2), tail)
    first[...] = pick(odd, head, tail)
    second[...] = pick(odd, tail, head)


def halo_z_kernel(counts, where_ref, one_ref, two_ref, zpack, *sends):
    at_x, _, at_z = position(where_ref)
    half = one_ref.shape[0]
    below, above = neighbours(counts[2], at_z, one_ref[...], two_ref[...])
    lane = lane_of(below.shape)
    zpack[:half] = jnp.where(lane < SIDE, above, turn(below, SIDE, 2))
    zpack[half:] = jnp.where(lane < SIDE, turn(above, SIDE, 2), below)
    for send, face in zip(sends, faces_x(zpack[...][None], at_x % 2, len(sends), HALO)):
        send[...] = face[0]


def corners_kernel(counts, where_ref, zpack, *refs):
    n_x = 1 if counts[0] == 2 else 2
    main_x, halos_x, (two_y, one_y) = refs[:n_x], refs[n_x:2 * n_x], refs[2 * n_x:]
    at_x, at_y, _ = position(where_ref)
    for a in range(7):
        if a < 6:
            below, above = neighbours(counts[0], at_x, main_x[0][a], main_x[-1][a])
        else:
            below, above = neighbours(counts[0], at_x, halos_x[0][...], halos_x[-1][...])
        for n, pair in enumerate(corner_sends(below, above, at_y % 2, False)):
            one_y[3 * a + n], two_y[3 * a + n] = pair
    one_y[21:], two_y[21:] = faces_y(zpack[...], at_y % 2, HALO)


def each(first, last, step, body):
    rounds = (last - first) // step

    def go(i, carry):
        for j in range(step):
            body(first + i * step + j)
        return carry

    if rounds:
        lax.fori_loop(0, rounds, go, 0)
    for x in range(first + rounds * step, last):
        body(x)


def ring_up(main, halo, lane):
    main_up, halo_up = turn(main, -1, 1), turn(halo, -1, 1)
    last = lane == LANES - 1
    return jnp.where(last, halo_up, main_up), jnp.where(last, main_up, halo_up)


def ring_down(main, halo, lane):
    main_down, halo_down = turn(main, 1, 1), turn(halo, 1, 1)
    zero = lane == 0
    return jnp.where(zero, halo_down, main_down), jnp.where(zero, main_down, halo_down)


def pull_slab(field, bx, by, bz, x, lane):
    centre = [half[x] for half in field]
    out = []
    for k in range(2):
        c, face = centre[k], by[k][x]
        t = bx[k][x] * field[k][x + 1] + bx[k][x - 1] * field[k][x - 1]
        out.append(t + (face * turn(c, -1, 0) + turn(face * c, 1, 0)))
    faces = [half[x] for half in bz]
    ups = ring_up(centre[0], centre[1], lane)
    downs = ring_down(faces[0] * centre[0], faces[1] * centre[1], lane)
    return centre, [out[k] + (faces[k] * ups[k] + downs[k]) for k in range(2)]


def unpacked(packed, a, lane):
    at, depth = PLACE[a], DEPTH[a]
    axis = packed.ndim - 1
    right, left = turn(packed, -at, axis), turn(packed, SIDE - depth - at, axis)
    return jnp.where(lane < depth, right, jnp.where(lane >= LANES - depth, left, 0.0))


def rows_of(source, x, firsts, seconds):
    total = None
    for p in firsts:
        for q in seconds:
            term = source[x + p, pl.ds(q, source.shape[1] // 2, stride=2), :]
            total = term if total is None else total + term
    return total


BOTH, ODD = (0, 1), (1,)


def to_level1(sums, first, count, table, factor):
    _, x1, y1, _ = sums.shape
    flat = sums[first:first + count].reshape(count * x1 * y1, 2 * LANES)
    return factor * times_table(flat, table).reshape(count, x1, y1, LANES)


def coefficient_kernel(counts, where_ref, *refs):
    ins, refs = refs[2:7], refs[7:]
    n_x = 1 if counts[0] == 2 else 2
    main_x, halos_x = refs[:n_x], refs[n_x:2 * n_x]
    coarse2, coeffs1, halo, sums, pairing = refs[2 * n_x:]
    sx, sy, sz = ins[0].shape
    at_x = position(where_ref)[0]
    x1, y1 = sx // 2, sy // 2
    lane = lane_of((sx, sy, LANES))
    lanes = [slice(k * LANES, (k + 1) * LANES) for k in range(2)]
    edge_lane = lane_of((1, sy, LANES))
    last = slice(HALO - 1, HALO)
    below, _ = neighbours(counts[0], at_x, main_x[0][3, last], main_x[-1][3, last])
    packed, _ = neighbours(counts[0], at_x, halos_x[0][last], halos_x[-1][last])
    for k, edge in enumerate((below, unpacked(packed, 3, edge_lane))):
        halo[k, 0:1] = edge
        sums[4, 0, :, lanes[k]] = rows_of(halo.at[k], 0, (0,), BOTH)
    for n, (firsts, seconds) in enumerate(((BOTH, BOTH), (ODD, BOTH), (BOTH, ODD), (BOTH, BOTH))):
        halo[0] = unpacked(ins[4][...], n + 2, lane)
        for i in range(x1):
            sums[n, i, :, lanes[0]] = rows_of(ins[n], 2 * i, firsts, seconds)
            sums[n, i, :, lanes[1]] = rows_of(halo.at[0], 2 * i, firsts, seconds)
    pairs = pair_table(2 * LANES, LANES, False)
    odds = pair_table(2 * LANES, LANES, True)
    paired = to_level1(sums, 0, 3, pairs, 0.0625)
    mass1 = (2.0 * WEIGHT) * paired[0]
    faces1 = (paired[1], paired[2], to_level1(sums, 3, 1, odds, 0.0625)[0])
    edge = 0.0625 * times_table(sums[4, 0], pairs)[None]
    diag1 = mass1 + faces1[0] + jnp.concatenate([edge, faces1[0][:-1]], axis=0)
    diag1 = diag1 + faces1[1] + faces1[2] + turn(faces1[2], 1, 2)
    for n, values in enumerate((mass1, diag1) + faces1):
        coeffs1[n] = values
    parts = (
        (mass1, False, False, False, 0.125),
        (faces1[0], True, False, False, 0.0625),
        (faces1[1], False, True, False, 0.0625),
        (faces1[2], False, False, True, 0.0625),
    )
    for n, (values, *odd_axes, factor) in enumerate(parts):
        pairing[n] = values
        coarse2[n] = level2_rows(pairing.at[n], odd_axes, factor, x1 // 2, y1 // 2, sz // 4)


def down_kernel(counts, where_ref, *refs):
    ins, refs = refs[:7], refs[7:]
    n_x = 1 if counts[0] == 2 else 2
    main_x, halos_x = refs[:n_x], refs[n_x:2 * n_x]
    main_two, main_one, rest_two, rest_one, coeffs1, own1 = refs[2 * n_x:6 + 2 * n_x]
    refs = refs[6 + 2 * n_x:]
    sends, near_two, near_one, refs = refs[:n_x], refs[n_x], refs[n_x + 1], refs[n_x + 2:]
    kept_m, kept_h, weight_m, weight_h = refs[:4]
    faces_out, scratch = refs[4:12], refs[12:]
    rhs, bx, by, bz = zip(faces_out[::2], faces_out[1::2])
    field, alpha = scratch[:2], scratch[2:4]
    packs, half_m, half_h, diag_m, diag_h, sums, left = scratch[4:]
    arrays = (field, rhs, alpha, bx, by, bz)
    sx, sy, sz = ins[0].shape
    ex, ey = sx + 2 * HALO, sy + 2 * HALO
    at_x, at_y, _ = position(where_ref)

    rest = neighbours(counts[1], at_y, rest_one[...], rest_two[...])
    rest = jnp.concatenate(rest[::-1], axis=1)
    for a in range(7):
        if a < 6:
            to = arrays[a][0]
            below, above = neighbours(counts[0], at_x, main_x[0][a], main_x[-1][a])
            rows = neighbours(counts[1], at_y, main_one[a], main_two[a])
            rows = jnp.concatenate(rows[::-1], axis=1)
        else:
            to = packs
            below, above = neighbours(counts[0], at_x, halos_x[0][...], halos_x[-1][...])
            rows = rest[21:]
        to[:HALO, :sy] = below
        to[HALO:HALO + sx, :sy] = ins[a][...]
        to[HALO + sx:, :sy] = above
        to[HALO:HALO + sx, sy:] = rows
        low, high = corner_tiles([rest[3 * a + n] for n in range(3)])
        for n in range(HALO):
            to[n, sy:] = low[n]
            to[HALO + sx + n, sy:] = high[n]
    lane = lane_of((ey, LANES))

    def unpack(x):
        packed = packs[x]
        for a in range(6):
            arrays[a][1][x] = unpacked(packed, a, lane)

    each(0, ex, 4, unpack)
    halfway, weight, kept = (half_m, half_h), (weight_m, weight_h), (kept_m, kept_h)
    diag = (diag_m, diag_h)

    def first_sweep(x):
        faces = [half[x] for half in bz]
        downs = ring_down(faces[0], faces[1], lane)
        centre, near = pull_slab(field, bx, by, bz, x, lane)
        for k in range(2):
            face = by[k][x]
            mass = WEIGHT * alpha[k][x]
            d = mass + bx[k][x] + bx[k][x - 1] + face + turn(face, 1, 0) + faces[k] + downs[k]
            w = relaxer(mass, d)
            diag[k][x] = d
            weight[k][x] = w
            halfway[k][x] = KEEP * centre[k] + w * (rhs[k][x] + near[k])

    each(1, ex - 1, 4, first_sweep)

    def second_sweep(x):
        centre, near = pull_slab(halfway, bx, by, bz, x, lane)
        for k in range(2):
            kept[k][x] = KEEP * centre[k] + weight[k][x] * (rhs[k][x] + near[k])

    each(2, ex - 2, 4, second_sweep)

    def residual(x):
        centre, near = pull_slab(kept, bx, by, bz, x, lane)
        for k in range(2):
            halfway[k][x] = rhs[k][x] - diag[k][x] * centre[k] + near[k]

    each(HALO, ex - HALO, 4, residual)

    x1, y1 = sx // 2, sy // 2
    for k in range(2):
        lanes = slice(k * LANES, (k + 1) * LANES)
        for i in range(x1):
            x = HALO + 2 * i
            total = None
            for p in BOTH:
                for q in BOTH:
                    term = halfway[k][x + p, pl.ds(q, y1, stride=2), :]
                    total = term if total is None else total + term
            sums[0, i, :, lanes] = total
            left[...] = turn(by[k][x] + by[k][x + 1], 1, 0)
            sums[1, i, :, lanes] = left[pl.ds(0, y1, stride=2), :]
    rhs1, low_y = to_level1(sums, 0, 2, pair_table(2 * LANES, LANES, False), 0.0625)
    weight1 = relaxer(coeffs1[0], coeffs1[1] + low_y)
    for n, values in enumerate((2.0 * rhs1, weight1, coeffs1[2], coeffs1[3], coeffs1[4])):
        own1[n] = values
        for send, face in zip(sends, faces_x(values[None], at_x % 2, n_x, NEAR)):
            send[n] = face[0]
        near_one[n], near_two[n] = faces_y(values, at_y % 2, NEAR)


def level2_rows(source, odd_axes, factor, x2, y2, z2):
    rows = []
    for i in range(x2):
        total = None
        for p in (1,) if odd_axes[0] else (0, 1):
            for q in (1,) if odd_axes[1] else (0, 1):
                term = source[2 * i + p, pl.ds(q, y2, stride=2), :]
                total = term if total is None else total + term
        rows.append(total)
    flat = jnp.concatenate(rows, axis=0)
    flat = factor * times_table(flat, pair_table(LANES, LANES, odd_axes[2]))
    lane = lane_of((y2, LANES))
    packed = jnp.zeros((y2, LANES), F32)
    for i in range(x2):
        mask = (lane >= i * z2) & (lane < (i + 1) * z2)
        packed = jnp.where(mask, turn(flat[i * y2:(i + 1) * y2], i * z2, 1), packed)
    return packed


def near_corners_kernel(counts, where_ref, *refs):
    halos_x, (two_y, one_y) = refs[:-2], refs[-2:]
    at_x, at_y, _ = position(where_ref)
    for a in range(halos_x[0].shape[0]):
        below, above = neighbours(counts[0], at_x, halos_x[0][a], halos_x[-1][a])
        for n, pair in enumerate(corner_sends(below, above, at_y % 2, True)):
            one_y[5 * a + n], two_y[5 * a + n] = pair


def near_kernel(counts, devices, where_ref, ring, *refs):
    n_x = 1 if counts[0] == 2 else 2
    halos_x = refs[:n_x]
    main_two, main_one, rest_two, rest_one, coarse2, copies, level1, left = refs[n_x:]
    n, bx1, by1, _ = ring.shape
    at_x, at_y, _ = position(where_ref)
    rest = neighbours(counts[1], at_y, rest_one[...], rest_two[...])
    rest = jnp.concatenate(rest[::-1], axis=1)
    whole = []
    for a in range(n):
        below, above = neighbours(counts[0], at_x, halos_x[0][a], halos_x[-1][a])
        rows = neighbours(counts[1], at_y, main_one[a], main_two[a])
        rows = jnp.concatenate(rows[::-1], axis=1)
        low, high = corner_tiles([rest[5 * a + k] for k in range(5)])
        rows = jnp.concatenate(
            [tile[None] for tile in low] + [rows] + [tile[None] for tile in high], axis=0
        )
        block = jnp.concatenate([below, ring[a], above], axis=0)
        whole.append(jnp.concatenate([block, rows], axis=1))
    rhs1, weight1 = whole[:2]
    faces1 = tuple(whole[2:])
    field1 = weight1 * rhs1
    field1 = sweep(field1, rhs1, weight1, faces1)
    for a, values in enumerate([field1] + whole):
        level1[a] = values
    mine = slice(NEAR, NEAR + bx1)
    inner = weight1[mine]
    diag1 = RELAX / jnp.where(inner > 0.0, inner, 1.0)
    remain = rhs1[mine] - diag1 * field1[mine] + pull(field1, faces1)[mine]
    left[...] = remain
    packed = level2_rows(left, (False,) * 3, 0.125, bx1 // 2, by1 // 2, LANES // 4)
    for d in range(devices):
        copies[d, 0] = packed
        for a in range(n - 1):
            copies[d, a + 1] = coarse2[a]


def halve(values, odd_axis, step):
    half = values.shape[0] // 2
    even = [values[2 * i:2 * i + 1] for i in range(half)]
    odd = [values[2 * i + 1:2 * i + 2] for i in range(half)]
    if odd_axis != 0:
        odd = [a + b for a, b in zip(even, odd)]
    values = jnp.concatenate(odd, axis=0)
    for axis in (1, 2):
        next_one = turn(values, -step, axis)
        values = next_one if odd_axis == axis else values + next_one
    return values


def double(values, step):
    values = values + turn(values, step, 1)
    values = values + turn(values, step, 2)
    return jnp.concatenate([values[i // 2:i // 2 + 1] for i in range(2 * values.shape[0])], axis=0)


def coarse_levels(mass, faces, y, z):
    levels = []
    for level in range(2, LEVELS):
        step = 2 ** (level - 2)
        bx, by, bz = faces
        row = lax.broadcasted_iota(jnp.int32, by.shape, 1)
        lane = lane_of(bz.shape)
        coupled = (
            bx,
            jnp.where(row == (y - 1) * step, 0.0, by),
            jnp.where(lane == (z - 1) * step, 0.0, bz),
        )
        mass = jnp.where((row % step == 0) & (lane % step == 0), mass, 0.0)
        diag = diagonal(mass, faces, coupled, step)
        levels.append((diag, relaxer(mass, diag), coupled))
        if level < LEVELS - 1:
            faces = tuple(0.0625 * halve(face, axis, step) for axis, face in enumerate(faces))
            mass = 0.125 * halve(mass, -1, step)
            y, z = y // 2, z // 2
    return levels


def coarse_cycle(level, rhs, levels):
    step = 2 ** (level - 2)
    diag, weight, faces = levels[level - 2]
    field = weight * rhs
    if level == LEVELS - 1:
        for _ in range(BOTTOM - 1):
            field = sweep(field, rhs, weight, faces, step)
        return field
    for _ in range(SWEEPS - 1):
        field = sweep(field, rhs, weight, faces, step)
    remain = rhs - diag * field + pull(field, faces, step)
    correction = coarse_cycle(level + 1, 0.125 * halve(remain, -1, step), levels)
    field = field + double(correction, step)
    for _ in range(SWEEPS):
        field = sweep(field, rhs, weight, faces, step)
    return field


def spread_out(counts, slots, whole):
    gx, gy, gz = counts
    y2 = slots.shape[-2]
    x2 = whole.shape[0] // gx
    z2 = LANES // x2
    lane = lane_of((y2, LANES))
    for i in range(gx):
        for j in range(gy):
            for x in range(x2):
                for part in range(whole.shape[2] // LANES):
                    total = jnp.zeros((y2, LANES), F32)
                    for k in range(LANES // z2):
                        column = part * (LANES // z2) + k
                        if column < gz:
                            block = slots[(i * gy + j) * gz + column]
                            mask = (lane >= k * z2) & (lane < (k + 1) * z2)
                            total = jnp.where(mask, turn(block, (k - x) * z2, 1), total)
                    lanes = slice(part * LANES, (part + 1) * LANES)
                    whole[i * x2 + x, j * y2:(j + 1) * y2, lanes] = total


def up_kernel(counts, where_ref, gathered, level1, *refs):
    kept, weight, rhs, bx, by, bz = zip(refs[0:12:2], refs[1:12:2])
    out, whole, second, spread_m, spread_h, field_m, field_h, half_m, half_h = refs[12:]
    gx, gy, gz = counts
    at_x, at_y, at_z = position(where_ref)
    sx, sy, sz = out.shape
    x1, y1 = sx // 2, sy // 2
    x2, y2, z2 = x1 // 2, y1 // 2, sz // 4
    columns = max(LANES, gz * z2)
    for a in range(5):
        spread_out(counts, gathered.at[:, a], whole.at[a])
    levels = coarse_levels(whole[1], (whole[2], whole[3], whole[4]), gy * y2, gz * z2)
    correction = coarse_cycle(2, whole[0], levels)

    wide = gx * x2
    half = NEAR // 2
    ex1, ey1 = x1 + 2 * NEAR, y1 + 2 * NEAR
    second[:half] = jnp.zeros((half,) + correction.shape[1:], F32)
    second[half:half + wide] = correction
    second[half + wide:] = jnp.zeros((half,) + correction.shape[1:], F32)
    window = second[pl.ds(at_x * x2, x2 + NEAR)]
    rows = correction.shape[1]
    row = iota2((ey1, rows), 0)
    col = iota2((ey1, rows), 1)
    place = jnp.where(row < y1 + NEAR, row, row - ey1)
    table_y = (col == at_y * y2 + lax.shift_right_arithmetic(place, 1)).astype(F32)
    row = iota2((columns, LANES), 0)
    col = iota2((columns, LANES), 1)
    place = jnp.where(col < LANES * 3 // 4, col, col - LANES)
    table_z = (row == at_z * z2 + lax.shift_right_arithmetic(place, 1)).astype(F32)
    flat = times_table(window.reshape((x2 + NEAR) * rows, columns), table_z)
    blocks = [table_times(table_y, flat[i * rows:(i + 1) * rows])[None] for i in range(x2 + NEAR)]
    lifted = jnp.concatenate([blocks[i // 2] for i in range(ex1)], axis=0)
    field1, rhs1, weight1 = level1[0], level1[1], level1[2]
    faces1 = (level1[3], level1[4], level1[5])
    field1 = field1 + jnp.where(weight1 > 0.0, lifted, 0.0)
    for _ in range(SWEEPS):
        field1 = sweep(field1, rhs1, weight1, faces1)

    ex, ey = sx + 2 * HALO, sy + 2 * HALO
    near = field1[NEAR - 1:NEAR + x1 + 1].reshape((x1 + 2) * ey1, LANES)
    row = iota2((LANES, 2 * LANES), 0)
    col = iota2((LANES, 2 * LANES), 1)
    lifted = times_table(near, (col // 2 == row).astype(F32))
    quarter = NEAR // 2
    for k, spread in enumerate((spread_m, spread_h)):
        block = lifted[:, k * LANES:(k + 1) * LANES].reshape(x1 + 2, ey1, LANES)
        for i in range(x1 + 2):
            for q in range(2):
                spread[i, pl.ds(q, y1, stride=2), :] = block[i, :y1]
                spread[i, pl.ds(sy + q, quarter, stride=2), :] = block[i, y1:y1 + quarter]
                spread[i, pl.ds(sy + HALO + q, quarter, stride=2), :] = block[i, ey1 - quarter:]
    before, after = (field_m, field_h), (half_m, half_h)
    first = HALO - 2
    for x in range(first, ex - first):
        for k, spread in enumerate((spread_m, spread_h)):
            before[k][x] = kept[k][x] + spread[(x - first) // 2]

    lane = lane_of((ey, LANES))

    def sweep_out(x):
        centre, around = pull_slab(before, bx, by, bz, x, lane)
        for k in range(2):
            after[k][x] = KEEP * centre[k] + weight[k][x] * (rhs[k][x] + around[k])

    each(first + 1, ex - first - 1, 4, sweep_out)

    def sweep_own(x):
        centre, around = pull_slab(after, bx, by, bz, x, lane)
        value = KEEP * centre[0] + weight[0][x] * (rhs[0][x] + around[0])
        out[x - HALO] = value[:sy]

    each(HALO, ex - HALO, 4, sweep_own)


def run(kernel, outs, where, arrays, scratch=(), grant=16, micros=1):
    return pl.pallas_call(
        kernel,
        out_shape=tuple(jax.ShapeDtypeStruct(shape, F32) for shape in outs),
        in_specs=[SM] * len(where) + [VM] * len(arrays),
        out_specs=tuple(VM for _ in outs),
        scratch_shapes=[pltpu.VMEM(shape, F32) for shape in scratch],
        compiler_params=pltpu.CompilerParams(vmem_limit_bytes=grant * 1024 * 1024),
        cost_estimate=pl.CostEstimate(
            flops=0, bytes_accessed=int(micros * 3.6e6), transcendentals=0
        ),
    )(*where, *arrays)


def swaps(axis, sends):
    count = lax.axis_size(axis)
    got = []
    for k, block in enumerate(sends):
        pairs = [(i, (i + 1) % count) for i in range(k, count, 2)]
        pairs = [pair for low, high in pairs for pair in ((low, high), (high, low))]
        got.append(lax.ppermute(block, axis, pairs))
    return got


def local(initial, right_side, alpha, beta_x, beta_y, beta_z):
    axes = ("gx", "gy", "gz")
    counts = tuple(lax.axis_size(axis) for axis in axes)
    devices = counts[0] * counts[1] * counts[2]
    where = (lax.axis_index("gx") * STRIDE + lax.axis_index("gy")) * STRIDE + lax.axis_index("gz")
    where = (where.astype(jnp.int32).reshape(1),)
    ins = (initial, right_side, alpha, beta_x, beta_y, beta_z)
    sx, sy, sz = initial.shape
    n_x = 1 if counts[0] == 2 else 2
    ex, ey = sx + 2 * HALO, sy + 2 * HALO
    fine = (ex, ey, LANES)

    *sends_x, two_y, one_y, first, second = run(
        functools.partial(faces_kernel, counts),
        [(6, HALO, sy, LANES)] * n_x
        + [(6, sx, HALO, LANES)] * 2
        + [(sx // 2, sy, LANES)] * 2,
        where,
        ins,
        grant=60,
    )
    main_x = tuple(swaps("gx", sends_x))
    main_y = tuple(swaps("gy", (one_y, two_y))[::-1])
    got = swaps("gz", (first, second))
    zpack, *sends = run(
        functools.partial(halo_z_kernel, counts),
        [(sx, sy, LANES)] + [(HALO, sy, LANES)] * n_x,
        where,
        tuple(got),
    )
    halos_x = tuple(swaps("gx", sends))
    two_y, one_y = run(
        functools.partial(corners_kernel, counts),
        [(21 + sx, HALO, LANES)] * 2,
        where,
        (zpack,) + main_x + halos_x,
    )
    rest_y = tuple(swaps("gy", (one_y, two_y))[::-1])
    x1, y1 = sx // 2, sy // 2
    ins = ins + (zpack,)
    coarse2, coeffs1 = run(
        functools.partial(coefficient_kernel, counts),
        [(4, y1 // 2, LANES), (5, x1, y1, LANES)],
        where,
        ins + main_x + halos_x,
        [(2, sx, sy, LANES), (5, x1, y1, 2 * LANES), (4, x1, y1, LANES)],
        micros=2,
    )
    own1, *outs = run(
        functools.partial(down_kernel, counts),
        [(5, x1, y1, LANES)]
        + [(5, NEAR, y1, LANES)] * n_x
        + [(5, x1, NEAR, LANES)] * 2
        + [fine] * 12,
        where,
        ins + main_x + halos_x + main_y + rest_y + (coeffs1,),
        [fine] * 9 + [(2, x1, y1, 2 * LANES), (ey, LANES)],
        24,
        micros=4,
    )
    sends_x, (two_y, one_y), fine_arrays = outs[:n_x], outs[n_x:n_x + 2], outs[n_x + 2:]

    near_x = tuple(swaps("gx", sends_x))
    near_y = tuple(swaps("gy", (one_y, two_y))[::-1])
    two_y, one_y = run(
        functools.partial(near_corners_kernel, counts), [(25, NEAR, LANES)] * 2, where, near_x
    )
    rest_y = tuple(swaps("gy", (one_y, two_y))[::-1])
    copies, level1 = run(
        functools.partial(near_kernel, counts, devices),
        [(devices, 5, y1 // 2, LANES), (6, x1 + 2 * NEAR, y1 + 2 * NEAR, LANES)],
        where,
        (own1,) + near_x + near_y + rest_y + (coarse2,),
        [(x1, y1 + 2 * NEAR, LANES)],
    )

    gathered = lax.all_to_all(copies, axes, 0, 0, tiled=True)
    wide, rows = counts[0] * x1 // 2, counts[1] * y1 // 2
    columns = max(LANES, counts[2] * sz // 4)
    (result,) = run(
        functools.partial(up_kernel, counts),
        [(sx, sy, sz)],
        where,
        (gathered, level1) + tuple(fine_arrays),
        [(5, wide, rows, columns), (wide + NEAR, rows, columns)]
        + [(x1 + 2, ey, LANES)] * 2
        + [fine] * 4,
        24,
        micros=4,
    )
    return result


def solution(mesh):
    spec = P("gx", "gy", "gz")
    return jax.shard_map(
        local, mesh=mesh, in_specs=(spec,) * 6, out_specs=spec, check_vma=False
    )
```

```python
import functools

import jax
import jax.numpy as jnp
from jax import lax
from jax.experimental import pallas as pl
from jax.experimental.pallas import tpu as pltpu
from jax.sharding import PartitionSpec as P

LEVELS = 6
SWEEPS = 2
BOTTOM = 8
WEIGHT = 0.25 ** (LEVELS - 1)
RELAX = 2.0 / 3.0
KEEP = 1.0 / 3.0

HALO = 4
NEAR = 4
LANES = 128
PLACE = (0, 11, 21, 31, 41, 51)
DEPTH = (11, 10, 10, 10, 10, 11)
SIDE = LANES // 2
STRIDE = 256

VM = pl.BlockSpec(memory_space=pltpu.VMEM)
SM = pl.BlockSpec(memory_space=pltpu.SMEM)
F32 = jnp.float32


def position(where_ref):
    code = where_ref[0]
    return code // (STRIDE * STRIDE), code // STRIDE % STRIDE, code % STRIDE


def lane_of(shape):
    return lax.broadcasted_iota(jnp.int32, shape, len(shape) - 1)


def pick(flag, yes, no):
    return jnp.where(jnp.full(yes.shape, flag, jnp.int32) == 1, yes, no)


def neighbours(count, place, one, two):
    if count == 2:
        two = jnp.zeros_like(one)
    else:
        ends = jnp.full(two.shape, place, jnp.int32)
        two = jnp.where((ends == 0) | (ends == count - 1), 0.0, two)
    return pick(place % 2, one, two), pick(place % 2, two, one)


def turn(values, shift, axis):
    return pltpu.roll(values, shift % values.shape[axis], axis)


def parts_of(values):
    high = values.astype(jnp.bfloat16)
    rest = values - high.astype(F32)
    middle = rest.astype(jnp.bfloat16)
    low = (rest - middle.astype(F32)).astype(jnp.bfloat16)
    return high, middle, low


def times_table(values, table):
    table = table.astype(jnp.bfloat16)
    total = None
    for part in reversed(parts_of(values)):
        term = jnp.dot(part, table, preferred_element_type=F32)
        total = term if total is None else total + term
    return total


def table_times(table, values):
    table = table.astype(jnp.bfloat16)
    total = None
    for part in reversed(parts_of(values)):
        term = jnp.dot(table, part, preferred_element_type=F32)
        total = term if total is None else total + term
    return total


def iota2(shape, axis):
    return lax.broadcasted_iota(jnp.int32, shape, axis)


def pair_table(rows, cols, odd):
    row = iota2((rows, cols), 0)
    col = iota2((rows, cols), 1)
    hit = (row == 2 * col + 1) if odd else (row // 2 == col)
    return hit.astype(F32)


def below_x(values):
    if values.shape[0] == 1:
        return jnp.zeros_like(values)
    return jnp.concatenate([jnp.zeros_like(values[:1]), values[:-1]], axis=0)


def above_x(values):
    if values.shape[0] == 1:
        return jnp.zeros_like(values)
    return jnp.concatenate([values[1:], jnp.zeros_like(values[:1])], axis=0)


def pull(values, faces, step=1):
    bx, by, bz = faces
    total = bx * above_x(values) + below_x(bx * values)
    total = total + (by * turn(values, -step, 1) + turn(by * values, step, 1))
    return total + (bz * turn(values, -step, 2) + turn(bz * values, step, 2))


def diagonal(mass, faces, coupled, step=1):
    bx, by, bz = faces
    _, cy, cz = coupled
    return mass + bx + below_x(bx) + by + turn(cy, step, 1) + bz + turn(cz, step, 2)


def relaxer(mass, diag):
    inside = mass > 0.0
    return jnp.where(inside, RELAX / jnp.where(inside, diag, 1.0), 0.0)


def sweep(values, rhs, weight, faces, step=1):
    return KEEP * values + weight * (rhs + pull(values, faces, step))


def faces_x(values, odd, n_x, width):
    head, tail = values[:, :width], values[:, values.shape[1] - width:]
    return [pick(odd, head, tail), pick(odd, tail, head)][:n_x]


def faces_y(values, odd, width):
    head, tail = values[:, :width], values[:, values.shape[1] - width:]
    return pick(odd, head, tail), pick(odd, tail, head)


def corner_sends(below, above, odd, corners):
    packs = []
    for rows, sign in ((slice(0, 8), 1), (slice(below.shape[1] - 8, below.shape[1]), -1)):
        low = [below[3 - i, rows] for i in range(4)]
        high = [above[i, rows] for i in range(4)]
        pack = []
        if corners:
            pack = [low[0], high[0]]
            low, high = low[1:], high[1:]
        row = iota2(low[0].shape, 0)
        row = row if sign == 1 else 7 - row
        pack += [
            jnp.where(row < 3, low[0], turn(low[2], 3 * sign, 0)),
            jnp.where(row < 2, low[1], turn(high[1], 2 * sign, 0)),
            jnp.where(row < 3, high[0], turn(high[2], 3 * sign, 0)),
        ]
        packs.append([p[:4] if sign == 1 else p[4:] for p in pack])
    return [(pick(odd, h, t), pick(odd, t, h)) for h, t in zip(*packs)]


def corner_tiles(tiles):
    first, second, third = tiles[-3:]
    upper = iota2(first.shape, 0) < 4

    def inner(tile, by):
        return jnp.where(upper, turn(tile, -by, 0), turn(tile, by, 0))

    low = [first, second, inner(first, 3)]
    high = [third, inner(second, 2), inner(third, 3)]
    if len(tiles) == 5:
        low, high = tiles[:1] + low, tiles[1:2] + high
    else:
        zero = jnp.zeros_like(first)
        low, high = low + [zero], high + [zero]
    return low[::-1], high


def faces_kernel(counts, where_ref, *refs):
    ins, refs = refs[:6], refs[6:]
    n_x = 1 if counts[0] == 2 else 2
    sends_x, (two_y, one_y, first, second) = refs[:n_x], refs[n_x:]
    odd_x, odd_y, odd = (place % 2 for place in position(where_ref))
    sx, sy, sz = ins[0].shape
    half = sx // 2
    lane = lane_of((half, sy, LANES))
    head = jnp.zeros((half, sy, LANES), F32)
    tail = head
    for a, ref in enumerate(ins):
        for send, face in zip(sends_x, faces_x(ref[...][None], odd_x, n_x, HALO)):
            send[a] = face[0]
        one_y[a], two_y[a] = faces_y(ref[...], odd_y, HALO)
        for g in range(2):
            values = ref[g * half:(g + 1) * half]
            at = SIDE * g + PLACE[a]
            mask = (lane >= at) & (lane < at + DEPTH[a])
            head = jnp.where(mask, turn(values, at, 2), head)
            tail = jnp.where(mask, turn(values, at + DEPTH[a], 2), tail)
    first[...] = pick(odd, head, tail)
    second[...] = pick(odd, tail, head)


def halo_z_kernel(counts, where_ref, one_ref, two_ref, zpack, *sends):
    at_x, _, at_z = position(where_ref)
    half = one_ref.shape[0]
    below, above = neighbours(counts[2], at_z, one_ref[...], two_ref[...])
    lane = lane_of(below.shape)
    zpack[:half] = jnp.where(lane < SIDE, above, turn(below, SIDE, 2))
    zpack[half:] = jnp.where(lane < SIDE, turn(above, SIDE, 2), below)
    for send, face in zip(sends, faces_x(zpack[...][None], at_x % 2, len(sends), HALO)):
        send[...] = face[0]


def corners_kernel(counts, where_ref, zpack, *refs):
    n_x = 1 if counts[0] == 2 else 2
    main_x, halos_x, (two_y, one_y) = refs[:n_x], refs[n_x:2 * n_x], refs[2 * n_x:]
    at_x, at_y, _ = position(where_ref)
    for a in range(7):
        if a < 6:
            below, above = neighbours(counts[0], at_x, main_x[0][a], main_x[-1][a])
        else:
            below, above = neighbours(counts[0], at_x, halos_x[0][...], halos_x[-1][...])
        for n, pair in enumerate(corner_sends(below, above, at_y % 2, False)):
            one_y[3 * a + n], two_y[3 * a + n] = pair
    one_y[21:], two_y[21:] = faces_y(zpack[...], at_y % 2, HALO)


def each(first, last, step, body):
    rounds = (last - first) // step

    def go(i, carry):
        for j in range(step):
            body(first + i * step + j)
        return carry

    if rounds:
        lax.fori_loop(0, rounds, go, 0)
    for x in range(first + rounds * step, last):
        body(x)


def ring_up(main, halo, lane):
    main_up, halo_up = turn(main, -1, 1), turn(halo, -1, 1)
    last = lane == LANES - 1
    return jnp.where(last, halo_up, main_up), jnp.where(last, main_up, halo_up)


def ring_down(main, halo, lane):
    main_down, halo_down = turn(main, 1, 1), turn(halo, 1, 1)
    zero = lane == 0
    return jnp.where(zero, halo_down, main_down), jnp.where(zero, main_down, halo_down)


def pull_slab(field, bx, by, bz, x, lane):
    centre = [half[x] for half in field]
    out = []
    for k in range(2):
        c, face = centre[k], by[k][x]
        t = bx[k][x] * field[k][x + 1] + bx[k][x - 1] * field[k][x - 1]
        out.append(t + (face * turn(c, -1, 0) + turn(face * c, 1, 0)))
    faces = [half[x] for half in bz]
    ups = ring_up(centre[0], centre[1], lane)
    downs = ring_down(faces[0] * centre[0], faces[1] * centre[1], lane)
    return centre, [out[k] + (faces[k] * ups[k] + downs[k]) for k in range(2)]


def unpacked(packed, a, lane):
    at, depth = PLACE[a], DEPTH[a]
    axis = packed.ndim - 1
    right, left = turn(packed, -at, axis), turn(packed, SIDE - depth - at, axis)
    return jnp.where(lane < depth, right, jnp.where(lane >= LANES - depth, left, 0.0))


def rows_of(source, x, firsts, seconds):
    total = None
    for p in firsts:
        for q in seconds:
            term = source[x + p, pl.ds(q, source.shape[1] // 2, stride=2), :]
            total = term if total is None else total + term
    return total


BOTH, ODD = (0, 1), (1,)


def to_level1(sums, first, count, table, factor):
    _, x1, y1, _ = sums.shape
    flat = sums[first:first + count].reshape(count * x1 * y1, 2 * LANES)
    return factor * times_table(flat, table).reshape(count, x1, y1, LANES)


def coefficient_kernel(counts, where_ref, *refs):
    ins, refs = refs[2:7], refs[7:]
    n_x = 1 if counts[0] == 2 else 2
    main_x, halos_x = refs[:n_x], refs[n_x:2 * n_x]
    coarse2, coeffs1, halo, sums, pairing = refs[2 * n_x:]
    sx, sy, sz = ins[0].shape
    at_x = position(where_ref)[0]
    x1, y1 = sx // 2, sy // 2
    lane = lane_of((sx, sy, LANES))
    lanes = [slice(k * LANES, (k + 1) * LANES) for k in range(2)]
    edge_lane = lane_of((1, sy, LANES))
    last = slice(HALO - 1, HALO)
    below, _ = neighbours(counts[0], at_x, main_x[0][3, last], main_x[-1][3, last])
    packed, _ = neighbours(counts[0], at_x, halos_x[0][last], halos_x[-1][last])
    for k, edge in enumerate((below, unpacked(packed, 3, edge_lane))):
        halo[k, 0:1] = edge
        sums[4, 0, :, lanes[k]] = rows_of(halo.at[k], 0, (0,), BOTH)
    for n, (firsts, seconds) in enumerate(((BOTH, BOTH), (ODD, BOTH), (BOTH, ODD), (BOTH, BOTH))):
        halo[0] = unpacked(ins[4][...], n + 2, lane)
        for i in range(x1):
            sums[n, i, :, lanes[0]] = rows_of(ins[n], 2 * i, firsts, seconds)
            sums[n, i, :, lanes[1]] = rows_of(halo.at[0], 2 * i, firsts, seconds)
    pairs = pair_table(2 * LANES, LANES, False)
    odds = pair_table(2 * LANES, LANES, True)
    paired = to_level1(sums, 0, 3, pairs, 0.0625)
    mass1 = (2.0 * WEIGHT) * paired[0]
    faces1 = (paired[1], paired[2], to_level1(sums, 3, 1, odds, 0.0625)[0])
    edge = 0.0625 * times_table(sums[4, 0], pairs)[None]
    diag1 = mass1 + faces1[0] + jnp.concatenate([edge, faces1[0][:-1]], axis=0)
    diag1 = diag1 + faces1[1] + faces1[2] + turn(faces1[2], 1, 2)
    for n, values in enumerate((mass1, diag1) + faces1):
        coeffs1[n] = values
    parts = (
        (mass1, False, False, False, 0.125),
        (faces1[0], True, False, False, 0.0625),
        (faces1[1], False, True, False, 0.0625),
        (faces1[2], False, False, True, 0.0625),
    )
    for n, (values, *odd_axes, factor) in enumerate(parts):
        pairing[n] = values
        coarse2[n] = level2_rows(pairing.at[n], odd_axes, factor, x1 // 2, y1 // 2, sz // 4)


def down_kernel(counts, where_ref, *refs):
    ins, refs = refs[:7], refs[7:]
    n_x = 1 if counts[0] == 2 else 2
    main_x, halos_x = refs[:n_x], refs[n_x:2 * n_x]
    main_two, main_one, rest_two, rest_one, coeffs1, own1 = refs[2 * n_x:6 + 2 * n_x]
    refs = refs[6 + 2 * n_x:]
    sends, near_two, near_one, refs = refs[:n_x], refs[n_x], refs[n_x + 1], refs[n_x + 2:]
    kept_m, kept_h, weight_m, weight_h = refs[:4]
    faces_out, scratch = refs[4:12], refs[12:]
    rhs, bx, by, bz = zip(faces_out[::2], faces_out[1::2])
    field, alpha = scratch[:2], scratch[2:4]
    packs, half_m, half_h, diag_m, diag_h, sums, left = scratch[4:]
    arrays = (field, rhs, alpha, bx, by, bz)
    sx, sy, sz = ins[0].shape
    ex, ey = sx + 2 * HALO, sy + 2 * HALO
    at_x, at_y, _ = position(where_ref)

    rest = neighbours(counts[1], at_y, rest_one[...], rest_two[...])
    rest = jnp.concatenate(rest[::-1], axis=1)
    for a in range(7):
        if a < 6:
            to = arrays[a][0]
            below, above = neighbours(counts[0], at_x, main_x[0][a], main_x[-1][a])
            rows = neighbours(counts[1], at_y, main_one[a], main_two[a])
            rows = jnp.concatenate(rows[::-1], axis=1)
        else:
            to = packs
            below, above = neighbours(counts[0], at_x, halos_x[0][...], halos_x[-1][...])
            rows = rest[21:]
        to[:HALO, :sy] = below
        to[HALO:HALO + sx, :sy] = ins[a][...]
        to[HALO + sx:, :sy] = above
        to[HALO:HALO + sx, sy:] = rows
        low, high = corner_tiles([rest[3 * a + n] for n in range(3)])
        for n in range(HALO):
            to[n, sy:] = low[n]
            to[HALO + sx + n, sy:] = high[n]
    lane = lane_of((ey, LANES))

    def unpack(x):
        packed = packs[x]
        for a in range(6):
            arrays[a][1][x] = unpacked(packed, a, lane)

    each(0, ex, 4, unpack)
    halfway, weight, kept = (half_m, half_h), (weight_m, weight_h), (kept_m, kept_h)
    diag = (diag_m, diag_h)

    def first_sweep(x):
        faces = [half[x] for half in bz]
        downs = ring_down(faces[0], faces[1], lane)
        centre, near = pull_slab(field, bx, by, bz, x, lane)
        for k in range(2):
            face = by[k][x]
            mass = WEIGHT * alpha[k][x]
            d = mass + bx[k][x] + bx[k][x - 1] + face + turn(face, 1, 0) + faces[k] + downs[k]
            w = relaxer(mass, d)
            diag[k][x] = d
            weight[k][x] = w
            halfway[k][x] = KEEP * centre[k] + w * (rhs[k][x] + near[k])

    each(1, ex - 1, 4, first_sweep)

    def second_sweep(x):
        centre, near = pull_slab(halfway, bx, by, bz, x, lane)
        for k in range(2):
            kept[k][x] = KEEP * centre[k] + weight[k][x] * (rhs[k][x] + near[k])

    each(2, ex - 2, 4, second_sweep)

    def residual(x):
        centre, near = pull_slab(kept, bx, by, bz, x, lane)
        for k in range(2):
            halfway[k][x] = rhs[k][x] - diag[k][x] * centre[k] + near[k]

    each(HALO, ex - HALO, 4, residual)

    x1, y1 = sx // 2, sy // 2
    for k in range(2):
        lanes = slice(k * LANES, (k + 1) * LANES)
        for i in range(x1):
            x = HALO + 2 * i
            total = None
            for p in BOTH:
                for q in BOTH:
                    term = halfway[k][x + p, pl.ds(q, y1, stride=2), :]
                    total = term if total is None else total + term
            sums[0, i, :, lanes] = total
            left[...] = turn(by[k][x] + by[k][x + 1], 1, 0)
            sums[1, i, :, lanes] = left[pl.ds(0, y1, stride=2), :]
    rhs1, low_y = to_level1(sums, 0, 2, pair_table(2 * LANES, LANES, False), 0.0625)
    weight1 = relaxer(coeffs1[0], coeffs1[1] + low_y)
    for n, values in enumerate((2.0 * rhs1, weight1, coeffs1[2], coeffs1[3], coeffs1[4])):
        own1[n] = values
        for send, face in zip(sends, faces_x(values[None], at_x % 2, n_x, NEAR)):
            send[n] = face[0]
        near_one[n], near_two[n] = faces_y(values, at_y % 2, NEAR)


def level2_rows(source, odd_axes, factor, x2, y2, z2):
    rows = []
    for i in range(x2):
        total = None
        for p in (1,) if odd_axes[0] else (0, 1):
            for q in (1,) if odd_axes[1] else (0, 1):
                term = source[2 * i + p, pl.ds(q, y2, stride=2), :]
                total = term if total is None else total + term
        rows.append(total)
    flat = jnp.concatenate(rows, axis=0)
    flat = factor * times_table(flat, pair_table(LANES, LANES, odd_axes[2]))
    lane = lane_of((y2, LANES))
    packed = jnp.zeros((y2, LANES), F32)
    for i in range(x2):
        mask = (lane >= i * z2) & (lane < (i + 1) * z2)
        packed = jnp.where(mask, turn(flat[i * y2:(i + 1) * y2], i * z2, 1), packed)
    return packed


def near_corners_kernel(counts, where_ref, *refs):
    halos_x, (two_y, one_y) = refs[:-2], refs[-2:]
    at_x, at_y, _ = position(where_ref)
    for a in range(halos_x[0].shape[0]):
        below, above = neighbours(counts[0], at_x, halos_x[0][a], halos_x[-1][a])
        for n, pair in enumerate(corner_sends(below, above, at_y % 2, True)):
            one_y[5 * a + n], two_y[5 * a + n] = pair


def near_kernel(counts, devices, where_ref, ring, *refs):
    n_x = 1 if counts[0] == 2 else 2
    halos_x = refs[:n_x]
    main_two, main_one, rest_two, rest_one, coarse2, copies, level1, left = refs[n_x:]
    n, bx1, by1, _ = ring.shape
    at_x, at_y, _ = position(where_ref)
    rest = neighbours(counts[1], at_y, rest_one[...], rest_two[...])
    rest = jnp.concatenate(rest[::-1], axis=1)
    whole = []
    for a in range(n):
        below, above = neighbours(counts[0], at_x, halos_x[0][a], halos_x[-1][a])
        rows = neighbours(counts[1], at_y, main_one[a], main_two[a])
        rows = jnp.concatenate(rows[::-1], axis=1)
        low, high = corner_tiles([rest[5 * a + k] for k in range(5)])
        rows = jnp.concatenate(
            [tile[None] for tile in low] + [rows] + [tile[None] for tile in high], axis=0
        )
        block = jnp.concatenate([below, ring[a], above], axis=0)
        whole.append(jnp.concatenate([block, rows], axis=1))
    rhs1, weight1 = whole[:2]
    faces1 = tuple(whole[2:])
    field1 = weight1 * rhs1
    field1 = sweep(field1, rhs1, weight1, faces1)
    for a, values in enumerate([field1] + whole):
        level1[a] = values
    mine = slice(NEAR, NEAR + bx1)
    inner = weight1[mine]
    diag1 = RELAX / jnp.where(inner > 0.0, inner, 1.0)
    remain = rhs1[mine] - diag1 * field1[mine] + pull(field1, faces1)[mine]
    left[...] = remain
    packed = level2_rows(left, (False,) * 3, 0.125, bx1 // 2, by1 // 2, LANES // 4)
    for d in range(devices):
        copies[d, 0] = packed
        for a in range(n - 1):
            copies[d, a + 1] = coarse2[a]


def halve(values, odd_axis, step):
    half = values.shape[0] // 2
    even = [values[2 * i:2 * i + 1] for i in range(half)]
    odd = [values[2 * i + 1:2 * i + 2] for i in range(half)]
    if odd_axis != 0:
        odd = [a + b for a, b in zip(even, odd)]
    values = jnp.concatenate(odd, axis=0)
    for axis in (1, 2):
        next_one = turn(values, -step, axis)
        values = next_one if odd_axis == axis else values + next_one
    return values


def double(values, step):
    values = values + turn(values, step, 1)
    values = values + turn(values, step, 2)
    return jnp.concatenate([values[i // 2:i // 2 + 1] for i in range(2 * values.shape[0])], axis=0)


def coarse_levels(mass, faces, y, z):
    levels = []
    for level in range(2, LEVELS):
        step = 2 ** (level - 2)
        bx, by, bz = faces
        row = lax.broadcasted_iota(jnp.int32, by.shape, 1)
        lane = lane_of(bz.shape)
        coupled = (
            bx,
            jnp.where(row == (y - 1) * step, 0.0, by),
            jnp.where(lane == (z - 1) * step, 0.0, bz),
        )
        mass = jnp.where((row % step == 0) & (lane % step == 0), mass, 0.0)
        diag = diagonal(mass, faces, coupled, step)
        levels.append((diag, relaxer(mass, diag), coupled))
        if level < LEVELS - 1:
            faces = tuple(0.0625 * halve(face, axis, step) for axis, face in enumerate(faces))
            mass = 0.125 * halve(mass, -1, step)
            y, z = y // 2, z // 2
    return levels


def coarse_cycle(level, rhs, levels):
    step = 2 ** (level - 2)
    diag, weight, faces = levels[level - 2]
    field = weight * rhs
    if level == LEVELS - 1:
        for _ in range(BOTTOM - 1):
            field = sweep(field, rhs, weight, faces, step)
        return field
    for _ in range(SWEEPS - 1):
        field = sweep(field, rhs, weight, faces, step)
    remain = rhs - diag * field + pull(field, faces, step)
    correction = coarse_cycle(level + 1, 0.125 * halve(remain, -1, step), levels)
    field = field + double(correction, step)
    for _ in range(SWEEPS):
        field = sweep(field, rhs, weight, faces, step)
    return field


def spread_out(counts, slots, whole):
    gx, gy, gz = counts
    y2 = slots.shape[-2]
    x2 = whole.shape[0] // gx
    z2 = LANES // x2
    lane = lane_of((y2, LANES))
    for i in range(gx):
        for j in range(gy):
            for x in range(x2):
                for part in range(whole.shape[2] // LANES):
                    total = jnp.zeros((y2, LANES), F32)
                    for k in range(LANES // z2):
                        column = part * (LANES // z2) + k
                        if column < gz:
                            block = slots[(i * gy + j) * gz + column]
                            mask = (lane >= k * z2) & (lane < (k + 1) * z2)
                            total = jnp.where(mask, turn(block, (k - x) * z2, 1), total)
                    lanes = slice(part * LANES, (part + 1) * LANES)
                    whole[i * x2 + x, j * y2:(j + 1) * y2, lanes] = total


def up_kernel(counts, where_ref, gathered, level1, *refs):
    kept, weight, rhs, bx, by, bz = zip(refs[0:12:2], refs[1:12:2])
    out, whole, second, spread_m, spread_h, field_m, field_h, half_m, half_h = refs[12:]
    gx, gy, gz = counts
    at_x, at_y, at_z = position(where_ref)
    sx, sy, sz = out.shape
    x1, y1 = sx // 2, sy // 2
    x2, y2, z2 = x1 // 2, y1 // 2, sz // 4
    columns = max(LANES, gz * z2)
    for a in range(5):
        spread_out(counts, gathered.at[:, a], whole.at[a])
    levels = coarse_levels(whole[1], (whole[2], whole[3], whole[4]), gy * y2, gz * z2)
    correction = coarse_cycle(2, whole[0], levels)

    wide = gx * x2
    half = NEAR // 2
    ex1, ey1 = x1 + 2 * NEAR, y1 + 2 * NEAR
    second[:half] = jnp.zeros((half,) + correction.shape[1:], F32)
    second[half:half + wide] = correction
    second[half + wide:] = jnp.zeros((half,) + correction.shape[1:], F32)
    window = second[pl.ds(at_x * x2, x2 + NEAR)]
    rows = correction.shape[1]
    row = iota2((ey1, rows), 0)
    col = iota2((ey1, rows), 1)
    place = jnp.where(row < y1 + NEAR, row, row - ey1)
    table_y = (col == at_y * y2 + lax.shift_right_arithmetic(place, 1)).astype(F32)
    row = iota2((columns, LANES), 0)
    col = iota2((columns, LANES), 1)
    place = jnp.where(col < LANES * 3 // 4, col, col - LANES)
    table_z = (row == at_z * z2 + lax.shift_right_arithmetic(place, 1)).astype(F32)
    flat = times_table(window.reshape((x2 + NEAR) * rows, columns), table_z)
    blocks = [table_times(table_y, flat[i * rows:(i + 1) * rows])[None] for i in range(x2 + NEAR)]
    lifted = jnp.concatenate([blocks[i // 2] for i in range(ex1)], axis=0)
    field1, rhs1, weight1 = level1[0], level1[1], level1[2]
    faces1 = (level1[3], level1[4], level1[5])
    field1 = field1 + jnp.where(weight1 > 0.0, lifted, 0.0)
    for _ in range(SWEEPS):
        field1 = sweep(field1, rhs1, weight1, faces1)

    ex, ey = sx + 2 * HALO, sy + 2 * HALO
    near = field1[NEAR - 1:NEAR + x1 + 1].reshape((x1 + 2) * ey1, LANES)
    row = iota2((LANES, 2 * LANES), 0)
    col = iota2((LANES, 2 * LANES), 1)
    lifted = times_table(near, (col // 2 == row).astype(F32))
    quarter = NEAR // 2
    for k, spread in enumerate((spread_m, spread_h)):
        block = lifted[:, k * LANES:(k + 1) * LANES].reshape(x1 + 2, ey1, LANES)
        for i in range(x1 + 2):
            for q in range(2):
                spread[i, pl.ds(q, y1, stride=2), :] = block[i, :y1]
                spread[i, pl.ds(sy + q, quarter, stride=2), :] = block[i, y1:y1 + quarter]
                spread[i, pl.ds(sy + HALO + q, quarter, stride=2), :] = block[i, ey1 - quarter:]
    before, after = (field_m, field_h), (half_m, half_h)
    first = HALO - 2
    for x in range(first, ex - first):
        for k, spread in enumerate((spread_m, spread_h)):
            before[k][x] = kept[k][x] + spread[(x - first) // 2]

    lane = lane_of((ey, LANES))

    def sweep_out(x):
        centre, around = pull_slab(before, bx, by, bz, x, lane)
        for k in range(2):
            after[k][x] = KEEP * centre[k] + weight[k][x] * (rhs[k][x] + around[k])

    each(first + 1, ex - first - 1, 4, sweep_out)

    def sweep_own(x):
        centre, around = pull_slab(after, bx, by, bz, x, lane)
        value = KEEP * centre[0] + weight[0][x] * (rhs[0][x] + around[0])
        out[x - HALO] = value[:sy]

    each(HALO, ex - HALO, 4, sweep_own)


def run(kernel, outs, where, arrays, scratch=(), grant=16, micros=1):
    return pl.pallas_call(
        kernel,
        out_shape=tuple(jax.ShapeDtypeStruct(shape, F32) for shape in outs),
        in_specs=[SM] * len(where) + [VM] * len(arrays),
        out_specs=tuple(VM for _ in outs),
        scratch_shapes=[pltpu.VMEM(shape, F32) for shape in scratch],
        compiler_params=pltpu.CompilerParams(vmem_limit_bytes=grant * 1024 * 1024),
        cost_estimate=pl.CostEstimate(
            flops=0, bytes_accessed=int(micros * 3.6e6), transcendentals=0
        ),
    )(*where, *arrays)


def swaps(axis, sends):
    count = lax.axis_size(axis)
    got = []
    for k, block in enumerate(sends):
        partner = list(range(count))
        for low in range(k, count - 1, 2):
            partner[low], partner[low + 1] = low + 1, low
        got.append(lax.ppermute(block, axis, list(enumerate(partner))))
    return got


def local(initial, right_side, alpha, beta_x, beta_y, beta_z):
    axes = ("gx", "gy", "gz")
    counts = tuple(lax.axis_size(axis) for axis in axes)
    devices = counts[0] * counts[1] * counts[2]
    where = (lax.axis_index("gx") * STRIDE + lax.axis_index("gy")) * STRIDE + lax.axis_index("gz")
    where = (where.astype(jnp.int32).reshape(1),)
    ins = (initial, right_side, alpha, beta_x, beta_y, beta_z)
    sx, sy, sz = initial.shape
    n_x = 1 if counts[0] == 2 else 2
    ex, ey = sx + 2 * HALO, sy + 2 * HALO
    fine = (ex, ey, LANES)

    *sends_x, two_y, one_y, first, second = run(
        functools.partial(faces_kernel, counts),
        [(6, HALO, sy, LANES)] * n_x
        + [(6, sx, HALO, LANES)] * 2
        + [(sx // 2, sy, LANES)] * 2,
        where,
        ins,
        grant=60,
    )
    main_x = tuple(swaps("gx", sends_x))
    main_y = tuple(swaps("gy", (one_y, two_y))[::-1])
    got = swaps("gz", (first, second))
    zpack, *sends = run(
        functools.partial(halo_z_kernel, counts),
        [(sx, sy, LANES)] + [(HALO, sy, LANES)] * n_x,
        where,
        tuple(got),
    )
    halos_x = tuple(swaps("gx", sends))
    two_y, one_y = run(
        functools.partial(corners_kernel, counts),
        [(21 + sx, HALO, LANES)] * 2,
        where,
        (zpack,) + main_x + halos_x,
    )
    rest_y = tuple(swaps("gy", (one_y, two_y))[::-1])
    x1, y1 = sx // 2, sy // 2
    ins = ins + (zpack,)
    coarse2, coeffs1 = run(
        functools.partial(coefficient_kernel, counts),
        [(4, y1 // 2, LANES), (5, x1, y1, LANES)],
        where,
        ins + main_x + halos_x,
        [(2, sx, sy, LANES), (5, x1, y1, 2 * LANES), (4, x1, y1, LANES)],
        micros=2,
    )
    own1, *outs = run(
        functools.partial(down_kernel, counts),
        [(5, x1, y1, LANES)]
        + [(5, NEAR, y1, LANES)] * n_x
        + [(5, x1, NEAR, LANES)] * 2
        + [fine] * 12,
        where,
        ins + main_x + halos_x + main_y + rest_y + (coeffs1,),
        [fine] * 9 + [(2, x1, y1, 2 * LANES), (ey, LANES)],
        24,
        micros=4,
    )
    sends_x, (two_y, one_y), fine_arrays = outs[:n_x], outs[n_x:n_x + 2], outs[n_x + 2:]

    near_x = tuple(swaps("gx", sends_x))
    near_y = tuple(swaps("gy", (one_y, two_y))[::-1])
    two_y, one_y = run(
        functools.partial(near_corners_kernel, counts), [(25, NEAR, LANES)] * 2, where, near_x
    )
    rest_y = tuple(swaps("gy", (one_y, two_y))[::-1])
    copies, level1 = run(
        functools.partial(near_kernel, counts, devices),
        [(devices, 5, y1 // 2, LANES), (6, x1 + 2 * NEAR, y1 + 2 * NEAR, LANES)],
        where,
        (own1,) + near_x + near_y + rest_y + (coarse2,),
        [(x1, y1 + 2 * NEAR, LANES)],
    )

    gathered = lax.all_to_all(copies, axes, 0, 0, tiled=True)
    wide, rows = counts[0] * x1 // 2, counts[1] * y1 // 2
    columns = max(LANES, counts[2] * sz // 4)
    (result,) = run(
        functools.partial(up_kernel, counts),
        [(sx, sy, sz)],
        where,
        (gathered, level1) + tuple(fine_arrays),
        [(5, wide, rows, columns), (wide + NEAR, rows, columns)]
        + [(x1 + 2, ey, LANES)] * 2
        + [fine] * 4,
        24,
        micros=4,
    )
    return result


def solution(mesh):
    spec = P("gx", "gy", "gz")
    return jax.shard_map(
        local, mesh=mesh, in_specs=(spec,) * 6, out_specs=spec, check_vma=False
    )
```

```python
import functools

import jax
import jax.numpy as jnp
from jax import lax
from jax.experimental import pallas as pl
from jax.experimental.pallas import tpu as pltpu
from jax.sharding import PartitionSpec as P

LEVELS = 6
SWEEPS = 2
BOTTOM = 8
WEIGHT = 0.25 ** (LEVELS - 1)
RELAX = 2.0 / 3.0
KEEP = 1.0 / 3.0

HALO = 4
NEAR = 4
LANES = 128
PLACE = (0, 11, 21, 31, 41, 51)
DEPTH = (11, 10, 10, 10, 10, 11)
SIDE = LANES // 2
STRIDE = 256

VM = pl.BlockSpec(memory_space=pltpu.VMEM)
SM = pl.BlockSpec(memory_space=pltpu.SMEM)
F32 = jnp.float32


def position(where_ref):
    code = where_ref[0]
    return code // (STRIDE * STRIDE), code // STRIDE % STRIDE, code % STRIDE


def lane_of(shape):
    return lax.broadcasted_iota(jnp.int32, shape, len(shape) - 1)


def pick(flag, yes, no):
    return jnp.where(jnp.full(yes.shape, flag, jnp.int32) == 1, yes, no)


def neighbours(count, place, one, two):
    if count == 2:
        two = jnp.zeros_like(one)
    else:
        ends = jnp.full(two.shape, place, jnp.int32)
        two = jnp.where((ends == 0) | (ends == count - 1), 0.0, two)
    return pick(place % 2, one, two), pick(place % 2, two, one)


def turn(values, shift, axis):
    return pltpu.roll(values, shift % values.shape[axis], axis)


def parts_of(values):
    high = values.astype(jnp.bfloat16)
    rest = values - high.astype(F32)
    middle = rest.astype(jnp.bfloat16)
    low = (rest - middle.astype(F32)).astype(jnp.bfloat16)
    return high, middle, low


def times_table(values, table):
    table = table.astype(jnp.bfloat16)
    total = None
    for part in reversed(parts_of(values)):
        term = jnp.dot(part, table, preferred_element_type=F32)
        total = term if total is None else total + term
    return total


def table_times(table, values):
    table = table.astype(jnp.bfloat16)
    total = None
    for part in reversed(parts_of(values)):
        term = jnp.dot(table, part, preferred_element_type=F32)
        total = term if total is None else total + term
    return total


def iota2(shape, axis):
    return lax.broadcasted_iota(jnp.int32, shape, axis)


def pair_table(rows, cols, odd):
    row = iota2((rows, cols), 0)
    col = iota2((rows, cols), 1)
    hit = (row == 2 * col + 1) if odd else (row // 2 == col)
    return hit.astype(F32)


def below_x(values):
    if values.shape[0] == 1:
        return jnp.zeros_like(values)
    return jnp.concatenate([jnp.zeros_like(values[:1]), values[:-1]], axis=0)


def above_x(values):
    if values.shape[0] == 1:
        return jnp.zeros_like(values)
    return jnp.concatenate([values[1:], jnp.zeros_like(values[:1])], axis=0)


def pull(values, faces, step=1):
    bx, by, bz = faces
    total = bx * above_x(values) + below_x(bx * values)
    total = total + (by * turn(values, -step, 1) + turn(by * values, step, 1))
    return total + (bz * turn(values, -step, 2) + turn(bz * values, step, 2))


def diagonal(mass, faces, coupled, step=1):
    bx, by, bz = faces
    _, cy, cz = coupled
    return mass + bx + below_x(bx) + by + turn(cy, step, 1) + bz + turn(cz, step, 2)


def relaxer(mass, diag):
    inside = mass > 0.0
    return jnp.where(inside, RELAX / jnp.where(inside, diag, 1.0), 0.0)


def sweep(values, rhs, weight, faces, step=1):
    return KEEP * values + weight * (rhs + pull(values, faces, step))


def faces_x(values, odd, n_x, width):
    head, tail = values[:, :width], values[:, values.shape[1] - width:]
    return [pick(odd, head, tail), pick(odd, tail, head)][:n_x]


def faces_y(values, odd, width):
    head, tail = values[:, :width], values[:, values.shape[1] - width:]
    return pick(odd, head, tail), pick(odd, tail, head)


def corner_sends(below, above, odd, corners):
    packs = []
    for rows, sign in ((slice(0, 8), 1), (slice(below.shape[1] - 8, below.shape[1]), -1)):
        low = [below[3 - i, rows] for i in range(4)]
        high = [above[i, rows] for i in range(4)]
        pack = []
        if corners:
            pack = [low[0], high[0]]
            low, high = low[1:], high[1:]
        row = iota2(low[0].shape, 0)
        row = row if sign == 1 else 7 - row
        pack += [
            jnp.where(row < 3, low[0], turn(low[2], 3 * sign, 0)),
            jnp.where(row < 2, low[1], turn(high[1], 2 * sign, 0)),
            jnp.where(row < 3, high[0], turn(high[2], 3 * sign, 0)),
        ]
        packs.append([p[:4] if sign == 1 else p[4:] for p in pack])
    return [(pick(odd, h, t), pick(odd, t, h)) for h, t in zip(*packs)]


def corner_tiles(tiles):
    first, second, third = tiles[-3:]
    upper = iota2(first.shape, 0) < 4

    def inner(tile, by):
        return jnp.where(upper, turn(tile, -by, 0), turn(tile, by, 0))

    low = [first, second, inner(first, 3)]
    high = [third, inner(second, 2), inner(third, 3)]
    if len(tiles) == 5:
        low, high = tiles[:1] + low, tiles[1:2] + high
    else:
        zero = jnp.zeros_like(first)
        low, high = low + [zero], high + [zero]
    return low[::-1], high


def faces_kernel(counts, where_ref, *refs):
    ins, refs = refs[:6], refs[6:]
    n_x = 1 if counts[0] == 2 else 2
    sends_x, (two_y, one_y, first, second) = refs[:n_x], refs[n_x:]
    odd_x, odd_y, odd = (place % 2 for place in position(where_ref))
    sx, sy, sz = ins[0].shape
    half = sx // 2
    lane = lane_of((half, sy, LANES))
    head = jnp.zeros((half, sy, LANES), F32)
    tail = head
    for a, ref in enumerate(ins):
        for send, face in zip(sends_x, faces_x(ref[...][None], odd_x, n_x, HALO)):
            send[a] = face[0]
        one_y[a], two_y[a] = faces_y(ref[...], odd_y, HALO)
        for g in range(2):
            values = ref[g * half:(g + 1) * half]
            at = SIDE * g + PLACE[a]
            mask = (lane >= at) & (lane < at + DEPTH[a])
            head = jnp.where(mask, turn(values, at, 2), head)
            tail = jnp.where(mask, turn(values, at + DEPTH[a], 2), tail)
    first[...] = pick(odd, head, tail)
    second[...] = pick(odd, tail, head)


def halo_z_kernel(counts, where_ref, one_ref, two_ref, zpack, *sends):
    at_x, _, at_z = position(where_ref)
    half = one_ref.shape[0]
    below, above = neighbours(counts[2], at_z, one_ref[...], two_ref[...])
    lane = lane_of(below.shape)
    zpack[:half] = jnp.where(lane < SIDE, above, turn(below, SIDE, 2))
    zpack[half:] = jnp.where(lane < SIDE, turn(above, SIDE, 2), below)
    for send, face in zip(sends, faces_x(zpack[...][None], at_x % 2, len(sends), HALO)):
        send[...] = face[0]


def corners_kernel(counts, where_ref, zpack, *refs):
    n_x = 1 if counts[0] == 2 else 2
    main_x, halos_x, (two_y, one_y) = refs[:n_x], refs[n_x:2 * n_x], refs[2 * n_x:]
    at_x, at_y, _ = position(where_ref)
    for a in range(7):
        if a < 6:
            below, above = neighbours(counts[0], at_x, main_x[0][a], main_x[-1][a])
        else:
            below, above = neighbours(counts[0], at_x, halos_x[0][...], halos_x[-1][...])
        for n, pair in enumerate(corner_sends(below, above, at_y % 2, False)):
            one_y[3 * a + n], two_y[3 * a + n] = pair
    one_y[21:], two_y[21:] = faces_y(zpack[...], at_y % 2, HALO)


def each(first, last, step, body):
    rounds = (last - first) // step

    def go(i, carry):
        for j in range(step):
            body(first + i * step + j)
        return carry

    if rounds:
        lax.fori_loop(0, rounds, go, 0)
    for x in range(first + rounds * step, last):
        body(x)


def ring_up(main, halo, lane):
    main_up, halo_up = turn(main, -1, 1), turn(halo, -1, 1)
    last = lane == LANES - 1
    return jnp.where(last, halo_up, main_up), jnp.where(last, main_up, halo_up)


def ring_down(main, halo, lane):
    main_down, halo_down = turn(main, 1, 1), turn(halo, 1, 1)
    zero = lane == 0
    return jnp.where(zero, halo_down, main_down), jnp.where(zero, main_down, halo_down)


def pull_slab(field, bx, by, bz, x, lane):
    centre = [half[x] for half in field]
    out = []
    for k in range(2):
        c, face = centre[k], by[k][x]
        t = bx[k][x] * field[k][x + 1] + bx[k][x - 1] * field[k][x - 1]
        out.append(t + (face * turn(c, -1, 0) + turn(face * c, 1, 0)))
    faces = [half[x] for half in bz]
    ups = ring_up(centre[0], centre[1], lane)
    downs = ring_down(faces[0] * centre[0], faces[1] * centre[1], lane)
    return centre, [out[k] + (faces[k] * ups[k] + downs[k]) for k in range(2)]


def unpacked(packed, a, lane):
    at, depth = PLACE[a], DEPTH[a]
    axis = packed.ndim - 1
    right, left = turn(packed, -at, axis), turn(packed, SIDE - depth - at, axis)
    return jnp.where(lane < depth, right, jnp.where(lane >= LANES - depth, left, 0.0))


def rows_of(source, x, firsts, seconds):
    total = None
    for p in firsts:
        for q in seconds:
            term = source[x + p, pl.ds(q, source.shape[1] // 2, stride=2), :]
            total = term if total is None else total + term
    return total


BOTH, ODD = (0, 1), (1,)


def to_level1(sums, first, count, table, factor):
    _, x1, y1, _ = sums.shape
    flat = sums[first:first + count].reshape(count * x1 * y1, 2 * LANES)
    return factor * times_table(flat, table).reshape(count, x1, y1, LANES)


def coefficient_kernel(counts, where_ref, *refs):
    ins, refs = refs[2:7], refs[7:]
    n_x = 1 if counts[0] == 2 else 2
    main_x, halos_x = refs[:n_x], refs[n_x:2 * n_x]
    coarse2, coeffs1, halo, sums, pairing = refs[2 * n_x:]
    sx, sy, sz = ins[0].shape
    at_x = position(where_ref)[0]
    x1, y1 = sx // 2, sy // 2
    lane = lane_of((sx, sy, LANES))
    lanes = [slice(k * LANES, (k + 1) * LANES) for k in range(2)]
    edge_lane = lane_of((1, sy, LANES))
    last = slice(HALO - 1, HALO)
    below, _ = neighbours(counts[0], at_x, main_x[0][3, last], main_x[-1][3, last])
    packed, _ = neighbours(counts[0], at_x, halos_x[0][last], halos_x[-1][last])
    for k, edge in enumerate((below, unpacked(packed, 3, edge_lane))):
        halo[k, 0:1] = edge
        sums[4, 0, :, lanes[k]] = rows_of(halo.at[k], 0, (0,), BOTH)
    for n, (firsts, seconds) in enumerate(((BOTH, BOTH), (ODD, BOTH), (BOTH, ODD), (BOTH, BOTH))):
        halo[0] = unpacked(ins[4][...], n + 2, lane)
        for i in range(x1):
            sums[n, i, :, lanes[0]] = rows_of(ins[n], 2 * i, firsts, seconds)
            sums[n, i, :, lanes[1]] = rows_of(halo.at[0], 2 * i, firsts, seconds)
    pairs = pair_table(2 * LANES, LANES, False)
    odds = pair_table(2 * LANES, LANES, True)
    paired = to_level1(sums, 0, 3, pairs, 0.0625)
    mass1 = (2.0 * WEIGHT) * paired[0]
    faces1 = (paired[1], paired[2], to_level1(sums, 3, 1, odds, 0.0625)[0])
    edge = 0.0625 * times_table(sums[4, 0], pairs)[None]
    diag1 = mass1 + faces1[0] + jnp.concatenate([edge, faces1[0][:-1]], axis=0)
    diag1 = diag1 + faces1[1] + faces1[2] + turn(faces1[2], 1, 2)
    for n, values in enumerate((mass1, diag1) + faces1):
        coeffs1[n] = values
    parts = (
        (mass1, False, False, False, 0.125),
        (faces1[0], True, False, False, 0.0625),
        (faces1[1], False, True, False, 0.0625),
        (faces1[2], False, False, True, 0.0625),
    )
    for n, (values, *odd_axes, factor) in enumerate(parts):
        pairing[n] = values
        coarse2[n] = level2_rows(pairing.at[n], odd_axes, factor, x1 // 2, y1 // 2, sz // 4)


def down_kernel(counts, where_ref, *refs):
    ins, refs = refs[:7], refs[7:]
    n_x = 1 if counts[0] == 2 else 2
    main_x, halos_x = refs[:n_x], refs[n_x:2 * n_x]
    main_two, main_one, rest_two, rest_one, coeffs1, own1 = refs[2 * n_x:6 + 2 * n_x]
    refs = refs[6 + 2 * n_x:]
    sends, near_two, near_one, refs = refs[:n_x], refs[n_x], refs[n_x + 1], refs[n_x + 2:]
    kept_m, kept_h, weight_m, weight_h = refs[:4]
    faces_out, scratch = refs[4:12], refs[12:]
    rhs, bx, by, bz = zip(faces_out[::2], faces_out[1::2])
    field, alpha = scratch[:2], scratch[2:4]
    packs, half_m, half_h, diag_m, diag_h, sums, left = scratch[4:]
    arrays = (field, rhs, alpha, bx, by, bz)
    sx, sy, sz = ins[0].shape
    ex, ey = sx + 2 * HALO, sy + 2 * HALO
    at_x, at_y, _ = position(where_ref)

    rest = neighbours(counts[1], at_y, rest_one[...], rest_two[...])
    rest = jnp.concatenate(rest[::-1], axis=1)
    for a in range(7):
        if a < 6:
            to = arrays[a][0]
            below, above = neighbours(counts[0], at_x, main_x[0][a], main_x[-1][a])
            rows = neighbours(counts[1], at_y, main_one[a], main_two[a])
            rows = jnp.concatenate(rows[::-1], axis=1)
        else:
            to = packs
            below, above = neighbours(counts[0], at_x, halos_x[0][...], halos_x[-1][...])
            rows = rest[21:]
        to[:HALO, :sy] = below
        to[HALO:HALO + sx, :sy] = ins[a][...]
        to[HALO + sx:, :sy] = above
        to[HALO:HALO + sx, sy:] = rows
        low, high = corner_tiles([rest[3 * a + n] for n in range(3)])
        for n in range(HALO):
            to[n, sy:] = low[n]
            to[HALO + sx + n, sy:] = high[n]
    lane = lane_of((ey, LANES))

    def unpack(x):
        packed = packs[x]
        for a in range(6):
            arrays[a][1][x] = unpacked(packed, a, lane)

    each(0, ex, 4, unpack)
    halfway, weight, kept = (half_m, half_h), (weight_m, weight_h), (kept_m, kept_h)
    diag = (diag_m, diag_h)

    def first_sweep(x):
        faces = [half[x] for half in bz]
        downs = ring_down(faces[0], faces[1], lane)
        centre, near = pull_slab(field, bx, by, bz, x, lane)
        for k in range(2):
            face = by[k][x]
            mass = WEIGHT * alpha[k][x]
            d = mass + bx[k][x] + bx[k][x - 1] + face + turn(face, 1, 0) + faces[k] + downs[k]
            w = relaxer(mass, d)
            diag[k][x] = d
            weight[k][x] = w
            halfway[k][x] = KEEP * centre[k] + w * (rhs[k][x] + near[k])

    each(1, ex - 1, 4, first_sweep)

    def second_sweep(x):
        centre, near = pull_slab(halfway, bx, by, bz, x, lane)
        for k in range(2):
            kept[k][x] = KEEP * centre[k] + weight[k][x] * (rhs[k][x] + near[k])

    each(2, ex - 2, 4, second_sweep)

    def residual(x):
        centre, near = pull_slab(kept, bx, by, bz, x, lane)
        for k in range(2):
            halfway[k][x] = rhs[k][x] - diag[k][x] * centre[k] + near[k]

    each(HALO, ex - HALO, 4, residual)

    x1, y1 = sx // 2, sy // 2
    for k in range(2):
        lanes = slice(k * LANES, (k + 1) * LANES)
        for i in range(x1):
            x = HALO + 2 * i
            total = None
            for p in BOTH:
                for q in BOTH:
                    term = halfway[k][x + p, pl.ds(q, y1, stride=2), :]
                    total = term if total is None else total + term
            sums[0, i, :, lanes] = total
            left[...] = turn(by[k][x] + by[k][x + 1], 1, 0)
            sums[1, i, :, lanes] = left[pl.ds(0, y1, stride=2), :]
    rhs1, low_y = to_level1(sums, 0, 2, pair_table(2 * LANES, LANES, False), 0.0625)
    weight1 = relaxer(coeffs1[0], coeffs1[1] + low_y)
    for n, values in enumerate((2.0 * rhs1, weight1, coeffs1[2], coeffs1[3], coeffs1[4])):
        own1[n] = values
        for send, face in zip(sends, faces_x(values[None], at_x % 2, n_x, NEAR)):
            send[n] = face[0]
        near_one[n], near_two[n] = faces_y(values, at_y % 2, NEAR)


def level2_rows(source, odd_axes, factor, x2, y2, z2):
    rows = []
    for i in range(x2):
        total = None
        for p in (1,) if odd_axes[0] else (0, 1):
            for q in (1,) if odd_axes[1] else (0, 1):
                term = source[2 * i + p, pl.ds(q, y2, stride=2), :]
                total = term if total is None else total + term
        rows.append(total)
    flat = jnp.concatenate(rows, axis=0)
    flat = factor * times_table(flat, pair_table(LANES, LANES, odd_axes[2]))
    lane = lane_of((y2, LANES))
    packed = jnp.zeros((y2, LANES), F32)
    for i in range(x2):
        mask = (lane >= i * z2) & (lane < (i + 1) * z2)
        packed = jnp.where(mask, turn(flat[i * y2:(i + 1) * y2], i * z2, 1), packed)
    return packed


def near_corners_kernel(counts, where_ref, *refs):
    halos_x, (two_y, one_y) = refs[:-2], refs[-2:]
    at_x, at_y, _ = position(where_ref)
    for a in range(halos_x[0].shape[0]):
        below, above = neighbours(counts[0], at_x, halos_x[0][a], halos_x[-1][a])
        for n, pair in enumerate(corner_sends(below, above, at_y % 2, True)):
            one_y[5 * a + n], two_y[5 * a + n] = pair


def near_kernel(counts, devices, where_ref, ring, *refs):
    n_x = 1 if counts[0] == 2 else 2
    halos_x = refs[:n_x]
    main_two, main_one, rest_two, rest_one, coarse2, copies, level1, left = refs[n_x:]
    n, bx1, by1, _ = ring.shape
    at_x, at_y, _ = position(where_ref)
    rest = neighbours(counts[1], at_y, rest_one[...], rest_two[...])
    rest = jnp.concatenate(rest[::-1], axis=1)
    whole = []
    for a in range(n):
        below, above = neighbours(counts[0], at_x, halos_x[0][a], halos_x[-1][a])
        rows = neighbours(counts[1], at_y, main_one[a], main_two[a])
        rows = jnp.concatenate(rows[::-1], axis=1)
        low, high = corner_tiles([rest[5 * a + k] for k in range(5)])
        rows = jnp.concatenate(
            [tile[None] for tile in low] + [rows] + [tile[None] for tile in high], axis=0
        )
        block = jnp.concatenate([below, ring[a], above], axis=0)
        whole.append(jnp.concatenate([block, rows], axis=1))
    rhs1, weight1 = whole[:2]
    faces1 = tuple(whole[2:])
    field1 = weight1 * rhs1
    field1 = sweep(field1, rhs1, weight1, faces1)
    for a, values in enumerate([field1] + whole):
        level1[a] = values
    mine = slice(NEAR, NEAR + bx1)
    inner = weight1[mine]
    diag1 = RELAX / jnp.where(inner > 0.0, inner, 1.0)
    remain = rhs1[mine] - diag1 * field1[mine] + pull(field1, faces1)[mine]
    left[...] = remain
    packed = level2_rows(left, (False,) * 3, 0.125, bx1 // 2, by1 // 2, LANES // 4)
    for d in range(devices):
        copies[d, 0] = packed
        for a in range(n - 1):
            copies[d, a + 1] = coarse2[a]


def halve(values, odd_axis, step):
    half = values.shape[0] // 2
    even = [values[2 * i:2 * i + 1] for i in range(half)]
    odd = [values[2 * i + 1:2 * i + 2] for i in range(half)]
    if odd_axis != 0:
        odd = [a + b for a, b in zip(even, odd)]
    values = jnp.concatenate(odd, axis=0)
    for axis in (1, 2):
        next_one = turn(values, -step, axis)
        values = next_one if odd_axis == axis else values + next_one
    return values


def double(values, step):
    values = values + turn(values, step, 1)
    values = values + turn(values, step, 2)
    return jnp.concatenate([values[i // 2:i // 2 + 1] for i in range(2 * values.shape[0])], axis=0)


def coarse_levels(mass, faces, y, z):
    levels = []
    for level in range(2, LEVELS):
        step = 2 ** (level - 2)
        bx, by, bz = faces
        row = lax.broadcasted_iota(jnp.int32, by.shape, 1)
        lane = lane_of(bz.shape)
        coupled = (
            bx,
            jnp.where(row == (y - 1) * step, 0.0, by),
            jnp.where(lane == (z - 1) * step, 0.0, bz),
        )
        mass = jnp.where((row % step == 0) & (lane % step == 0), mass, 0.0)
        diag = diagonal(mass, faces, coupled, step)
        levels.append((diag, relaxer(mass, diag), coupled))
        if level < LEVELS - 1:
            faces = tuple(0.0625 * halve(face, axis, step) for axis, face in enumerate(faces))
            mass = 0.125 * halve(mass, -1, step)
            y, z = y // 2, z // 2
    return levels


def coarse_cycle(level, rhs, levels):
    step = 2 ** (level - 2)
    diag, weight, faces = levels[level - 2]
    field = weight * rhs
    if level == LEVELS - 1:
        for _ in range(BOTTOM - 1):
            field = sweep(field, rhs, weight, faces, step)
        return field
    for _ in range(SWEEPS - 1):
        field = sweep(field, rhs, weight, faces, step)
    remain = rhs - diag * field + pull(field, faces, step)
    correction = coarse_cycle(level + 1, 0.125 * halve(remain, -1, step), levels)
    field = field + double(correction, step)
    for _ in range(SWEEPS):
        field = sweep(field, rhs, weight, faces, step)
    return field


def spread_out(counts, slots, whole):
    gx, gy, gz = counts
    y2 = slots.shape[-2]
    x2 = whole.shape[0] // gx
    z2 = LANES // x2
    lane = lane_of((y2, LANES))
    for i in range(gx):
        for j in range(gy):
            for x in range(x2):
                for part in range(whole.shape[2] // LANES):
                    total = jnp.zeros((y2, LANES), F32)
                    for k in range(LANES // z2):
                        column = part * (LANES // z2) + k
                        if column < gz:
                            block = slots[(i * gy + j) * gz + column]
                            mask = (lane >= k * z2) & (lane < (k + 1) * z2)
                            total = jnp.where(mask, turn(block, (k - x) * z2, 1), total)
                    lanes = slice(part * LANES, (part + 1) * LANES)
                    whole[i * x2 + x, j * y2:(j + 1) * y2, lanes] = total


def up_kernel(counts, where_ref, gathered, level1, *refs):
    kept, weight, rhs, bx, by, bz = zip(refs[0:12:2], refs[1:12:2])
    out, whole, second, spread_m, spread_h, field_m, field_h, half_m, half_h = refs[12:]
    gx, gy, gz = counts
    at_x, at_y, at_z = position(where_ref)
    sx, sy, sz = out.shape
    x1, y1 = sx // 2, sy // 2
    x2, y2, z2 = x1 // 2, y1 // 2, sz // 4
    columns = max(LANES, gz * z2)
    for a in range(5):
        spread_out(counts, gathered.at[:, a], whole.at[a])
    levels = coarse_levels(whole[1], (whole[2], whole[3], whole[4]), gy * y2, gz * z2)
    correction = coarse_cycle(2, whole[0], levels)

    wide = gx * x2
    half = NEAR // 2
    ex1, ey1 = x1 + 2 * NEAR, y1 + 2 * NEAR
    second[:half] = jnp.zeros((half,) + correction.shape[1:], F32)
    second[half:half + wide] = correction
    second[half + wide:] = jnp.zeros((half,) + correction.shape[1:], F32)
    window = second[pl.ds(at_x * x2, x2 + NEAR)]
    rows = correction.shape[1]
    row = iota2((ey1, rows), 0)
    col = iota2((ey1, rows), 1)
    place = jnp.where(row < y1 + NEAR, row, row - ey1)
    table_y = (col == at_y * y2 + lax.shift_right_arithmetic(place, 1)).astype(F32)
    row = iota2((columns, LANES), 0)
    col = iota2((columns, LANES), 1)
    place = jnp.where(col < LANES * 3 // 4, col, col - LANES)
    table_z = (row == at_z * z2 + lax.shift_right_arithmetic(place, 1)).astype(F32)
    flat = times_table(window.reshape((x2 + NEAR) * rows, columns), table_z)
    blocks = [table_times(table_y, flat[i * rows:(i + 1) * rows])[None] for i in range(x2 + NEAR)]
    lifted = jnp.concatenate([blocks[i // 2] for i in range(ex1)], axis=0)
    field1, rhs1, weight1 = level1[0], level1[1], level1[2]
    faces1 = (level1[3], level1[4], level1[5])
    field1 = field1 + jnp.where(weight1 > 0.0, lifted, 0.0)
    for _ in range(SWEEPS):
        field1 = sweep(field1, rhs1, weight1, faces1)

    ex, ey = sx + 2 * HALO, sy + 2 * HALO
    near = field1[NEAR - 1:NEAR + x1 + 1].reshape((x1 + 2) * ey1, LANES)
    row = iota2((LANES, 2 * LANES), 0)
    col = iota2((LANES, 2 * LANES), 1)
    lifted = times_table(near, (col // 2 == row).astype(F32))
    quarter = NEAR // 2
    for k, spread in enumerate((spread_m, spread_h)):
        block = lifted[:, k * LANES:(k + 1) * LANES].reshape(x1 + 2, ey1, LANES)
        for i in range(x1 + 2):
            for q in range(2):
                spread[i, pl.ds(q, y1, stride=2), :] = block[i, :y1]
                spread[i, pl.ds(sy + q, quarter, stride=2), :] = block[i, y1:y1 + quarter]
                spread[i, pl.ds(sy + HALO + q, quarter, stride=2), :] = block[i, ey1 - quarter:]
    before, after = (field_m, field_h), (half_m, half_h)
    first = HALO - 2
    for x in range(first, ex - first):
        for k, spread in enumerate((spread_m, spread_h)):
            before[k][x] = kept[k][x] + spread[(x - first) // 2]

    lane = lane_of((ey, LANES))

    def sweep_out(x):
        centre, around = pull_slab(before, bx, by, bz, x, lane)
        for k in range(2):
            after[k][x] = KEEP * centre[k] + weight[k][x] * (rhs[k][x] + around[k])

    each(first + 1, ex - first - 1, 4, sweep_out)

    def sweep_own(x):
        centre, around = pull_slab(after, bx, by, bz, x, lane)
        value = KEEP * centre[0] + weight[0][x] * (rhs[0][x] + around[0])
        out[x - HALO] = value[:sy]

    each(HALO, ex - HALO, 4, sweep_own)


def run(kernel, outs, where, arrays, scratch=(), grant=16, micros=1):
    return pl.pallas_call(
        kernel,
        out_shape=tuple(jax.ShapeDtypeStruct(shape, F32) for shape in outs),
        in_specs=[SM] * len(where) + [VM] * len(arrays),
        out_specs=tuple(VM for _ in outs),
        scratch_shapes=[pltpu.VMEM(shape, F32) for shape in scratch],
        compiler_params=pltpu.CompilerParams(vmem_limit_bytes=grant * 1024 * 1024),
        cost_estimate=pl.CostEstimate(
            flops=0, bytes_accessed=int(micros * 3.6e6), transcendentals=0
        ),
    )(*where, *arrays)


def swaps(axis, sends, other=None):
    count = lax.axis_size(axis)
    got = []
    for k, block in enumerate(sends):
        partner = list(range(count))
        for low in range(k, count - 1, 2):
            partner[low], partner[low + 1] = low + 1, low
        if k == 0:
            got.append(lax.ppermute(block, axis, list(enumerate(partner))))
            continue
        rows = lax.axis_size(other)
        pairs = []
        for row in range(rows):
            for i in range(count):
                ends = [(row, i), (min(row ^ 1, rows - 1) if partner[i] == i else row, partner[i])]
                if axis < other:
                    pairs.append(tuple(at * rows + line for line, at in ends))
                else:
                    pairs.append(tuple(line * count + at for line, at in ends))
        got.append(lax.ppermute(block, tuple(sorted((axis, other))), pairs))
    return got


def local(initial, right_side, alpha, beta_x, beta_y, beta_z):
    axes = ("gx", "gy", "gz")
    counts = tuple(lax.axis_size(axis) for axis in axes)
    devices = counts[0] * counts[1] * counts[2]
    where = (lax.axis_index("gx") * STRIDE + lax.axis_index("gy")) * STRIDE + lax.axis_index("gz")
    where = (where.astype(jnp.int32).reshape(1),)
    ins = (initial, right_side, alpha, beta_x, beta_y, beta_z)
    sx, sy, sz = initial.shape
    n_x = 1 if counts[0] == 2 else 2
    ex, ey = sx + 2 * HALO, sy + 2 * HALO
    fine = (ex, ey, LANES)

    *sends_x, two_y, one_y, first, second = run(
        functools.partial(faces_kernel, counts),
        [(6, HALO, sy, LANES)] * n_x
        + [(6, sx, HALO, LANES)] * 2
        + [(sx // 2, sy, LANES)] * 2,
        where,
        ins,
        grant=60,
    )
    main_x = tuple(swaps("gx", sends_x, "gy"))
    main_y = tuple(swaps("gy", (one_y, two_y), "gz")[::-1])
    got = swaps("gz", (first, second), "gy")
    zpack, *sends = run(
        functools.partial(halo_z_kernel, counts),
        [(sx, sy, LANES)] + [(HALO, sy, LANES)] * n_x,
        where,
        tuple(got),
    )
    halos_x = tuple(swaps("gx", sends, "gy"))
    two_y, one_y = run(
        functools.partial(corners_kernel, counts),
        [(21 + sx, HALO, LANES)] * 2,
        where,
        (zpack,) + main_x + halos_x,
    )
    rest_y = tuple(swaps("gy", (one_y, two_y), "gz")[::-1])
    x1, y1 = sx // 2, sy // 2
    ins = ins + (zpack,)
    coarse2, coeffs1 = run(
        functools.partial(coefficient_kernel, counts),
        [(4, y1 // 2, LANES), (5, x1, y1, LANES)],
        where,
        ins + main_x + halos_x,
        [(2, sx, sy, LANES), (5, x1, y1, 2 * LANES), (4, x1, y1, LANES)],
        micros=2,
    )
    own1, *outs = run(
        functools.partial(down_kernel, counts),
        [(5, x1, y1, LANES)]
        + [(5, NEAR, y1, LANES)] * n_x
        + [(5, x1, NEAR, LANES)] * 2
        + [fine] * 12,
        where,
        ins + main_x + halos_x + main_y + rest_y + (coeffs1,),
        [fine] * 9 + [(2, x1, y1, 2 * LANES), (ey, LANES)],
        24,
        micros=4,
    )
    sends_x, (two_y, one_y), fine_arrays = outs[:n_x], outs[n_x:n_x + 2], outs[n_x + 2:]

    near_x = tuple(swaps("gx", sends_x, "gy"))
    near_y = tuple(swaps("gy", (one_y, two_y), "gz")[::-1])
    two_y, one_y = run(
        functools.partial(near_corners_kernel, counts), [(25, NEAR, LANES)] * 2, where, near_x
    )
    rest_y = tuple(swaps("gy", (one_y, two_y), "gz")[::-1])
    copies, level1 = run(
        functools.partial(near_kernel, counts, devices),
        [(devices, 5, y1 // 2, LANES), (6, x1 + 2 * NEAR, y1 + 2 * NEAR, LANES)],
        where,
        (own1,) + near_x + near_y + rest_y + (coarse2,),
        [(x1, y1 + 2 * NEAR, LANES)],
    )

    gathered = lax.all_to_all(copies, axes, 0, 0, tiled=True)
    wide, rows = counts[0] * x1 // 2, counts[1] * y1 // 2
    columns = max(LANES, counts[2] * sz // 4)
    (result,) = run(
        functools.partial(up_kernel, counts),
        [(sx, sy, sz)],
        where,
        (gathered, level1) + tuple(fine_arrays),
        [(5, wide, rows, columns), (wide + NEAR, rows, columns)]
        + [(x1 + 2, ey, LANES)] * 2
        + [fine] * 4,
        24,
        micros=4,
    )
    return result


def solution(mesh):
    spec = P("gx", "gy", "gz")
    return jax.shard_map(
        local, mesh=mesh, in_specs=(spec,) * 6, out_specs=spec, check_vma=False
    )
```

```python
import functools

import jax
import jax.numpy as jnp
from jax import lax
from jax.experimental import pallas as pl
from jax.experimental.pallas import tpu as pltpu
from jax.sharding import PartitionSpec as P

LEVELS = 6
SWEEPS = 2
BOTTOM = 8
WEIGHT = 0.25 ** (LEVELS - 1)
RELAX = 2.0 / 3.0
KEEP = 1.0 / 3.0

HALO = 4
NEAR = 4
LANES = 128
PLACE = (0, 11, 21, 31, 41, 51)
DEPTH = (11, 10, 10, 10, 10, 11)
SIDE = LANES // 2
STRIDE = 256

VM = pl.BlockSpec(memory_space=pltpu.VMEM)
SM = pl.BlockSpec(memory_space=pltpu.SMEM)
F32 = jnp.float32


def position(where_ref):
    code = where_ref[0]
    return code // (STRIDE * STRIDE), code // STRIDE % STRIDE, code % STRIDE


def lane_of(shape):
    return lax.broadcasted_iota(jnp.int32, shape, len(shape) - 1)


def pick(flag, yes, no):
    return jnp.where(jnp.full(yes.shape, flag, jnp.int32) == 1, yes, no)


def neighbours(count, place, one, two):
    if count == 2:
        two = jnp.zeros_like(one)
    else:
        ends = jnp.full(two.shape, place, jnp.int32)
        two = jnp.where((ends == 0) | (ends == count - 1), 0.0, two)
    return pick(place % 2, one, two), pick(place % 2, two, one)


def turn(values, shift, axis):
    return pltpu.roll(values, shift % values.shape[axis], axis)


def parts_of(values):
    high = values.astype(jnp.bfloat16)
    rest = values - high.astype(F32)
    middle = rest.astype(jnp.bfloat16)
    low = (rest - middle.astype(F32)).astype(jnp.bfloat16)
    return high, middle, low


def times_table(values, table):
    table = table.astype(jnp.bfloat16)
    total = None
    for part in reversed(parts_of(values)):
        term = jnp.dot(part, table, preferred_element_type=F32)
        total = term if total is None else total + term
    return total


def table_times(table, values):
    table = table.astype(jnp.bfloat16)
    total = None
    for part in reversed(parts_of(values)):
        term = jnp.dot(table, part, preferred_element_type=F32)
        total = term if total is None else total + term
    return total


def iota2(shape, axis):
    return lax.broadcasted_iota(jnp.int32, shape, axis)


def pair_table(rows, cols, odd):
    row = iota2((rows, cols), 0)
    col = iota2((rows, cols), 1)
    hit = (row == 2 * col + 1) if odd else (row // 2 == col)
    return hit.astype(F32)


def below_x(values):
    if values.shape[0] == 1:
        return jnp.zeros_like(values)
    return jnp.concatenate([jnp.zeros_like(values[:1]), values[:-1]], axis=0)


def above_x(values):
    if values.shape[0] == 1:
        return jnp.zeros_like(values)
    return jnp.concatenate([values[1:], jnp.zeros_like(values[:1])], axis=0)


def pull(values, faces, step=1):
    bx, by, bz = faces
    total = bx * above_x(values) + below_x(bx * values)
    total = total + (by * turn(values, -step, 1) + turn(by * values, step, 1))
    return total + (bz * turn(values, -step, 2) + turn(bz * values, step, 2))


def diagonal(mass, faces, coupled, step=1):
    bx, by, bz = faces
    _, cy, cz = coupled
    return mass + bx + below_x(bx) + by + turn(cy, step, 1) + bz + turn(cz, step, 2)


def relaxer(mass, diag):
    inside = mass > 0.0
    return jnp.where(inside, RELAX / jnp.where(inside, diag, 1.0), 0.0)


def sweep(values, rhs, weight, faces, step=1):
    return KEEP * values + weight * (rhs + pull(values, faces, step))


def faces_x(values, odd, n_x, width):
    head, tail = values[:, :width], values[:, values.shape[1] - width:]
    return [pick(odd, head, tail), pick(odd, tail, head)][:n_x]


def faces_y(values, odd, width):
    head, tail = values[:, :width], values[:, values.shape[1] - width:]
    return pick(odd, head, tail), pick(odd, tail, head)


def corner_sends(below, above, odd, corners):
    packs = []
    for rows, sign in ((slice(0, 8), 1), (slice(below.shape[1] - 8, below.shape[1]), -1)):
        low = [below[3 - i, rows] for i in range(4)]
        high = [above[i, rows] for i in range(4)]
        pack = []
        if corners:
            pack = [low[0], high[0]]
            low, high = low[1:], high[1:]
        row = iota2(low[0].shape, 0)
        row = row if sign == 1 else 7 - row
        pack += [
            jnp.where(row < 3, low[0], turn(low[2], 3 * sign, 0)),
            jnp.where(row < 2, low[1], turn(high[1], 2 * sign, 0)),
            jnp.where(row < 3, high[0], turn(high[2], 3 * sign, 0)),
        ]
        packs.append([p[:4] if sign == 1 else p[4:] for p in pack])
    return [(pick(odd, h, t), pick(odd, t, h)) for h, t in zip(*packs)]


def corner_tiles(tiles):
    first, second, third = tiles[-3:]
    upper = iota2(first.shape, 0) < 4

    def inner(tile, by):
        return jnp.where(upper, turn(tile, -by, 0), turn(tile, by, 0))

    low = [first, second, inner(first, 3)]
    high = [third, inner(second, 2), inner(third, 3)]
    if len(tiles) == 5:
        low, high = tiles[:1] + low, tiles[1:2] + high
    else:
        zero = jnp.zeros_like(first)
        low, high = low + [zero], high + [zero]
    return low[::-1], high


def faces_kernel(counts, where_ref, *refs):
    ins, refs = refs[:6], refs[6:]
    n_x = 1 if counts[0] == 2 else 2
    sends_x, (two_y, one_y, first, second) = refs[:n_x], refs[n_x:]
    odd_x, odd_y, odd = (place % 2 for place in position(where_ref))
    sx, sy, sz = ins[0].shape
    half = sx // 2
    lane = lane_of((half, sy, LANES))
    head = jnp.zeros((half, sy, LANES), F32)
    tail = head
    for a, ref in enumerate(ins):
        for send, face in zip(sends_x, faces_x(ref[...][None], odd_x, n_x, HALO)):
            send[a] = face[0]
        one_y[a], two_y[a] = faces_y(ref[...], odd_y, HALO)
        for g in range(2):
            values = ref[g * half:(g + 1) * half]
            at = SIDE * g + PLACE[a]
            mask = (lane >= at) & (lane < at + DEPTH[a])
            head = jnp.where(mask, turn(values, at, 2), head)
            tail = jnp.where(mask, turn(values, at + DEPTH[a], 2), tail)
    first[...] = pick(odd, head, tail)
    second[...] = pick(odd, tail, head)


def halo_z_kernel(counts, where_ref, one_ref, two_ref, zpack, *sends):
    at_x, _, at_z = position(where_ref)
    half = one_ref.shape[0]
    below, above = neighbours(counts[2], at_z, one_ref[...], two_ref[...])
    lane = lane_of(below.shape)
    zpack[:half] = jnp.where(lane < SIDE, above, turn(below, SIDE, 2))
    zpack[half:] = jnp.where(lane < SIDE, turn(above, SIDE, 2), below)
    for send, face in zip(sends, faces_x(zpack[...][None], at_x % 2, len(sends), HALO)):
        send[...] = face[0]


def corners_kernel(counts, where_ref, zpack, *refs):
    n_x = 1 if counts[0] == 2 else 2
    main_x, halos_x, (two_y, one_y) = refs[:n_x], refs[n_x:2 * n_x], refs[2 * n_x + 1:]
    at_x, at_y, _ = position(where_ref)
    for a in range(7):
        if a < 6:
            below, above = neighbours(counts[0], at_x, main_x[0][a], main_x[-1][a])
        else:
            below, above = neighbours(counts[0], at_x, halos_x[0][...], halos_x[-1][...])
        for n, pair in enumerate(corner_sends(below, above, at_y % 2, False)):
            one_y[3 * a + n], two_y[3 * a + n] = pair
    one_y[21:], two_y[21:] = faces_y(zpack[...], at_y % 2, HALO)


def each(first, last, step, body):
    rounds = (last - first) // step

    def go(i, carry):
        for j in range(step):
            body(first + i * step + j)
        return carry

    if rounds:
        lax.fori_loop(0, rounds, go, 0)
    for x in range(first + rounds * step, last):
        body(x)


def ring_up(main, halo, lane):
    main_up, halo_up = turn(main, -1, 1), turn(halo, -1, 1)
    last = lane == LANES - 1
    return jnp.where(last, halo_up, main_up), jnp.where(last, main_up, halo_up)


def ring_down(main, halo, lane):
    main_down, halo_down = turn(main, 1, 1), turn(halo, 1, 1)
    zero = lane == 0
    return jnp.where(zero, halo_down, main_down), jnp.where(zero, main_down, halo_down)


def pull_slab(field, bx, by, bz, x, lane):
    centre = [half[x] for half in field]
    out = []
    for k in range(2):
        c, face = centre[k], by[k][x]
        t = bx[k][x] * field[k][x + 1] + bx[k][x - 1] * field[k][x - 1]
        out.append(t + (face * turn(c, -1, 0) + turn(face * c, 1, 0)))
    faces = [half[x] for half in bz]
    ups = ring_up(centre[0], centre[1], lane)
    downs = ring_down(faces[0] * centre[0], faces[1] * centre[1], lane)
    return centre, [out[k] + (faces[k] * ups[k] + downs[k]) for k in range(2)]


def unpacked(packed, a, lane):
    at, depth = PLACE[a], DEPTH[a]
    axis = packed.ndim - 1
    right, left = turn(packed, -at, axis), turn(packed, SIDE - depth - at, axis)
    return jnp.where(lane < depth, right, jnp.where(lane >= LANES - depth, left, 0.0))


def rows_of(source, x, count, firsts, seconds):
    total = None
    for p in firsts:
        for q in seconds:
            term = source[x + p, pl.ds(q, count, stride=2), :]
            total = term if total is None else total + term
    return total


BOTH, ODD = (0, 1), (1,)


def to_level1(sums, first, count, table, factor):
    _, x1, y1, _ = sums.shape
    flat = sums[first:first + count].reshape(count * x1 * y1, 2 * LANES)
    return factor * times_table(flat, table).reshape(count, x1, y1, LANES)


def coefficient_kernel(counts, where_ref, *refs):
    ins, refs = refs[:7], refs[7:]
    n_x = 1 if counts[0] == 2 else 2
    main_x, refs = refs[:n_x], refs[n_x:]
    arrays, (coarse2, coeffs1, sums, pairing) = refs[:12], refs[12:]
    sx, sy, sz = ins[0].shape
    at_x = position(where_ref)[0]
    x1, y1 = sx // 2, sy // 2
    lane = lane_of((sx, sy, LANES))
    lanes = [slice(k * LANES, (k + 1) * LANES) for k in range(2)]
    mine = slice(HALO, HALO + sx)
    for a in range(6):
        to = arrays[2 * a]
        below, above = neighbours(counts[0], at_x, main_x[0][a], main_x[-1][a])
        to[:HALO, :sy] = below
        to[mine, :sy] = ins[a][...]
        to[HALO + sx:, :sy] = above
        arrays[2 * a + 1][mine, :sy] = unpacked(ins[6][...], a, lane)
    for n, (firsts, seconds) in enumerate(((BOTH, BOTH), (ODD, BOTH), (BOTH, ODD), (BOTH, BOTH))):
        for k in range(2):
            for i in range(x1):
                source = arrays[2 * (n + 2) + k]
                sums[n, i, :, lanes[k]] = rows_of(source, HALO + 2 * i, y1, firsts, seconds)
    pairs = pair_table(2 * LANES, LANES, False)
    odds = pair_table(2 * LANES, LANES, True)
    paired = to_level1(sums, 0, 3, pairs, 0.0625)
    mass1 = (2.0 * WEIGHT) * paired[0]
    faces1 = (paired[1], paired[2], to_level1(sums, 3, 1, odds, 0.0625)[0])
    diag1 = mass1 + faces1[0] + below_x(faces1[0])
    diag1 = diag1 + faces1[1] + faces1[2] + turn(faces1[2], 1, 2)
    for n, values in enumerate((mass1, diag1) + faces1):
        coeffs1[n] = values
    parts = (
        (mass1, False, False, False, 0.125),
        (faces1[0], True, False, False, 0.0625),
        (faces1[1], False, True, False, 0.0625),
        (faces1[2], False, False, True, 0.0625),
    )
    for n, (values, *odd_axes, factor) in enumerate(parts):
        pairing[n] = values
        coarse2[n] = level2_rows(pairing.at[n], odd_axes, factor, x1 // 2, y1 // 2, sz // 4)


def down_kernel(counts, where_ref, zpack, *refs):
    refs = refs[12:]
    n_x = 1 if counts[0] == 2 else 2
    halos_x = refs[:n_x]
    main_two, main_one, rest_two, rest_one, coeffs1 = refs[n_x:5 + n_x]
    flat, refs = refs[5 + n_x:17 + n_x], refs[17 + n_x:]
    arrays = tuple(zip(flat[::2], flat[1::2]))
    own1, refs = refs[0], refs[1:]
    sends, near_two, near_one, refs = refs[:n_x], refs[n_x], refs[n_x + 1], refs[n_x + 2:]
    kept_m, kept_h, weight_m, weight_h = refs[:4]
    packs, half_m, half_h, diag_m, diag_h, sums, left = refs[4:]
    field, rhs, alpha, bx, by, bz = arrays
    sx, sy, sz = zpack.shape
    ex, ey = sx + 2 * HALO, sy + 2 * HALO
    at_x, at_y, _ = position(where_ref)

    rest = neighbours(counts[1], at_y, rest_one[...], rest_two[...])
    rest = jnp.concatenate(rest[::-1], axis=1)
    for a in range(7):
        if a < 6:
            to = arrays[a][0]
            rows = neighbours(counts[1], at_y, main_one[a], main_two[a])
            rows = jnp.concatenate(rows[::-1], axis=1)
        else:
            to = packs
            rows = rest[21:]
            below, above = neighbours(counts[0], at_x, halos_x[0][...], halos_x[-1][...])
            to[:HALO, :sy] = below
            to[HALO + sx:, :sy] = above
        to[HALO:HALO + sx, sy:] = rows
        low, high = corner_tiles([rest[3 * a + n] for n in range(3)])
        for n in range(HALO):
            to[n, sy:] = low[n]
            to[HALO + sx + n, sy:] = high[n]
    lane = lane_of((ey, LANES))
    lane_low = lane_of((2 * HALO, LANES))

    def unpack_rows(x):
        packed = packs[x, sy:]
        for a in range(6):
            arrays[a][1][x, sy:] = unpacked(packed, a, lane_low)

    def unpack(x):
        packed = packs[x]
        for a in range(6):
            arrays[a][1][x] = unpacked(packed, a, lane)

    each(0, HALO, HALO, unpack)
    each(HALO, HALO + sx, 8, unpack_rows)
    each(HALO + sx, ex, HALO, unpack)
    halfway, weight, kept = (half_m, half_h), (weight_m, weight_h), (kept_m, kept_h)
    diag = (diag_m, diag_h)

    def first_sweep(x):
        faces = [half[x] for half in bz]
        downs = ring_down(faces[0], faces[1], lane)
        centre, near = pull_slab(field, bx, by, bz, x, lane)
        for k in range(2):
            face = by[k][x]
            mass = WEIGHT * alpha[k][x]
            d = mass + bx[k][x] + bx[k][x - 1] + face + turn(face, 1, 0) + faces[k] + downs[k]
            w = relaxer(mass, d)
            diag[k][x] = d
            weight[k][x] = w
            halfway[k][x] = KEEP * centre[k] + w * (rhs[k][x] + near[k])

    each(1, ex - 1, 4, first_sweep)

    def second_sweep(x):
        centre, near = pull_slab(halfway, bx, by, bz, x, lane)
        for k in range(2):
            kept[k][x] = KEEP * centre[k] + weight[k][x] * (rhs[k][x] + near[k])

    each(2, ex - 2, 4, second_sweep)

    def residual(x):
        centre, near = pull_slab(kept, bx, by, bz, x, lane)
        for k in range(2):
            halfway[k][x] = rhs[k][x] - diag[k][x] * centre[k] + near[k]

    each(HALO, ex - HALO, 4, residual)

    x1, y1 = sx // 2, sy // 2
    for k in range(2):
        lanes = slice(k * LANES, (k + 1) * LANES)
        for i in range(x1):
            x = HALO + 2 * i
            sums[0, i, :, lanes] = rows_of(halfway[k], x, y1, BOTH, BOTH)
            left[...] = turn(by[k][x] + by[k][x + 1], 1, 0)
            sums[1, i, :, lanes] = left[pl.ds(0, y1, stride=2), :]
        sums[2, 0, :, lanes] = rows_of(bx[k], HALO - 1, y1, (0,), BOTH)
        sums[2, 1:, :, lanes] = jnp.zeros((x1 - 1, y1, LANES), F32)
    rhs1, low_y, low_x = to_level1(sums, 0, 3, pair_table(2 * LANES, LANES, False), 0.0625)
    weight1 = relaxer(coeffs1[0], coeffs1[1] + low_y + low_x)
    for n, values in enumerate((2.0 * rhs1, weight1, coeffs1[2], coeffs1[3], coeffs1[4])):
        own1[n] = values
        for send, face in zip(sends, faces_x(values[None], at_x % 2, n_x, NEAR)):
            send[n] = face[0]
        near_one[n], near_two[n] = faces_y(values, at_y % 2, NEAR)


def level2_rows(source, odd_axes, factor, x2, y2, z2):
    rows = []
    for i in range(x2):
        total = None
        for p in (1,) if odd_axes[0] else (0, 1):
            for q in (1,) if odd_axes[1] else (0, 1):
                term = source[2 * i + p, pl.ds(q, y2, stride=2), :]
                total = term if total is None else total + term
        rows.append(total)
    flat = jnp.concatenate(rows, axis=0)
    flat = factor * times_table(flat, pair_table(LANES, LANES, odd_axes[2]))
    lane = lane_of((y2, LANES))
    packed = jnp.zeros((y2, LANES), F32)
    for i in range(x2):
        mask = (lane >= i * z2) & (lane < (i + 1) * z2)
        packed = jnp.where(mask, turn(flat[i * y2:(i + 1) * y2], i * z2, 1), packed)
    return packed


def near_corners_kernel(counts, where_ref, *refs):
    halos_x, (two_y, one_y) = refs[:-2], refs[-2:]
    at_x, at_y, _ = position(where_ref)
    for a in range(halos_x[0].shape[0]):
        below, above = neighbours(counts[0], at_x, halos_x[0][a], halos_x[-1][a])
        for n, pair in enumerate(corner_sends(below, above, at_y % 2, True)):
            one_y[5 * a + n], two_y[5 * a + n] = pair


def near_kernel(counts, devices, where_ref, ring, *refs):
    n_x = 1 if counts[0] == 2 else 2
    halos_x = refs[:n_x]
    main_two, main_one, rest_two, rest_one, coarse2, copies, level1, left = refs[n_x:]
    n, bx1, by1, _ = ring.shape
    at_x, at_y, _ = position(where_ref)
    rest = neighbours(counts[1], at_y, rest_one[...], rest_two[...])
    rest = jnp.concatenate(rest[::-1], axis=1)
    whole = []
    for a in range(n):
        below, above = neighbours(counts[0], at_x, halos_x[0][a], halos_x[-1][a])
        rows = neighbours(counts[1], at_y, main_one[a], main_two[a])
        rows = jnp.concatenate(rows[::-1], axis=1)
        low, high = corner_tiles([rest[5 * a + k] for k in range(5)])
        rows = jnp.concatenate(
            [tile[None] for tile in low] + [rows] + [tile[None] for tile in high], axis=0
        )
        block = jnp.concatenate([below, ring[a], above], axis=0)
        whole.append(jnp.concatenate([block, rows], axis=1))
    rhs1, weight1 = whole[:2]
    faces1 = tuple(whole[2:])
    field1 = weight1 * rhs1
    field1 = sweep(field1, rhs1, weight1, faces1)
    for a, values in enumerate([field1] + whole):
        level1[a] = values
    mine = slice(NEAR, NEAR + bx1)
    inner = weight1[mine]
    diag1 = RELAX / jnp.where(inner > 0.0, inner, 1.0)
    remain = rhs1[mine] - diag1 * field1[mine] + pull(field1, faces1)[mine]
    left[...] = remain
    packed = level2_rows(left, (False,) * 3, 0.125, bx1 // 2, by1 // 2, LANES // 4)
    for d in range(devices):
        copies[d, 0] = packed
        for a in range(n - 1):
            copies[d, a + 1] = coarse2[a]


def halve(values, odd_axis, step):
    half = values.shape[0] // 2
    even = [values[2 * i:2 * i + 1] for i in range(half)]
    odd = [values[2 * i + 1:2 * i + 2] for i in range(half)]
    if odd_axis != 0:
        odd = [a + b for a, b in zip(even, odd)]
    values = jnp.concatenate(odd, axis=0)
    for axis in (1, 2):
        next_one = turn(values, -step, axis)
        values = next_one if odd_axis == axis else values + next_one
    return values


def double(values, step):
    values = values + turn(values, step, 1)
    values = values + turn(values, step, 2)
    return jnp.concatenate([values[i // 2:i // 2 + 1] for i in range(2 * values.shape[0])], axis=0)


def coarse_levels(mass, faces, y, z):
    levels = []
    for level in range(2, LEVELS):
        step = 2 ** (level - 2)
        bx, by, bz = faces
        row = lax.broadcasted_iota(jnp.int32, by.shape, 1)
        lane = lane_of(bz.shape)
        coupled = (
            bx,
            jnp.where(row == (y - 1) * step, 0.0, by),
            jnp.where(lane == (z - 1) * step, 0.0, bz),
        )
        mass = jnp.where((row % step == 0) & (lane % step == 0), mass, 0.0)
        diag = diagonal(mass, faces, coupled, step)
        levels.append((diag, relaxer(mass, diag), coupled))
        if level < LEVELS - 1:
            faces = tuple(0.0625 * halve(face, axis, step) for axis, face in enumerate(faces))
            mass = 0.125 * halve(mass, -1, step)
            y, z = y // 2, z // 2
    return levels


def coarse_cycle(level, rhs, levels):
    step = 2 ** (level - 2)
    diag, weight, faces = levels[level - 2]
    field = weight * rhs
    if level == LEVELS - 1:
        for _ in range(BOTTOM - 1):
            field = sweep(field, rhs, weight, faces, step)
        return field
    for _ in range(SWEEPS - 1):
        field = sweep(field, rhs, weight, faces, step)
    remain = rhs - diag * field + pull(field, faces, step)
    correction = coarse_cycle(level + 1, 0.125 * halve(remain, -1, step), levels)
    field = field + double(correction, step)
    for _ in range(SWEEPS):
        field = sweep(field, rhs, weight, faces, step)
    return field


def spread_out(counts, slots, whole):
    gx, gy, gz = counts
    y2 = slots.shape[-2]
    x2 = whole.shape[0] // gx
    z2 = LANES // x2
    lane = lane_of((y2, LANES))
    for i in range(gx):
        for j in range(gy):
            for x in range(x2):
                for part in range(whole.shape[2] // LANES):
                    total = jnp.zeros((y2, LANES), F32)
                    for k in range(LANES // z2):
                        column = part * (LANES // z2) + k
                        if column < gz:
                            block = slots[(i * gy + j) * gz + column]
                            mask = (lane >= k * z2) & (lane < (k + 1) * z2)
                            total = jnp.where(mask, turn(block, (k - x) * z2, 1), total)
                    lanes = slice(part * LANES, (part + 1) * LANES)
                    whole[i * x2 + x, j * y2:(j + 1) * y2, lanes] = total


def up_kernel(counts, where_ref, gathered, level1, *refs):
    kept, weight, rhs, bx, by, bz = zip(refs[0:12:2], refs[1:12:2])
    out, whole, second, spread_m, spread_h, field_m, field_h, half_m, half_h = refs[12:]
    gx, gy, gz = counts
    at_x, at_y, at_z = position(where_ref)
    sx, sy, sz = out.shape
    x1, y1 = sx // 2, sy // 2
    x2, y2, z2 = x1 // 2, y1 // 2, sz // 4
    columns = max(LANES, gz * z2)
    for a in range(5):
        spread_out(counts, gathered.at[:, a], whole.at[a])
    levels = coarse_levels(whole[1], (whole[2], whole[3], whole[4]), gy * y2, gz * z2)
    correction = coarse_cycle(2, whole[0], levels)

    wide = gx * x2
    half = NEAR // 2
    ex1, ey1 = x1 + 2 * NEAR, y1 + 2 * NEAR
    second[:half] = jnp.zeros((half,) + correction.shape[1:], F32)
    second[half:half + wide] = correction
    second[half + wide:] = jnp.zeros((half,) + correction.shape[1:], F32)
    window = second[pl.ds(at_x * x2, x2 + NEAR)]
    rows = correction.shape[1]
    row = iota2((ey1, rows), 0)
    col = iota2((ey1, rows), 1)
    place = jnp.where(row < y1 + NEAR, row, row - ey1)
    table_y = (col == at_y * y2 + lax.shift_right_arithmetic(place, 1)).astype(F32)
    row = iota2((columns, LANES), 0)
    col = iota2((columns, LANES), 1)
    place = jnp.where(col < LANES * 3 // 4, col, col - LANES)
    table_z = (row == at_z * z2 + lax.shift_right_arithmetic(place, 1)).astype(F32)
    flat = times_table(window.reshape((x2 + NEAR) * rows, columns), table_z)
    blocks = [table_times(table_y, flat[i * rows:(i + 1) * rows])[None] for i in range(x2 + NEAR)]
    lifted = jnp.concatenate([blocks[i // 2] for i in range(ex1)], axis=0)
    field1, rhs1, weight1 = level1[0], level1[1], level1[2]
    faces1 = (level1[3], level1[4], level1[5])
    field1 = field1 + jnp.where(weight1 > 0.0, lifted, 0.0)
    for _ in range(SWEEPS):
        field1 = sweep(field1, rhs1, weight1, faces1)

    ex, ey = sx + 2 * HALO, sy + 2 * HALO
    near = field1[NEAR - 1:NEAR + x1 + 1].reshape((x1 + 2) * ey1, LANES)
    row = iota2((LANES, 2 * LANES), 0)
    col = iota2((LANES, 2 * LANES), 1)
    lifted = times_table(near, (col // 2 == row).astype(F32))
    quarter = NEAR // 2
    for k, spread in enumerate((spread_m, spread_h)):
        block = lifted[:, k * LANES:(k + 1) * LANES].reshape(x1 + 2, ey1, LANES)
        for i in range(x1 + 2):
            for q in range(2):
                spread[i, pl.ds(q, y1, stride=2), :] = block[i, :y1]
                spread[i, pl.ds(sy + q, quarter, stride=2), :] = block[i, y1:y1 + quarter]
                spread[i, pl.ds(sy + HALO + q, quarter, stride=2), :] = block[i, ey1 - quarter:]
    before, after = (field_m, field_h), (half_m, half_h)
    first = HALO - 2
    for x in range(first, ex - first):
        for k, spread in enumerate((spread_m, spread_h)):
            before[k][x] = kept[k][x] + spread[(x - first) // 2]

    lane = lane_of((ey, LANES))

    def sweep_out(x):
        centre, around = pull_slab(before, bx, by, bz, x, lane)
        for k in range(2):
            after[k][x] = KEEP * centre[k] + weight[k][x] * (rhs[k][x] + around[k])

    each(first + 1, ex - first - 1, 4, sweep_out)

    def sweep_own(x):
        centre, around = pull_slab(after, bx, by, bz, x, lane)
        value = KEEP * centre[0] + weight[0][x] * (rhs[0][x] + around[0])
        out[x - HALO] = value[:sy]

    each(HALO, ex - HALO, 4, sweep_own)


def run(kernel, outs, where, arrays, scratch=(), grant=16, micros=1, aliases={}):
    return pl.pallas_call(
        kernel,
        out_shape=tuple(jax.ShapeDtypeStruct(shape, F32) for shape in outs),
        in_specs=[SM] * len(where) + [VM] * len(arrays),
        out_specs=tuple(VM for _ in outs),
        input_output_aliases=aliases,
        scratch_shapes=[pltpu.VMEM(shape, F32) for shape in scratch],
        compiler_params=pltpu.CompilerParams(vmem_limit_bytes=grant * 1024 * 1024),
        cost_estimate=pl.CostEstimate(
            flops=0, bytes_accessed=int(micros * 3.6e6), transcendentals=0
        ),
    )(*where, *arrays)


def swaps(axis, sends, other=None):
    count = lax.axis_size(axis)
    got = []
    for k, block in enumerate(sends):
        partner = list(range(count))
        for low in range(k, count - 1, 2):
            partner[low], partner[low + 1] = low + 1, low
        if k == 0:
            got.append(lax.ppermute(block, axis, list(enumerate(partner))))
            continue
        rows = lax.axis_size(other)
        pairs = []
        for row in range(rows):
            for i in range(count):
                ends = [(row, i), (min(row ^ 1, rows - 1) if partner[i] == i else row, partner[i])]
                if axis < other:
                    pairs.append(tuple(at * rows + line for line, at in ends))
                else:
                    pairs.append(tuple(line * count + at for line, at in ends))
        got.append(lax.ppermute(block, tuple(sorted((axis, other))), pairs))
    return got


def local(initial, right_side, alpha, beta_x, beta_y, beta_z):
    axes = ("gx", "gy", "gz")
    counts = tuple(lax.axis_size(axis) for axis in axes)
    devices = counts[0] * counts[1] * counts[2]
    where = (lax.axis_index("gx") * STRIDE + lax.axis_index("gy")) * STRIDE + lax.axis_index("gz")
    where = (where.astype(jnp.int32).reshape(1),)
    ins = (initial, right_side, alpha, beta_x, beta_y, beta_z)
    sx, sy, sz = initial.shape
    n_x = 1 if counts[0] == 2 else 2
    ex, ey = sx + 2 * HALO, sy + 2 * HALO
    fine = (ex, ey, LANES)

    *sends_x, two_y, one_y, first, second = run(
        functools.partial(faces_kernel, counts),
        [(6, HALO, sy, LANES)] * n_x
        + [(6, sx, HALO, LANES)] * 2
        + [(sx // 2, sy, LANES)] * 2,
        where,
        ins,
        grant=60,
    )
    main_x = tuple(swaps("gx", sends_x, "gy"))
    main_y = tuple(swaps("gy", (one_y, two_y), "gz")[::-1])
    got = swaps("gz", (first, second), "gy")
    zpack, *sends = run(
        functools.partial(halo_z_kernel, counts),
        [(sx, sy, LANES)] + [(HALO, sy, LANES)] * n_x,
        where,
        tuple(got),
    )
    halos_x = tuple(swaps("gx", sends, "gy"))
    x1, y1 = sx // 2, sy // 2
    *laid, coarse2, coeffs1 = run(
        functools.partial(coefficient_kernel, counts),
        [fine] * 12 + [(4, y1 // 2, LANES), (5, x1, y1, LANES)],
        where,
        ins + (zpack,) + main_x,
        [(4, x1, y1, 2 * LANES), (4, x1, y1, LANES)],
        micros=2,
    )
    two_y, one_y = run(
        functools.partial(corners_kernel, counts),
        [(21 + sx, HALO, LANES)] * 2,
        where,
        (zpack,) + main_x + halos_x + (coarse2,),
    )
    rest_y = tuple(swaps("gy", (one_y, two_y), "gz")[::-1])
    outs = run(
        functools.partial(down_kernel, counts),
        [fine] * 12
        + [(5, x1, y1, LANES)]
        + [(5, NEAR, y1, LANES)] * n_x
        + [(5, x1, NEAR, LANES)] * 2
        + [fine] * 4,
        where,
        (zpack,) + tuple(laid) + halos_x + main_y + rest_y + (coeffs1,),
        [fine] * 5 + [(3, x1, y1, 2 * LANES), (ey, LANES)],
        24,
        micros=4,
        aliases={n + 2: n for n in range(12)},
    )
    laid, own1, outs = outs[:12], outs[12], outs[13:]
    sends_x, (two_y, one_y), fine_arrays = outs[:n_x], outs[n_x:n_x + 2], outs[n_x + 2:]
    fine_arrays = tuple(fine_arrays) + tuple(laid[2:4]) + tuple(laid[6:])

    near_x = tuple(swaps("gx", sends_x, "gy"))
    near_y = tuple(swaps("gy", (one_y, two_y), "gz")[::-1])
    two_y, one_y = run(
        functools.partial(near_corners_kernel, counts), [(25, NEAR, LANES)] * 2, where, near_x
    )
    rest_y = tuple(swaps("gy", (one_y, two_y), "gz")[::-1])
    copies, level1 = run(
        functools.partial(near_kernel, counts, devices),
        [(devices, 5, y1 // 2, LANES), (6, x1 + 2 * NEAR, y1 + 2 * NEAR, LANES)],
        where,
        (own1,) + near_x + near_y + rest_y + (coarse2,),
        [(x1, y1 + 2 * NEAR, LANES)],
    )

    gathered = lax.all_to_all(copies, axes, 0, 0, tiled=True)
    wide, rows = counts[0] * x1 // 2, counts[1] * y1 // 2
    columns = max(LANES, counts[2] * sz // 4)
    (result,) = run(
        functools.partial(up_kernel, counts),
        [(sx, sy, sz)],
        where,
        (gathered, level1) + tuple(fine_arrays),
        [(5, wide, rows, columns), (wide + NEAR, rows, columns)]
        + [(x1 + 2, ey, LANES)] * 2
        + [fine] * 4,
        24,
        micros=4,
    )
    return result


def solution(mesh):
    spec = P("gx", "gy", "gz")
    return jax.shard_map(
        local, mesh=mesh, in_specs=(spec,) * 6, out_specs=spec, check_vma=False
    )
```

```python
import functools

import jax
import jax.numpy as jnp
from jax import lax
from jax.experimental import pallas as pl
from jax.experimental.pallas import tpu as pltpu
from jax.sharding import PartitionSpec as P

LEVELS = 6
SWEEPS = 2
BOTTOM = 8
WEIGHT = 0.25 ** (LEVELS - 1)
RELAX = 2.0 / 3.0
KEEP = 1.0 / 3.0

HALO = 4
NEAR = 4
LANES = 128
PLACE = (0, 11, 21, 31, 41, 51)
DEPTH = (11, 10, 10, 10, 10, 11)
SIDE = LANES // 2
STRIDE = 256

VM = pl.BlockSpec(memory_space=pltpu.VMEM)
SM = pl.BlockSpec(memory_space=pltpu.SMEM)
F32 = jnp.float32


def position(where_ref):
    code = where_ref[0]
    return code // (STRIDE * STRIDE), code // STRIDE % STRIDE, code % STRIDE


def lane_of(shape):
    return lax.broadcasted_iota(jnp.int32, shape, len(shape) - 1)


def pick(flag, yes, no):
    return jnp.where(jnp.full(yes.shape, flag, jnp.int32) == 1, yes, no)


def neighbours(count, place, one, two):
    if count == 2:
        two = jnp.zeros_like(one)
    else:
        ends = jnp.full(two.shape, place, jnp.int32)
        two = jnp.where((ends == 0) | (ends == count - 1), 0.0, two)
    return pick(place % 2, one, two), pick(place % 2, two, one)


def turn(values, shift, axis):
    return pltpu.roll(values, shift % values.shape[axis], axis)


def parts_of(values):
    high = values.astype(jnp.bfloat16)
    rest = values - high.astype(F32)
    middle = rest.astype(jnp.bfloat16)
    low = (rest - middle.astype(F32)).astype(jnp.bfloat16)
    return high, middle, low


def times_table(values, table):
    table = table.astype(jnp.bfloat16)
    total = None
    for part in reversed(parts_of(values)):
        term = jnp.dot(part, table, preferred_element_type=F32)
        total = term if total is None else total + term
    return total


def table_times(table, values):
    table = table.astype(jnp.bfloat16)
    total = None
    for part in reversed(parts_of(values)):
        term = jnp.dot(table, part, preferred_element_type=F32)
        total = term if total is None else total + term
    return total


def iota2(shape, axis):
    return lax.broadcasted_iota(jnp.int32, shape, axis)


def pair_table(rows, cols, odd):
    row = iota2((rows, cols), 0)
    col = iota2((rows, cols), 1)
    hit = (row == 2 * col + 1) if odd else (row // 2 == col)
    return hit.astype(F32)


def below_x(values):
    if values.shape[0] == 1:
        return jnp.zeros_like(values)
    return jnp.concatenate([jnp.zeros_like(values[:1]), values[:-1]], axis=0)


def above_x(values):
    if values.shape[0] == 1:
        return jnp.zeros_like(values)
    return jnp.concatenate([values[1:], jnp.zeros_like(values[:1])], axis=0)


def pull(values, faces, step=1):
    bx, by, bz = faces
    total = bx * above_x(values) + below_x(bx * values)
    total = total + (by * turn(values, -step, 1) + turn(by * values, step, 1))
    return total + (bz * turn(values, -step, 2) + turn(bz * values, step, 2))


def diagonal(mass, faces, coupled, step=1):
    bx, by, bz = faces
    _, cy, cz = coupled
    return mass + bx + below_x(bx) + by + turn(cy, step, 1) + bz + turn(cz, step, 2)


def relaxer(mass, diag):
    inside = mass > 0.0
    return jnp.where(inside, RELAX / jnp.where(inside, diag, 1.0), 0.0)


def sweep(values, rhs, weight, faces, step=1):
    return KEEP * values + weight * (rhs + pull(values, faces, step))


def faces_x(values, odd, n_x, width):
    head, tail = values[:, :width], values[:, values.shape[1] - width:]
    return [pick(odd, head, tail), pick(odd, tail, head)][:n_x]


def faces_y(values, odd, width):
    head, tail = values[:, :width], values[:, values.shape[1] - width:]
    return pick(odd, head, tail), pick(odd, tail, head)


def corner_sends(below, above, odd):
    packs = []
    for rows, sign in ((slice(0, 8), 1), (slice(below.shape[1] - 8, below.shape[1]), -1)):
        low = [below[3 - i, rows] for i in range(3)]
        high = [above[i, rows] for i in range(3)]
        row = iota2(low[0].shape, 0)
        row = row if sign == 1 else 7 - row
        pack = (
            jnp.where(row < 3, low[0], turn(low[2], 3 * sign, 0)),
            jnp.where(row < 2, low[1], turn(high[1], 2 * sign, 0)),
            jnp.where(row < 3, high[0], turn(high[2], 3 * sign, 0)),
        )
        packs.append([p[:4] if sign == 1 else p[4:] for p in pack])
    return [(pick(odd, h, t), pick(odd, t, h)) for h, t in zip(*packs)]


def inner_rows(tile, by):
    upper = iota2(tile.shape, 0) < 4
    return jnp.where(upper, turn(tile, -by, 0), turn(tile, by, 0))


def corner_tiles(first, second, third):
    zero = jnp.zeros_like(first)
    low = (zero, inner_rows(first, 3), second, first)
    return low, (third, inner_rows(second, 2), inner_rows(third, 3), zero)


def diagonal_sends(values, n_x, odd_x, odd_y):
    corners = []
    for slabs in ([values[i] for i in range(4)], [values[values.shape[0] - 1 - i] for i in range(4)]):
        for sign in (1, -1):
            row = iota2(slabs[0].shape, 0)
            row = row if sign == 1 else 7 - row
            tiles = (slabs[0], jnp.where(row < 3, slabs[1], turn(slabs[3], 3 * sign, 0)), slabs[2])
            corners.append([t[:4] if sign == 1 else t[4:] for t in tiles])
    sends = []
    for k_x in range(n_x):
        for k_y in range(2):
            head_x = odd_x if k_x == 0 else 1 - odd_x
            head_y = odd_y if k_y == 0 else 1 - odd_y
            sends.append(
                [
                    pick(head_x, pick(head_y, hh, ht), pick(head_y, th, tt))
                    for hh, ht, th, tt in zip(*corners)
                ]
            )
    return sends


def diagonal_tiles(first, second, third):
    return [first, second, third, inner_rows(second, 3)]


def faces_kernel(counts, where_ref, *refs):
    ins, refs = refs[:6], refs[6:]
    n_x = 1 if counts[0] == 2 else 2
    sends_x, (two_y, one_y, first, second) = refs[:n_x], refs[n_x:]
    odd_x, odd_y, odd = (place % 2 for place in position(where_ref))
    sx, sy, sz = ins[0].shape
    half = sx // 2
    lane = lane_of((half, sy, LANES))
    head = jnp.zeros((half, sy, LANES), F32)
    tail = head
    for a, ref in enumerate(ins):
        for send, face in zip(sends_x, faces_x(ref[...][None], odd_x, n_x, HALO)):
            send[a] = face[0]
        one_y[a], two_y[a] = faces_y(ref[...], odd_y, HALO)
        for g in range(2):
            values = ref[g * half:(g + 1) * half]
            at = SIDE * g + PLACE[a]
            mask = (lane >= at) & (lane < at + DEPTH[a])
            head = jnp.where(mask, turn(values, at, 2), head)
            tail = jnp.where(mask, turn(values, at + DEPTH[a], 2), tail)
    first[...] = pick(odd, head, tail)
    second[...] = pick(odd, tail, head)


def halo_z_kernel(counts, where_ref, one_ref, two_ref, zpack, *sends):
    at_x, _, at_z = position(where_ref)
    half = one_ref.shape[0]
    below, above = neighbours(counts[2], at_z, one_ref[...], two_ref[...])
    lane = lane_of(below.shape)
    zpack[:half] = jnp.where(lane < SIDE, above, turn(below, SIDE, 2))
    zpack[half:] = jnp.where(lane < SIDE, turn(above, SIDE, 2), below)
    for send, face in zip(sends, faces_x(zpack[...][None], at_x % 2, len(sends), HALO)):
        send[...] = face[0]


def corners_kernel(counts, where_ref, zpack, *refs):
    n_x = 1 if counts[0] == 2 else 2
    main_x, halos_x, (two_y, one_y) = refs[:n_x], refs[n_x:2 * n_x], refs[2 * n_x + 1:]
    at_x, at_y, _ = position(where_ref)
    for a in range(7):
        if a < 6:
            below, above = neighbours(counts[0], at_x, main_x[0][a], main_x[-1][a])
        else:
            below, above = neighbours(counts[0], at_x, halos_x[0][...], halos_x[-1][...])
        for n, pair in enumerate(corner_sends(below, above, at_y % 2)):
            one_y[3 * a + n], two_y[3 * a + n] = pair
    one_y[21:], two_y[21:] = faces_y(zpack[...], at_y % 2, HALO)


def each(first, last, step, body):
    rounds = (last - first) // step

    def go(i, carry):
        for j in range(step):
            body(first + i * step + j)
        return carry

    if rounds:
        lax.fori_loop(0, rounds, go, 0)
    for x in range(first + rounds * step, last):
        body(x)


def ring_up(main, halo, lane):
    main_up, halo_up = turn(main, -1, 1), turn(halo, -1, 1)
    last = lane == LANES - 1
    return jnp.where(last, halo_up, main_up), jnp.where(last, main_up, halo_up)


def ring_down(main, halo, lane):
    main_down, halo_down = turn(main, 1, 1), turn(halo, 1, 1)
    zero = lane == 0
    return jnp.where(zero, halo_down, main_down), jnp.where(zero, main_down, halo_down)


def pull_slab(field, bx, by, bz, x, lane):
    centre = [half[x] for half in field]
    out = []
    for k in range(2):
        c, face = centre[k], by[k][x]
        t = bx[k][x] * field[k][x + 1] + bx[k][x - 1] * field[k][x - 1]
        out.append(t + (face * turn(c, -1, 0) + turn(face * c, 1, 0)))
    faces = [half[x] for half in bz]
    ups = ring_up(centre[0], centre[1], lane)
    downs = ring_down(faces[0] * centre[0], faces[1] * centre[1], lane)
    return centre, [out[k] + (faces[k] * ups[k] + downs[k]) for k in range(2)]


def unpacked(packed, a, lane):
    at, depth = PLACE[a], DEPTH[a]
    axis = packed.ndim - 1
    right, left = turn(packed, -at, axis), turn(packed, SIDE - depth - at, axis)
    return jnp.where(lane < depth, right, jnp.where(lane >= LANES - depth, left, 0.0))


def rows_of(source, x, count, firsts, seconds):
    total = None
    for p in firsts:
        for q in seconds:
            term = source[x + p, pl.ds(q, count, stride=2), :]
            total = term if total is None else total + term
    return total


BOTH, ODD = (0, 1), (1,)


def to_level1(sums, first, count, table, factor):
    _, x1, y1, _ = sums.shape
    flat = sums[first:first + count].reshape(count * x1 * y1, 2 * LANES)
    return factor * times_table(flat, table).reshape(count, x1, y1, LANES)


def coefficient_kernel(counts, where_ref, *refs):
    ins, refs = refs[:7], refs[7:]
    n_x = 1 if counts[0] == 2 else 2
    main_x, refs = refs[:n_x], refs[n_x:]
    arrays, (coarse2, coeffs1, sums, pairing) = refs[:12], refs[12:]
    sx, sy, sz = ins[0].shape
    at_x = position(where_ref)[0]
    x1, y1 = sx // 2, sy // 2
    lane = lane_of((sx, sy, LANES))
    lanes = [slice(k * LANES, (k + 1) * LANES) for k in range(2)]
    mine = slice(HALO, HALO + sx)
    for a in range(6):
        to = arrays[2 * a]
        below, above = neighbours(counts[0], at_x, main_x[0][a], main_x[-1][a])
        to[:HALO, :sy] = below
        to[mine, :sy] = ins[a][...]
        to[HALO + sx:, :sy] = above
        arrays[2 * a + 1][mine, :sy] = unpacked(ins[6][...], a, lane)
    for n, (firsts, seconds) in enumerate(((BOTH, BOTH), (ODD, BOTH), (BOTH, ODD), (BOTH, BOTH))):
        for k in range(2):
            for i in range(x1):
                source = arrays[2 * (n + 2) + k]
                sums[n, i, :, lanes[k]] = rows_of(source, HALO + 2 * i, y1, firsts, seconds)
    pairs = pair_table(2 * LANES, LANES, False)
    odds = pair_table(2 * LANES, LANES, True)
    paired = to_level1(sums, 0, 3, pairs, 0.0625)
    mass1 = (2.0 * WEIGHT) * paired[0]
    faces1 = (paired[1], paired[2], to_level1(sums, 3, 1, odds, 0.0625)[0])
    diag1 = mass1 + faces1[0] + below_x(faces1[0])
    diag1 = diag1 + faces1[1] + faces1[2] + turn(faces1[2], 1, 2)
    for n, values in enumerate((mass1, diag1) + faces1):
        coeffs1[n] = values
    parts = (
        (mass1, False, False, False, 0.125),
        (faces1[0], True, False, False, 0.0625),
        (faces1[1], False, True, False, 0.0625),
        (faces1[2], False, False, True, 0.0625),
    )
    for n, (values, *odd_axes, factor) in enumerate(parts):
        pairing[n] = values
        coarse2[n] = level2_rows(pairing.at[n], odd_axes, factor, x1 // 2, y1 // 2, sz // 4)


def down_kernel(counts, where_ref, zpack, *refs):
    refs = refs[12:]
    n_x = 1 if counts[0] == 2 else 2
    halos_x = refs[:n_x]
    main_two, main_one, rest_two, rest_one, coeffs1 = refs[n_x:5 + n_x]
    flat, refs = refs[5 + n_x:17 + n_x], refs[17 + n_x:]
    arrays = tuple(zip(flat[::2], flat[1::2]))
    own1, refs = refs[0], refs[1:]
    sends, near_two, near_one, refs = refs[:n_x], refs[n_x], refs[n_x + 1], refs[n_x + 2:]
    sends_xy, refs = refs[:2 * n_x], refs[2 * n_x:]
    kept_m, kept_h, weight_m, weight_h = refs[:4]
    packs, half_m, half_h, diag_m, diag_h, sums, left = refs[4:]
    field, rhs, alpha, bx, by, bz = arrays
    sx, sy, sz = zpack.shape
    ex, ey = sx + 2 * HALO, sy + 2 * HALO
    at_x, at_y, _ = position(where_ref)

    rest = neighbours(counts[1], at_y, rest_one[...], rest_two[...])
    rest = jnp.concatenate(rest[::-1], axis=1)
    for a in range(7):
        if a < 6:
            to = arrays[a][0]
            rows = neighbours(counts[1], at_y, main_one[a], main_two[a])
            rows = jnp.concatenate(rows[::-1], axis=1)
        else:
            to = packs
            rows = rest[21:]
            below, above = neighbours(counts[0], at_x, halos_x[0][...], halos_x[-1][...])
            to[:HALO, :sy] = below
            to[HALO + sx:, :sy] = above
        to[HALO:HALO + sx, sy:] = rows
        low, high = corner_tiles(*(rest[3 * a + n] for n in range(3)))
        for n in range(HALO):
            to[n, sy:] = low[n]
            to[HALO + sx + n, sy:] = high[n]
    lane = lane_of((ey, LANES))
    lane_low = lane_of((2 * HALO, LANES))

    def unpack_rows(x):
        packed = packs[x, sy:]
        for a in range(6):
            arrays[a][1][x, sy:] = unpacked(packed, a, lane_low)

    def unpack(x):
        packed = packs[x]
        for a in range(6):
            arrays[a][1][x] = unpacked(packed, a, lane)

    each(0, HALO, HALO, unpack)
    each(HALO, HALO + sx, 8, unpack_rows)
    each(HALO + sx, ex, HALO, unpack)
    halfway, weight, kept = (half_m, half_h), (weight_m, weight_h), (kept_m, kept_h)
    diag = (diag_m, diag_h)

    def first_sweep(x):
        faces = [half[x] for half in bz]
        downs = ring_down(faces[0], faces[1], lane)
        centre, near = pull_slab(field, bx, by, bz, x, lane)
        for k in range(2):
            face = by[k][x]
            mass = WEIGHT * alpha[k][x]
            d = mass + bx[k][x] + bx[k][x - 1] + face + turn(face, 1, 0) + faces[k] + downs[k]
            w = relaxer(mass, d)
            diag[k][x] = d
            weight[k][x] = w
            halfway[k][x] = KEEP * centre[k] + w * (rhs[k][x] + near[k])

    each(1, ex - 1, 4, first_sweep)

    def second_sweep(x):
        centre, near = pull_slab(halfway, bx, by, bz, x, lane)
        for k in range(2):
            kept[k][x] = KEEP * centre[k] + weight[k][x] * (rhs[k][x] + near[k])

    each(2, ex - 2, 4, second_sweep)

    def residual(x):
        centre, near = pull_slab(kept, bx, by, bz, x, lane)
        for k in range(2):
            halfway[k][x] = rhs[k][x] - diag[k][x] * centre[k] + near[k]

    each(HALO, ex - HALO, 4, residual)

    x1, y1 = sx // 2, sy // 2
    for k in range(2):
        lanes = slice(k * LANES, (k + 1) * LANES)
        for i in range(x1):
            x = HALO + 2 * i
            sums[0, i, :, lanes] = rows_of(halfway[k], x, y1, BOTH, BOTH)
            left[...] = turn(by[k][x] + by[k][x + 1], 1, 0)
            sums[1, i, :, lanes] = left[pl.ds(0, y1, stride=2), :]
        sums[2, 0, :, lanes] = rows_of(bx[k], HALO - 1, y1, (0,), BOTH)
        sums[2, 1:, :, lanes] = jnp.zeros((x1 - 1, y1, LANES), F32)
    rhs1, low_y, low_x = to_level1(sums, 0, 3, pair_table(2 * LANES, LANES, False), 0.0625)
    weight1 = relaxer(coeffs1[0], coeffs1[1] + low_y + low_x)
    for n, values in enumerate((2.0 * rhs1, weight1, coeffs1[2], coeffs1[3], coeffs1[4])):
        own1[n] = values
        for send, face in zip(sends, faces_x(values[None], at_x % 2, n_x, NEAR)):
            send[n] = face[0]
        near_one[n], near_two[n] = faces_y(values, at_y % 2, NEAR)
        for send, tiles in zip(sends_xy, diagonal_sends(values, n_x, at_x % 2, at_y % 2)):
            for t in range(3):
                send[3 * n + t] = tiles[t]


def level2_rows(source, odd_axes, factor, x2, y2, z2):
    rows = []
    for i in range(x2):
        total = None
        for p in (1,) if odd_axes[0] else (0, 1):
            for q in (1,) if odd_axes[1] else (0, 1):
                term = source[2 * i + p, pl.ds(q, y2, stride=2), :]
                total = term if total is None else total + term
        rows.append(total)
    flat = jnp.concatenate(rows, axis=0)
    flat = factor * times_table(flat, pair_table(LANES, LANES, odd_axes[2]))
    lane = lane_of((y2, LANES))
    packed = jnp.zeros((y2, LANES), F32)
    for i in range(x2):
        mask = (lane >= i * z2) & (lane < (i + 1) * z2)
        packed = jnp.where(mask, turn(flat[i * y2:(i + 1) * y2], i * z2, 1), packed)
    return packed


def near_kernel(counts, devices, where_ref, ring, *refs):
    n_x = 1 if counts[0] == 2 else 2
    halos_x = refs[:n_x]
    main_two, main_one = refs[n_x:n_x + 2]
    diagonals, (coarse2, copies, level1, left) = refs[n_x + 2:3 * n_x + 2], refs[3 * n_x + 2:]
    n, bx1, by1, _ = ring.shape
    at_x, at_y, _ = position(where_ref)
    sides = [
        neighbours(counts[0], at_x, diagonals[k][...], diagonals[k - 2][...]) for k in range(2)
    ]
    rest = []
    for one, two in zip(*sides):
        rows = neighbours(counts[1], at_y, one, two)
        rest.append(jnp.concatenate(rows[::-1], axis=1))
    whole = []
    for a in range(n):
        below, above = neighbours(counts[0], at_x, halos_x[0][a], halos_x[-1][a])
        rows = neighbours(counts[1], at_y, main_one[a], main_two[a])
        rows = jnp.concatenate(rows[::-1], axis=1)
        low, high = (diagonal_tiles(*(side[3 * a + k] for k in range(3))) for side in rest)
        low = low[::-1]
        rows = jnp.concatenate(
            [tile[None] for tile in low] + [rows] + [tile[None] for tile in high], axis=0
        )
        block = jnp.concatenate([below, ring[a], above], axis=0)
        whole.append(jnp.concatenate([block, rows], axis=1))
    rhs1, weight1 = whole[:2]
    faces1 = tuple(whole[2:])
    field1 = weight1 * rhs1
    field1 = sweep(field1, rhs1, weight1, faces1)
    for a, values in enumerate([field1] + whole):
        level1[a] = values
    mine = slice(NEAR, NEAR + bx1)
    inner = weight1[mine]
    diag1 = RELAX / jnp.where(inner > 0.0, inner, 1.0)
    remain = rhs1[mine] - diag1 * field1[mine] + pull(field1, faces1)[mine]
    left[...] = remain
    packed = level2_rows(left, (False,) * 3, 0.125, bx1 // 2, by1 // 2, LANES // 4)
    for d in range(devices):
        copies[d, 0] = packed
        for a in range(n - 1):
            copies[d, a + 1] = coarse2[a]


def halve(values, odd_axis, step):
    half = values.shape[0] // 2
    even = [values[2 * i:2 * i + 1] for i in range(half)]
    odd = [values[2 * i + 1:2 * i + 2] for i in range(half)]
    if odd_axis != 0:
        odd = [a + b for a, b in zip(even, odd)]
    values = jnp.concatenate(odd, axis=0)
    for axis in (1, 2):
        next_one = turn(values, -step, axis)
        values = next_one if odd_axis == axis else values + next_one
    return values


def double(values, step):
    values = values + turn(values, step, 1)
    values = values + turn(values, step, 2)
    return jnp.concatenate([values[i // 2:i // 2 + 1] for i in range(2 * values.shape[0])], axis=0)


def coarse_levels(mass, faces, y, z):
    levels = []
    for level in range(2, LEVELS):
        step = 2 ** (level - 2)
        bx, by, bz = faces
        row = lax.broadcasted_iota(jnp.int32, by.shape, 1)
        lane = lane_of(bz.shape)
        coupled = (
            bx,
            jnp.where(row == (y - 1) * step, 0.0, by),
            jnp.where(lane == (z - 1) * step, 0.0, bz),
        )
        mass = jnp.where((row % step == 0) & (lane % step == 0), mass, 0.0)
        diag = diagonal(mass, faces, coupled, step)
        levels.append((diag, relaxer(mass, diag), coupled))
        if level < LEVELS - 1:
            faces = tuple(0.0625 * halve(face, axis, step) for axis, face in enumerate(faces))
            mass = 0.125 * halve(mass, -1, step)
            y, z = y // 2, z // 2
    return levels


def coarse_cycle(level, rhs, levels):
    step = 2 ** (level - 2)
    diag, weight, faces = levels[level - 2]
    field = weight * rhs
    if level == LEVELS - 1:
        for _ in range(BOTTOM - 1):
            field = sweep(field, rhs, weight, faces, step)
        return field
    for _ in range(SWEEPS - 1):
        field = sweep(field, rhs, weight, faces, step)
    remain = rhs - diag * field + pull(field, faces, step)
    correction = coarse_cycle(level + 1, 0.125 * halve(remain, -1, step), levels)
    field = field + double(correction, step)
    for _ in range(SWEEPS):
        field = sweep(field, rhs, weight, faces, step)
    return field


def spread_out(counts, slots, whole):
    gx, gy, gz = counts
    y2 = slots.shape[-2]
    x2 = whole.shape[0] // gx
    z2 = LANES // x2
    lane = lane_of((y2, LANES))
    for i in range(gx):
        for j in range(gy):
            for x in range(x2):
                for part in range(whole.shape[2] // LANES):
                    total = jnp.zeros((y2, LANES), F32)
                    for k in range(LANES // z2):
                        column = part * (LANES // z2) + k
                        if column < gz:
                            block = slots[(i * gy + j) * gz + column]
                            mask = (lane >= k * z2) & (lane < (k + 1) * z2)
                            total = jnp.where(mask, turn(block, (k - x) * z2, 1), total)
                    lanes = slice(part * LANES, (part + 1) * LANES)
                    whole[i * x2 + x, j * y2:(j + 1) * y2, lanes] = total


def up_kernel(counts, where_ref, gathered, level1, *refs):
    kept, weight, rhs, bx, by, bz = zip(refs[0:12:2], refs[1:12:2])
    out, whole, second, spread_m, spread_h, field_m, field_h, half_m, half_h = refs[12:]
    gx, gy, gz = counts
    at_x, at_y, at_z = position(where_ref)
    sx, sy, sz = out.shape
    x1, y1 = sx // 2, sy // 2
    x2, y2, z2 = x1 // 2, y1 // 2, sz // 4
    columns = max(LANES, gz * z2)
    for a in range(5):
        spread_out(counts, gathered.at[:, a], whole.at[a])
    levels = coarse_levels(whole[1], (whole[2], whole[3], whole[4]), gy * y2, gz * z2)
    correction = coarse_cycle(2, whole[0], levels)

    wide = gx * x2
    half = NEAR // 2
    ex1, ey1 = x1 + 2 * NEAR, y1 + 2 * NEAR
    second[:half] = jnp.zeros((half,) + correction.shape[1:], F32)
    second[half:half + wide] = correction
    second[half + wide:] = jnp.zeros((half,) + correction.shape[1:], F32)
    window = second[pl.ds(at_x * x2, x2 + NEAR)]
    rows = correction.shape[1]
    row = iota2((ey1, rows), 0)
    col = iota2((ey1, rows), 1)
    place = jnp.where(row < y1 + NEAR, row, row - ey1)
    table_y = (col == at_y * y2 + lax.shift_right_arithmetic(place, 1)).astype(F32)
    row = iota2((columns, LANES), 0)
    col = iota2((columns, LANES), 1)
    place = jnp.where(col < LANES * 3 // 4, col, col - LANES)
    table_z = (row == at_z * z2 + lax.shift_right_arithmetic(place, 1)).astype(F32)
    flat = times_table(window.reshape((x2 + NEAR) * rows, columns), table_z)
    blocks = [table_times(table_y, flat[i * rows:(i + 1) * rows])[None] for i in range(x2 + NEAR)]
    lifted = jnp.concatenate([blocks[i // 2] for i in range(ex1)], axis=0)
    field1, rhs1, weight1 = level1[0], level1[1], level1[2]
    faces1 = (level1[3], level1[4], level1[5])
    field1 = field1 + jnp.where(weight1 > 0.0, lifted, 0.0)
    for _ in range(SWEEPS):
        field1 = sweep(field1, rhs1, weight1, faces1)

    ex, ey = sx + 2 * HALO, sy + 2 * HALO
    near = field1[NEAR - 1:NEAR + x1 + 1].reshape((x1 + 2) * ey1, LANES)
    row = iota2((LANES, 2 * LANES), 0)
    col = iota2((LANES, 2 * LANES), 1)
    lifted = times_table(near, (col // 2 == row).astype(F32))
    quarter = NEAR // 2
    for k, spread in enumerate((spread_m, spread_h)):
        block = lifted[:, k * LANES:(k + 1) * LANES].reshape(x1 + 2, ey1, LANES)
        for i in range(x1 + 2):
            for q in range(2):
                spread[i, pl.ds(q, y1, stride=2), :] = block[i, :y1]
                spread[i, pl.ds(sy + q, quarter, stride=2), :] = block[i, y1:y1 + quarter]
                spread[i, pl.ds(sy + HALO + q, quarter, stride=2), :] = block[i, ey1 - quarter:]
    before, after = (field_m, field_h), (half_m, half_h)
    first = HALO - 2
    for x in range(first, ex - first):
        for k, spread in enumerate((spread_m, spread_h)):
            before[k][x] = kept[k][x] + spread[(x - first) // 2]

    lane = lane_of((ey, LANES))

    def sweep_out(x):
        centre, around = pull_slab(before, bx, by, bz, x, lane)
        for k in range(2):
            after[k][x] = KEEP * centre[k] + weight[k][x] * (rhs[k][x] + around[k])

    each(first + 1, ex - first - 1, 4, sweep_out)

    def sweep_own(x):
        centre, around = pull_slab(after, bx, by, bz, x, lane)
        value = KEEP * centre[0] + weight[0][x] * (rhs[0][x] + around[0])
        out[x - HALO] = value[:sy]

    each(HALO, ex - HALO, 4, sweep_own)


def run(kernel, outs, where, arrays, scratch=(), grant=16, micros=1, aliases={}):
    return pl.pallas_call(
        kernel,
        out_shape=tuple(jax.ShapeDtypeStruct(shape, F32) for shape in outs),
        in_specs=[SM] * len(where) + [VM] * len(arrays),
        out_specs=tuple(VM for _ in outs),
        input_output_aliases=aliases,
        scratch_shapes=[pltpu.VMEM(shape, F32) for shape in scratch],
        compiler_params=pltpu.CompilerParams(vmem_limit_bytes=grant * 1024 * 1024),
        cost_estimate=pl.CostEstimate(
            flops=0, bytes_accessed=int(micros * 3.6e6), transcendentals=0
        ),
    )(*where, *arrays)


def partners(count, k):
    partner = list(range(count))
    for low in range(k, count - 1, 2):
        partner[low], partner[low + 1] = low + 1, low
    return partner


def swaps(axis, sends, other=None):
    count = lax.axis_size(axis)
    got = []
    for k, block in enumerate(sends):
        partner = partners(count, k)
        if k == 1 and other is None:
            partner[0], partner[-1] = count - 1, 0
        if k == 0 or other is None:
            got.append(lax.ppermute(block, axis, list(enumerate(partner))))
            continue
        rows = lax.axis_size(other)
        pairs = []
        for row in range(rows):
            for i in range(count):
                ends = [(row, i), (min(row ^ 1, rows - 1) if partner[i] == i else row, partner[i])]
                if axis < other:
                    pairs.append(tuple(at * rows + line for line, at in ends))
                else:
                    pairs.append(tuple(line * count + at for line, at in ends))
        got.append(lax.ppermute(block, tuple(sorted((axis, other))), pairs))
    return got


def diagonal_swaps(sends):
    count_x, count_y = lax.axis_size("gx"), lax.axis_size("gy")
    got = []
    for n, block in enumerate(sends):
        xs, ys = partners(count_x, n // 2), partners(count_y, n % 2)
        pairs = [
            (x * count_y + y, xs[x] * count_y + ys[y])
            for x in range(count_x)
            for y in range(count_y)
        ]
        got.append(lax.ppermute(block, ("gx", "gy"), pairs))
    return got


def local(initial, right_side, alpha, beta_x, beta_y, beta_z):
    axes = ("gx", "gy", "gz")
    counts = tuple(lax.axis_size(axis) for axis in axes)
    devices = counts[0] * counts[1] * counts[2]
    where = (lax.axis_index("gx") * STRIDE + lax.axis_index("gy")) * STRIDE + lax.axis_index("gz")
    where = (where.astype(jnp.int32).reshape(1),)
    ins = (initial, right_side, alpha, beta_x, beta_y, beta_z)
    sx, sy, sz = initial.shape
    n_x = 1 if counts[0] == 2 else 2
    ex, ey = sx + 2 * HALO, sy + 2 * HALO
    fine = (ex, ey, LANES)

    *sends_x, two_y, one_y, first, second = run(
        functools.partial(faces_kernel, counts),
        [(6, HALO, sy, LANES)] * n_x
        + [(6, sx, HALO, LANES)] * 2
        + [(sx // 2, sy, LANES)] * 2,
        where,
        ins,
        grant=60,
    )
    main_x = tuple(swaps("gx", sends_x, "gy"))
    main_y = tuple(swaps("gy", (one_y, two_y))[::-1])
    got = swaps("gz", (first, second), "gy")
    zpack, *sends = run(
        functools.partial(halo_z_kernel, counts),
        [(sx, sy, LANES)] + [(HALO, sy, LANES)] * n_x,
        where,
        tuple(got),
    )
    halos_x = tuple(swaps("gx", sends, "gy"))
    x1, y1 = sx // 2, sy // 2
    *laid, coarse2, coeffs1 = run(
        functools.partial(coefficient_kernel, counts),
        [fine] * 12 + [(4, y1 // 2, LANES), (5, x1, y1, LANES)],
        where,
        ins + (zpack,) + main_x,
        [(4, x1, y1, 2 * LANES), (4, x1, y1, LANES)],
        micros=2,
    )
    two_y, one_y = run(
        functools.partial(corners_kernel, counts),
        [(21 + sx, HALO, LANES)] * 2,
        where,
        (zpack,) + main_x + halos_x + (coarse2,),
    )
    rest_y = tuple(swaps("gy", (one_y, two_y), "gz")[::-1])
    outs = run(
        functools.partial(down_kernel, counts),
        [fine] * 12
        + [(5, x1, y1, LANES)]
        + [(5, NEAR, y1, LANES)] * n_x
        + [(5, x1, NEAR, LANES)] * 2
        + [(15, NEAR, LANES)] * (2 * n_x)
        + [fine] * 4,
        where,
        (zpack,) + tuple(laid) + halos_x + main_y + rest_y + (coeffs1,),
        [fine] * 5 + [(3, x1, y1, 2 * LANES), (ey, LANES)],
        24,
        micros=4,
        aliases={n + 2: n for n in range(12)},
    )
    laid, own1, outs = outs[:12], outs[12], outs[13:]
    sends_x, (two_y, one_y), outs = outs[:n_x], outs[n_x:n_x + 2], outs[n_x + 2:]
    sends_xy, fine_arrays = outs[:2 * n_x], outs[2 * n_x:]
    fine_arrays = tuple(fine_arrays) + tuple(laid[2:4]) + tuple(laid[6:])

    near_x = tuple(swaps("gx", sends_x, "gy"))
    near_y = tuple(swaps("gy", (one_y, two_y), "gz")[::-1])
    near_xy = tuple(diagonal_swaps(sends_xy))
    copies, level1 = run(
        functools.partial(near_kernel, counts, devices),
        [(devices, 5, y1 // 2, LANES), (6, x1 + 2 * NEAR, y1 + 2 * NEAR, LANES)],
        where,
        (own1,) + near_x + near_y + near_xy + (coarse2,),
        [(x1, y1 + 2 * NEAR, LANES)],
    )

    gathered = lax.all_to_all(copies, axes, 0, 0, tiled=True)
    wide, rows = counts[0] * x1 // 2, counts[1] * y1 // 2
    columns = max(LANES, counts[2] * sz // 4)
    (result,) = run(
        functools.partial(up_kernel, counts),
        [(sx, sy, sz)],
        where,
        (gathered, level1) + tuple(fine_arrays),
        [(5, wide, rows, columns), (wide + NEAR, rows, columns)]
        + [(x1 + 2, ey, LANES)] * 2
        + [fine] * 4,
        24,
        micros=4,
    )
    return result


def solution(mesh):
    spec = P("gx", "gy", "gz")
    return jax.shard_map(
        local, mesh=mesh, in_specs=(spec,) * 6, out_specs=spec, check_vma=False
    )
```

```python
import functools

import jax
import jax.numpy as jnp
from jax import lax
from jax.experimental import pallas as pl
from jax.experimental.pallas import tpu as pltpu
from jax.sharding import PartitionSpec as P

LEVELS = 6
SWEEPS = 2
BOTTOM = 8
WEIGHT = 0.25 ** (LEVELS - 1)
RELAX = 2.0 / 3.0
KEEP = 1.0 / 3.0

HALO = 4
NEAR = 4
LANES = 128
PLACE = (0, 11, 21, 31, 41, 51)
DEPTH = (11, 10, 10, 10, 10, 11)
SIDE = LANES // 2
STRIDE = 256

VM = pl.BlockSpec(memory_space=pltpu.VMEM)
SM = pl.BlockSpec(memory_space=pltpu.SMEM)
F32 = jnp.float32


def position(where_ref):
    code = where_ref[0]
    return code // (STRIDE * STRIDE), code // STRIDE % STRIDE, code % STRIDE


def lane_of(shape):
    return lax.broadcasted_iota(jnp.int32, shape, len(shape) - 1)


def pick(flag, yes, no):
    return jnp.where(jnp.full(yes.shape, flag, jnp.int32) == 1, yes, no)


def neighbours(count, place, one, two):
    if count == 2:
        two = jnp.zeros_like(one)
    else:
        ends = jnp.full(two.shape, place, jnp.int32)
        two = jnp.where((ends == 0) | (ends == count - 1), 0.0, two)
    return pick(place % 2, one, two), pick(place % 2, two, one)


def turn(values, shift, axis):
    return pltpu.roll(values, shift % values.shape[axis], axis)


def parts_of(values):
    high = values.astype(jnp.bfloat16)
    rest = values - high.astype(F32)
    middle = rest.astype(jnp.bfloat16)
    low = (rest - middle.astype(F32)).astype(jnp.bfloat16)
    return high, middle, low


def times_table(values, table):
    table = table.astype(jnp.bfloat16)
    total = None
    for part in reversed(parts_of(values)):
        term = jnp.dot(part, table, preferred_element_type=F32)
        total = term if total is None else total + term
    return total


def table_times(table, values):
    table = table.astype(jnp.bfloat16)
    total = None
    for part in reversed(parts_of(values)):
        term = jnp.dot(table, part, preferred_element_type=F32)
        total = term if total is None else total + term
    return total


def iota2(shape, axis):
    return lax.broadcasted_iota(jnp.int32, shape, axis)


def pair_table(rows, cols, odd):
    row = iota2((rows, cols), 0)
    col = iota2((rows, cols), 1)
    hit = (row == 2 * col + 1) if odd else (row // 2 == col)
    return hit.astype(F32)


def below_x(values):
    if values.shape[0] == 1:
        return jnp.zeros_like(values)
    return jnp.concatenate([jnp.zeros_like(values[:1]), values[:-1]], axis=0)


def above_x(values):
    if values.shape[0] == 1:
        return jnp.zeros_like(values)
    return jnp.concatenate([values[1:], jnp.zeros_like(values[:1])], axis=0)


def pull(values, faces, step=1):
    bx, by, bz = faces
    total = bx * above_x(values) + below_x(bx * values)
    total = total + (by * turn(values, -step, 1) + turn(by * values, step, 1))
    return total + (bz * turn(values, -step, 2) + turn(bz * values, step, 2))


def diagonal(mass, faces, coupled, step=1):
    bx, by, bz = faces
    _, cy, cz = coupled
    return mass + bx + below_x(bx) + by + turn(cy, step, 1) + bz + turn(cz, step, 2)


def relaxer(mass, diag):
    inside = mass > 0.0
    return jnp.where(inside, RELAX / jnp.where(inside, diag, 1.0), 0.0)


def sweep(values, rhs, weight, faces, step=1):
    return KEEP * values + weight * (rhs + pull(values, faces, step))


def faces_x(values, odd, n_x, width):
    head, tail = values[:, :width], values[:, values.shape[1] - width:]
    return [pick(odd, head, tail), pick(odd, tail, head)][:n_x]


def faces_y(values, odd, width):
    head, tail = values[:, :width], values[:, values.shape[1] - width:]
    return pick(odd, head, tail), pick(odd, tail, head)


def corner_sends(below, above, odd):
    packs = []
    for rows, sign in ((slice(0, 8), 1), (slice(below.shape[1] - 8, below.shape[1]), -1)):
        low = [below[3 - i, rows] for i in range(3)]
        high = [above[i, rows] for i in range(3)]
        row = iota2(low[0].shape, 0)
        row = row if sign == 1 else 7 - row
        pack = (
            jnp.where(row < 3, low[0], turn(low[2], 3 * sign, 0)),
            jnp.where(row < 2, low[1], turn(high[1], 2 * sign, 0)),
            jnp.where(row < 3, high[0], turn(high[2], 3 * sign, 0)),
        )
        packs.append([p[:4] if sign == 1 else p[4:] for p in pack])
    return [(pick(odd, h, t), pick(odd, t, h)) for h, t in zip(*packs)]


def inner_rows(tile, by):
    upper = iota2(tile.shape, 0) < 4
    return jnp.where(upper, turn(tile, -by, 0), turn(tile, by, 0))


def corner_tiles(first, second, third):
    zero = jnp.zeros_like(first)
    low = (zero, inner_rows(first, 3), second, first)
    return low, (third, inner_rows(second, 2), inner_rows(third, 3), zero)


def diagonal_sends(values, n_x, odd_x, odd_y):
    corners = []
    for slabs in ([values[i] for i in range(4)], [values[values.shape[0] - 1 - i] for i in range(4)]):
        for sign in (1, -1):
            row = iota2(slabs[0].shape, 0)
            row = row if sign == 1 else 7 - row
            tiles = (slabs[0], jnp.where(row < 3, slabs[1], turn(slabs[3], 3 * sign, 0)), slabs[2])
            corners.append([t[:4] if sign == 1 else t[4:] for t in tiles])
    sends = []
    for k_x in range(n_x):
        for k_y in range(2):
            head_x = odd_x if k_x == 0 else 1 - odd_x
            head_y = odd_y if k_y == 0 else 1 - odd_y
            sends.append(
                [
                    pick(head_x, pick(head_y, hh, ht), pick(head_y, th, tt))
                    for hh, ht, th, tt in zip(*corners)
                ]
            )
    return sends


def halo_lanes(n):
    return SIDE + 2 * NEAR * n


def pack_level1(values):
    lane = lane_of(values[0].shape)
    axis = values[0].ndim - 1
    packs = [
        jnp.where(lane < SIDE, values[0], turn(values[1], SIDE, axis)),
        jnp.where(lane < SIDE, values[2], turn(values[3], SIDE, axis)),
    ]
    last = jnp.where(lane < SIDE, values[4], 0.0)
    for n, array in enumerate(values):
        at = halo_lanes(n)
        right = turn(array, at - SIDE, axis)
        left = turn(array, at + 2 * NEAR, axis)
        last = jnp.where((lane >= at) & (lane < at + NEAR), right, last)
        last = jnp.where((lane >= at + NEAR) & (lane < at + 2 * NEAR), left, last)
    return packs + [last]


def unpack_level1(packs):
    first, second, last = packs
    lane = lane_of(first.shape)
    axis = first.ndim - 1
    blocks = (first, turn(first, SIDE, axis), second, turn(second, SIDE, axis), last)
    values = []
    for n, block in enumerate(blocks):
        at = halo_lanes(n)
        right = turn(last, SIDE - at, axis)
        left = turn(last, -at - 2 * NEAR, axis)
        halo = jnp.where(lane < SIDE + NEAR, right, jnp.where(lane >= LANES - NEAR, left, 0.0))
        values.append(jnp.where(lane < SIDE, block, halo))
    return values


def diagonal_tiles(first, second, third):
    return [first, second, third, inner_rows(second, 3)]


def faces_kernel(counts, where_ref, *refs):
    ins, refs = refs[:6], refs[6:]
    n_x = 1 if counts[0] == 2 else 2
    sends_x, (two_y, one_y, first, second), sends_xz = refs[:n_x], refs[n_x:n_x + 4], refs[n_x + 4:]
    odd_x, odd_y, odd = (place % 2 for place in position(where_ref))
    sx, sy, sz = ins[0].shape
    half = sx // 2
    lane = lane_of((half, sy, LANES))
    head = jnp.zeros((half, sy, LANES), F32)
    tail = head
    for a, ref in enumerate(ins):
        for send, face in zip(sends_x, faces_x(ref[...][None], odd_x, n_x, HALO)):
            send[a] = face[0]
        one_y[a], two_y[a] = faces_y(ref[...], odd_y, HALO)
        for g in range(2):
            values = ref[g * half:(g + 1) * half]
            at = SIDE * g + PLACE[a]
            mask = (lane >= at) & (lane < at + DEPTH[a])
            head = jnp.where(mask, turn(values, at, 2), head)
            tail = jnp.where(mask, turn(values, at + DEPTH[a], 2), tail)
    swapped = (pick(odd, head, tail), pick(odd, tail, head))
    first[...], second[...] = swapped
    lane = lane_of((2, sy, LANES))
    for k_z, values in enumerate(swapped):
        low = jnp.where(lane < SIDE, values[:2], turn(values[2:4], SIDE, 2))
        high = jnp.where(lane < SIDE, turn(values[half - 4:half - 2], SIDE, 2), values[half - 2:])
        for k_x in range(n_x):
            sends_xz[2 * k_x + k_z][...] = pick(odd_x if k_x == 0 else 1 - odd_x, low, high)


def halo_z_kernel(counts, where_ref, one_ref, two_ref, *refs):
    n_x = 1 if counts[0] == 2 else 2
    diagonals, main_x = refs[:2 * n_x], refs[2 * n_x:3 * n_x]
    zpack, two_y, one_y = refs[3 * n_x:]
    at_x, at_y, at_z = position(where_ref)
    half = one_ref.shape[0]
    sx = 2 * half
    below, above = neighbours(counts[2], at_z, one_ref[...], two_ref[...])
    lane = lane_of(below.shape)
    own = slice(HALO, HALO + half), slice(HALO + half, HALO + sx)
    zpack[own[0]] = jnp.where(lane < SIDE, above, turn(below, SIDE, 2))
    zpack[own[1]] = jnp.where(lane < SIDE, turn(above, SIDE, 2), below)
    sides = [
        neighbours(counts[0], at_x, diagonals[k][...], diagonals[k - 2][...]) for k in range(2)
    ]
    lane = lane_of(sides[0][0].shape)
    for at, (one, two) in zip((0, HALO + sx), zip(*sides)):
        below, above = neighbours(counts[2], at_z, one, two)
        zpack[at:at + 2] = jnp.where(lane < SIDE, above, turn(below, SIDE, 2))
        zpack[at + 2:at + 4] = jnp.where(lane < SIDE, turn(above, SIDE, 2), below)
    odd = at_y % 2
    for a in range(7):
        if a < 6:
            below, above = neighbours(counts[0], at_x, main_x[0][a], main_x[-1][a])
        else:
            below, above = zpack[:HALO], zpack[HALO + sx:]
        for n, pair in enumerate(corner_sends(below, above, odd)):
            one_y[3 * a + n], two_y[3 * a + n] = pair
    one_y[21:], two_y[21:] = faces_y(zpack[HALO:HALO + sx], odd, HALO)


def each(first, last, step, body):
    rounds = (last - first) // step

    def go(i, carry):
        for j in range(step):
            body(first + i * step + j)
        return carry

    if rounds:
        lax.fori_loop(0, rounds, go, 0)
    for x in range(first + rounds * step, last):
        body(x)


def ring_up(main, halo, lane):
    main_up, halo_up = turn(main, -1, 1), turn(halo, -1, 1)
    last = lane == LANES - 1
    return jnp.where(last, halo_up, main_up), jnp.where(last, main_up, halo_up)


def ring_down(main, halo, lane):
    main_down, halo_down = turn(main, 1, 1), turn(halo, 1, 1)
    zero = lane == 0
    return jnp.where(zero, halo_down, main_down), jnp.where(zero, main_down, halo_down)


def pull_slab(field, bx, by, bz, x, lane):
    centre = [half[x] for half in field]
    out = []
    for k in range(2):
        c, face = centre[k], by[k][x]
        t = bx[k][x] * field[k][x + 1] + bx[k][x - 1] * field[k][x - 1]
        out.append(t + (face * turn(c, -1, 0) + turn(face * c, 1, 0)))
    faces = [half[x] for half in bz]
    ups = ring_up(centre[0], centre[1], lane)
    downs = ring_down(faces[0] * centre[0], faces[1] * centre[1], lane)
    return centre, [out[k] + (faces[k] * ups[k] + downs[k]) for k in range(2)]


def unpacked(packed, a, lane):
    at, depth = PLACE[a], DEPTH[a]
    axis = packed.ndim - 1
    right, left = turn(packed, -at, axis), turn(packed, SIDE - depth - at, axis)
    return jnp.where(lane < depth, right, jnp.where(lane >= LANES - depth, left, 0.0))


def rows_of(source, x, count, firsts, seconds):
    total = None
    for p in firsts:
        for q in seconds:
            term = source[x + p, pl.ds(q, count, stride=2), :]
            total = term if total is None else total + term
    return total


BOTH, ODD = (0, 1), (1,)


def to_level1(sums, first, count, table, factor):
    _, x1, y1, _ = sums.shape
    flat = sums[first:first + count].reshape(count * x1 * y1, 2 * LANES)
    return factor * times_table(flat, table).reshape(count, x1, y1, LANES)


def coefficient_kernel(counts, where_ref, *refs):
    ins, zpack, refs = refs[:6], refs[6], refs[7:]
    n_x = 1 if counts[0] == 2 else 2
    main_x, refs = refs[:n_x], refs[n_x:]
    arrays, (coarse2, coeffs1, sums, pairing) = refs[:12], refs[12:]
    sx, sy, sz = ins[0].shape
    at_x = position(where_ref)[0]
    x1, y1 = sx // 2, sy // 2
    lane = lane_of(zpack.shape)
    lanes = [slice(k * LANES, (k + 1) * LANES) for k in range(2)]
    mine = slice(HALO, HALO + sx)
    for a in range(6):
        to = arrays[2 * a]
        below, above = neighbours(counts[0], at_x, main_x[0][a], main_x[-1][a])
        to[:HALO, :sy] = below
        to[mine, :sy] = ins[a][...]
        to[HALO + sx:, :sy] = above
        arrays[2 * a + 1][:, :sy] = unpacked(zpack[...], a, lane)
    for n, (firsts, seconds) in enumerate(((BOTH, BOTH), (ODD, BOTH), (BOTH, ODD), (BOTH, BOTH))):
        for k in range(2):
            for i in range(x1):
                source = arrays[2 * (n + 2) + k]
                sums[n, i, :, lanes[k]] = rows_of(source, HALO + 2 * i, y1, firsts, seconds)
    pairs = pair_table(2 * LANES, LANES, False)
    odds = pair_table(2 * LANES, LANES, True)
    paired = to_level1(sums, 0, 3, pairs, 0.0625)
    mass1 = (2.0 * WEIGHT) * paired[0]
    faces1 = (paired[1], paired[2], to_level1(sums, 3, 1, odds, 0.0625)[0])
    diag1 = mass1 + faces1[0] + below_x(faces1[0])
    diag1 = diag1 + faces1[1] + faces1[2] + turn(faces1[2], 1, 2)
    for n, values in enumerate((mass1, diag1) + faces1):
        coeffs1[n] = values
    parts = (
        (mass1, False, False, False, 0.125),
        (faces1[0], True, False, False, 0.0625),
        (faces1[1], False, True, False, 0.0625),
        (faces1[2], False, False, True, 0.0625),
    )
    for n, (values, *odd_axes, factor) in enumerate(parts):
        pairing[n] = values
        coarse2[n] = level2_rows(pairing.at[n], odd_axes, factor, x1 // 2, y1 // 2, sz // 4)


def down_kernel(counts, where_ref, *refs):
    refs = refs[12:]
    n_x = 1 if counts[0] == 2 else 2
    main_two, main_one, rest_two, rest_one, coeffs1 = refs[:5]
    flat, refs = refs[5:17], refs[17:]
    arrays = tuple(zip(flat[::2], flat[1::2]))
    own1, refs = refs[0], refs[1:]
    sends, near_two, near_one, refs = refs[:n_x], refs[n_x], refs[n_x + 1], refs[n_x + 2:]
    sends_xy, refs = refs[:2 * n_x], refs[2 * n_x:]
    kept_m, kept_h, weight_m, weight_h = refs[:4]
    packs, half_m, half_h, diag_m, diag_h, sums, left = refs[4:]
    field, rhs, alpha, bx, by, bz = arrays
    ex, ey, _ = flat[0].shape
    sx, sy = ex - 2 * HALO, ey - 2 * HALO
    at_x, at_y, _ = position(where_ref)

    rest = neighbours(counts[1], at_y, rest_one[...], rest_two[...])
    rest = jnp.concatenate(rest[::-1], axis=1)
    for a in range(7):
        if a < 6:
            to = arrays[a][0]
            rows = neighbours(counts[1], at_y, main_one[a], main_two[a])
            rows = jnp.concatenate(rows[::-1], axis=1)
        else:
            to = packs
            rows = rest[21:]
        first = 0 if a == 6 else sy
        to[HALO:HALO + sx, first:] = rows
        low, high = corner_tiles(*(rest[3 * a + n] for n in range(3)))
        for n in range(HALO):
            to[n, first:] = low[n]
            to[HALO + sx + n, first:] = high[n]
    lane = lane_of((ey, LANES))
    lane_low = lane_of((2 * HALO, LANES))

    def unpack(x):
        packed = packs[x]
        for a in range(6):
            arrays[a][1][x, sy:] = unpacked(packed, a, lane_low)

    each(0, ex, 8, unpack)
    halfway, weight, kept = (half_m, half_h), (weight_m, weight_h), (kept_m, kept_h)
    diag = (diag_m, diag_h)

    def first_sweep(x):
        faces = [half[x] for half in bz]
        downs = ring_down(faces[0], faces[1], lane)
        centre, near = pull_slab(field, bx, by, bz, x, lane)
        for k in range(2):
            face = by[k][x]
            mass = WEIGHT * alpha[k][x]
            d = mass + bx[k][x] + bx[k][x - 1] + face + turn(face, 1, 0) + faces[k] + downs[k]
            w = relaxer(mass, d)
            diag[k][x] = d
            weight[k][x] = w
            halfway[k][x] = KEEP * centre[k] + w * (rhs[k][x] + near[k])

    each(1, ex - 1, 4, first_sweep)

    def second_sweep(x):
        centre, near = pull_slab(halfway, bx, by, bz, x, lane)
        for k in range(2):
            kept[k][x] = KEEP * centre[k] + weight[k][x] * (rhs[k][x] + near[k])

    each(2, ex - 2, 4, second_sweep)

    def residual(x):
        centre, near = pull_slab(kept, bx, by, bz, x, lane)
        for k in range(2):
            halfway[k][x] = rhs[k][x] - diag[k][x] * centre[k] + near[k]

    each(HALO, ex - HALO, 4, residual)

    x1, y1 = sx // 2, sy // 2
    for k in range(2):
        lanes = slice(k * LANES, (k + 1) * LANES)
        for i in range(x1):
            x = HALO + 2 * i
            sums[0, i, :, lanes] = rows_of(halfway[k], x, y1, BOTH, BOTH)
            left[...] = turn(by[k][x] + by[k][x + 1], 1, 0)
            sums[1, i, :, lanes] = left[pl.ds(0, y1, stride=2), :]
        sums[2, 0, :, lanes] = rows_of(bx[k], HALO - 1, y1, (0,), BOTH)
        sums[2, 1:, :, lanes] = jnp.zeros((x1 - 1, y1, LANES), F32)
    rhs1, low_y, low_x = to_level1(sums, 0, 3, pair_table(2 * LANES, LANES, False), 0.0625)
    weight1 = relaxer(coeffs1[0], coeffs1[1] + low_y + low_x)
    packed = pack_level1((2.0 * rhs1, weight1, coeffs1[2], coeffs1[3], coeffs1[4]))
    for n, values in enumerate(packed):
        own1[n] = values
        for send, face in zip(sends, faces_x(values[None], at_x % 2, n_x, NEAR)):
            send[n] = face[0]
        near_one[n], near_two[n] = faces_y(values, at_y % 2, NEAR)
        for send, tiles in zip(sends_xy, diagonal_sends(values, n_x, at_x % 2, at_y % 2)):
            for t in range(3):
                send[3 * n + t] = tiles[t]


def level2_rows(source, odd_axes, factor, x2, y2, z2):
    rows = []
    for i in range(x2):
        total = None
        for p in (1,) if odd_axes[0] else (0, 1):
            for q in (1,) if odd_axes[1] else (0, 1):
                term = source[2 * i + p, pl.ds(q, y2, stride=2), :]
                total = term if total is None else total + term
        rows.append(total)
    flat = jnp.concatenate(rows, axis=0)
    flat = factor * times_table(flat, pair_table(LANES, LANES, odd_axes[2]))
    lane = lane_of((y2, LANES))
    packed = jnp.zeros((y2, LANES), F32)
    for i in range(x2):
        mask = (lane >= i * z2) & (lane < (i + 1) * z2)
        packed = jnp.where(mask, turn(flat[i * y2:(i + 1) * y2], i * z2, 1), packed)
    return packed


def near_kernel(counts, devices, where_ref, ring, *refs):
    n_x = 1 if counts[0] == 2 else 2
    halos_x = refs[:n_x]
    main_two, main_one = refs[n_x:n_x + 2]
    diagonals, (coarse2, copies, level1, left) = refs[n_x + 2:3 * n_x + 2], refs[3 * n_x + 2:]
    n, bx1, by1, _ = ring.shape
    at_x, at_y, _ = position(where_ref)
    sides = [
        neighbours(counts[0], at_x, diagonals[k][...], diagonals[k - 2][...]) for k in range(2)
    ]
    rest = []
    for one, two in zip(*sides):
        rows = neighbours(counts[1], at_y, one, two)
        rest.append(jnp.concatenate(rows[::-1], axis=1))
    whole = []
    for a in range(n):
        below, above = neighbours(counts[0], at_x, halos_x[0][a], halos_x[-1][a])
        rows = neighbours(counts[1], at_y, main_one[a], main_two[a])
        rows = jnp.concatenate(rows[::-1], axis=1)
        low, high = (diagonal_tiles(*(side[3 * a + k] for k in range(3))) for side in rest)
        low = low[::-1]
        rows = jnp.concatenate(
            [tile[None] for tile in low] + [rows] + [tile[None] for tile in high], axis=0
        )
        block = jnp.concatenate([below, ring[a], above], axis=0)
        whole.append(jnp.concatenate([block, rows], axis=1))
    whole = unpack_level1(whole)
    rhs1, weight1 = whole[:2]
    faces1 = tuple(whole[2:])
    field1 = weight1 * rhs1
    field1 = sweep(field1, rhs1, weight1, faces1)
    for a, values in enumerate([field1] + whole):
        level1[a] = values
    mine = slice(NEAR, NEAR + bx1)
    inner = weight1[mine]
    diag1 = RELAX / jnp.where(inner > 0.0, inner, 1.0)
    remain = rhs1[mine] - diag1 * field1[mine] + pull(field1, faces1)[mine]
    left[...] = remain
    packed = level2_rows(left, (False,) * 3, 0.125, bx1 // 2, by1 // 2, LANES // 4)
    for d in range(devices):
        copies[d, 0] = packed
        for a in range(4):
            copies[d, a + 1] = coarse2[a]


def halve(values, odd_axis, step):
    half = values.shape[0] // 2
    even = [values[2 * i:2 * i + 1] for i in range(half)]
    odd = [values[2 * i + 1:2 * i + 2] for i in range(half)]
    if odd_axis != 0:
        odd = [a + b for a, b in zip(even, odd)]
    values = jnp.concatenate(odd, axis=0)
    for axis in (1, 2):
        next_one = turn(values, -step, axis)
        values = next_one if odd_axis == axis else values + next_one
    return values


def double(values, step):
    values = values + turn(values, step, 1)
    values = values + turn(values, step, 2)
    return jnp.concatenate([values[i // 2:i // 2 + 1] for i in range(2 * values.shape[0])], axis=0)


def coarse_levels(mass, faces, y, z):
    levels = []
    for level in range(2, LEVELS):
        step = 2 ** (level - 2)
        bx, by, bz = faces
        row = lax.broadcasted_iota(jnp.int32, by.shape, 1)
        lane = lane_of(bz.shape)
        coupled = (
            bx,
            jnp.where(row == (y - 1) * step, 0.0, by),
            jnp.where(lane == (z - 1) * step, 0.0, bz),
        )
        mass = jnp.where((row % step == 0) & (lane % step == 0), mass, 0.0)
        diag = diagonal(mass, faces, coupled, step)
        levels.append((diag, relaxer(mass, diag), coupled))
        if level < LEVELS - 1:
            faces = tuple(0.0625 * halve(face, axis, step) for axis, face in enumerate(faces))
            mass = 0.125 * halve(mass, -1, step)
            y, z = y // 2, z // 2
    return levels


def coarse_cycle(level, rhs, levels):
    step = 2 ** (level - 2)
    diag, weight, faces = levels[level - 2]
    field = weight * rhs
    if level == LEVELS - 1:
        for _ in range(BOTTOM - 1):
            field = sweep(field, rhs, weight, faces, step)
        return field
    for _ in range(SWEEPS - 1):
        field = sweep(field, rhs, weight, faces, step)
    remain = rhs - diag * field + pull(field, faces, step)
    correction = coarse_cycle(level + 1, 0.125 * halve(remain, -1, step), levels)
    field = field + double(correction, step)
    for _ in range(SWEEPS):
        field = sweep(field, rhs, weight, faces, step)
    return field


def spread_out(counts, slots, whole):
    gx, gy, gz = counts
    y2 = slots.shape[-2]
    x2 = whole.shape[0] // gx
    z2 = LANES // x2
    lane = lane_of((y2, LANES))
    for i in range(gx):
        for j in range(gy):
            for x in range(x2):
                for part in range(whole.shape[2] // LANES):
                    total = jnp.zeros((y2, LANES), F32)
                    for k in range(LANES // z2):
                        column = part * (LANES // z2) + k
                        if column < gz:
                            block = slots[(i * gy + j) * gz + column]
                            mask = (lane >= k * z2) & (lane < (k + 1) * z2)
                            total = jnp.where(mask, turn(block, (k - x) * z2, 1), total)
                    lanes = slice(part * LANES, (part + 1) * LANES)
                    whole[i * x2 + x, j * y2:(j + 1) * y2, lanes] = total


def up_kernel(counts, where_ref, gathered, level1, *refs):
    kept, weight, rhs, bx, by, bz = zip(refs[0:12:2], refs[1:12:2])
    out, whole, second, spread_m, spread_h, field_m, field_h, half_m, half_h = refs[12:]
    gx, gy, gz = counts
    at_x, at_y, at_z = position(where_ref)
    sx, sy, sz = out.shape
    x1, y1 = sx // 2, sy // 2
    x2, y2, z2 = x1 // 2, y1 // 2, sz // 4
    columns = max(LANES, gz * z2)
    for a in range(5):
        spread_out(counts, gathered.at[:, a], whole.at[a])
    levels = coarse_levels(whole[1], (whole[2], whole[3], whole[4]), gy * y2, gz * z2)
    correction = coarse_cycle(2, whole[0], levels)

    wide = gx * x2
    half = NEAR // 2
    ex1, ey1 = x1 + 2 * NEAR, y1 + 2 * NEAR
    second[:half] = jnp.zeros((half,) + correction.shape[1:], F32)
    second[half:half + wide] = correction
    second[half + wide:] = jnp.zeros((half,) + correction.shape[1:], F32)
    window = second[pl.ds(at_x * x2, x2 + NEAR)]
    rows = correction.shape[1]
    row = iota2((ey1, rows), 0)
    col = iota2((ey1, rows), 1)
    place = jnp.where(row < y1 + NEAR, row, row - ey1)
    table_y = (col == at_y * y2 + lax.shift_right_arithmetic(place, 1)).astype(F32)
    row = iota2((columns, LANES), 0)
    col = iota2((columns, LANES), 1)
    place = jnp.where(col < LANES * 3 // 4, col, col - LANES)
    table_z = (row == at_z * z2 + lax.shift_right_arithmetic(place, 1)).astype(F32)
    flat = times_table(window.reshape((x2 + NEAR) * rows, columns), table_z)
    blocks = [table_times(table_y, flat[i * rows:(i + 1) * rows])[None] for i in range(x2 + NEAR)]
    lifted = jnp.concatenate([blocks[i // 2] for i in range(ex1)], axis=0)
    field1, rhs1, weight1 = level1[0], level1[1], level1[2]
    faces1 = (level1[3], level1[4], level1[5])
    field1 = field1 + jnp.where(weight1 > 0.0, lifted, 0.0)
    for _ in range(SWEEPS):
        field1 = sweep(field1, rhs1, weight1, faces1)

    ex, ey = sx + 2 * HALO, sy + 2 * HALO
    near = field1[NEAR - 1:NEAR + x1 + 1].reshape((x1 + 2) * ey1, LANES)
    row = iota2((LANES, 2 * LANES), 0)
    col = iota2((LANES, 2 * LANES), 1)
    lifted = times_table(near, (col // 2 == row).astype(F32))
    quarter = NEAR // 2
    for k, spread in enumerate((spread_m, spread_h)):
        block = lifted[:, k * LANES:(k + 1) * LANES].reshape(x1 + 2, ey1, LANES)
        for i in range(x1 + 2):
            for q in range(2):
                spread[i, pl.ds(q, y1, stride=2), :] = block[i, :y1]
                spread[i, pl.ds(sy + q, quarter, stride=2), :] = block[i, y1:y1 + quarter]
                spread[i, pl.ds(sy + HALO + q, quarter, stride=2), :] = block[i, ey1 - quarter:]
    before, after = (field_m, field_h), (half_m, half_h)
    first = HALO - 2
    for x in range(first, ex - first):
        for k, spread in enumerate((spread_m, spread_h)):
            before[k][x] = kept[k][x] + spread[(x - first) // 2]

    lane = lane_of((ey, LANES))

    def sweep_out(x):
        centre, around = pull_slab(before, bx, by, bz, x, lane)
        for k in range(2):
            after[k][x] = KEEP * centre[k] + weight[k][x] * (rhs[k][x] + around[k])

    each(first + 1, ex - first - 1, 4, sweep_out)

    def sweep_own(x):
        centre, around = pull_slab(after, bx, by, bz, x, lane)
        value = KEEP * centre[0] + weight[0][x] * (rhs[0][x] + around[0])
        out[x - HALO] = value[:sy]

    each(HALO, ex - HALO, 4, sweep_own)


def run(kernel, outs, where, arrays, scratch=(), grant=16, micros=1, aliases={}):
    return pl.pallas_call(
        kernel,
        out_shape=tuple(jax.ShapeDtypeStruct(shape, F32) for shape in outs),
        in_specs=[SM] * len(where) + [VM] * len(arrays),
        out_specs=tuple(VM for _ in outs),
        input_output_aliases=aliases,
        scratch_shapes=[pltpu.VMEM(shape, F32) for shape in scratch],
        compiler_params=pltpu.CompilerParams(vmem_limit_bytes=grant * 1024 * 1024),
        cost_estimate=pl.CostEstimate(
            flops=0, bytes_accessed=int(micros * 3.6e6), transcendentals=0
        ),
    )(*where, *arrays)


def partners(count, k):
    partner = list(range(count))
    for low in range(k, count - 1, 2):
        partner[low], partner[low + 1] = low + 1, low
    return partner


def swaps(axis, sends, other=None):
    count = lax.axis_size(axis)
    got = []
    for k, block in enumerate(sends):
        partner = partners(count, k)
        if k == 1 and other is None:
            partner[0], partner[-1] = count - 1, 0
        if k == 0 or other is None:
            got.append(lax.ppermute(block, axis, list(enumerate(partner))))
            continue
        rows = lax.axis_size(other)
        pairs = []
        for row in range(rows):
            for i in range(count):
                ends = [(row, i), (min(row ^ 1, rows - 1) if partner[i] == i else row, partner[i])]
                if axis < other:
                    pairs.append(tuple(at * rows + line for line, at in ends))
                else:
                    pairs.append(tuple(line * count + at for line, at in ends))
        got.append(lax.ppermute(block, tuple(sorted((axis, other))), pairs))
    return got


def diagonal_swaps(sends, other):
    count_x, count = lax.axis_size("gx"), lax.axis_size(other)
    got = []
    for n, block in enumerate(sends):
        xs, others = partners(count_x, n // 2), partners(count, n % 2)
        pairs = [
            (x * count + y, xs[x] * count + others[y]) for x in range(count_x) for y in range(count)
        ]
        got.append(lax.ppermute(block, ("gx", other), pairs))
    return got


def local(initial, right_side, alpha, beta_x, beta_y, beta_z):
    axes = ("gx", "gy", "gz")
    counts = tuple(lax.axis_size(axis) for axis in axes)
    devices = counts[0] * counts[1] * counts[2]
    where = (lax.axis_index("gx") * STRIDE + lax.axis_index("gy")) * STRIDE + lax.axis_index("gz")
    where = (where.astype(jnp.int32).reshape(1),)
    ins = (initial, right_side, alpha, beta_x, beta_y, beta_z)
    sx, sy, sz = initial.shape
    n_x = 1 if counts[0] == 2 else 2
    ex, ey = sx + 2 * HALO, sy + 2 * HALO
    fine = (ex, ey, LANES)

    sends = run(
        functools.partial(faces_kernel, counts),
        [(6, HALO, sy, LANES)] * n_x
        + [(6, sx, HALO, LANES)] * 2
        + [(sx // 2, sy, LANES)] * 2
        + [(2, sy, LANES)] * (2 * n_x),
        where,
        ins,
        grant=60,
    )
    main_x = tuple(swaps("gx", sends[:n_x], "gy"))
    main_y = tuple(swaps("gy", sends[n_x:n_x + 2][::-1])[::-1])
    got = tuple(swaps("gz", sends[n_x + 2:n_x + 4], "gy"))
    got_xz = tuple(diagonal_swaps(sends[n_x + 4:], "gz"))
    zpack, two_y, one_y = run(
        functools.partial(halo_z_kernel, counts),
        [(ex, sy, LANES)] + [(21 + sx, HALO, LANES)] * 2,
        where,
        got + got_xz + main_x,
    )
    x1, y1 = sx // 2, sy // 2
    *laid, coarse2, coeffs1 = run(
        functools.partial(coefficient_kernel, counts),
        [fine] * 12 + [(4, y1 // 2, LANES), (5, x1, y1, LANES)],
        where,
        ins + (zpack,) + main_x,
        [(4, x1, y1, 2 * LANES), (4, x1, y1, LANES)],
        micros=2,
    )
    rest_y = tuple(swaps("gy", (one_y, two_y), "gz")[::-1])
    outs = run(
        functools.partial(down_kernel, counts),
        [fine] * 12
        + [(3, x1, y1, LANES)]
        + [(3, NEAR, y1, LANES)] * n_x
        + [(3, x1, NEAR, LANES)] * 2
        + [(9, NEAR, LANES)] * (2 * n_x)
        + [fine] * 4,
        where,
        tuple(laid) + main_y + rest_y + (coeffs1,),
        [(ex, 2 * HALO, LANES)] + [fine] * 4 + [(3, x1, y1, 2 * LANES), (ey, LANES)],
        24,
        micros=4,
        aliases={n + 1: n for n in range(12)},
    )
    laid, own1, outs = outs[:12], outs[12], outs[13:]
    sends_x, (two_y, one_y), outs = outs[:n_x], outs[n_x:n_x + 2], outs[n_x + 2:]
    sends_xy, fine_arrays = outs[:2 * n_x], outs[2 * n_x:]
    fine_arrays = tuple(fine_arrays) + tuple(laid[2:4]) + tuple(laid[6:])

    near_x = tuple(swaps("gx", sends_x, "gy"))
    near_y = tuple(swaps("gy", (one_y, two_y), "gz")[::-1])
    near_xy = tuple(diagonal_swaps(sends_xy, "gy"))
    copies, level1 = run(
        functools.partial(near_kernel, counts, devices),
        [(devices, 5, y1 // 2, LANES), (6, x1 + 2 * NEAR, y1 + 2 * NEAR, LANES)],
        where,
        (own1,) + near_x + near_y + near_xy + (coarse2,),
        [(x1, y1 + 2 * NEAR, LANES)],
    )

    gathered = lax.all_to_all(copies, axes, 0, 0, tiled=True)
    wide, rows = counts[0] * x1 // 2, counts[1] * y1 // 2
    columns = max(LANES, counts[2] * sz // 4)
    (result,) = run(
        functools.partial(up_kernel, counts),
        [(sx, sy, sz)],
        where,
        (gathered, level1) + tuple(fine_arrays),
        [(5, wide, rows, columns), (wide + NEAR, rows, columns)]
        + [(x1 + 2, ey, LANES)] * 2
        + [fine] * 4,
        24,
        micros=4,
    )
    return result


def solution(mesh):
    spec = P("gx", "gy", "gz")
    return jax.shard_map(
        local, mesh=mesh, in_specs=(spec,) * 6, out_specs=spec, check_vma=False
    )
```

```python
import functools

import jax
import jax.numpy as jnp
from jax import lax
from jax.experimental import pallas as pl
from jax.experimental.pallas import tpu as pltpu
from jax.sharding import PartitionSpec as P

LEVELS = 6
SWEEPS = 2
BOTTOM = 8
WEIGHT = 0.25 ** (LEVELS - 1)
RELAX = 2.0 / 3.0
KEEP = 1.0 / 3.0

HALO = 4
NEAR = 4
LANES = 128
PLACE = (0, 11, 21, 31, 41, 51)
DEPTH = (11, 10, 10, 10, 10, 11)
SIDE = LANES // 2
STRIDE = 256

VM = pl.BlockSpec(memory_space=pltpu.VMEM)
SM = pl.BlockSpec(memory_space=pltpu.SMEM)
F32 = jnp.float32


def position(where_ref):
    code = where_ref[0]
    return code // (STRIDE * STRIDE), code // STRIDE % STRIDE, code % STRIDE


def lane_of(shape):
    return lax.broadcasted_iota(jnp.int32, shape, len(shape) - 1)


def pick(flag, yes, no):
    return jnp.where(jnp.full(yes.shape, flag, jnp.int32) == 1, yes, no)


def neighbours(count, place, one, two):
    if count == 2:
        two = jnp.zeros_like(one)
    else:
        ends = jnp.full(two.shape, place, jnp.int32)
        two = jnp.where((ends == 0) | (ends == count - 1), 0.0, two)
    return pick(place % 2, one, two), pick(place % 2, two, one)


def turn(values, shift, axis):
    return pltpu.roll(values, shift % values.shape[axis], axis)


def parts_of(values):
    high = values.astype(jnp.bfloat16)
    rest = values - high.astype(F32)
    middle = rest.astype(jnp.bfloat16)
    low = (rest - middle.astype(F32)).astype(jnp.bfloat16)
    return high, middle, low


def times_table(values, table):
    table = table.astype(jnp.bfloat16)
    total = None
    for part in reversed(parts_of(values)):
        term = jnp.dot(part, table, preferred_element_type=F32)
        total = term if total is None else total + term
    return total


def table_times(table, values):
    table = table.astype(jnp.bfloat16)
    total = None
    for part in reversed(parts_of(values)):
        term = jnp.dot(table, part, preferred_element_type=F32)
        total = term if total is None else total + term
    return total


def iota2(shape, axis):
    return lax.broadcasted_iota(jnp.int32, shape, axis)


def pair_table(rows, cols, odd):
    row = iota2((rows, cols), 0)
    col = iota2((rows, cols), 1)
    hit = (row == 2 * col + 1) if odd else (row // 2 == col)
    return hit.astype(F32)


def below_x(values):
    if values.shape[0] == 1:
        return jnp.zeros_like(values)
    return jnp.concatenate([jnp.zeros_like(values[:1]), values[:-1]], axis=0)


def above_x(values):
    if values.shape[0] == 1:
        return jnp.zeros_like(values)
    return jnp.concatenate([values[1:], jnp.zeros_like(values[:1])], axis=0)


def pull(values, faces, step=1):
    bx, by, bz = faces
    total = bx * above_x(values) + below_x(bx * values)
    total = total + (by * turn(values, -step, 1) + turn(by * values, step, 1))
    return total + (bz * turn(values, -step, 2) + turn(bz * values, step, 2))


def diagonal(mass, faces, coupled, step=1):
    bx, by, bz = faces
    _, cy, cz = coupled
    return mass + bx + below_x(bx) + by + turn(cy, step, 1) + bz + turn(cz, step, 2)


def relaxer(mass, diag):
    inside = mass > 0.0
    return jnp.where(inside, RELAX / jnp.where(inside, diag, 1.0), 0.0)


def sweep(values, rhs, weight, faces, step=1):
    return KEEP * values + weight * (rhs + pull(values, faces, step))


def faces_x(values, odd, n_x, width):
    head, tail = values[:, :width], values[:, values.shape[1] - width:]
    return [pick(odd, head, tail), pick(odd, tail, head)][:n_x]


def faces_y(values, odd, width):
    head, tail = values[:, :width], values[:, values.shape[1] - width:]
    return pick(odd, head, tail), pick(odd, tail, head)


def corner_sends(below, above, odd):
    packs = []
    for rows, sign in ((slice(0, 8), 1), (slice(below.shape[1] - 8, below.shape[1]), -1)):
        low = [below[3 - i, rows] for i in range(3)]
        high = [above[i, rows] for i in range(3)]
        row = iota2(low[0].shape, 0)
        row = row if sign == 1 else 7 - row
        pack = (
            jnp.where(row < 3, low[0], turn(low[2], 3 * sign, 0)),
            jnp.where(row < 2, low[1], turn(high[1], 2 * sign, 0)),
            jnp.where(row < 3, high[0], turn(high[2], 3 * sign, 0)),
        )
        packs.append([p[:4] if sign == 1 else p[4:] for p in pack])
    return [(pick(odd, h, t), pick(odd, t, h)) for h, t in zip(*packs)]


def inner_rows(tile, by):
    upper = iota2(tile.shape, 0) < 4
    return jnp.where(upper, turn(tile, -by, 0), turn(tile, by, 0))


def corner_tiles(first, second, third):
    zero = jnp.zeros_like(first)
    low = (zero, inner_rows(first, 3), second, first)
    return low, (third, inner_rows(second, 2), inner_rows(third, 3), zero)


def diagonal_sends(values, n_x, odd_x, odd_y):
    corners = []
    for slabs in ([values[i] for i in range(4)], [values[values.shape[0] - 1 - i] for i in range(4)]):
        for sign in (1, -1):
            row = iota2(slabs[0].shape, 0)
            row = row if sign == 1 else 7 - row
            tiles = (slabs[0], jnp.where(row < 3, slabs[1], turn(slabs[3], 3 * sign, 0)), slabs[2])
            corners.append([t[:4] if sign == 1 else t[4:] for t in tiles])
    sends = []
    for k_x in range(n_x):
        for k_y in range(2):
            head_x = odd_x if k_x == 0 else 1 - odd_x
            head_y = odd_y if k_y == 0 else 1 - odd_y
            sends.append(
                [
                    pick(head_x, pick(head_y, hh, ht), pick(head_y, th, tt))
                    for hh, ht, th, tt in zip(*corners)
                ]
            )
    return sends


def diagonal_tiles(first, second, third):
    return [first, second, third, inner_rows(second, 3)]


def faces_kernel(counts, where_ref, *refs):
    ins, refs = refs[:6], refs[6:]
    sends_x, (first, second) = refs[:-2], refs[-2:]
    odd_x, _, odd = (place % 2 for place in position(where_ref))
    sx, sy, sz = ins[0].shape
    half = sx // 2
    lane = lane_of((half, sy, LANES))
    head = jnp.zeros((half, sy, LANES), F32)
    tail = head
    for a, ref in enumerate(ins):
        for send, face in zip(sends_x, faces_x(ref[...][None], odd_x, len(sends_x), HALO)):
            send[a] = face[0]
        for g in range(2):
            values = ref[g * half:(g + 1) * half]
            at = SIDE * g + PLACE[a]
            mask = (lane >= at) & (lane < at + DEPTH[a])
            head = jnp.where(mask, turn(values, at, 2), head)
            tail = jnp.where(mask, turn(values, at + DEPTH[a], 2), tail)
    first[...] = pick(odd, head, tail)
    second[...] = pick(odd, tail, head)


def halo_z_kernel(counts, where_ref, one_ref, two_ref, zpack, *sends):
    at_x, _, at_z = position(where_ref)
    half = one_ref.shape[0]
    below, above = neighbours(counts[2], at_z, one_ref[...], two_ref[...])
    lane = lane_of(below.shape)
    zpack[:half] = jnp.where(lane < SIDE, above, turn(below, SIDE, 2))
    zpack[half:] = jnp.where(lane < SIDE, turn(above, SIDE, 2), below)
    for send, face in zip(sends, faces_x(zpack[...][None], at_x % 2, len(sends), HALO)):
        send[...] = face[0]


def corners_kernel(counts, where_ref, zpack, *refs):
    n_x = 1 if counts[0] == 2 else 2
    main_x, halos_x, (two_y, one_y) = refs[:n_x], refs[n_x:2 * n_x], refs[2 * n_x + 1:]
    at_x, at_y, _ = position(where_ref)
    for a in range(7):
        if a < 6:
            below, above = neighbours(counts[0], at_x, main_x[0][a], main_x[-1][a])
        else:
            below, above = neighbours(counts[0], at_x, halos_x[0][...], halos_x[-1][...])
        for n, pair in enumerate(corner_sends(below, above, at_y % 2)):
            one_y[3 * a + n], two_y[3 * a + n] = pair
    one_y[21:], two_y[21:] = faces_y(zpack[...], at_y % 2, HALO)


def each(first, last, step, body):
    rounds = (last - first) // step

    def go(i, carry):
        for j in range(step):
            body(first + i * step + j)
        return carry

    if rounds:
        lax.fori_loop(0, rounds, go, 0)
    for x in range(first + rounds * step, last):
        body(x)


def ring_up(main, halo, lane):
    main_up, halo_up = turn(main, -1, 1), turn(halo, -1, 1)
    last = lane == LANES - 1
    return jnp.where(last, halo_up, main_up), jnp.where(last, main_up, halo_up)


def ring_down(main, halo, lane):
    main_down, halo_down = turn(main, 1, 1), turn(halo, 1, 1)
    zero = lane == 0
    return jnp.where(zero, halo_down, main_down), jnp.where(zero, main_down, halo_down)


def pull_slab(field, bx, by, bz, x, lane):
    centre = [half[x] for half in field]
    out = []
    for k in range(2):
        c, face = centre[k], by[k][x]
        t = bx[k][x] * field[k][x + 1] + bx[k][x - 1] * field[k][x - 1]
        out.append(t + (face * turn(c, -1, 0) + turn(face * c, 1, 0)))
    faces = [half[x] for half in bz]
    ups = ring_up(centre[0], centre[1], lane)
    downs = ring_down(faces[0] * centre[0], faces[1] * centre[1], lane)
    return centre, [out[k] + (faces[k] * ups[k] + downs[k]) for k in range(2)]


def unpacked(packed, a, lane):
    at, depth = PLACE[a], DEPTH[a]
    axis = packed.ndim - 1
    right, left = turn(packed, -at, axis), turn(packed, SIDE - depth - at, axis)
    return jnp.where(lane < depth, right, jnp.where(lane >= LANES - depth, left, 0.0))


def rows_of(source, x, count, firsts, seconds):
    total = None
    for p in firsts:
        for q in seconds:
            term = source[x + p, pl.ds(q, count, stride=2), :]
            total = term if total is None else total + term
    return total


BOTH, ODD = (0, 1), (1,)


def to_level1(sums, first, count, table, factor):
    _, x1, y1, _ = sums.shape
    flat = sums[first:first + count].reshape(count * x1 * y1, 2 * LANES)
    return factor * times_table(flat, table).reshape(count, x1, y1, LANES)


def coefficient_kernel(counts, where_ref, *refs):
    ins, refs = refs[:7], refs[7:]
    n_x = 1 if counts[0] == 2 else 2
    main_x, refs = refs[:n_x], refs[n_x:]
    two_y, one_y, refs = refs[0], refs[1], refs[2:]
    arrays, (coarse2, coeffs1, sums, pairing) = refs[:12], refs[12:]
    sx, sy, sz = ins[0].shape
    at_x, at_y, _ = position(where_ref)
    x1, y1 = sx // 2, sy // 2
    lane = lane_of((sx, sy, LANES))
    lanes = [slice(k * LANES, (k + 1) * LANES) for k in range(2)]
    mine = slice(HALO, HALO + sx)
    for a in range(6):
        to = arrays[2 * a]
        below, above = neighbours(counts[0], at_x, main_x[0][a], main_x[-1][a])
        to[:HALO, :sy] = below
        to[mine, :sy] = ins[a][...]
        to[HALO + sx:, :sy] = above
        arrays[2 * a + 1][mine, :sy] = unpacked(ins[6][...], a, lane)
        one_y[a], two_y[a] = faces_y(ins[a][...], at_y % 2, HALO)
    for n, (firsts, seconds) in enumerate(((BOTH, BOTH), (ODD, BOTH), (BOTH, ODD), (BOTH, BOTH))):
        for k in range(2):
            for i in range(x1):
                source = arrays[2 * (n + 2) + k]
                sums[n, i, :, lanes[k]] = rows_of(source, HALO + 2 * i, y1, firsts, seconds)
    pairs = pair_table(2 * LANES, LANES, False)
    odds = pair_table(2 * LANES, LANES, True)
    paired = to_level1(sums, 0, 3, pairs, 0.0625)
    mass1 = (2.0 * WEIGHT) * paired[0]
    faces1 = (paired[1], paired[2], to_level1(sums, 3, 1, odds, 0.0625)[0])
    diag1 = mass1 + faces1[0] + below_x(faces1[0])
    diag1 = diag1 + faces1[1] + faces1[2] + turn(faces1[2], 1, 2)
    for n, values in enumerate((mass1, diag1) + faces1):
        coeffs1[n] = values
    parts = (
        (mass1, False, False, False, 0.125),
        (faces1[0], True, False, False, 0.0625),
        (faces1[1], False, True, False, 0.0625),
        (faces1[2], False, False, True, 0.0625),
    )
    for n, (values, *odd_axes, factor) in enumerate(parts):
        pairing[n] = values
        coarse2[n] = level2_rows(pairing.at[n], odd_axes, factor, x1 // 2, y1 // 2, sz // 4)


def down_kernel(counts, where_ref, zpack, *refs):
    refs = refs[12:]
    n_x = 1 if counts[0] == 2 else 2
    halos_x = refs[:n_x]
    main_two, main_one, rest_two, rest_one, coeffs1 = refs[n_x:5 + n_x]
    flat, refs = refs[5 + n_x:17 + n_x], refs[17 + n_x:]
    arrays = tuple(zip(flat[::2], flat[1::2]))
    own1, refs = refs[0], refs[1:]
    sends, near_two, near_one, refs = refs[:n_x], refs[n_x], refs[n_x + 1], refs[n_x + 2:]
    sends_xy, refs = refs[:2 * n_x], refs[2 * n_x:]
    kept_m, kept_h, weight_m, weight_h = refs[:4]
    packs, half_m, half_h, diag_m, diag_h, sums, left = refs[4:]
    field, rhs, alpha, bx, by, bz = arrays
    sx, sy, sz = zpack.shape
    ex, ey = sx + 2 * HALO, sy + 2 * HALO
    at_x, at_y, _ = position(where_ref)

    rest = neighbours(counts[1], at_y, rest_one[...], rest_two[...])
    rest = jnp.concatenate(rest[::-1], axis=1)
    for a in range(7):
        if a < 6:
            to = arrays[a][0]
            rows = neighbours(counts[1], at_y, main_one[a], main_two[a])
            rows = jnp.concatenate(rows[::-1], axis=1)
        else:
            to = packs
            rows = rest[21:]
            below, above = neighbours(counts[0], at_x, halos_x[0][...], halos_x[-1][...])
            to[:HALO, :sy] = below
            to[HALO + sx:, :sy] = above
        to[HALO:HALO + sx, sy:] = rows
        low, high = corner_tiles(*(rest[3 * a + n] for n in range(3)))
        for n in range(HALO):
            to[n, sy:] = low[n]
            to[HALO + sx + n, sy:] = high[n]
    lane = lane_of((ey, LANES))
    lane_low = lane_of((2 * HALO, LANES))

    def unpack_rows(x):
        packed = packs[x, sy:]
        for a in range(6):
            arrays[a][1][x, sy:] = unpacked(packed, a, lane_low)

    def unpack(x):
        packed = packs[x]
        for a in range(6):
            arrays[a][1][x] = unpacked(packed, a, lane)

    each(0, HALO, HALO, unpack)
    each(HALO, HALO + sx, 8, unpack_rows)
    each(HALO + sx, ex, HALO, unpack)
    halfway, weight, kept = (half_m, half_h), (weight_m, weight_h), (kept_m, kept_h)
    diag = (diag_m, diag_h)

    def first_sweep(x):
        faces = [half[x] for half in bz]
        downs = ring_down(faces[0], faces[1], lane)
        centre, near = pull_slab(field, bx, by, bz, x, lane)
        for k in range(2):
            face = by[k][x]
            mass = WEIGHT * alpha[k][x]
            d = mass + bx[k][x] + bx[k][x - 1] + face + turn(face, 1, 0) + faces[k] + downs[k]
            w = relaxer(mass, d)
            diag[k][x] = d
            weight[k][x] = w
            halfway[k][x] = KEEP * centre[k] + w * (rhs[k][x] + near[k])

    each(1, ex - 1, 4, first_sweep)

    def second_sweep(x):
        centre, near = pull_slab(halfway, bx, by, bz, x, lane)
        for k in range(2):
            kept[k][x] = KEEP * centre[k] + weight[k][x] * (rhs[k][x] + near[k])

    each(2, ex - 2, 4, second_sweep)

    def residual(x):
        centre, near = pull_slab(kept, bx, by, bz, x, lane)
        for k in range(2):
            halfway[k][x] = rhs[k][x] - diag[k][x] * centre[k] + near[k]

    each(HALO, ex - HALO, 4, residual)

    x1, y1 = sx // 2, sy // 2
    for k in range(2):
        lanes = slice(k * LANES, (k + 1) * LANES)
        for i in range(x1):
            x = HALO + 2 * i
            sums[0, i, :, lanes] = rows_of(halfway[k], x, y1, BOTH, BOTH)
            left[...] = turn(by[k][x] + by[k][x + 1], 1, 0)
            sums[1, i, :, lanes] = left[pl.ds(0, y1, stride=2), :]
        sums[2, 0, :, lanes] = rows_of(bx[k], HALO - 1, y1, (0,), BOTH)
        sums[2, 1:, :, lanes] = jnp.zeros((x1 - 1, y1, LANES), F32)
    rhs1, low_y, low_x = to_level1(sums, 0, 3, pair_table(2 * LANES, LANES, False), 0.0625)
    weight1 = relaxer(coeffs1[0], coeffs1[1] + low_y + low_x)
    for n, values in enumerate((2.0 * rhs1, weight1, coeffs1[2], coeffs1[3], coeffs1[4])):
        own1[n] = values
        for send, face in zip(sends, faces_x(values[None], at_x % 2, n_x, NEAR)):
            send[n] = face[0]
        near_one[n], near_two[n] = faces_y(values, at_y % 2, NEAR)
        for send, tiles in zip(sends_xy, diagonal_sends(values, n_x, at_x % 2, at_y % 2)):
            for t in range(3):
                send[3 * n + t] = tiles[t]


def level2_rows(source, odd_axes, factor, x2, y2, z2):
    rows = []
    for i in range(x2):
        total = None
        for p in (1,) if odd_axes[0] else (0, 1):
            for q in (1,) if odd_axes[1] else (0, 1):
                term = source[2 * i + p, pl.ds(q, y2, stride=2), :]
                total = term if total is None else total + term
        rows.append(total)
    flat = jnp.concatenate(rows, axis=0)
    flat = factor * times_table(flat, pair_table(LANES, LANES, odd_axes[2]))
    lane = lane_of((y2, LANES))
    packed = jnp.zeros((y2, LANES), F32)
    for i in range(x2):
        mask = (lane >= i * z2) & (lane < (i + 1) * z2)
        packed = jnp.where(mask, turn(flat[i * y2:(i + 1) * y2], i * z2, 1), packed)
    return packed


def near_kernel(counts, devices, where_ref, ring, *refs):
    n_x = 1 if counts[0] == 2 else 2
    halos_x = refs[:n_x]
    main_two, main_one = refs[n_x:n_x + 2]
    diagonals, (coarse2, copies, level1, left) = refs[n_x + 2:3 * n_x + 2], refs[3 * n_x + 2:]
    n, bx1, by1, _ = ring.shape
    at_x, at_y, _ = position(where_ref)
    sides = [
        neighbours(counts[0], at_x, diagonals[k][...], diagonals[k - 2][...]) for k in range(2)
    ]
    rest = []
    for one, two in zip(*sides):
        rows = neighbours(counts[1], at_y, one, two)
        rest.append(jnp.concatenate(rows[::-1], axis=1))
    whole = []
    for a in range(n):
        below, above = neighbours(counts[0], at_x, halos_x[0][a], halos_x[-1][a])
        rows = neighbours(counts[1], at_y, main_one[a], main_two[a])
        rows = jnp.concatenate(rows[::-1], axis=1)
        low, high = (diagonal_tiles(*(side[3 * a + k] for k in range(3))) for side in rest)
        low = low[::-1]
        rows = jnp.concatenate(
            [tile[None] for tile in low] + [rows] + [tile[None] for tile in high], axis=0
        )
        block = jnp.concatenate([below, ring[a], above], axis=0)
        whole.append(jnp.concatenate([block, rows], axis=1))
    rhs1, weight1 = whole[:2]
    faces1 = tuple(whole[2:])
    field1 = weight1 * rhs1
    field1 = sweep(field1, rhs1, weight1, faces1)
    for a, values in enumerate([field1] + whole):
        level1[a] = values
    mine = slice(NEAR, NEAR + bx1)
    inner = weight1[mine]
    diag1 = RELAX / jnp.where(inner > 0.0, inner, 1.0)
    remain = rhs1[mine] - diag1 * field1[mine] + pull(field1, faces1)[mine]
    left[...] = remain
    packed = level2_rows(left, (False,) * 3, 0.125, bx1 // 2, by1 // 2, LANES // 4)
    for d in range(devices):
        copies[d, 0] = packed
        for a in range(n - 1):
            copies[d, a + 1] = coarse2[a]


def halve(values, odd_axis, step):
    half = values.shape[0] // 2
    even = [values[2 * i:2 * i + 1] for i in range(half)]
    odd = [values[2 * i + 1:2 * i + 2] for i in range(half)]
    if odd_axis != 0:
        odd = [a + b for a, b in zip(even, odd)]
    values = jnp.concatenate(odd, axis=0)
    for axis in (1, 2):
        next_one = turn(values, -step, axis)
        values = next_one if odd_axis == axis else values + next_one
    return values


def double(values, step):
    values = values + turn(values, step, 1)
    values = values + turn(values, step, 2)
    return jnp.concatenate([values[i // 2:i // 2 + 1] for i in range(2 * values.shape[0])], axis=0)


def coarse_levels(mass, faces, y, z):
    levels = []
    for level in range(2, LEVELS):
        step = 2 ** (level - 2)
        bx, by, bz = faces
        row = lax.broadcasted_iota(jnp.int32, by.shape, 1)
        lane = lane_of(bz.shape)
        coupled = (
            bx,
            jnp.where(row == (y - 1) * step, 0.0, by),
            jnp.where(lane == (z - 1) * step, 0.0, bz),
        )
        mass = jnp.where((row % step == 0) & (lane % step == 0), mass, 0.0)
        diag = diagonal(mass, faces, coupled, step)
        levels.append((diag, relaxer(mass, diag), coupled))
        if level < LEVELS - 1:
            faces = tuple(0.0625 * halve(face, axis, step) for axis, face in enumerate(faces))
            mass = 0.125 * halve(mass, -1, step)
            y, z = y // 2, z // 2
    return levels


def coarse_cycle(level, rhs, levels):
    step = 2 ** (level - 2)
    diag, weight, faces = levels[level - 2]
    field = weight * rhs
    if level == LEVELS - 1:
        for _ in range(BOTTOM - 1):
            field = sweep(field, rhs, weight, faces, step)
        return field
    for _ in range(SWEEPS - 1):
        field = sweep(field, rhs, weight, faces, step)
    remain = rhs - diag * field + pull(field, faces, step)
    correction = coarse_cycle(level + 1, 0.125 * halve(remain, -1, step), levels)
    field = field + double(correction, step)
    for _ in range(SWEEPS):
        field = sweep(field, rhs, weight, faces, step)
    return field


def spread_out(counts, slots, whole):
    gx, gy, gz = counts
    y2 = slots.shape[-2]
    x2 = whole.shape[0] // gx
    z2 = LANES // x2
    lane = lane_of((y2, LANES))
    for i in range(gx):
        for j in range(gy):
            for x in range(x2):
                for part in range(whole.shape[2] // LANES):
                    total = jnp.zeros((y2, LANES), F32)
                    for k in range(LANES // z2):
                        column = part * (LANES // z2) + k
                        if column < gz:
                            block = slots[(i * gy + j) * gz + column]
                            mask = (lane >= k * z2) & (lane < (k + 1) * z2)
                            total = jnp.where(mask, turn(block, (k - x) * z2, 1), total)
                    lanes = slice(part * LANES, (part + 1) * LANES)
                    whole[i * x2 + x, j * y2:(j + 1) * y2, lanes] = total


def up_kernel(counts, where_ref, gathered, level1, *refs):
    kept, weight, rhs, bx, by, bz = zip(refs[0:12:2], refs[1:12:2])
    out, whole, second, spread_m, spread_h, field_m, field_h, half_m, half_h = refs[12:]
    gx, gy, gz = counts
    at_x, at_y, at_z = position(where_ref)
    sx, sy, sz = out.shape
    x1, y1 = sx // 2, sy // 2
    x2, y2, z2 = x1 // 2, y1 // 2, sz // 4
    columns = max(LANES, gz * z2)
    for a in range(5):
        spread_out(counts, gathered.at[:, a], whole.at[a])
    levels = coarse_levels(whole[1], (whole[2], whole[3], whole[4]), gy * y2, gz * z2)
    correction = coarse_cycle(2, whole[0], levels)

    wide = gx * x2
    half = NEAR // 2
    ex1, ey1 = x1 + 2 * NEAR, y1 + 2 * NEAR
    second[:half] = jnp.zeros((half,) + correction.shape[1:], F32)
    second[half:half + wide] = correction
    second[half + wide:] = jnp.zeros((half,) + correction.shape[1:], F32)
    window = second[pl.ds(at_x * x2, x2 + NEAR)]
    rows = correction.shape[1]
    row = iota2((ey1, rows), 0)
    col = iota2((ey1, rows), 1)
    place = jnp.where(row < y1 + NEAR, row, row - ey1)
    table_y = (col == at_y * y2 + lax.shift_right_arithmetic(place, 1)).astype(F32)
    row = iota2((columns, LANES), 0)
    col = iota2((columns, LANES), 1)
    place = jnp.where(col < LANES * 3 // 4, col, col - LANES)
    table_z = (row == at_z * z2 + lax.shift_right_arithmetic(place, 1)).astype(F32)
    flat = times_table(window.reshape((x2 + NEAR) * rows, columns), table_z)
    blocks = [table_times(table_y, flat[i * rows:(i + 1) * rows])[None] for i in range(x2 + NEAR)]
    lifted = jnp.concatenate([blocks[i // 2] for i in range(ex1)], axis=0)
    field1, rhs1, weight1 = level1[0], level1[1], level1[2]
    faces1 = (level1[3], level1[4], level1[5])
    field1 = field1 + jnp.where(weight1 > 0.0, lifted, 0.0)
    for _ in range(SWEEPS):
        field1 = sweep(field1, rhs1, weight1, faces1)

    ex, ey = sx + 2 * HALO, sy + 2 * HALO
    near = field1[NEAR - 1:NEAR + x1 + 1].reshape((x1 + 2) * ey1, LANES)
    row = iota2((LANES, 2 * LANES), 0)
    col = iota2((LANES, 2 * LANES), 1)
    lifted = times_table(near, (col // 2 == row).astype(F32))
    quarter = NEAR // 2
    for k, spread in enumerate((spread_m, spread_h)):
        block = lifted[:, k * LANES:(k + 1) * LANES].reshape(x1 + 2, ey1, LANES)
        for i in range(x1 + 2):
            for q in range(2):
                spread[i, pl.ds(q, y1, stride=2), :] = block[i, :y1]
                spread[i, pl.ds(sy + q, quarter, stride=2), :] = block[i, y1:y1 + quarter]
                spread[i, pl.ds(sy + HALO + q, quarter, stride=2), :] = block[i, ey1 - quarter:]
    before, after = (field_m, field_h), (half_m, half_h)
    first = HALO - 2
    for x in range(first, ex - first):
        for k, spread in enumerate((spread_m, spread_h)):
            before[k][x] = kept[k][x] + spread[(x - first) // 2]

    lane = lane_of((ey, LANES))

    def sweep_out(x):
        centre, around = pull_slab(before, bx, by, bz, x, lane)
        for k in range(2):
            after[k][x] = KEEP * centre[k] + weight[k][x] * (rhs[k][x] + around[k])

    each(first + 1, ex - first - 1, 4, sweep_out)

    def sweep_own(x):
        centre, around = pull_slab(after, bx, by, bz, x, lane)
        value = KEEP * centre[0] + weight[0][x] * (rhs[0][x] + around[0])
        out[x - HALO] = value[:sy]

    each(HALO, ex - HALO, 4, sweep_own)


def run(kernel, outs, where, arrays, scratch=(), grant=16, micros=1, aliases={}):
    return pl.pallas_call(
        kernel,
        out_shape=tuple(jax.ShapeDtypeStruct(shape, F32) for shape in outs),
        in_specs=[SM] * len(where) + [VM] * len(arrays),
        out_specs=tuple(VM for _ in outs),
        input_output_aliases=aliases,
        scratch_shapes=[pltpu.VMEM(shape, F32) for shape in scratch],
        compiler_params=pltpu.CompilerParams(vmem_limit_bytes=grant * 1024 * 1024),
        cost_estimate=pl.CostEstimate(
            flops=0, bytes_accessed=int(micros * 3.6e6), transcendentals=0
        ),
    )(*where, *arrays)


def partners(count, k):
    partner = list(range(count))
    for low in range(k, count - 1, 2):
        partner[low], partner[low + 1] = low + 1, low
    return partner


def swaps(axis, sends, other=None):
    count = lax.axis_size(axis)
    got = []
    for k, block in enumerate(sends):
        partner = partners(count, k)
        if k == 1 and other is None:
            partner[0], partner[-1] = count - 1, 0
        if k == 0 or other is None:
            got.append(lax.ppermute(block, axis, list(enumerate(partner))))
            continue
        rows = lax.axis_size(other)
        pairs = []
        for row in range(rows):
            for i in range(count):
                ends = [(row, i), (min(row ^ 1, rows - 1) if partner[i] == i else row, partner[i])]
                if axis < other:
                    pairs.append(tuple(at * rows + line for line, at in ends))
                else:
                    pairs.append(tuple(line * count + at for line, at in ends))
        got.append(lax.ppermute(block, tuple(sorted((axis, other))), pairs))
    return got


def diagonal_swaps(sends):
    count_x, count_y = lax.axis_size("gx"), lax.axis_size("gy")
    got = []
    for n, block in enumerate(sends):
        xs, ys = partners(count_x, n // 2), partners(count_y, n % 2)
        pairs = [
            (x * count_y + y, xs[x] * count_y + ys[y])
            for x in range(count_x)
            for y in range(count_y)
        ]
        got.append(lax.ppermute(block, ("gx", "gy"), pairs))
    return got


def local(initial, right_side, alpha, beta_x, beta_y, beta_z):
    axes = ("gx", "gy", "gz")
    counts = tuple(lax.axis_size(axis) for axis in axes)
    devices = counts[0] * counts[1] * counts[2]
    where = (lax.axis_index("gx") * STRIDE + lax.axis_index("gy")) * STRIDE + lax.axis_index("gz")
    where = (where.astype(jnp.int32).reshape(1),)
    ins = (initial, right_side, alpha, beta_x, beta_y, beta_z)
    sx, sy, sz = initial.shape
    n_x = 1 if counts[0] == 2 else 2
    ex, ey = sx + 2 * HALO, sy + 2 * HALO
    fine = (ex, ey, LANES)

    *sends_x, first, second = run(
        functools.partial(faces_kernel, counts),
        [(6, HALO, sy, LANES)] * n_x + [(sx // 2, sy, LANES)] * 2,
        where,
        ins,
        grant=60,
    )
    main_x = tuple(swaps("gx", sends_x, "gy"))
    got = swaps("gz", (first, second), "gy")
    zpack, *sends = run(
        functools.partial(halo_z_kernel, counts),
        [(sx, sy, LANES)] + [(HALO, sy, LANES)] * n_x,
        where,
        tuple(got),
    )
    halos_x = tuple(swaps("gx", sends, "gy"))
    x1, y1 = sx // 2, sy // 2
    two_y, one_y, *laid, coarse2, coeffs1 = run(
        functools.partial(coefficient_kernel, counts),
        [(6, sx, HALO, LANES)] * 2 + [fine] * 12 + [(4, y1 // 2, LANES), (5, x1, y1, LANES)],
        where,
        ins + (zpack,) + main_x,
        [(4, x1, y1, 2 * LANES), (4, x1, y1, LANES)],
        micros=2,
    )
    main_y = tuple(swaps("gy", (one_y, two_y), "gz")[::-1])
    two_y, one_y = run(
        functools.partial(corners_kernel, counts),
        [(21 + sx, HALO, LANES)] * 2,
        where,
        (zpack,) + main_x + halos_x + (coarse2,),
    )
    rest_y = tuple(swaps("gy", (one_y, two_y), "gz")[::-1])
    outs = run(
        functools.partial(down_kernel, counts),
        [fine] * 12
        + [(5, x1, y1, LANES)]
        + [(5, NEAR, y1, LANES)] * n_x
        + [(5, x1, NEAR, LANES)] * 2
        + [(15, NEAR, LANES)] * (2 * n_x)
        + [fine] * 4,
        where,
        (zpack,) + tuple(laid) + halos_x + main_y + rest_y + (coeffs1,),
        [fine] * 5 + [(3, x1, y1, 2 * LANES), (ey, LANES)],
        24,
        micros=4,
        aliases={n + 2: n for n in range(12)},
    )
    laid, own1, outs = outs[:12], outs[12], outs[13:]
    sends_x, (two_y, one_y), outs = outs[:n_x], outs[n_x:n_x + 2], outs[n_x + 2:]
    sends_xy, fine_arrays = outs[:2 * n_x], outs[2 * n_x:]
    fine_arrays = tuple(fine_arrays) + tuple(laid[2:4]) + tuple(laid[6:])

    near_x = tuple(swaps("gx", sends_x, "gy"))
    near_y = tuple(swaps("gy", (one_y, two_y), "gz")[::-1])
    near_xy = tuple(diagonal_swaps(sends_xy))
    copies, level1 = run(
        functools.partial(near_kernel, counts, devices),
        [(devices, 5, y1 // 2, LANES), (6, x1 + 2 * NEAR, y1 + 2 * NEAR, LANES)],
        where,
        (own1,) + near_x + near_y + near_xy + (coarse2,),
        [(x1, y1 + 2 * NEAR, LANES)],
    )

    gathered = lax.all_to_all(copies, axes, 0, 0, tiled=True)
    wide, rows = counts[0] * x1 // 2, counts[1] * y1 // 2
    columns = max(LANES, counts[2] * sz // 4)
    (result,) = run(
        functools.partial(up_kernel, counts),
        [(sx, sy, sz)],
        where,
        (gathered, level1) + tuple(fine_arrays),
        [(5, wide, rows, columns), (wide + NEAR, rows, columns)]
        + [(x1 + 2, ey, LANES)] * 2
        + [fine] * 4,
        24,
        micros=4,
    )
    return result


def solution(mesh):
    spec = P("gx", "gy", "gz")
    return jax.shard_map(
        local, mesh=mesh, in_specs=(spec,) * 6, out_specs=spec, check_vma=False
    )
```

```python
import functools

import jax
import jax.numpy as jnp
from jax import lax
from jax.experimental import pallas as pl
from jax.experimental.pallas import tpu as pltpu
from jax.sharding import PartitionSpec as P

LEVELS = 6
SWEEPS = 2
BOTTOM = 8
WEIGHT = 0.25 ** (LEVELS - 1)
RELAX = 2.0 / 3.0
KEEP = 1.0 / 3.0

HALO = 4
NEAR = 4
LANES = 128
PLACE = (0, 11, 21, 31, 41, 51)
DEPTH = (11, 10, 10, 10, 10, 11)
SIDE = LANES // 2
STRIDE = 256

VM = pl.BlockSpec(memory_space=pltpu.VMEM)
SM = pl.BlockSpec(memory_space=pltpu.SMEM)
F32 = jnp.float32


def position(where_ref):
    code = where_ref[0]
    return code // (STRIDE * STRIDE), code // STRIDE % STRIDE, code % STRIDE


def lane_of(shape):
    return lax.broadcasted_iota(jnp.int32, shape, len(shape) - 1)


def pick(flag, yes, no):
    return jnp.where(jnp.full(yes.shape, flag, jnp.int32) == 1, yes, no)


def neighbours(count, place, one, two):
    if count == 2:
        two = jnp.zeros_like(one)
    else:
        ends = jnp.full(two.shape, place, jnp.int32)
        two = jnp.where((ends == 0) | (ends == count - 1), 0.0, two)
    return pick(place % 2, one, two), pick(place % 2, two, one)


def turn(values, shift, axis):
    return pltpu.roll(values, shift % values.shape[axis], axis)


def parts_of(values):
    high = values.astype(jnp.bfloat16)
    return high, (values - high.astype(F32)).astype(jnp.bfloat16)


def times_table(values, table):
    table = table.astype(jnp.bfloat16)
    total = None
    for part in reversed(parts_of(values)):
        term = jnp.dot(part, table, preferred_element_type=F32)
        total = term if total is None else total + term
    return total


def table_times(table, values):
    table = table.astype(jnp.bfloat16)
    total = None
    for part in reversed(parts_of(values)):
        term = jnp.dot(table, part, preferred_element_type=F32)
        total = term if total is None else total + term
    return total


def iota2(shape, axis):
    return lax.broadcasted_iota(jnp.int32, shape, axis)


def pair_table(rows, cols, odd):
    row = iota2((rows, cols), 0)
    col = iota2((rows, cols), 1)
    hit = (row == 2 * col + 1) if odd else (row // 2 == col)
    return hit.astype(F32)


def below_x(values):
    if values.shape[0] == 1:
        return jnp.zeros_like(values)
    return jnp.concatenate([jnp.zeros_like(values[:1]), values[:-1]], axis=0)


def above_x(values):
    if values.shape[0] == 1:
        return jnp.zeros_like(values)
    return jnp.concatenate([values[1:], jnp.zeros_like(values[:1])], axis=0)


def pull(values, faces, step=1):
    bx, by, bz = faces
    total = bx * above_x(values) + below_x(bx * values)
    total = total + (by * turn(values, -step, 1) + turn(by * values, step, 1))
    return total + (bz * turn(values, -step, 2) + turn(bz * values, step, 2))


def diagonal(mass, faces, coupled, step=1):
    bx, by, bz = faces
    _, cy, cz = coupled
    return mass + bx + below_x(bx) + by + turn(cy, step, 1) + bz + turn(cz, step, 2)


def relaxer(mass, diag):
    inside = mass > 0.0
    return jnp.where(inside, RELAX / jnp.where(inside, diag, 1.0), 0.0)


def sweep(values, rhs, weight, faces, step=1):
    return KEEP * values + weight * (rhs + pull(values, faces, step))


def faces_x(values, odd, n_x, width):
    head, tail = values[:, :width], values[:, values.shape[1] - width:]
    return [pick(odd, head, tail), pick(odd, tail, head)][:n_x]


def faces_y(values, odd, width):
    head, tail = values[:, :width], values[:, values.shape[1] - width:]
    return pick(odd, head, tail), pick(odd, tail, head)


def corner_sends(below, above, odd):
    packs = []
    for rows, sign in ((slice(0, 8), 1), (slice(below.shape[1] - 8, below.shape[1]), -1)):
        low = [below[3 - i, rows] for i in range(3)]
        high = [above[i, rows] for i in range(3)]
        row = iota2(low[0].shape, 0)
        row = row if sign == 1 else 7 - row
        pack = (
            jnp.where(row < 3, low[0], turn(low[2], 3 * sign, 0)),
            jnp.where(row < 2, low[1], turn(high[1], 2 * sign, 0)),
            jnp.where(row < 3, high[0], turn(high[2], 3 * sign, 0)),
        )
        packs.append([p[:4] if sign == 1 else p[4:] for p in pack])
    return [(pick(odd, h, t), pick(odd, t, h)) for h, t in zip(*packs)]


def inner_rows(tile, by):
    upper = iota2(tile.shape, 0) < 4
    return jnp.where(upper, turn(tile, -by, 0), turn(tile, by, 0))


def corner_tiles(first, second, third):
    zero = jnp.zeros_like(first)
    low = (zero, inner_rows(first, 3), second, first)
    return low, (third, inner_rows(second, 2), inner_rows(third, 3), zero)


def diagonal_sends(values, n_x, odd_x, odd_y):
    corners = []
    for slabs in ([values[i] for i in range(4)], [values[values.shape[0] - 1 - i] for i in range(4)]):
        for sign in (1, -1):
            row = iota2(slabs[0].shape, 0)
            row = row if sign == 1 else 7 - row
            tiles = (slabs[0], jnp.where(row < 3, slabs[1], turn(slabs[3], 3 * sign, 0)), slabs[2])
            corners.append([t[:4] if sign == 1 else t[4:] for t in tiles])
    sends = []
    for k_x in range(n_x):
        for k_y in range(2):
            head_x = odd_x if k_x == 0 else 1 - odd_x
            head_y = odd_y if k_y == 0 else 1 - odd_y
            sends.append(
                [
                    pick(head_x, pick(head_y, hh, ht), pick(head_y, th, tt))
                    for hh, ht, th, tt in zip(*corners)
                ]
            )
    return sends


def diagonal_tiles(first, second, third):
    return [first, second, third, inner_rows(second, 3)]


def faces_kernel(counts, where_ref, *refs):
    ins, refs = refs[:6], refs[6:]
    n_x = 1 if counts[0] == 2 else 2
    sends_x, (two_y, one_y, first, second) = refs[:n_x], refs[n_x:]
    odd_x, odd_y, odd = (place % 2 for place in position(where_ref))
    sx, sy, sz = ins[0].shape
    half = sx // 2
    lane = lane_of((half, sy, LANES))
    head = jnp.zeros((half, sy, LANES), F32)
    tail = head
    for a, ref in enumerate(ins):
        for send, face in zip(sends_x, faces_x(ref[...][None], odd_x, n_x, HALO)):
            send[a] = face[0]
        one_y[a], two_y[a] = faces_y(ref[...], odd_y, HALO)
        for g in range(2):
            values = ref[g * half:(g + 1) * half]
            at = SIDE * g + PLACE[a]
            mask = (lane >= at) & (lane < at + DEPTH[a])
            head = jnp.where(mask, turn(values, at, 2), head)
            tail = jnp.where(mask, turn(values, at + DEPTH[a], 2), tail)
    first[...] = pick(odd, head, tail)
    second[...] = pick(odd, tail, head)


def halo_z_kernel(counts, where_ref, one_ref, two_ref, zpack, *sends):
    at_x, _, at_z = position(where_ref)
    half = one_ref.shape[0]
    below, above = neighbours(counts[2], at_z, one_ref[...], two_ref[...])
    lane = lane_of(below.shape)
    zpack[:half] = jnp.where(lane < SIDE, above, turn(below, SIDE, 2))
    zpack[half:] = jnp.where(lane < SIDE, turn(above, SIDE, 2), below)
    for send, face in zip(sends, faces_x(zpack[...][None], at_x % 2, len(sends), HALO)):
        send[...] = face[0]


def corners_kernel(counts, where_ref, zpack, *refs):
    n_x = 1 if counts[0] == 2 else 2
    main_x, halos_x, (two_y, one_y) = refs[:n_x], refs[n_x:2 * n_x], refs[2 * n_x + 1:]
    at_x, at_y, _ = position(where_ref)
    for a in range(7):
        if a < 6:
            below, above = neighbours(counts[0], at_x, main_x[0][a], main_x[-1][a])
        else:
            below, above = neighbours(counts[0], at_x, halos_x[0][...], halos_x[-1][...])
        for n, pair in enumerate(corner_sends(below, above, at_y % 2)):
            one_y[3 * a + n], two_y[3 * a + n] = pair
    one_y[21:], two_y[21:] = faces_y(zpack[...], at_y % 2, HALO)


def each(first, last, step, body):
    rounds = (last - first) // step

    def go(i, carry):
        for j in range(step):
            body(first + i * step + j)
        return carry

    if rounds:
        lax.fori_loop(0, rounds, go, 0)
    for x in range(first + rounds * step, last):
        body(x)


def ring_up(main, halo, lane):
    main_up, halo_up = turn(main, -1, 1), turn(halo, -1, 1)
    last = lane == LANES - 1
    return jnp.where(last, halo_up, main_up), jnp.where(last, main_up, halo_up)


def ring_down(main, halo, lane):
    main_down, halo_down = turn(main, 1, 1), turn(halo, 1, 1)
    zero = lane == 0
    return jnp.where(zero, halo_down, main_down), jnp.where(zero, main_down, halo_down)


def pull_slab(field, bx, by, bz, x, lane):
    centre = [half[x] for half in field]
    out = []
    for k in range(2):
        c, face = centre[k], by[k][x]
        t = bx[k][x] * field[k][x + 1] + bx[k][x - 1] * field[k][x - 1]
        out.append(t + (face * turn(c, -1, 0) + turn(face * c, 1, 0)))
    faces = [half[x] for half in bz]
    ups = ring_up(centre[0], centre[1], lane)
    downs = ring_down(faces[0] * centre[0], faces[1] * centre[1], lane)
    return centre, [out[k] + (faces[k] * ups[k] + downs[k]) for k in range(2)]


def unpacked(packed, a, lane):
    at, depth = PLACE[a], DEPTH[a]
    axis = packed.ndim - 1
    right, left = turn(packed, -at, axis), turn(packed, SIDE - depth - at, axis)
    return jnp.where(lane < depth, right, jnp.where(lane >= LANES - depth, left, 0.0))


def rows_of(source, x, count, firsts, seconds):
    total = None
    for p in firsts:
        for q in seconds:
            term = source[x + p, pl.ds(q, count, stride=2), :]
            total = term if total is None else total + term
    return total


BOTH, ODD = (0, 1), (1,)


def to_level1(sums, first, count, table, factor):
    _, x1, y1, _ = sums.shape
    flat = sums[first:first + count].reshape(count * x1 * y1, 2 * LANES)
    return factor * times_table(flat, table).reshape(count, x1, y1, LANES)


def coefficient_kernel(counts, where_ref, *refs):
    ins, refs = refs[:7], refs[7:]
    n_x = 1 if counts[0] == 2 else 2
    main_x, refs = refs[:n_x], refs[n_x:]
    arrays, (coarse2, coeffs1, sums, pairing) = refs[:12], refs[12:]
    sx, sy, sz = ins[0].shape
    at_x = position(where_ref)[0]
    x1, y1 = sx // 2, sy // 2
    lane = lane_of((sx, sy, LANES))
    lanes = [slice(k * LANES, (k + 1) * LANES) for k in range(2)]
    mine = slice(HALO, HALO + sx)
    for a in range(6):
        to = arrays[2 * a]
        below, above = neighbours(counts[0], at_x, main_x[0][a], main_x[-1][a])
        to[:HALO, :sy] = below
        to[mine, :sy] = ins[a][...]
        to[HALO + sx:, :sy] = above
        arrays[2 * a + 1][mine, :sy] = unpacked(ins[6][...], a, lane)
    for n, (firsts, seconds) in enumerate(((BOTH, BOTH), (ODD, BOTH), (BOTH, ODD), (BOTH, BOTH))):
        for k in range(2):
            for i in range(x1):
                source = arrays[2 * (n + 2) + k]
                sums[n, i, :, lanes[k]] = rows_of(source, HALO + 2 * i, y1, firsts, seconds)
    pairs = pair_table(2 * LANES, LANES, False)
    odds = pair_table(2 * LANES, LANES, True)
    paired = to_level1(sums, 0, 3, pairs, 0.0625)
    mass1 = (2.0 * WEIGHT) * paired[0]
    faces1 = (paired[1], paired[2], to_level1(sums, 3, 1, odds, 0.0625)[0])
    diag1 = mass1 + faces1[0] + below_x(faces1[0])
    diag1 = diag1 + faces1[1] + faces1[2] + turn(faces1[2], 1, 2)
    for n, values in enumerate((mass1, diag1) + faces1):
        coeffs1[n] = values
    parts = (
        (mass1, False, False, False, 0.125),
        (faces1[0], True, False, False, 0.0625),
        (faces1[1], False, True, False, 0.0625),
        (faces1[2], False, False, True, 0.0625),
    )
    for n, (values, *odd_axes, factor) in enumerate(parts):
        pairing[n] = values
        coarse2[n] = level2_rows(pairing.at[n], odd_axes, factor, x1 // 2, y1 // 2, sz // 4)


def down_kernel(counts, where_ref, zpack, *refs):
    refs = refs[12:]
    n_x = 1 if counts[0] == 2 else 2
    halos_x = refs[:n_x]
    main_two, main_one, rest_two, rest_one, coeffs1 = refs[n_x:5 + n_x]
    flat, refs = refs[5 + n_x:17 + n_x], refs[17 + n_x:]
    arrays = tuple(zip(flat[::2], flat[1::2]))
    own1, refs = refs[0], refs[1:]
    sends, near_two, near_one, refs = refs[:n_x], refs[n_x], refs[n_x + 1], refs[n_x + 2:]
    sends_xy, refs = refs[:2 * n_x], refs[2 * n_x:]
    kept_m, kept_h, weight_m, weight_h = refs[:4]
    packs, half_m, half_h, diag_m, diag_h, sums, left = refs[4:]
    field, rhs, alpha, bx, by, bz = arrays
    sx, sy, sz = zpack.shape
    ex, ey = sx + 2 * HALO, sy + 2 * HALO
    at_x, at_y, _ = position(where_ref)

    rest = neighbours(counts[1], at_y, rest_one[...], rest_two[...])
    rest = jnp.concatenate(rest[::-1], axis=1)
    for a in range(7):
        if a < 6:
            to = arrays[a][0]
            rows = neighbours(counts[1], at_y, main_one[a], main_two[a])
            rows = jnp.concatenate(rows[::-1], axis=1)
        else:
            to = packs
            rows = rest[21:]
            below, above = neighbours(counts[0], at_x, halos_x[0][...], halos_x[-1][...])
            to[:HALO, :sy] = below
            to[HALO + sx:, :sy] = above
        to[HALO:HALO + sx, sy:] = rows
        low, high = corner_tiles(*(rest[3 * a + n] for n in range(3)))
        for n in range(HALO):
            to[n, sy:] = low[n]
            to[HALO + sx + n, sy:] = high[n]
    lane = lane_of((ey, LANES))
    lane_low = lane_of((2 * HALO, LANES))

    def unpack_rows(x):
        packed = packs[x, sy:]
        for a in range(6):
            arrays[a][1][x, sy:] = unpacked(packed, a, lane_low)

    def unpack(x):
        packed = packs[x]
        for a in range(6):
            arrays[a][1][x] = unpacked(packed, a, lane)

    each(0, HALO, HALO, unpack)
    each(HALO, HALO + sx, 8, unpack_rows)
    each(HALO + sx, ex, HALO, unpack)
    halfway, weight, kept = (half_m, half_h), (weight_m, weight_h), (kept_m, kept_h)
    diag = (diag_m, diag_h)

    def first_sweep(x):
        faces = [half[x] for half in bz]
        downs = ring_down(faces[0], faces[1], lane)
        centre, near = pull_slab(field, bx, by, bz, x, lane)
        for k in range(2):
            face = by[k][x]
            mass = WEIGHT * alpha[k][x]
            d = mass + bx[k][x] + bx[k][x - 1] + face + turn(face, 1, 0) + faces[k] + downs[k]
            w = relaxer(mass, d)
            diag[k][x] = d
            weight[k][x] = w
            halfway[k][x] = KEEP * centre[k] + w * (rhs[k][x] + near[k])

    each(1, ex - 1, 11, first_sweep)

    def second_sweep(x):
        centre, near = pull_slab(halfway, bx, by, bz, x, lane)
        for k in range(2):
            kept[k][x] = KEEP * centre[k] + weight[k][x] * (rhs[k][x] + near[k])

    each(2, ex - 2, 10, second_sweep)

    def residual(x):
        centre, near = pull_slab(kept, bx, by, bz, x, lane)
        for k in range(2):
            halfway[k][x] = rhs[k][x] - diag[k][x] * centre[k] + near[k]

    each(HALO, ex - HALO, 8, residual)

    x1, y1 = sx // 2, sy // 2
    for k in range(2):
        lanes = slice(k * LANES, (k + 1) * LANES)
        for i in range(x1):
            x = HALO + 2 * i
            sums[0, i, :, lanes] = rows_of(halfway[k], x, y1, BOTH, BOTH)
            left[...] = turn(by[k][x] + by[k][x + 1], 1, 0)
            sums[1, i, :, lanes] = left[pl.ds(0, y1, stride=2), :]
        sums[2, 0, :, lanes] = rows_of(bx[k], HALO - 1, y1, (0,), BOTH)
        sums[2, 1:, :, lanes] = jnp.zeros((x1 - 1, y1, LANES), F32)
    rhs1, low_y, low_x = to_level1(sums, 0, 3, pair_table(2 * LANES, LANES, False), 0.0625)
    weight1 = relaxer(coeffs1[0], coeffs1[1] + low_y + low_x)
    for n, values in enumerate((2.0 * rhs1, weight1, coeffs1[2], coeffs1[3], coeffs1[4])):
        own1[n] = values
        for send, face in zip(sends, faces_x(values[None], at_x % 2, n_x, NEAR)):
            send[n] = face[0]
        near_one[n], near_two[n] = faces_y(values, at_y % 2, NEAR)
        for send, tiles in zip(sends_xy, diagonal_sends(values, n_x, at_x % 2, at_y % 2)):
            for t in range(3):
                send[3 * n + t] = tiles[t]


def level2_rows(source, odd_axes, factor, x2, y2, z2):
    rows = []
    for i in range(x2):
        total = None
        for p in (1,) if odd_axes[0] else (0, 1):
            for q in (1,) if odd_axes[1] else (0, 1):
                term = source[2 * i + p, pl.ds(q, y2, stride=2), :]
                total = term if total is None else total + term
        rows.append(total)
    flat = jnp.concatenate(rows, axis=0)
    flat = factor * times_table(flat, pair_table(LANES, LANES, odd_axes[2]))
    lane = lane_of((y2, LANES))
    packed = jnp.zeros((y2, LANES), F32)
    for i in range(x2):
        mask = (lane >= i * z2) & (lane < (i + 1) * z2)
        packed = jnp.where(mask, turn(flat[i * y2:(i + 1) * y2], i * z2, 1), packed)
    return packed


def near_kernel(counts, devices, where_ref, ring, *refs):
    n_x = 1 if counts[0] == 2 else 2
    halos_x = refs[:n_x]
    main_two, main_one = refs[n_x:n_x + 2]
    diagonals, (coarse2, copies, level1, left) = refs[n_x + 2:3 * n_x + 2], refs[3 * n_x + 2:]
    n, bx1, by1, _ = ring.shape
    at_x, at_y, _ = position(where_ref)
    sides = [
        neighbours(counts[0], at_x, diagonals[k][...], diagonals[k - 2][...]) for k in range(2)
    ]
    rest = []
    for one, two in zip(*sides):
        rows = neighbours(counts[1], at_y, one, two)
        rest.append(jnp.concatenate(rows[::-1], axis=1))
    whole = []
    for a in range(n):
        below, above = neighbours(counts[0], at_x, halos_x[0][a], halos_x[-1][a])
        rows = neighbours(counts[1], at_y, main_one[a], main_two[a])
        rows = jnp.concatenate(rows[::-1], axis=1)
        low, high = (diagonal_tiles(*(side[3 * a + k] for k in range(3))) for side in rest)
        low = low[::-1]
        rows = jnp.concatenate(
            [tile[None] for tile in low] + [rows] + [tile[None] for tile in high], axis=0
        )
        block = jnp.concatenate([below, ring[a], above], axis=0)
        whole.append(jnp.concatenate([block, rows], axis=1))
    rhs1, weight1 = whole[:2]
    faces1 = tuple(whole[2:])
    field1 = weight1 * rhs1
    field1 = sweep(field1, rhs1, weight1, faces1)
    for a, values in enumerate([field1] + whole):
        level1[a] = values
    mine = slice(NEAR, NEAR + bx1)
    inner = weight1[mine]
    diag1 = RELAX / jnp.where(inner > 0.0, inner, 1.0)
    remain = rhs1[mine] - diag1 * field1[mine] + pull(field1, faces1)[mine]
    left[...] = remain
    packed = level2_rows(left, (False,) * 3, 0.125, bx1 // 2, by1 // 2, LANES // 4)
    blocks = LANES // (LANES // 4)
    shift = position(where_ref)[2] % blocks * (LANES // blocks)
    slots = [pltpu.roll(values, shift, 1) for values in [packed] + [coarse2[a] for a in range(4)]]
    for d in range(devices):
        for a in range(n):
            copies[d, a] = slots[a]


def inner_sweep(values, rhs, weight, faces, first):
    part = slice(first, rhs.shape[0] - first)
    below = slice(first - 1, rhs.shape[0] - first - 1)
    bx, by, bz = faces
    centre = values[1:-1]
    near = bx[part] * values[2:] + bx[below] * values[:-2]
    near = near + (by[part] * turn(centre, -1, 1) + turn(by[part] * centre, 1, 1))
    near = near + (bz[part] * turn(centre, -1, 2) + turn(bz[part] * centre, 1, 2))
    return KEEP * centre + weight[part] * (rhs[part] + near)


def halve(values, odd_axis, step):
    half = values.shape[0] // 2
    even = [values[2 * i:2 * i + 1] for i in range(half)]
    odd = [values[2 * i + 1:2 * i + 2] for i in range(half)]
    if odd_axis != 0:
        odd = [a + b for a, b in zip(even, odd)]
    values = jnp.concatenate(odd, axis=0)
    for axis in (1, 2):
        next_one = turn(values, -step, axis)
        values = next_one if odd_axis == axis else values + next_one
    return values


def double(values, step):
    values = values + turn(values, step, 1)
    values = values + turn(values, step, 2)
    return jnp.concatenate([values[i // 2:i // 2 + 1] for i in range(2 * values.shape[0])], axis=0)


def coarse_levels(mass, faces, y, z):
    levels = []
    for level in range(2, LEVELS):
        step = 2 ** (level - 2)
        bx, by, bz = faces
        row = lax.broadcasted_iota(jnp.int32, by.shape, 1)
        lane = lane_of(bz.shape)
        upper = (
            bx,
            jnp.where(row == (y - 1) * step, 0.0, by),
            jnp.where(lane == (z - 1) * step, 0.0, bz),
        )
        lower = (below_x(bx), turn(upper[1], step, 1), turn(upper[2], step, 2))
        mass = jnp.where((row % step == 0) & (lane % step == 0), mass, 0.0)
        diag = mass + bx + lower[0] + by + lower[1] + bz + lower[2]
        levels.append((diag, relaxer(mass, diag), upper, lower))
        if level < LEVELS - 1:
            faces = tuple(0.0625 * halve(face, axis, step) for axis, face in enumerate(faces))
            mass = 0.125 * halve(mass, -1, step)
            y, z = y // 2, z // 2
    return levels


def coupled(values, upper, lower, step):
    ups = (above_x(values), turn(values, -step, 1), turn(values, -step, 2))
    downs = (below_x(values), turn(values, step, 1), turn(values, step, 2))
    x, y, z = (u * up + l * down for u, up, l, down in zip(upper, ups, lower, downs))
    return (y + z) + x if values.shape[0] > 1 else y + z


def coarse_cycle(level, rhs, levels):
    step = 2 ** (level - 2)
    diag, weight, upper, lower = levels[level - 2]
    scaled = tuple(tuple(weight * b for b in faces) for faces in (upper, lower))
    source = weight * rhs

    def relax(field):
        return (KEEP * field + source) + coupled(field, *scaled, step)

    field = source
    if level == LEVELS - 1:
        for _ in range(BOTTOM - 1):
            field = relax(field)
        return field
    for _ in range(SWEEPS - 1):
        field = relax(field)
    remain = (rhs - diag * field) + coupled(field, upper, lower, step)
    correction = coarse_cycle(level + 1, 0.125 * halve(remain, -1, step), levels)
    field = field + double(correction, step)
    for _ in range(SWEEPS):
        field = relax(field)
    return field


def spread_out(counts, slots, whole):
    gx, gy, gz = counts
    y2 = slots.shape[-2]
    x2 = whole.shape[0] // gx
    z2 = LANES // x2
    lane = lane_of((y2, LANES))
    for i in range(gx):
        for j in range(gy):
            for x in range(x2):
                for part in range(whole.shape[2] // LANES):
                    total = None
                    for k in range(LANES // z2):
                        column = part * (LANES // z2) + k
                        if column < gz:
                            block = slots[(i * gy + j) * gz + column]
                            at = (x + k) * z2 % LANES
                            mask = (lane >= at) & (lane < at + z2)
                            if total is None:
                                total = jnp.where(mask, block, 0.0)
                            total = jnp.where(mask, block, total)
                    if x:
                        total = turn(total, -x * z2, 1)
                    lanes = slice(part * LANES, (part + 1) * LANES)
                    whole[i * x2 + x, j * y2:(j + 1) * y2, lanes] = total


def up_kernel(counts, where_ref, gathered, level1, *refs):
    kept, weight, rhs, bx, by, bz = zip(refs[0:12:2], refs[1:12:2])
    out, whole, second, spread_m, spread_h, field_m, field_h, half_m, half_h = refs[12:]
    gx, gy, gz = counts
    at_x, at_y, at_z = position(where_ref)
    sx, sy, sz = out.shape
    x1, y1 = sx // 2, sy // 2
    x2, y2, z2 = x1 // 2, y1 // 2, sz // 4
    columns = max(LANES, gz * z2)
    for a in range(5):
        spread_out(counts, gathered.at[:, a], whole.at[a])
    levels = coarse_levels(whole[1], (whole[2], whole[3], whole[4]), gy * y2, gz * z2)
    correction = coarse_cycle(2, whole[0], levels)

    wide = gx * x2
    half = NEAR // 2
    ex1, ey1 = x1 + 2 * NEAR, y1 + 2 * NEAR
    second[:half] = jnp.zeros((half,) + correction.shape[1:], F32)
    second[half:half + wide] = correction
    second[half + wide:] = jnp.zeros((half,) + correction.shape[1:], F32)
    window = second[pl.ds(at_x * x2, x2 + NEAR)]
    rows = correction.shape[1]
    row = iota2((ey1, rows), 0)
    col = iota2((ey1, rows), 1)
    place = jnp.where(row < y1 + NEAR, row, row - ey1)
    table_y = (col == at_y * y2 + lax.shift_right_arithmetic(place, 1)).astype(F32)
    row = iota2((columns, LANES), 0)
    col = iota2((columns, LANES), 1)
    place = jnp.where(col < LANES * 3 // 4, col, col - LANES)
    table_z = (row == at_z * z2 + lax.shift_right_arithmetic(place, 1)).astype(F32)
    flat = times_table(window.reshape((x2 + NEAR) * rows, columns), table_z)
    blocks = [table_times(table_y, flat[i * rows:(i + 1) * rows])[None] for i in range(x2 + NEAR)]
    lifted = jnp.concatenate([blocks[i // 2] for i in range(ex1)], axis=0)
    field1, rhs1, weight1 = level1[0], level1[1], level1[2]
    faces1 = (level1[3], level1[4], level1[5])
    field1 = (field1 + jnp.where(weight1 > 0.0, lifted, 0.0))[1:-1]
    for n in range(SWEEPS):
        field1 = inner_sweep(field1, rhs1, weight1, faces1, 2 + n)

    ex, ey = sx + 2 * HALO, sy + 2 * HALO
    near = field1.reshape((x1 + 2) * ey1, LANES)
    row = iota2((LANES, 2 * LANES), 0)
    col = iota2((LANES, 2 * LANES), 1)
    lifted = times_table(near, (col // 2 == row).astype(F32))
    quarter = NEAR // 2
    for k, spread in enumerate((spread_m, spread_h)):
        block = lifted[:, k * LANES:(k + 1) * LANES].reshape(x1 + 2, ey1, LANES)
        for i in range(x1 + 2):
            for q in range(2):
                spread[i, pl.ds(q, y1, stride=2), :] = block[i, :y1]
                spread[i, pl.ds(sy + q, quarter, stride=2), :] = block[i, y1:y1 + quarter]
                spread[i, pl.ds(sy + HALO + q, quarter, stride=2), :] = block[i, ey1 - quarter:]
    before, after = (field_m, field_h), (half_m, half_h)
    first = HALO - 2
    for x in range(first, ex - first):
        for k, spread in enumerate((spread_m, spread_h)):
            before[k][x] = kept[k][x] + spread[(x - first) // 2]

    lane = lane_of((ey, LANES))

    def sweep_out(x):
        centre, around = pull_slab(before, bx, by, bz, x, lane)
        for k in range(2):
            after[k][x] = KEEP * centre[k] + weight[k][x] * (rhs[k][x] + around[k])

    each(first + 1, ex - first - 1, 9, sweep_out)

    def sweep_own(x):
        centre, around = pull_slab(after, bx, by, bz, x, lane)
        value = KEEP * centre[0] + weight[0][x] * (rhs[0][x] + around[0])
        out[x - HALO] = value[:sy]

    each(HALO, ex - HALO, 8, sweep_own)


def run(kernel, outs, where, arrays, scratch=(), grant=16, micros=1, aliases={}):
    return pl.pallas_call(
        kernel,
        out_shape=tuple(jax.ShapeDtypeStruct(shape, F32) for shape in outs),
        in_specs=[SM] * len(where) + [VM] * len(arrays),
        out_specs=tuple(VM for _ in outs),
        input_output_aliases=aliases,
        scratch_shapes=[pltpu.VMEM(shape, F32) for shape in scratch],
        compiler_params=pltpu.CompilerParams(vmem_limit_bytes=grant * 1024 * 1024),
        cost_estimate=pl.CostEstimate(
            flops=0, bytes_accessed=int(micros * 3.6e6), transcendentals=0
        ),
    )(*where, *arrays)


def partners(count, k):
    partner = list(range(count))
    for low in range(k, count - 1, 2):
        partner[low], partner[low + 1] = low + 1, low
    return partner


def swaps(axis, sends, other=None):
    count = lax.axis_size(axis)
    got = []
    for k, block in enumerate(sends):
        partner = partners(count, k)
        if k == 1 and other is None:
            partner[0], partner[-1] = count - 1, 0
        if k == 0 or other is None:
            got.append(lax.ppermute(block, axis, list(enumerate(partner))))
            continue
        rows = lax.axis_size(other)
        pairs = []
        for row in range(rows):
            for i in range(count):
                ends = [(row, i), (min(row ^ 1, rows - 1) if partner[i] == i else row, partner[i])]
                if axis < other:
                    pairs.append(tuple(at * rows + line for line, at in ends))
                else:
                    pairs.append(tuple(line * count + at for line, at in ends))
        got.append(lax.ppermute(block, tuple(sorted((axis, other))), pairs))
    return got


def diagonal_swaps(sends):
    count_x, count_y = lax.axis_size("gx"), lax.axis_size("gy")
    got = []
    for n, block in enumerate(sends):
        xs, ys = partners(count_x, n // 2), partners(count_y, n % 2)
        pairs = [
            (x * count_y + y, xs[x] * count_y + ys[y])
            for x in range(count_x)
            for y in range(count_y)
        ]
        got.append(lax.ppermute(block, ("gx", "gy"), pairs))
    return got


def local(initial, right_side, alpha, beta_x, beta_y, beta_z):
    axes = ("gx", "gy", "gz")
    counts = tuple(lax.axis_size(axis) for axis in axes)
    devices = counts[0] * counts[1] * counts[2]
    where = (lax.axis_index("gx") * STRIDE + lax.axis_index("gy")) * STRIDE + lax.axis_index("gz")
    where = (where.astype(jnp.int32).reshape(1),)
    ins = (initial, right_side, alpha, beta_x, beta_y, beta_z)
    sx, sy, sz = initial.shape
    n_x = 1 if counts[0] == 2 else 2
    ex, ey = sx + 2 * HALO, sy + 2 * HALO
    fine = (ex, ey, LANES)

    *sends_x, two_y, one_y, first, second = run(
        functools.partial(faces_kernel, counts),
        [(6, HALO, sy, LANES)] * n_x
        + [(6, sx, HALO, LANES)] * 2
        + [(sx // 2, sy, LANES)] * 2,
        where,
        ins,
        grant=60,
    )
    main_x = tuple(swaps("gx", sends_x, "gy"))
    main_y = tuple(swaps("gy", (one_y, two_y))[::-1])
    got = swaps("gz", (first, second), "gy")
    zpack, *sends = run(
        functools.partial(halo_z_kernel, counts),
        [(sx, sy, LANES)] + [(HALO, sy, LANES)] * n_x,
        where,
        tuple(got),
    )
    halos_x = tuple(swaps("gx", sends, "gy"))
    x1, y1 = sx // 2, sy // 2
    *laid, coarse2, coeffs1 = run(
        functools.partial(coefficient_kernel, counts),
        [fine] * 12 + [(4, y1 // 2, LANES), (5, x1, y1, LANES)],
        where,
        ins + (zpack,) + main_x,
        [(4, x1, y1, 2 * LANES), (4, x1, y1, LANES)],
        micros=2,
    )
    two_y, one_y = run(
        functools.partial(corners_kernel, counts),
        [(21 + sx, HALO, LANES)] * 2,
        where,
        (zpack,) + main_x + halos_x + (coarse2,),
    )
    rest_y = tuple(swaps("gy", (one_y, two_y), "gz")[::-1])
    outs = run(
        functools.partial(down_kernel, counts),
        [fine] * 12
        + [(5, x1, y1, LANES)]
        + [(5, NEAR, y1, LANES)] * n_x
        + [(5, x1, NEAR, LANES)] * 2
        + [(15, NEAR, LANES)] * (2 * n_x)
        + [fine] * 4,
        where,
        (zpack,) + tuple(laid) + halos_x + main_y + rest_y + (coeffs1,),
        [fine] * 5 + [(3, x1, y1, 2 * LANES), (ey, LANES)],
        24,
        micros=4,
        aliases={n + 2: n for n in range(12)},
    )
    laid, own1, outs = outs[:12], outs[12], outs[13:]
    sends_x, (two_y, one_y), outs = outs[:n_x], outs[n_x:n_x + 2], outs[n_x + 2:]
    sends_xy, fine_arrays = outs[:2 * n_x], outs[2 * n_x:]
    fine_arrays = tuple(fine_arrays) + tuple(laid[2:4]) + tuple(laid[6:])

    near_x = tuple(swaps("gx", sends_x, "gy"))
    near_y = tuple(swaps("gy", (one_y, two_y), "gz")[::-1])
    near_xy = tuple(diagonal_swaps(sends_xy))
    copies, level1 = run(
        functools.partial(near_kernel, counts, devices),
        [(devices, 5, y1 // 2, LANES), (6, x1 + 2 * NEAR, y1 + 2 * NEAR, LANES)],
        where,
        (own1,) + near_x + near_y + near_xy + (coarse2,),
        [(x1, y1 + 2 * NEAR, LANES)],
    )

    gathered = lax.all_to_all(copies, axes, 0, 0, tiled=True)
    wide, rows = counts[0] * x1 // 2, counts[1] * y1 // 2
    columns = max(LANES, counts[2] * sz // 4)
    (result,) = run(
        functools.partial(up_kernel, counts),
        [(sx, sy, sz)],
        where,
        (gathered, level1) + tuple(fine_arrays),
        [(5, wide, rows, columns), (wide + NEAR, rows, columns)]
        + [(x1 + 2, ey, LANES)] * 2
        + [fine] * 4,
        24,
        micros=4,
    )
    return result


def solution(mesh):
    spec = P("gx", "gy", "gz")
    return jax.shard_map(
        local, mesh=mesh, in_specs=(spec,) * 6, out_specs=spec, check_vma=False
    )
```

```python
import functools

import jax
import jax.numpy as jnp
from jax import lax
from jax.experimental import pallas as pl
from jax.experimental.pallas import tpu as pltpu
from jax.sharding import PartitionSpec as P

LEVELS = 6
SWEEPS = 2
BOTTOM = 8
WEIGHT = 0.25 ** (LEVELS - 1)
RELAX = 2.0 / 3.0
KEEP = 1.0 / 3.0

HALO = 4
NEAR = 4
LANES = 128
PLACE = (0, 11, 21, 31, 41, 51)
DEPTH = (11, 10, 10, 10, 10, 11)
SIDE = LANES // 2
STRIDE = 256

VM = pl.BlockSpec(memory_space=pltpu.VMEM)
SM = pl.BlockSpec(memory_space=pltpu.SMEM)
F32 = jnp.float32


def position(where_ref):
    code = where_ref[0]
    return code // (STRIDE * STRIDE), code // STRIDE % STRIDE, code % STRIDE


def lane_of(shape):
    return lax.broadcasted_iota(jnp.int32, shape, len(shape) - 1)


def pick(flag, yes, no):
    return jnp.where(jnp.full(yes.shape, flag, jnp.int32) == 1, yes, no)


def neighbours(count, place, one, two):
    if count == 2:
        two = jnp.zeros_like(one)
    else:
        ends = jnp.full(two.shape, place, jnp.int32)
        two = jnp.where((ends == 0) | (ends == count - 1), 0.0, two)
    return pick(place % 2, one, two), pick(place % 2, two, one)


def turn(values, shift, axis):
    return pltpu.roll(values, shift % values.shape[axis], axis)


def parts_of(values):
    high = values.astype(jnp.bfloat16)
    return high, (values - high.astype(F32)).astype(jnp.bfloat16)


def times_table(values, table):
    table = table.astype(jnp.bfloat16)
    total = None
    for part in reversed(parts_of(values)):
        term = jnp.dot(part, table, preferred_element_type=F32)
        total = term if total is None else total + term
    return total


def table_times(table, values):
    table = table.astype(jnp.bfloat16)
    total = None
    for part in reversed(parts_of(values)):
        term = jnp.dot(table, part, preferred_element_type=F32)
        total = term if total is None else total + term
    return total


def iota2(shape, axis):
    return lax.broadcasted_iota(jnp.int32, shape, axis)


def pair_table(rows, cols, odd):
    row = iota2((rows, cols), 0)
    col = iota2((rows, cols), 1)
    hit = (row == 2 * col + 1) if odd else (row // 2 == col)
    return hit.astype(F32)


def below_x(values):
    if values.shape[0] == 1:
        return jnp.zeros_like(values)
    return jnp.concatenate([jnp.zeros_like(values[:1]), values[:-1]], axis=0)


def above_x(values):
    if values.shape[0] == 1:
        return jnp.zeros_like(values)
    return jnp.concatenate([values[1:], jnp.zeros_like(values[:1])], axis=0)


def pull(values, faces, step=1):
    bx, by, bz = faces
    total = bx * above_x(values) + below_x(bx * values)
    total = total + (by * turn(values, -step, 1) + turn(by * values, step, 1))
    return total + (bz * turn(values, -step, 2) + turn(bz * values, step, 2))


def diagonal(mass, faces, coupled, step=1):
    bx, by, bz = faces
    _, cy, cz = coupled
    return mass + bx + below_x(bx) + by + turn(cy, step, 1) + bz + turn(cz, step, 2)


def relaxer(mass, diag):
    inside = mass > 0.0
    return jnp.where(inside, RELAX / jnp.where(inside, diag, 1.0), 0.0)


def sweep(values, rhs, weight, faces, step=1):
    return KEEP * values + weight * (rhs + pull(values, faces, step))


def faces_x(values, odd, n_x, width):
    head, tail = values[:, :width], values[:, values.shape[1] - width:]
    return [pick(odd, head, tail), pick(odd, tail, head)][:n_x]


def faces_y(values, odd, width):
    head, tail = values[:, :width], values[:, values.shape[1] - width:]
    return pick(odd, head, tail), pick(odd, tail, head)


def corner_sends(below, above, odd):
    packs = []
    for rows, sign in ((slice(0, 8), 1), (slice(below.shape[1] - 8, below.shape[1]), -1)):
        low = [below[3 - i, rows] for i in range(3)]
        high = [above[i, rows] for i in range(3)]
        row = iota2(low[0].shape, 0)
        row = row if sign == 1 else 7 - row
        pack = (
            jnp.where(row < 3, low[0], turn(low[2], 3 * sign, 0)),
            jnp.where(row < 2, low[1], turn(high[1], 2 * sign, 0)),
            jnp.where(row < 3, high[0], turn(high[2], 3 * sign, 0)),
        )
        packs.append([p[:4] if sign == 1 else p[4:] for p in pack])
    return [(pick(odd, h, t), pick(odd, t, h)) for h, t in zip(*packs)]


def inner_rows(tile, by):
    upper = iota2(tile.shape, 0) < 4
    return jnp.where(upper, turn(tile, -by, 0), turn(tile, by, 0))


def corner_tiles(first, second, third):
    zero = jnp.zeros_like(first)
    low = (zero, inner_rows(first, 3), second, first)
    return low, (third, inner_rows(second, 2), inner_rows(third, 3), zero)


def diagonal_sends(values, n_x, odd_x, odd_y):
    corners = []
    for slabs in ([values[i] for i in range(4)], [values[values.shape[0] - 1 - i] for i in range(4)]):
        for sign in (1, -1):
            row = iota2(slabs[0].shape, 0)
            row = row if sign == 1 else 7 - row
            tiles = (slabs[0], jnp.where(row < 3, slabs[1], turn(slabs[3], 3 * sign, 0)), slabs[2])
            corners.append([t[:4] if sign == 1 else t[4:] for t in tiles])
    sends = []
    for k_x in range(n_x):
        for k_y in range(2):
            head_x = odd_x if k_x == 0 else 1 - odd_x
            head_y = odd_y if k_y == 0 else 1 - odd_y
            sends.append(
                [
                    pick(head_x, pick(head_y, hh, ht), pick(head_y, th, tt))
                    for hh, ht, th, tt in zip(*corners)
                ]
            )
    return sends


def diagonal_tiles(first, second, third):
    return [first, second, third, inner_rows(second, 3)]


def faces_kernel(counts, where_ref, *refs):
    ins, refs = refs[:6], refs[6:]
    n_x = 1 if counts[0] == 2 else 2
    sends_x, (two_y, one_y, first, second) = refs[:n_x], refs[n_x:]
    odd_x, odd_y, odd = (place % 2 for place in position(where_ref))
    sx, sy, sz = ins[0].shape
    half = sx // 2
    lane = lane_of((half, sy, LANES))
    head = jnp.zeros((half, sy, LANES), F32)
    tail = head
    for a, ref in enumerate(ins):
        for send, face in zip(sends_x, faces_x(ref[...][None], odd_x, n_x, HALO)):
            send[a] = face[0]
        one_y[a], two_y[a] = faces_y(ref[...], odd_y, HALO)
        for g in range(2):
            values = ref[g * half:(g + 1) * half]
            at = SIDE * g + PLACE[a]
            mask = (lane >= at) & (lane < at + DEPTH[a])
            head = jnp.where(mask, turn(values, at, 2), head)
            tail = jnp.where(mask, turn(values, at + DEPTH[a], 2), tail)
    first[...] = pick(odd, head, tail)
    second[...] = pick(odd, tail, head)


def halo_z_kernel(counts, where_ref, one_ref, two_ref, zpack, *sends):
    at_x, _, at_z = position(where_ref)
    half = one_ref.shape[0]
    below, above = neighbours(counts[2], at_z, one_ref[...], two_ref[...])
    lane = lane_of(below.shape)
    zpack[:half] = jnp.where(lane < SIDE, above, turn(below, SIDE, 2))
    zpack[half:] = jnp.where(lane < SIDE, turn(above, SIDE, 2), below)
    for send, face in zip(sends, faces_x(zpack[...][None], at_x % 2, len(sends), HALO)):
        send[...] = face[0]


def corners_kernel(counts, where_ref, zpack, *refs):
    n_x = 1 if counts[0] == 2 else 2
    main_x, halos_x, (two_y, one_y) = refs[:n_x], refs[n_x:2 * n_x], refs[2 * n_x + 1:]
    at_x, at_y, _ = position(where_ref)
    for a in range(7):
        if a < 6:
            below, above = neighbours(counts[0], at_x, main_x[0][a], main_x[-1][a])
        else:
            below, above = neighbours(counts[0], at_x, halos_x[0][...], halos_x[-1][...])
        for n, pair in enumerate(corner_sends(below, above, at_y % 2)):
            one_y[3 * a + n], two_y[3 * a + n] = pair
    one_y[21:], two_y[21:] = faces_y(zpack[...], at_y % 2, HALO)


def each(first, last, body):
    for x in range(first, last):
        body(x)


def ring_up(main, halo, lane):
    main_up, halo_up = turn(main, -1, 1), turn(halo, -1, 1)
    last = lane == LANES - 1
    return jnp.where(last, halo_up, main_up), jnp.where(last, main_up, halo_up)


def ring_down(main, halo, lane):
    main_down, halo_down = turn(main, 1, 1), turn(halo, 1, 1)
    zero = lane == 0
    return jnp.where(zero, halo_down, main_down), jnp.where(zero, main_down, halo_down)


def pull_slab(field, bx, by, bz, x, lane):
    centre = [half[x] for half in field]
    out = []
    for k in range(2):
        c, face = centre[k], by[k][x]
        t = bx[k][x] * field[k][x + 1] + bx[k][x - 1] * field[k][x - 1]
        out.append(t + (face * turn(c, -1, 0) + turn(face * c, 1, 0)))
    faces = [half[x] for half in bz]
    ups = ring_up(centre[0], centre[1], lane)
    downs = ring_down(faces[0] * centre[0], faces[1] * centre[1], lane)
    return centre, [out[k] + (faces[k] * ups[k] + downs[k]) for k in range(2)]


def unpacked(packed, a, lane):
    at, depth = PLACE[a], DEPTH[a]
    axis = packed.ndim - 1
    right, left = turn(packed, -at, axis), turn(packed, SIDE - depth - at, axis)
    return jnp.where(lane < depth, right, jnp.where(lane >= LANES - depth, left, 0.0))


def rows_of(source, x, count, firsts, seconds):
    total = None
    for p in firsts:
        for q in seconds:
            term = source[x + p, pl.ds(q, count, stride=2), :]
            total = term if total is None else total + term
    return total


BOTH, ODD = (0, 1), (1,)


def to_level1(sums, first, count, table, factor):
    _, x1, y1, _ = sums.shape
    flat = sums[first:first + count].reshape(count * x1 * y1, 2 * LANES)
    return factor * times_table(flat, table).reshape(count, x1, y1, LANES)


def coefficient_kernel(counts, where_ref, *refs):
    ins, refs = refs[:7], refs[7:]
    n_x = 1 if counts[0] == 2 else 2
    main_x, refs = refs[:n_x], refs[n_x:]
    arrays, (coarse2, coeffs1, sums, pairing) = refs[:12], refs[12:]
    sx, sy, sz = ins[0].shape
    at_x = position(where_ref)[0]
    x1, y1 = sx // 2, sy // 2
    lane = lane_of((sx, sy, LANES))
    lanes = [slice(k * LANES, (k + 1) * LANES) for k in range(2)]
    mine = slice(HALO, HALO + sx)
    for a in range(6):
        to = arrays[2 * a]
        below, above = neighbours(counts[0], at_x, main_x[0][a], main_x[-1][a])
        to[:HALO, :sy] = below
        to[mine, :sy] = ins[a][...]
        to[HALO + sx:, :sy] = above
        arrays[2 * a + 1][mine, :sy] = unpacked(ins[6][...], a, lane)
    for n, (firsts, seconds) in enumerate(((BOTH, BOTH), (ODD, BOTH), (BOTH, ODD), (BOTH, BOTH))):
        for k in range(2):
            for i in range(x1):
                source = arrays[2 * (n + 2) + k]
                sums[n, i, :, lanes[k]] = rows_of(source, HALO + 2 * i, y1, firsts, seconds)
    pairs = pair_table(2 * LANES, LANES, False)
    odds = pair_table(2 * LANES, LANES, True)
    paired = to_level1(sums, 0, 3, pairs, 0.0625)
    mass1 = (2.0 * WEIGHT) * paired[0]
    faces1 = (paired[1], paired[2], to_level1(sums, 3, 1, odds, 0.0625)[0])
    diag1 = mass1 + faces1[0] + below_x(faces1[0])
    diag1 = diag1 + faces1[1] + faces1[2] + turn(faces1[2], 1, 2)
    for n, values in enumerate((mass1, diag1) + faces1):
        coeffs1[n] = values
    parts = (
        (mass1, False, False, False, 0.125),
        (faces1[0], True, False, False, 0.0625),
        (faces1[1], False, True, False, 0.0625),
        (faces1[2], False, False, True, 0.0625),
    )
    for n, (values, *odd_axes, factor) in enumerate(parts):
        pairing[n] = values
        coarse2[n] = level2_rows(pairing.at[n], odd_axes, factor, x1 // 2, y1 // 2, sz // 4)


def down_kernel(counts, where_ref, zpack, *refs):
    refs = refs[12:]
    n_x = 1 if counts[0] == 2 else 2
    halos_x = refs[:n_x]
    main_two, main_one, rest_two, rest_one, coeffs1 = refs[n_x:5 + n_x]
    flat, refs = refs[5 + n_x:17 + n_x], refs[17 + n_x:]
    arrays = tuple(zip(flat[::2], flat[1::2]))
    own1, refs = refs[0], refs[1:]
    sends, near_two, near_one, refs = refs[:n_x], refs[n_x], refs[n_x + 1], refs[n_x + 2:]
    sends_xy, refs = refs[:2 * n_x], refs[2 * n_x:]
    kept_m, kept_h, weight_m, weight_h = refs[:4]
    packs, half_m, half_h, diag_m, diag_h, sums, left = refs[4:]
    field, rhs, alpha, bx, by, bz = arrays
    sx, sy, sz = zpack.shape
    ex, ey = sx + 2 * HALO, sy + 2 * HALO
    at_x, at_y, _ = position(where_ref)

    rest = neighbours(counts[1], at_y, rest_one[...], rest_two[...])
    rest = jnp.concatenate(rest[::-1], axis=1)
    for a in range(7):
        if a < 6:
            to = arrays[a][0]
            rows = neighbours(counts[1], at_y, main_one[a], main_two[a])
            rows = jnp.concatenate(rows[::-1], axis=1)
        else:
            to = packs
            rows = rest[21:]
            below, above = neighbours(counts[0], at_x, halos_x[0][...], halos_x[-1][...])
            to[:HALO, :sy] = below
            to[HALO + sx:, :sy] = above
        to[HALO:HALO + sx, sy:] = rows
        low, high = corner_tiles(*(rest[3 * a + n] for n in range(3)))
        for n in range(HALO):
            to[n, sy:] = low[n]
            to[HALO + sx + n, sy:] = high[n]
    lane = lane_of((ey, LANES))
    lane_low = lane_of((2 * HALO, LANES))

    def unpack_rows(x):
        packed = packs[x, sy:]
        for a in range(6):
            arrays[a][1][x, sy:] = unpacked(packed, a, lane_low)

    def unpack(x):
        packed = packs[x]
        for a in range(6):
            arrays[a][1][x] = unpacked(packed, a, lane)

    each(0, HALO, unpack)
    each(HALO, HALO + sx, unpack_rows)
    each(HALO + sx, ex, unpack)
    halfway, weight, kept = (half_m, half_h), (weight_m, weight_h), (kept_m, kept_h)
    diag = (diag_m, diag_h)

    def first_sweep(x):
        faces = [half[x] for half in bz]
        downs = ring_down(faces[0], faces[1], lane)
        centre, near = pull_slab(field, bx, by, bz, x, lane)
        for k in range(2):
            face = by[k][x]
            mass = WEIGHT * alpha[k][x]
            d = mass + bx[k][x] + bx[k][x - 1] + face + turn(face, 1, 0) + faces[k] + downs[k]
            w = relaxer(mass, d)
            diag[k][x] = d
            weight[k][x] = w
            halfway[k][x] = KEEP * centre[k] + w * (rhs[k][x] + near[k])

    each(1, ex - 1, first_sweep)

    def second_sweep(x):
        centre, near = pull_slab(halfway, bx, by, bz, x, lane)
        for k in range(2):
            kept[k][x] = KEEP * centre[k] + weight[k][x] * (rhs[k][x] + near[k])

    each(2, ex - 2, second_sweep)

    def residual(x):
        centre, near = pull_slab(kept, bx, by, bz, x, lane)
        for k in range(2):
            halfway[k][x] = rhs[k][x] - diag[k][x] * centre[k] + near[k]

    each(HALO, ex - HALO, residual)

    x1, y1 = sx // 2, sy // 2
    for k in range(2):
        lanes = slice(k * LANES, (k + 1) * LANES)
        for i in range(x1):
            x = HALO + 2 * i
            sums[0, i, :, lanes] = rows_of(halfway[k], x, y1, BOTH, BOTH)
            left[...] = turn(by[k][x] + by[k][x + 1], 1, 0)
            sums[1, i, :, lanes] = left[pl.ds(0, y1, stride=2), :]
        sums[2, 0, :, lanes] = rows_of(bx[k], HALO - 1, y1, (0,), BOTH)
        sums[2, 1:, :, lanes] = jnp.zeros((x1 - 1, y1, LANES), F32)
    rhs1, low_y, low_x = to_level1(sums, 0, 3, pair_table(2 * LANES, LANES, False), 0.0625)
    weight1 = relaxer(coeffs1[0], coeffs1[1] + low_y + low_x)
    for n, values in enumerate((2.0 * rhs1, weight1, coeffs1[2], coeffs1[3], coeffs1[4])):
        own1[n] = values
        for send, face in zip(sends, faces_x(values[None], at_x % 2, n_x, NEAR)):
            send[n] = face[0]
        near_one[n], near_two[n] = faces_y(values, at_y % 2, NEAR)
        for send, tiles in zip(sends_xy, diagonal_sends(values, n_x, at_x % 2, at_y % 2)):
            for t in range(3):
                send[3 * n + t] = tiles[t]


def level2_rows(source, odd_axes, factor, x2, y2, z2):
    rows = []
    for i in range(x2):
        total = None
        for p in (1,) if odd_axes[0] else (0, 1):
            for q in (1,) if odd_axes[1] else (0, 1):
                term = source[2 * i + p, pl.ds(q, y2, stride=2), :]
                total = term if total is None else total + term
        rows.append(total)
    flat = jnp.concatenate(rows, axis=0)
    flat = factor * times_table(flat, pair_table(LANES, LANES, odd_axes[2]))
    lane = lane_of((y2, LANES))
    packed = jnp.zeros((y2, LANES), F32)
    for i in range(x2):
        mask = (lane >= i * z2) & (lane < (i + 1) * z2)
        packed = jnp.where(mask, turn(flat[i * y2:(i + 1) * y2], i * z2, 1), packed)
    return packed


def near_kernel(counts, devices, where_ref, ring, *refs):
    n_x = 1 if counts[0] == 2 else 2
    halos_x = refs[:n_x]
    main_two, main_one = refs[n_x:n_x + 2]
    diagonals, (coarse2, copies, level1, left) = refs[n_x + 2:3 * n_x + 2], refs[3 * n_x + 2:]
    n, bx1, by1, _ = ring.shape
    at_x, at_y, _ = position(where_ref)
    sides = [
        neighbours(counts[0], at_x, diagonals[k][...], diagonals[k - 2][...]) for k in range(2)
    ]
    rest = []
    for one, two in zip(*sides):
        rows = neighbours(counts[1], at_y, one, two)
        rest.append(jnp.concatenate(rows[::-1], axis=1))
    whole = []
    for a in range(n):
        below, above = neighbours(counts[0], at_x, halos_x[0][a], halos_x[-1][a])
        rows = neighbours(counts[1], at_y, main_one[a], main_two[a])
        rows = jnp.concatenate(rows[::-1], axis=1)
        low, high = (diagonal_tiles(*(side[3 * a + k] for k in range(3))) for side in rest)
        low = low[::-1]
        rows = jnp.concatenate(
            [tile[None] for tile in low] + [rows] + [tile[None] for tile in high], axis=0
        )
        block = jnp.concatenate([below, ring[a], above], axis=0)
        whole.append(jnp.concatenate([block, rows], axis=1))
    rhs1, weight1 = whole[:2]
    faces1 = tuple(whole[2:])
    field1 = weight1 * rhs1
    field1 = sweep(field1, rhs1, weight1, faces1)
    for a, values in enumerate([field1] + whole):
        level1[a] = values
    mine = slice(NEAR, NEAR + bx1)
    inner = weight1[mine]
    diag1 = RELAX / jnp.where(inner > 0.0, inner, 1.0)
    remain = rhs1[mine] - diag1 * field1[mine] + pull(field1, faces1)[mine]
    left[...] = remain
    packed = level2_rows(left, (False,) * 3, 0.125, bx1 // 2, by1 // 2, LANES // 4)
    blocks = LANES // (LANES // 4)
    shift = position(where_ref)[2] % blocks * (LANES // blocks)
    slots = [pltpu.roll(values, shift, 1) for values in [packed] + [coarse2[a] for a in range(4)]]
    for d in range(devices):
        for a in range(n):
            copies[d, a] = slots[a]


def inner_sweep(values, rhs, weight, faces, first):
    part = slice(first, rhs.shape[0] - first)
    below = slice(first - 1, rhs.shape[0] - first - 1)
    bx, by, bz = faces
    centre = values[1:-1]
    near = bx[part] * values[2:] + bx[below] * values[:-2]
    near = near + (by[part] * turn(centre, -1, 1) + turn(by[part] * centre, 1, 1))
    near = near + (bz[part] * turn(centre, -1, 2) + turn(bz[part] * centre, 1, 2))
    return KEEP * centre + weight[part] * (rhs[part] + near)


def halve(values, odd_axis, step):
    half = values.shape[0] // 2
    even = [values[2 * i:2 * i + 1] for i in range(half)]
    odd = [values[2 * i + 1:2 * i + 2] for i in range(half)]
    if odd_axis != 0:
        odd = [a + b for a, b in zip(even, odd)]
    values = jnp.concatenate(odd, axis=0)
    for axis in (1, 2):
        next_one = turn(values, -step, axis)
        values = next_one if odd_axis == axis else values + next_one
    return values


def double(values, step):
    values = values + turn(values, step, 1)
    values = values + turn(values, step, 2)
    return jnp.concatenate([values[i // 2:i // 2 + 1] for i in range(2 * values.shape[0])], axis=0)


def coarse_levels(mass, faces, y, z):
    levels = []
    for level in range(2, LEVELS):
        step = 2 ** (level - 2)
        bx, by, bz = faces
        row = lax.broadcasted_iota(jnp.int32, by.shape, 1)
        lane = lane_of(bz.shape)
        upper = (
            bx,
            jnp.where(row == (y - 1) * step, 0.0, by),
            jnp.where(lane == (z - 1) * step, 0.0, bz),
        )
        lower = (below_x(bx), turn(upper[1], step, 1), turn(upper[2], step, 2))
        mass = jnp.where((row % step == 0) & (lane % step == 0), mass, 0.0)
        diag = mass + bx + lower[0] + by + lower[1] + bz + lower[2]
        levels.append((diag, relaxer(mass, diag), upper, lower))
        if level < LEVELS - 1:
            faces = tuple(0.0625 * halve(face, axis, step) for axis, face in enumerate(faces))
            mass = 0.125 * halve(mass, -1, step)
            y, z = y // 2, z // 2
    return levels


def coupled(values, upper, lower, step):
    ups = (above_x(values), turn(values, -step, 1), turn(values, -step, 2))
    downs = (below_x(values), turn(values, step, 1), turn(values, step, 2))
    x, y, z = (u * up + l * down for u, up, l, down in zip(upper, ups, lower, downs))
    return (y + z) + x if values.shape[0] > 1 else y + z


def coarse_cycle(level, rhs, levels):
    step = 2 ** (level - 2)
    diag, weight, upper, lower = levels[level - 2]
    scaled = tuple(tuple(weight * b for b in faces) for faces in (upper, lower))
    source = weight * rhs

    def relax(field):
        return (KEEP * field + source) + coupled(field, *scaled, step)

    field = source
    if level == LEVELS - 1:
        for _ in range(BOTTOM - 1):
            field = relax(field)
        return field
    for _ in range(SWEEPS - 1):
        field = relax(field)
    remain = (rhs - diag * field) + coupled(field, upper, lower, step)
    correction = coarse_cycle(level + 1, 0.125 * halve(remain, -1, step), levels)
    field = field + double(correction, step)
    for _ in range(SWEEPS):
        field = relax(field)
    return field


def spread_out(counts, slots, whole):
    gx, gy, gz = counts
    y2 = slots.shape[-2]
    x2 = whole.shape[0] // gx
    z2 = LANES // x2
    lane = lane_of((y2, LANES))
    for i in range(gx):
        for j in range(gy):
            for x in range(x2):
                for part in range(whole.shape[2] // LANES):
                    total = None
                    for k in range(LANES // z2):
                        column = part * (LANES // z2) + k
                        if column < gz:
                            block = slots[(i * gy + j) * gz + column]
                            at = (x + k) * z2 % LANES
                            mask = (lane >= at) & (lane < at + z2)
                            if total is None:
                                total = jnp.where(mask, block, 0.0)
                            total = jnp.where(mask, block, total)
                    if x:
                        total = turn(total, -x * z2, 1)
                    lanes = slice(part * LANES, (part + 1) * LANES)
                    whole[i * x2 + x, j * y2:(j + 1) * y2, lanes] = total


def up_kernel(counts, where_ref, gathered, level1, *refs):
    kept, weight, rhs, bx, by, bz = zip(refs[0:12:2], refs[1:12:2])
    out, whole, second, spread_m, spread_h, field_m, field_h, half_m, half_h = refs[12:]
    gx, gy, gz = counts
    at_x, at_y, at_z = position(where_ref)
    sx, sy, sz = out.shape
    x1, y1 = sx // 2, sy // 2
    x2, y2, z2 = x1 // 2, y1 // 2, sz // 4
    columns = max(LANES, gz * z2)
    for a in range(5):
        spread_out(counts, gathered.at[:, a], whole.at[a])
    levels = coarse_levels(whole[1], (whole[2], whole[3], whole[4]), gy * y2, gz * z2)
    correction = coarse_cycle(2, whole[0], levels)

    wide = gx * x2
    half = NEAR // 2
    ex1, ey1 = x1 + 2 * NEAR, y1 + 2 * NEAR
    second[:half] = jnp.zeros((half,) + correction.shape[1:], F32)
    second[half:half + wide] = correction
    second[half + wide:] = jnp.zeros((half,) + correction.shape[1:], F32)
    window = second[pl.ds(at_x * x2, x2 + NEAR)]
    rows = correction.shape[1]
    row = iota2((ey1, rows), 0)
    col = iota2((ey1, rows), 1)
    place = jnp.where(row < y1 + NEAR, row, row - ey1)
    table_y = (col == at_y * y2 + lax.shift_right_arithmetic(place, 1)).astype(F32)
    row = iota2((columns, LANES), 0)
    col = iota2((columns, LANES), 1)
    place = jnp.where(col < LANES * 3 // 4, col, col - LANES)
    table_z = (row == at_z * z2 + lax.shift_right_arithmetic(place, 1)).astype(F32)
    flat = times_table(window.reshape((x2 + NEAR) * rows, columns), table_z)
    blocks = [table_times(table_y, flat[i * rows:(i + 1) * rows])[None] for i in range(x2 + NEAR)]
    lifted = jnp.concatenate([blocks[i // 2] for i in range(ex1)], axis=0)
    field1, rhs1, weight1 = level1[0], level1[1], level1[2]
    faces1 = (level1[3], level1[4], level1[5])
    field1 = (field1 + jnp.where(weight1 > 0.0, lifted, 0.0))[1:-1]
    for n in range(SWEEPS):
        field1 = inner_sweep(field1, rhs1, weight1, faces1, 2 + n)

    ex, ey = sx + 2 * HALO, sy + 2 * HALO
    near = field1.reshape((x1 + 2) * ey1, LANES)
    row = iota2((LANES, 2 * LANES), 0)
    col = iota2((LANES, 2 * LANES), 1)
    lifted = times_table(near, (col // 2 == row).astype(F32))
    quarter = NEAR // 2
    for k, spread in enumerate((spread_m, spread_h)):
        block = lifted[:, k * LANES:(k + 1) * LANES].reshape(x1 + 2, ey1, LANES)
        for i in range(x1 + 2):
            for q in range(2):
                spread[i, pl.ds(q, y1, stride=2), :] = block[i, :y1]
                spread[i, pl.ds(sy + q, quarter, stride=2), :] = block[i, y1:y1 + quarter]
                spread[i, pl.ds(sy + HALO + q, quarter, stride=2), :] = block[i, ey1 - quarter:]
    before, after = (field_m, field_h), (half_m, half_h)
    first = HALO - 2
    for x in range(first, ex - first):
        for k, spread in enumerate((spread_m, spread_h)):
            before[k][x] = kept[k][x] + spread[(x - first) // 2]

    lane = lane_of((ey, LANES))

    def sweep_out(x):
        centre, around = pull_slab(before, bx, by, bz, x, lane)
        for k in range(2):
            after[k][x] = KEEP * centre[k] + weight[k][x] * (rhs[k][x] + around[k])

    each(first + 1, ex - first - 1, sweep_out)

    def sweep_own(x):
        centre, around = pull_slab(after, bx, by, bz, x, lane)
        value = KEEP * centre[0] + weight[0][x] * (rhs[0][x] + around[0])
        out[x - HALO] = value[:sy]

    each(HALO, ex - HALO, sweep_own)


def run(kernel, outs, where, arrays, scratch=(), grant=16, micros=1, aliases={}):
    return pl.pallas_call(
        kernel,
        out_shape=tuple(jax.ShapeDtypeStruct(shape, F32) for shape in outs),
        in_specs=[SM] * len(where) + [VM] * len(arrays),
        out_specs=tuple(VM for _ in outs),
        input_output_aliases=aliases,
        scratch_shapes=[pltpu.VMEM(shape, F32) for shape in scratch],
        compiler_params=pltpu.CompilerParams(vmem_limit_bytes=grant * 1024 * 1024),
        cost_estimate=pl.CostEstimate(
            flops=0, bytes_accessed=int(micros * 3.6e6), transcendentals=0
        ),
    )(*where, *arrays)


def partners(count, k):
    partner = list(range(count))
    for low in range(k, count - 1, 2):
        partner[low], partner[low + 1] = low + 1, low
    return partner


def swaps(axis, sends, other=None):
    count = lax.axis_size(axis)
    got = []
    for k, block in enumerate(sends):
        partner = partners(count, k)
        if k == 1 and other is None:
            partner[0], partner[-1] = count - 1, 0
        if k == 0 or other is None:
            got.append(lax.ppermute(block, axis, list(enumerate(partner))))
            continue
        rows = lax.axis_size(other)
        pairs = []
        for row in range(rows):
            for i in range(count):
                ends = [(row, i), (min(row ^ 1, rows - 1) if partner[i] == i else row, partner[i])]
                if axis < other:
                    pairs.append(tuple(at * rows + line for line, at in ends))
                else:
                    pairs.append(tuple(line * count + at for line, at in ends))
        got.append(lax.ppermute(block, tuple(sorted((axis, other))), pairs))
    return got


def diagonal_swaps(sends):
    count_x, count_y = lax.axis_size("gx"), lax.axis_size("gy")
    got = []
    for n, block in enumerate(sends):
        xs, ys = partners(count_x, n // 2), partners(count_y, n % 2)
        pairs = [
            (x * count_y + y, xs[x] * count_y + ys[y])
            for x in range(count_x)
            for y in range(count_y)
        ]
        got.append(lax.ppermute(block, ("gx", "gy"), pairs))
    return got


def local(initial, right_side, alpha, beta_x, beta_y, beta_z):
    axes = ("gx", "gy", "gz")
    counts = tuple(lax.axis_size(axis) for axis in axes)
    devices = counts[0] * counts[1] * counts[2]
    where = (lax.axis_index("gx") * STRIDE + lax.axis_index("gy")) * STRIDE + lax.axis_index("gz")
    where = (where.astype(jnp.int32).reshape(1),)
    ins = (initial, right_side, alpha, beta_x, beta_y, beta_z)
    sx, sy, sz = initial.shape
    n_x = 1 if counts[0] == 2 else 2
    ex, ey = sx + 2 * HALO, sy + 2 * HALO
    fine = (ex, ey, LANES)

    *sends_x, two_y, one_y, first, second = run(
        functools.partial(faces_kernel, counts),
        [(6, HALO, sy, LANES)] * n_x
        + [(6, sx, HALO, LANES)] * 2
        + [(sx // 2, sy, LANES)] * 2,
        where,
        ins,
        grant=60,
    )
    main_x = tuple(swaps("gx", sends_x, "gy"))
    main_y = tuple(swaps("gy", (one_y, two_y))[::-1])
    got = swaps("gz", (first, second), "gy")
    zpack, *sends = run(
        functools.partial(halo_z_kernel, counts),
        [(sx, sy, LANES)] + [(HALO, sy, LANES)] * n_x,
        where,
        tuple(got),
    )
    halos_x = tuple(swaps("gx", sends, "gy"))
    x1, y1 = sx // 2, sy // 2
    *laid, coarse2, coeffs1 = run(
        functools.partial(coefficient_kernel, counts),
        [fine] * 12 + [(4, y1 // 2, LANES), (5, x1, y1, LANES)],
        where,
        ins + (zpack,) + main_x,
        [(4, x1, y1, 2 * LANES), (4, x1, y1, LANES)],
        micros=2,
    )
    two_y, one_y = run(
        functools.partial(corners_kernel, counts),
        [(21 + sx, HALO, LANES)] * 2,
        where,
        (zpack,) + main_x + halos_x + (coarse2,),
    )
    rest_y = tuple(swaps("gy", (one_y, two_y), "gz")[::-1])
    outs = run(
        functools.partial(down_kernel, counts),
        [fine] * 12
        + [(5, x1, y1, LANES)]
        + [(5, NEAR, y1, LANES)] * n_x
        + [(5, x1, NEAR, LANES)] * 2
        + [(15, NEAR, LANES)] * (2 * n_x)
        + [fine] * 4,
        where,
        (zpack,) + tuple(laid) + halos_x + main_y + rest_y + (coeffs1,),
        [fine] * 5 + [(3, x1, y1, 2 * LANES), (ey, LANES)],
        24,
        micros=4,
        aliases={n + 2: n for n in range(12)},
    )
    laid, own1, outs = outs[:12], outs[12], outs[13:]
    sends_x, (two_y, one_y), outs = outs[:n_x], outs[n_x:n_x + 2], outs[n_x + 2:]
    sends_xy, fine_arrays = outs[:2 * n_x], outs[2 * n_x:]
    fine_arrays = tuple(fine_arrays) + tuple(laid[2:4]) + tuple(laid[6:])

    near_x = tuple(swaps("gx", sends_x, "gy"))
    near_y = tuple(swaps("gy", (one_y, two_y), "gz")[::-1])
    near_xy = tuple(diagonal_swaps(sends_xy))
    copies, level1 = run(
        functools.partial(near_kernel, counts, devices),
        [(devices, 5, y1 // 2, LANES), (6, x1 + 2 * NEAR, y1 + 2 * NEAR, LANES)],
        where,
        (own1,) + near_x + near_y + near_xy + (coarse2,),
        [(x1, y1 + 2 * NEAR, LANES)],
    )

    gathered = lax.all_to_all(copies, axes, 0, 0, tiled=True)
    wide, rows = counts[0] * x1 // 2, counts[1] * y1 // 2
    columns = max(LANES, counts[2] * sz // 4)
    (result,) = run(
        functools.partial(up_kernel, counts),
        [(sx, sy, sz)],
        where,
        (gathered, level1) + tuple(fine_arrays),
        [(5, wide, rows, columns), (wide + NEAR, rows, columns)]
        + [(x1 + 2, ey, LANES)] * 2
        + [fine] * 4,
        24,
        micros=4,
    )
    return result


def solution(mesh):
    spec = P("gx", "gy", "gz")
    return jax.shard_map(
        local, mesh=mesh, in_specs=(spec,) * 6, out_specs=spec, check_vma=False
    )
```

```python
import functools

import jax
import jax.numpy as jnp
from jax import lax
from jax.experimental import pallas as pl
from jax.experimental.pallas import tpu as pltpu
from jax.sharding import PartitionSpec as P

LEVELS = 6
SWEEPS = 2
BOTTOM = 8
WEIGHT = 0.25 ** (LEVELS - 1)
RELAX = 2.0 / 3.0
KEEP = 1.0 / 3.0

HALO = 4
NEAR = 4
LANES = 128
PLACE = (0, 11, 21, 31, 41, 51)
DEPTH = (11, 10, 10, 10, 10, 11)
SIDE = LANES // 2
STRIDE = 256

VM = pl.BlockSpec(memory_space=pltpu.VMEM)
SM = pl.BlockSpec(memory_space=pltpu.SMEM)
F32 = jnp.float32


def position(where_ref):
    code = where_ref[0]
    return code // (STRIDE * STRIDE), code // STRIDE % STRIDE, code % STRIDE


def lane_of(shape):
    return lax.broadcasted_iota(jnp.int32, shape, len(shape) - 1)


def pick(flag, yes, no):
    return jnp.where(jnp.full(yes.shape, flag, jnp.int32) == 1, yes, no)


def neighbours(count, place, one, two):
    if count == 2:
        two = jnp.zeros_like(one)
    else:
        ends = jnp.full(two.shape, place, jnp.int32)
        two = jnp.where((ends == 0) | (ends == count - 1), 0.0, two)
    return pick(place % 2, one, two), pick(place % 2, two, one)


def turn(values, shift, axis):
    return pltpu.roll(values, shift % values.shape[axis], axis)


def parts_of(values):
    high = values.astype(jnp.bfloat16)
    return high, (values - high.astype(F32)).astype(jnp.bfloat16)


def times_table(values, table):
    table = table.astype(jnp.bfloat16)
    total = None
    for part in reversed(parts_of(values)):
        term = jnp.dot(part, table, preferred_element_type=F32)
        total = term if total is None else total + term
    return total


def iota2(shape, axis):
    return lax.broadcasted_iota(jnp.int32, shape, axis)


def pair_table(rows, cols, odd):
    row = iota2((rows, cols), 0)
    col = iota2((rows, cols), 1)
    hit = (row == 2 * col + 1) if odd else (row // 2 == col)
    return hit.astype(F32)


def below_x(values):
    if values.shape[0] == 1:
        return jnp.zeros_like(values)
    return jnp.concatenate([jnp.zeros_like(values[:1]), values[:-1]], axis=0)


def above_x(values):
    if values.shape[0] == 1:
        return jnp.zeros_like(values)
    return jnp.concatenate([values[1:], jnp.zeros_like(values[:1])], axis=0)


def pull(values, faces, step=1):
    bx, by, bz = faces
    total = bx * above_x(values) + below_x(bx * values)
    total = total + (by * turn(values, -step, 1) + turn(by * values, step, 1))
    return total + (bz * turn(values, -step, 2) + turn(bz * values, step, 2))


def diagonal(mass, faces, coupled, step=1):
    bx, by, bz = faces
    _, cy, cz = coupled
    return mass + bx + below_x(bx) + by + turn(cy, step, 1) + bz + turn(cz, step, 2)


def relaxer(mass, diag):
    inside = mass > 0.0
    return jnp.where(inside, RELAX / jnp.where(inside, diag, 1.0), 0.0)


def sweep(values, rhs, weight, faces, step=1):
    return KEEP * values + weight * (rhs + pull(values, faces, step))


def faces_x(values, odd, n_x, width):
    head, tail = values[:, :width], values[:, values.shape[1] - width:]
    return [pick(odd, head, tail), pick(odd, tail, head)][:n_x]


def faces_y(values, odd, width):
    head, tail = values[:, :width], values[:, values.shape[1] - width:]
    return pick(odd, head, tail), pick(odd, tail, head)


def corner_sends(below, above, odd):
    packs = []
    for rows, sign in ((slice(0, 8), 1), (slice(below.shape[1] - 8, below.shape[1]), -1)):
        low = [below[3 - i, rows] for i in range(3)]
        high = [above[i, rows] for i in range(3)]
        row = iota2(low[0].shape, 0)
        row = row if sign == 1 else 7 - row
        pack = (
            jnp.where(row < 3, low[0], turn(low[2], 3 * sign, 0)),
            jnp.where(row < 2, low[1], turn(high[1], 2 * sign, 0)),
            jnp.where(row < 3, high[0], turn(high[2], 3 * sign, 0)),
        )
        packs.append([p[:4] if sign == 1 else p[4:] for p in pack])
    return [(pick(odd, h, t), pick(odd, t, h)) for h, t in zip(*packs)]


def inner_rows(tile, by):
    upper = iota2(tile.shape, 0) < 4
    return jnp.where(upper, turn(tile, -by, 0), turn(tile, by, 0))


def corner_tiles(first, second, third):
    zero = jnp.zeros_like(first)
    low = (zero, inner_rows(first, 3), second, first)
    return low, (third, inner_rows(second, 2), inner_rows(third, 3), zero)


def diagonal_sends(values, n_x, odd_x, odd_y):
    corners = []
    for slabs in ([values[i] for i in range(4)], [values[values.shape[0] - 1 - i] for i in range(4)]):
        for sign in (1, -1):
            row = iota2(slabs[0].shape, 0)
            row = row if sign == 1 else 7 - row
            tiles = (slabs[0], jnp.where(row < 3, slabs[1], turn(slabs[3], 3 * sign, 0)), slabs[2])
            corners.append([t[:4] if sign == 1 else t[4:] for t in tiles])
    sends = []
    for k_x in range(n_x):
        for k_y in range(2):
            head_x = odd_x if k_x == 0 else 1 - odd_x
            head_y = odd_y if k_y == 0 else 1 - odd_y
            sends.append(
                [
                    pick(head_x, pick(head_y, hh, ht), pick(head_y, th, tt))
                    for hh, ht, th, tt in zip(*corners)
                ]
            )
    return sends


def diagonal_tiles(first, second, third):
    return [first, second, third, inner_rows(second, 3)]


def faces_kernel(counts, where_ref, *refs):
    ins, refs = refs[:6], refs[6:]
    n_x = 1 if counts[0] == 2 else 2
    sends_x, (two_y, one_y, first, second) = refs[:n_x], refs[n_x:]
    odd_x, odd_y, odd = (place % 2 for place in position(where_ref))
    sx, sy, sz = ins[0].shape
    half = sx // 2
    lane = lane_of((half, sy, LANES))
    head = jnp.zeros((half, sy, LANES), F32)
    tail = head
    for a, ref in enumerate(ins):
        for send, face in zip(sends_x, faces_x(ref[...][None], odd_x, n_x, HALO)):
            send[a] = face[0]
        one_y[a], two_y[a] = faces_y(ref[...], odd_y, HALO)
        for g in range(2):
            values = ref[g * half:(g + 1) * half]
            at = SIDE * g + PLACE[a]
            mask = (lane >= at) & (lane < at + DEPTH[a])
            head = jnp.where(mask, turn(values, at, 2), head)
            tail = jnp.where(mask, turn(values, at + DEPTH[a], 2), tail)
    first[...] = pick(odd, head, tail)
    second[...] = pick(odd, tail, head)


def halo_z_kernel(counts, where_ref, one_ref, two_ref, zpack, *sends):
    at_x, _, at_z = position(where_ref)
    half = one_ref.shape[0]
    below, above = neighbours(counts[2], at_z, one_ref[...], two_ref[...])
    lane = lane_of(below.shape)
    zpack[:half] = jnp.where(lane < SIDE, above, turn(below, SIDE, 2))
    zpack[half:] = jnp.where(lane < SIDE, turn(above, SIDE, 2), below)
    for send, face in zip(sends, faces_x(zpack[...][None], at_x % 2, len(sends), HALO)):
        send[...] = face[0]


def corners_kernel(counts, where_ref, zpack, *refs):
    n_x = 1 if counts[0] == 2 else 2
    main_x, halos_x, (two_y, one_y) = refs[:n_x], refs[n_x:2 * n_x], refs[2 * n_x + 1:]
    at_x, at_y, _ = position(where_ref)
    for a in range(7):
        if a < 6:
            below, above = neighbours(counts[0], at_x, main_x[0][a], main_x[-1][a])
        else:
            below, above = neighbours(counts[0], at_x, halos_x[0][...], halos_x[-1][...])
        for n, pair in enumerate(corner_sends(below, above, at_y % 2)):
            one_y[3 * a + n], two_y[3 * a + n] = pair
    one_y[21:], two_y[21:] = faces_y(zpack[...], at_y % 2, HALO)


def each(first, last, body):
    for x in range(first, last):
        body(x)


def ring_up(main, halo, lane):
    main_up, halo_up = turn(main, -1, 1), turn(halo, -1, 1)
    last = lane == LANES - 1
    return jnp.where(last, halo_up, main_up), jnp.where(last, main_up, halo_up)


def ring_down(main, halo, lane):
    main_down, halo_down = turn(main, 1, 1), turn(halo, 1, 1)
    zero = lane == 0
    return jnp.where(zero, halo_down, main_down), jnp.where(zero, main_down, halo_down)


def pull_slab(field, bx, by, bz, x, lane):
    centre = [half[x] for half in field]
    out = []
    for k in range(2):
        c, face = centre[k], by[k][x]
        t = bx[k][x] * field[k][x + 1] + bx[k][x - 1] * field[k][x - 1]
        out.append(t + (face * turn(c, -1, 0) + turn(face * c, 1, 0)))
    faces = [half[x] for half in bz]
    ups = ring_up(centre[0], centre[1], lane)
    downs = ring_down(faces[0] * centre[0], faces[1] * centre[1], lane)
    return centre, [out[k] + (faces[k] * ups[k] + downs[k]) for k in range(2)]


def unpacked(packed, a, lane):
    at, depth = PLACE[a], DEPTH[a]
    axis = packed.ndim - 1
    right, left = turn(packed, -at, axis), turn(packed, SIDE - depth - at, axis)
    return jnp.where(lane < depth, right, jnp.where(lane >= LANES - depth, left, 0.0))


def rows_of(source, x, count, firsts, seconds):
    total = None
    for p in firsts:
        for q in seconds:
            term = source[x + p, pl.ds(q, count, stride=2), :]
            total = term if total is None else total + term
    return total


BOTH, ODD = (0, 1), (1,)


def to_level1(sums, first, count, table, factor):
    _, x1, y1, _ = sums.shape
    flat = sums[first:first + count].reshape(count * x1 * y1, 2 * LANES)
    return factor * times_table(flat, table).reshape(count, x1, y1, LANES)


def coefficient_kernel(counts, where_ref, *refs):
    ins, refs = refs[:7], refs[7:]
    n_x = 1 if counts[0] == 2 else 2
    main_x, refs = refs[:n_x], refs[n_x:]
    arrays, (coarse2, coeffs1, sums, pairing) = refs[:12], refs[12:]
    sx, sy, sz = ins[0].shape
    at_x = position(where_ref)[0]
    x1, y1 = sx // 2, sy // 2
    lane = lane_of((sx, sy, LANES))
    lanes = [slice(k * LANES, (k + 1) * LANES) for k in range(2)]
    mine = slice(HALO, HALO + sx)
    for a in range(6):
        to = arrays[2 * a]
        below, above = neighbours(counts[0], at_x, main_x[0][a], main_x[-1][a])
        to[:HALO, :sy] = below
        to[mine, :sy] = ins[a][...]
        to[HALO + sx:, :sy] = above
        arrays[2 * a + 1][mine, :sy] = unpacked(ins[6][...], a, lane)
    for n, (firsts, seconds) in enumerate(((BOTH, BOTH), (ODD, BOTH), (BOTH, ODD), (BOTH, BOTH))):
        for k in range(2):
            for i in range(x1):
                source = arrays[2 * (n + 2) + k]
                sums[n, i, :, lanes[k]] = rows_of(source, HALO + 2 * i, y1, firsts, seconds)
    pairs = pair_table(2 * LANES, LANES, False)
    odds = pair_table(2 * LANES, LANES, True)
    paired = to_level1(sums, 0, 3, pairs, 0.0625)
    mass1 = (2.0 * WEIGHT) * paired[0]
    faces1 = (paired[1], paired[2], to_level1(sums, 3, 1, odds, 0.0625)[0])
    diag1 = mass1 + faces1[0] + below_x(faces1[0])
    diag1 = diag1 + faces1[1] + faces1[2] + turn(faces1[2], 1, 2)
    for n, values in enumerate((mass1, diag1) + faces1):
        coeffs1[n] = values
    parts = (
        (mass1, False, False, False, 0.125),
        (faces1[0], True, False, False, 0.0625),
        (faces1[1], False, True, False, 0.0625),
        (faces1[2], False, False, True, 0.0625),
    )
    for n, (values, *odd_axes, factor) in enumerate(parts):
        pairing[n] = values
        coarse2[n] = level2_rows(pairing.at[n], odd_axes, factor, x1 // 2, y1 // 2, sz // 4)


def down_kernel(counts, where_ref, zpack, *refs):
    refs = refs[12:]
    n_x = 1 if counts[0] == 2 else 2
    halos_x = refs[:n_x]
    main_two, main_one, rest_two, rest_one, coeffs1 = refs[n_x:5 + n_x]
    flat, refs = refs[5 + n_x:17 + n_x], refs[17 + n_x:]
    arrays = tuple(zip(flat[::2], flat[1::2]))
    own1, refs = refs[0], refs[1:]
    sends, near_two, near_one, refs = refs[:n_x], refs[n_x], refs[n_x + 1], refs[n_x + 2:]
    sends_xy, refs = refs[:2 * n_x], refs[2 * n_x:]
    kept_m, kept_h, weight_m, weight_h = refs[:4]
    packs, half_m, half_h, diag_m, diag_h, sums, left = refs[4:]
    field, rhs, alpha, bx, by, bz = arrays
    sx, sy, sz = zpack.shape
    ex, ey = sx + 2 * HALO, sy + 2 * HALO
    at_x, at_y, _ = position(where_ref)

    rest = neighbours(counts[1], at_y, rest_one[...], rest_two[...])
    rest = jnp.concatenate(rest[::-1], axis=1)
    for a in range(7):
        if a < 6:
            to = arrays[a][0]
            rows = neighbours(counts[1], at_y, main_one[a], main_two[a])
            rows = jnp.concatenate(rows[::-1], axis=1)
        else:
            to = packs
            rows = rest[21:]
            below, above = neighbours(counts[0], at_x, halos_x[0][...], halos_x[-1][...])
            to[:HALO, :sy] = below
            to[HALO + sx:, :sy] = above
        to[HALO:HALO + sx, sy:] = rows
        low, high = corner_tiles(*(rest[3 * a + n] for n in range(3)))
        for n in range(HALO):
            to[n, sy:] = low[n]
            to[HALO + sx + n, sy:] = high[n]
    lane = lane_of((ey, LANES))
    lane_low = lane_of((2 * HALO, LANES))

    def unpack_rows(x):
        packed = packs[x, sy:]
        for a in range(6):
            arrays[a][1][x, sy:] = unpacked(packed, a, lane_low)

    def unpack(x):
        packed = packs[x]
        for a in range(6):
            arrays[a][1][x] = unpacked(packed, a, lane)

    each(0, HALO, unpack)
    each(HALO, HALO + sx, unpack_rows)
    each(HALO + sx, ex, unpack)
    halfway, weight, kept = (half_m, half_h), (weight_m, weight_h), (kept_m, kept_h)
    diag = (diag_m, diag_h)

    def first_sweep(x):
        faces = [half[x] for half in bz]
        downs = ring_down(faces[0], faces[1], lane)
        centre, near = pull_slab(field, bx, by, bz, x, lane)
        for k in range(2):
            face = by[k][x]
            mass = WEIGHT * alpha[k][x]
            d = mass + bx[k][x] + bx[k][x - 1] + face + turn(face, 1, 0) + faces[k] + downs[k]
            w = relaxer(mass, d)
            diag[k][x] = d
            weight[k][x] = w
            halfway[k][x] = KEEP * centre[k] + w * (rhs[k][x] + near[k])

    each(1, ex - 1, first_sweep)

    def second_sweep(x):
        centre, near = pull_slab(halfway, bx, by, bz, x, lane)
        for k in range(2):
            kept[k][x] = KEEP * centre[k] + weight[k][x] * (rhs[k][x] + near[k])

    each(2, ex - 2, second_sweep)

    def residual(x):
        centre, near = pull_slab(kept, bx, by, bz, x, lane)
        for k in range(2):
            halfway[k][x] = rhs[k][x] - diag[k][x] * centre[k] + near[k]

    each(HALO, ex - HALO, residual)

    x1, y1 = sx // 2, sy // 2
    for k in range(2):
        lanes = slice(k * LANES, (k + 1) * LANES)
        for i in range(x1):
            x = HALO + 2 * i
            sums[0, i, :, lanes] = rows_of(halfway[k], x, y1, BOTH, BOTH)
            left[...] = turn(by[k][x] + by[k][x + 1], 1, 0)
            sums[1, i, :, lanes] = left[pl.ds(0, y1, stride=2), :]
        sums[2, 0, :, lanes] = rows_of(bx[k], HALO - 1, y1, (0,), BOTH)
        sums[2, 1:, :, lanes] = jnp.zeros((x1 - 1, y1, LANES), F32)
    rhs1, low_y, low_x = to_level1(sums, 0, 3, pair_table(2 * LANES, LANES, False), 0.0625)
    weight1 = relaxer(coeffs1[0], coeffs1[1] + low_y + low_x)
    for n, values in enumerate((2.0 * rhs1, weight1, coeffs1[2], coeffs1[3], coeffs1[4])):
        own1[n] = values
        for send, face in zip(sends, faces_x(values[None], at_x % 2, n_x, NEAR)):
            send[n] = face[0]
        near_one[n], near_two[n] = faces_y(values, at_y % 2, NEAR)
        for send, tiles in zip(sends_xy, diagonal_sends(values, n_x, at_x % 2, at_y % 2)):
            for t in range(3):
                send[3 * n + t] = tiles[t]


def level2_rows(source, odd_axes, factor, x2, y2, z2):
    rows = []
    for i in range(x2):
        total = None
        for p in (1,) if odd_axes[0] else (0, 1):
            for q in (1,) if odd_axes[1] else (0, 1):
                term = source[2 * i + p, pl.ds(q, y2, stride=2), :]
                total = term if total is None else total + term
        rows.append(total)
    flat = jnp.concatenate(rows, axis=0)
    flat = factor * times_table(flat, pair_table(LANES, LANES, odd_axes[2]))
    lane = lane_of((y2, LANES))
    packed = jnp.zeros((y2, LANES), F32)
    for i in range(x2):
        mask = (lane >= i * z2) & (lane < (i + 1) * z2)
        packed = jnp.where(mask, turn(flat[i * y2:(i + 1) * y2], i * z2, 1), packed)
    return packed


def near_kernel(counts, devices, where_ref, ring, *refs):
    n_x = 1 if counts[0] == 2 else 2
    halos_x = refs[:n_x]
    main_two, main_one = refs[n_x:n_x + 2]
    diagonals, (coarse2, copies, level1, left) = refs[n_x + 2:3 * n_x + 2], refs[3 * n_x + 2:]
    n, bx1, by1, _ = ring.shape
    at_x, at_y, _ = position(where_ref)
    sides = [
        neighbours(counts[0], at_x, diagonals[k][...], diagonals[k - 2][...]) for k in range(2)
    ]
    rest = []
    for one, two in zip(*sides):
        rows = neighbours(counts[1], at_y, one, two)
        rest.append(jnp.concatenate(rows[::-1], axis=1))
    whole = []
    for a in range(n):
        below, above = neighbours(counts[0], at_x, halos_x[0][a], halos_x[-1][a])
        rows = neighbours(counts[1], at_y, main_one[a], main_two[a])
        rows = jnp.concatenate(rows[::-1], axis=1)
        low, high = (diagonal_tiles(*(side[3 * a + k] for k in range(3))) for side in rest)
        low = low[::-1]
        rows = jnp.concatenate(
            [tile[None] for tile in low] + [rows] + [tile[None] for tile in high], axis=0
        )
        block = jnp.concatenate([below, ring[a], above], axis=0)
        whole.append(jnp.concatenate([block, rows], axis=1))
    rhs1, weight1 = whole[:2]
    faces1 = tuple(whole[2:])
    field1 = weight1 * rhs1
    field1 = sweep(field1, rhs1, weight1, faces1)
    for a, values in enumerate([field1] + whole):
        level1[a] = values
    mine = slice(NEAR, NEAR + bx1)
    inner = weight1[mine]
    diag1 = RELAX / jnp.where(inner > 0.0, inner, 1.0)
    remain = rhs1[mine] - diag1 * field1[mine] + pull(field1, faces1)[mine]
    left[...] = remain
    packed = level2_rows(left, (False,) * 3, 0.125, bx1 // 2, by1 // 2, LANES // 4)
    blocks = LANES // (LANES // 4)
    shift = position(where_ref)[2] % blocks * (LANES // blocks)
    slots = [pltpu.roll(values, shift, 1) for values in [packed] + [coarse2[a] for a in range(4)]]
    for d in range(devices):
        for a in range(n):
            copies[d, a] = slots[a]


def inner_sweep(values, rhs, weight, faces, first):
    part = slice(first, rhs.shape[0] - first)
    below = slice(first - 1, rhs.shape[0] - first - 1)
    bx, by, bz = faces
    centre = values[1:-1]
    near = bx[part] * values[2:] + bx[below] * values[:-2]
    near = near + (by[part] * turn(centre, -1, 1) + turn(by[part] * centre, 1, 1))
    near = near + (bz[part] * turn(centre, -1, 2) + turn(bz[part] * centre, 1, 2))
    return KEEP * centre + weight[part] * (rhs[part] + near)


def halve(values, odd_axis, step):
    half = values.shape[0] // 2
    even = [values[2 * i:2 * i + 1] for i in range(half)]
    odd = [values[2 * i + 1:2 * i + 2] for i in range(half)]
    if odd_axis != 0:
        odd = [a + b for a, b in zip(even, odd)]
    values = jnp.concatenate(odd, axis=0)
    for axis in (1, 2):
        next_one = turn(values, -step, axis)
        values = next_one if odd_axis == axis else values + next_one
    return values


def double(values, step):
    values = values + turn(values, step, 1)
    values = values + turn(values, step, 2)
    return jnp.concatenate([values[i // 2:i // 2 + 1] for i in range(2 * values.shape[0])], axis=0)


def coarse_levels(mass, faces, y, z):
    levels = []
    for level in range(2, LEVELS):
        step = 2 ** (level - 2)
        bx, by, bz = faces
        row = lax.broadcasted_iota(jnp.int32, by.shape, 1)
        lane = lane_of(bz.shape)
        upper = (
            bx,
            jnp.where(row == (y - 1) * step, 0.0, by),
            jnp.where(lane == (z - 1) * step, 0.0, bz),
        )
        lower = (below_x(bx), turn(upper[1], step, 1), turn(upper[2], step, 2))
        mass = jnp.where((row % step == 0) & (lane % step == 0), mass, 0.0)
        diag = mass + bx + lower[0] + by + lower[1] + bz + lower[2]
        levels.append((diag, relaxer(mass, diag), upper, lower))
        if level < LEVELS - 1:
            faces = tuple(0.0625 * halve(face, axis, step) for axis, face in enumerate(faces))
            mass = 0.125 * halve(mass, -1, step)
            y, z = y // 2, z // 2
    return levels


def coupled(values, upper, lower, step):
    ups = (above_x(values), turn(values, -step, 1), turn(values, -step, 2))
    downs = (below_x(values), turn(values, step, 1), turn(values, step, 2))
    x, y, z = (u * up + l * down for u, up, l, down in zip(upper, ups, lower, downs))
    return (y + z) + x if values.shape[0] > 1 else y + z


def coarse_cycle(level, rhs, levels):
    step = 2 ** (level - 2)
    diag, weight, upper, lower = levels[level - 2]
    scaled = tuple(tuple(weight * b for b in faces) for faces in (upper, lower))
    source = weight * rhs

    def relax(field):
        return (KEEP * field + source) + coupled(field, *scaled, step)

    field = source
    if level == LEVELS - 1:
        for _ in range(BOTTOM - 1):
            field = relax(field)
        return field
    for _ in range(SWEEPS - 1):
        field = relax(field)
    remain = (rhs - diag * field) + coupled(field, upper, lower, step)
    correction = coarse_cycle(level + 1, 0.125 * halve(remain, -1, step), levels)
    field = field + double(correction, step)
    for _ in range(SWEEPS):
        field = relax(field)
    return field


def spread_out(counts, slots, whole):
    gx, gy, gz = counts
    y2 = slots.shape[-2]
    x2 = whole.shape[0] // gx
    z2 = LANES // x2
    lane = lane_of((y2, LANES))
    for i in range(gx):
        for j in range(gy):
            for x in range(x2):
                for part in range(whole.shape[2] // LANES):
                    total = None
                    for k in range(LANES // z2):
                        column = part * (LANES // z2) + k
                        if column < gz:
                            block = slots[(i * gy + j) * gz + column]
                            at = (x + k) * z2 % LANES
                            mask = (lane >= at) & (lane < at + z2)
                            if total is None:
                                total = jnp.where(mask, block, 0.0)
                            total = jnp.where(mask, block, total)
                    if x:
                        total = turn(total, -x * z2, 1)
                    lanes = slice(part * LANES, (part + 1) * LANES)
                    whole[i * x2 + x, j * y2:(j + 1) * y2, lanes] = total


def up_kernel(counts, where_ref, gathered, level1, *refs):
    kept, weight, rhs, bx, by, bz = zip(refs[0:12:2], refs[1:12:2])
    out, whole, second, lift, spread_m, spread_h, field_m, field_h, half_m, half_h = refs[12:]
    gx, gy, gz = counts
    at_x, at_y, at_z = position(where_ref)
    sx, sy, sz = out.shape
    x1, y1 = sx // 2, sy // 2
    x2, y2, z2 = x1 // 2, y1 // 2, sz // 4
    columns = max(LANES, gz * z2)
    for a in range(5):
        spread_out(counts, gathered.at[:, a], whole.at[a])
    levels = coarse_levels(whole[1], (whole[2], whole[3], whole[4]), gy * y2, gz * z2)
    correction = coarse_cycle(2, whole[0], levels)

    wide = gx * x2
    half = NEAR // 2
    ex1, ey1 = x1 + 2 * NEAR, y1 + 2 * NEAR
    second[:half] = jnp.zeros((half,) + correction.shape[1:], F32)
    second[half:half + wide] = correction
    second[half + wide:] = jnp.zeros((half,) + correction.shape[1:], F32)
    window = second[pl.ds(at_x * x2, x2 + NEAR)]
    rows = correction.shape[1]
    row = iota2((columns, LANES), 0)
    col = iota2((columns, LANES), 1)
    place = jnp.where(col < LANES * 3 // 4, col, col - LANES)
    table_z = (row == at_z * z2 + lax.shift_right_arithmetic(place, 1)).astype(F32)
    flat = times_table(window.reshape((x2 + NEAR) * rows, columns), table_z)
    flat = flat.reshape(x2 + NEAR, rows, LANES)
    flat = pltpu.roll(flat, (rows - at_y * y2) % rows, 1)
    for i in range(x2 + NEAR):
        for q in range(2):
            lift[i, pl.ds(q, y2, stride=2), :] = flat[i, :y2]
            lift[i, pl.ds(y1 + q, half, stride=2), :] = flat[i, y2:y2 + half]
            lift[i, pl.ds(y1 + NEAR + q, half, stride=2), :] = flat[i, rows - half:]
    lifted = jnp.concatenate([lift[i // 2][None] for i in range(ex1)], axis=0)
    field1, rhs1, weight1 = level1[0], level1[1], level1[2]
    faces1 = (level1[3], level1[4], level1[5])
    field1 = (field1 + jnp.where(weight1 > 0.0, lifted, 0.0))[1:-1]
    for n in range(SWEEPS):
        field1 = inner_sweep(field1, rhs1, weight1, faces1, 2 + n)

    ex, ey = sx + 2 * HALO, sy + 2 * HALO
    near = field1.reshape((x1 + 2) * ey1, LANES)
    row = iota2((LANES, 2 * LANES), 0)
    col = iota2((LANES, 2 * LANES), 1)
    lifted = times_table(near, (col // 2 == row).astype(F32))
    quarter = NEAR // 2
    for k, spread in enumerate((spread_m, spread_h)):
        block = lifted[:, k * LANES:(k + 1) * LANES].reshape(x1 + 2, ey1, LANES)
        for i in range(x1 + 2):
            for q in range(2):
                spread[i, pl.ds(q, y1, stride=2), :] = block[i, :y1]
                spread[i, pl.ds(sy + q, quarter, stride=2), :] = block[i, y1:y1 + quarter]
                spread[i, pl.ds(sy + HALO + q, quarter, stride=2), :] = block[i, ey1 - quarter:]
    before, after = (field_m, field_h), (half_m, half_h)
    first = HALO - 2
    for x in range(first, ex - first):
        for k, spread in enumerate((spread_m, spread_h)):
            before[k][x] = kept[k][x] + spread[(x - first) // 2]

    lane = lane_of((ey, LANES))

    def sweep_out(x):
        centre, around = pull_slab(before, bx, by, bz, x, lane)
        for k in range(2):
            after[k][x] = KEEP * centre[k] + weight[k][x] * (rhs[k][x] + around[k])

    each(first + 1, ex - first - 1, sweep_out)

    def sweep_own(x):
        centre, around = pull_slab(after, bx, by, bz, x, lane)
        value = KEEP * centre[0] + weight[0][x] * (rhs[0][x] + around[0])
        out[x - HALO] = value[:sy]

    each(HALO, ex - HALO, sweep_own)


def run(kernel, outs, where, arrays, scratch=(), grant=16, micros=1, aliases={}):
    return pl.pallas_call(
        kernel,
        out_shape=tuple(jax.ShapeDtypeStruct(shape, F32) for shape in outs),
        in_specs=[SM] * len(where) + [VM] * len(arrays),
        out_specs=tuple(VM for _ in outs),
        input_output_aliases=aliases,
        scratch_shapes=[pltpu.VMEM(shape, F32) for shape in scratch],
        compiler_params=pltpu.CompilerParams(vmem_limit_bytes=grant * 1024 * 1024),
        cost_estimate=pl.CostEstimate(
            flops=0, bytes_accessed=int(micros * 3.6e6), transcendentals=0
        ),
    )(*where, *arrays)


def partners(count, k):
    partner = list(range(count))
    for low in range(k, count - 1, 2):
        partner[low], partner[low + 1] = low + 1, low
    return partner


def swaps(axis, sends, other=None):
    count = lax.axis_size(axis)
    got = []
    for k, block in enumerate(sends):
        partner = partners(count, k)
        if k == 1 and other is None:
            partner[0], partner[-1] = count - 1, 0
        if k == 0 or other is None:
            got.append(lax.ppermute(block, axis, list(enumerate(partner))))
            continue
        rows = lax.axis_size(other)
        pairs = []
        for row in range(rows):
            for i in range(count):
                ends = [(row, i), (min(row ^ 1, rows - 1) if partner[i] == i else row, partner[i])]
                if axis < other:
                    pairs.append(tuple(at * rows + line for line, at in ends))
                else:
                    pairs.append(tuple(line * count + at for line, at in ends))
        got.append(lax.ppermute(block, tuple(sorted((axis, other))), pairs))
    return got


def diagonal_swaps(sends):
    count_x, count_y = lax.axis_size("gx"), lax.axis_size("gy")
    got = []
    for n, block in enumerate(sends):
        xs, ys = partners(count_x, n // 2), partners(count_y, n % 2)
        pairs = [
            (x * count_y + y, xs[x] * count_y + ys[y])
            for x in range(count_x)
            for y in range(count_y)
        ]
        got.append(lax.ppermute(block, ("gx", "gy"), pairs))
    return got


def local(initial, right_side, alpha, beta_x, beta_y, beta_z):
    axes = ("gx", "gy", "gz")
    counts = tuple(lax.axis_size(axis) for axis in axes)
    devices = counts[0] * counts[1] * counts[2]
    where = (lax.axis_index("gx") * STRIDE + lax.axis_index("gy")) * STRIDE + lax.axis_index("gz")
    where = (where.astype(jnp.int32).reshape(1),)
    ins = (initial, right_side, alpha, beta_x, beta_y, beta_z)
    sx, sy, sz = initial.shape
    n_x = 1 if counts[0] == 2 else 2
    ex, ey = sx + 2 * HALO, sy + 2 * HALO
    fine = (ex, ey, LANES)

    *sends_x, two_y, one_y, first, second = run(
        functools.partial(faces_kernel, counts),
        [(6, HALO, sy, LANES)] * n_x
        + [(6, sx, HALO, LANES)] * 2
        + [(sx // 2, sy, LANES)] * 2,
        where,
        ins,
        grant=60,
    )
    main_x = tuple(swaps("gx", sends_x, "gy"))
    main_y = tuple(swaps("gy", (one_y, two_y))[::-1])
    got = swaps("gz", (first, second), "gy")
    zpack, *sends = run(
        functools.partial(halo_z_kernel, counts),
        [(sx, sy, LANES)] + [(HALO, sy, LANES)] * n_x,
        where,
        tuple(got),
    )
    halos_x = tuple(swaps("gx", sends, "gy"))
    x1, y1 = sx // 2, sy // 2
    *laid, coarse2, coeffs1 = run(
        functools.partial(coefficient_kernel, counts),
        [fine] * 12 + [(4, y1 // 2, LANES), (5, x1, y1, LANES)],
        where,
        ins + (zpack,) + main_x,
        [(4, x1, y1, 2 * LANES), (4, x1, y1, LANES)],
        micros=2,
    )
    two_y, one_y = run(
        functools.partial(corners_kernel, counts),
        [(21 + sx, HALO, LANES)] * 2,
        where,
        (zpack,) + main_x + halos_x + (coarse2,),
    )
    rest_y = tuple(swaps("gy", (one_y, two_y), "gz")[::-1])
    outs = run(
        functools.partial(down_kernel, counts),
        [fine] * 12
        + [(5, x1, y1, LANES)]
        + [(5, NEAR, y1, LANES)] * n_x
        + [(5, x1, NEAR, LANES)] * 2
        + [(15, NEAR, LANES)] * (2 * n_x)
        + [fine] * 4,
        where,
        (zpack,) + tuple(laid) + halos_x + main_y + rest_y + (coeffs1,),
        [fine] * 5 + [(3, x1, y1, 2 * LANES), (ey, LANES)],
        24,
        micros=4,
        aliases={n + 2: n for n in range(12)},
    )
    laid, own1, outs = outs[:12], outs[12], outs[13:]
    sends_x, (two_y, one_y), outs = outs[:n_x], outs[n_x:n_x + 2], outs[n_x + 2:]
    sends_xy, fine_arrays = outs[:2 * n_x], outs[2 * n_x:]
    fine_arrays = tuple(fine_arrays) + tuple(laid[2:4]) + tuple(laid[6:])

    near_x = tuple(swaps("gx", sends_x, "gy"))
    near_y = tuple(swaps("gy", (one_y, two_y), "gz")[::-1])
    near_xy = tuple(diagonal_swaps(sends_xy))
    copies, level1 = run(
        functools.partial(near_kernel, counts, devices),
        [(devices, 5, y1 // 2, LANES), (6, x1 + 2 * NEAR, y1 + 2 * NEAR, LANES)],
        where,
        (own1,) + near_x + near_y + near_xy + (coarse2,),
        [(x1, y1 + 2 * NEAR, LANES)],
    )

    gathered = lax.all_to_all(copies, axes, 0, 0, tiled=True)
    wide, rows = counts[0] * x1 // 2, counts[1] * y1 // 2
    columns = max(LANES, counts[2] * sz // 4)
    (result,) = run(
        functools.partial(up_kernel, counts),
        [(sx, sy, sz)],
        where,
        (gathered, level1) + tuple(fine_arrays),
        [(5, wide, rows, columns), (wide + NEAR, rows, columns)]
        + [(x1 // 2 + NEAR, y1 + 2 * NEAR, LANES)]
        + [(x1 + 2, ey, LANES)] * 2
        + [fine] * 4,
        24,
        micros=4,
    )
    return result


def solution(mesh):
    spec = P("gx", "gy", "gz")
    return jax.shard_map(
        local, mesh=mesh, in_specs=(spec,) * 6, out_specs=spec, check_vma=False
    )
```

```python
import functools

import jax
import jax.numpy as jnp
from jax import lax
from jax.experimental import pallas as pl
from jax.experimental.pallas import tpu as pltpu
from jax.sharding import PartitionSpec as P

LEVELS = 6
SWEEPS = 2
BOTTOM = 8
WEIGHT = 0.25 ** (LEVELS - 1)
RELAX = 2.0 / 3.0
KEEP = 1.0 / 3.0

HALO = 4
NEAR = 4
LANES = 128
PLACE = (0, 11, 21, 31, 41, 51)
DEPTH = (11, 10, 10, 10, 10, 11)
SIDE = LANES // 2
STRIDE = 256

VM = pl.BlockSpec(memory_space=pltpu.VMEM)
SM = pl.BlockSpec(memory_space=pltpu.SMEM)
F32 = jnp.float32


def position(where_ref):
    code = where_ref[0]
    return code // (STRIDE * STRIDE), code // STRIDE % STRIDE, code % STRIDE


def lane_of(shape):
    return lax.broadcasted_iota(jnp.int32, shape, len(shape) - 1)


def pick(flag, yes, no):
    return jnp.where(jnp.full(yes.shape, flag, jnp.int32) == 1, yes, no)


def neighbours(count, place, one, two):
    if count == 2:
        two = jnp.zeros_like(one)
    else:
        ends = jnp.full(two.shape, place, jnp.int32)
        two = jnp.where((ends == 0) | (ends == count - 1), 0.0, two)
    return pick(place % 2, one, two), pick(place % 2, two, one)


def turn(values, shift, axis):
    return pltpu.roll(values, shift % values.shape[axis], axis)


def parts_of(values):
    high = values.astype(jnp.bfloat16)
    return high, (values - high.astype(F32)).astype(jnp.bfloat16)


def times_table(values, table):
    table = table.astype(jnp.bfloat16)
    total = None
    for part in reversed(parts_of(values)):
        term = jnp.dot(part, table, preferred_element_type=F32)
        total = term if total is None else total + term
    return total


def iota2(shape, axis):
    return lax.broadcasted_iota(jnp.int32, shape, axis)


def pair_table(rows, cols, odd):
    row = iota2((rows, cols), 0)
    col = iota2((rows, cols), 1)
    hit = (row == 2 * col + 1) if odd else (row // 2 == col)
    return hit.astype(F32)


def below_x(values):
    if values.shape[0] == 1:
        return jnp.zeros_like(values)
    return jnp.concatenate([jnp.zeros_like(values[:1]), values[:-1]], axis=0)


def above_x(values):
    if values.shape[0] == 1:
        return jnp.zeros_like(values)
    return jnp.concatenate([values[1:], jnp.zeros_like(values[:1])], axis=0)


def pull(values, faces, step=1):
    bx, by, bz = faces
    total = bx * above_x(values) + below_x(bx * values)
    total = total + (by * turn(values, -step, 1) + turn(by * values, step, 1))
    return total + (bz * turn(values, -step, 2) + turn(bz * values, step, 2))


def diagonal(mass, faces, coupled, step=1):
    bx, by, bz = faces
    _, cy, cz = coupled
    return mass + bx + below_x(bx) + by + turn(cy, step, 1) + bz + turn(cz, step, 2)


def relaxer(mass, diag):
    inside = mass > 0.0
    return jnp.where(inside, RELAX / jnp.where(inside, diag, 1.0), 0.0)


def sweep(values, rhs, weight, faces, step=1):
    return KEEP * values + weight * (rhs + pull(values, faces, step))


def faces_x(values, odd, n_x, width):
    head, tail = values[:, :width], values[:, values.shape[1] - width:]
    return [pick(odd, head, tail), pick(odd, tail, head)][:n_x]


def faces_y(values, odd, width):
    head, tail = values[:, :width], values[:, values.shape[1] - width:]
    return pick(odd, head, tail), pick(odd, tail, head)


def corner_sends(below, above, odd):
    packs = []
    for rows, sign in ((slice(0, 8), 1), (slice(below.shape[1] - 8, below.shape[1]), -1)):
        low = [below[3 - i, rows] for i in range(3)]
        high = [above[i, rows] for i in range(3)]
        row = iota2(low[0].shape, 0)
        row = row if sign == 1 else 7 - row
        pack = (
            jnp.where(row < 3, low[0], turn(low[2], 3 * sign, 0)),
            jnp.where(row < 2, low[1], turn(high[1], 2 * sign, 0)),
            jnp.where(row < 3, high[0], turn(high[2], 3 * sign, 0)),
        )
        packs.append([p[:4] if sign == 1 else p[4:] for p in pack])
    return [(pick(odd, h, t), pick(odd, t, h)) for h, t in zip(*packs)]


def inner_rows(tile, by):
    upper = iota2(tile.shape, 0) < 4
    return jnp.where(upper, turn(tile, -by, 0), turn(tile, by, 0))


def corner_tiles(first, second, third):
    zero = jnp.zeros_like(first)
    low = (zero, inner_rows(first, 3), second, first)
    return low, (third, inner_rows(second, 2), inner_rows(third, 3), zero)


def diagonal_sends(values, n_x, odd_x, odd_y):
    corners = []
    for slabs in ([values[i] for i in range(4)], [values[values.shape[0] - 1 - i] for i in range(4)]):
        for sign in (1, -1):
            row = iota2(slabs[0].shape, 0)
            row = row if sign == 1 else 7 - row
            tiles = (slabs[0], jnp.where(row < 3, slabs[1], turn(slabs[3], 3 * sign, 0)), slabs[2])
            corners.append([t[:4] if sign == 1 else t[4:] for t in tiles])
    sends = []
    for k_x in range(n_x):
        for k_y in range(2):
            head_x = odd_x if k_x == 0 else 1 - odd_x
            head_y = odd_y if k_y == 0 else 1 - odd_y
            sends.append(
                [
                    pick(head_x, pick(head_y, hh, ht), pick(head_y, th, tt))
                    for hh, ht, th, tt in zip(*corners)
                ]
            )
    return sends


def halo_lanes(n):
    return SIDE + 2 * NEAR * n


def pack_level1(values):
    lane = lane_of(values[0].shape)
    axis = values[0].ndim - 1
    packs = [
        jnp.where(lane < SIDE, values[0], turn(values[1], SIDE, axis)),
        jnp.where(lane < SIDE, values[2], turn(values[3], SIDE, axis)),
    ]
    last = jnp.where(lane < SIDE, values[4], 0.0)
    for n, array in enumerate(values):
        at = halo_lanes(n)
        right = turn(array, at - SIDE, axis)
        left = turn(array, at + 2 * NEAR, axis)
        last = jnp.where((lane >= at) & (lane < at + NEAR), right, last)
        last = jnp.where((lane >= at + NEAR) & (lane < at + 2 * NEAR), left, last)
    return packs + [last]


def unpack_level1(packs):
    first, second, last = packs
    lane = lane_of(first.shape)
    axis = first.ndim - 1
    blocks = (first, turn(first, SIDE, axis), second, turn(second, SIDE, axis), last)
    values = []
    for n, block in enumerate(blocks):
        at = halo_lanes(n)
        right = turn(last, SIDE - at, axis)
        left = turn(last, -at - 2 * NEAR, axis)
        halo = jnp.where(lane < SIDE + NEAR, right, jnp.where(lane >= LANES - NEAR, left, 0.0))
        values.append(jnp.where(lane < SIDE, block, halo))
    return values


def diagonal_tiles(first, second, third):
    return [first, second, third, inner_rows(second, 3)]


def faces_kernel(counts, where_ref, *refs):
    ins, refs = refs[:6], refs[6:]
    n_x = 1 if counts[0] == 2 else 2
    sends_x, (two_y, one_y, first, second) = refs[:n_x], refs[n_x:]
    odd_x, odd_y, odd = (place % 2 for place in position(where_ref))
    sx, sy, sz = ins[0].shape
    half = sx // 2
    lane = lane_of((half, sy, LANES))
    head = jnp.zeros((half, sy, LANES), F32)
    tail = head
    for a, ref in enumerate(ins):
        for send, face in zip(sends_x, faces_x(ref[...][None], odd_x, n_x, HALO)):
            send[a] = face[0]
        one_y[a], two_y[a] = faces_y(ref[...], odd_y, HALO)
        for g in range(2):
            values = ref[g * half:(g + 1) * half]
            at = SIDE * g + PLACE[a]
            mask = (lane >= at) & (lane < at + DEPTH[a])
            head = jnp.where(mask, turn(values, at, 2), head)
            tail = jnp.where(mask, turn(values, at + DEPTH[a], 2), tail)
    first[...] = pick(odd, head, tail)
    second[...] = pick(odd, tail, head)


def halo_z_kernel(counts, where_ref, one_ref, two_ref, zpack, *sends):
    at_x, _, at_z = position(where_ref)
    half = one_ref.shape[0]
    below, above = neighbours(counts[2], at_z, one_ref[...], two_ref[...])
    lane = lane_of(below.shape)
    zpack[:half] = jnp.where(lane < SIDE, above, turn(below, SIDE, 2))
    zpack[half:] = jnp.where(lane < SIDE, turn(above, SIDE, 2), below)
    for send, face in zip(sends, faces_x(zpack[...][None], at_x % 2, len(sends), HALO)):
        send[...] = face[0]


def corners_kernel(counts, where_ref, zpack, *refs):
    n_x = 1 if counts[0] == 2 else 2
    main_x, halos_x, (two_y, one_y) = refs[:n_x], refs[n_x:2 * n_x], refs[2 * n_x + 1:]
    at_x, at_y, _ = position(where_ref)
    for a in range(7):
        if a < 6:
            below, above = neighbours(counts[0], at_x, main_x[0][a], main_x[-1][a])
        else:
            below, above = neighbours(counts[0], at_x, halos_x[0][...], halos_x[-1][...])
        for n, pair in enumerate(corner_sends(below, above, at_y % 2)):
            one_y[3 * a + n], two_y[3 * a + n] = pair
    one_y[21:], two_y[21:] = faces_y(zpack[...], at_y % 2, HALO)


def each(first, last, body):
    for x in range(first, last):
        body(x)


def ring_up(main, halo, lane):
    main_up, halo_up = turn(main, -1, 1), turn(halo, -1, 1)
    last = lane == LANES - 1
    return jnp.where(last, halo_up, main_up), jnp.where(last, main_up, halo_up)


def ring_down(main, halo, lane):
    main_down, halo_down = turn(main, 1, 1), turn(halo, 1, 1)
    zero = lane == 0
    return jnp.where(zero, halo_down, main_down), jnp.where(zero, main_down, halo_down)


def pull_slab(field, bx, by, bz, x, lane):
    centre = [half[x] for half in field]
    out = []
    for k in range(2):
        c, face = centre[k], by[k][x]
        t = bx[k][x] * field[k][x + 1] + bx[k][x - 1] * field[k][x - 1]
        out.append(t + (face * turn(c, -1, 0) + turn(face * c, 1, 0)))
    faces = [half[x] for half in bz]
    ups = ring_up(centre[0], centre[1], lane)
    downs = ring_down(faces[0] * centre[0], faces[1] * centre[1], lane)
    return centre, [out[k] + (faces[k] * ups[k] + downs[k]) for k in range(2)]


def unpacked(packed, a, lane):
    at, depth = PLACE[a], DEPTH[a]
    axis = packed.ndim - 1
    right, left = turn(packed, -at, axis), turn(packed, SIDE - depth - at, axis)
    return jnp.where(lane < depth, right, jnp.where(lane >= LANES - depth, left, 0.0))


def rows_of(source, x, count, firsts, seconds):
    total = None
    for p in firsts:
        for q in seconds:
            term = source[x + p, pl.ds(q, count, stride=2), :]
            total = term if total is None else total + term
    return total


BOTH, ODD = (0, 1), (1,)


def to_level1(sums, first, count, table, factor):
    _, x1, y1, _ = sums.shape
    flat = sums[first:first + count].reshape(count * x1 * y1, 2 * LANES)
    return factor * times_table(flat, table).reshape(count, x1, y1, LANES)


def coefficient_kernel(counts, where_ref, *refs):
    ins, refs = refs[:7], refs[7:]
    n_x = 1 if counts[0] == 2 else 2
    main_x, refs = refs[:n_x], refs[n_x:]
    arrays, (coarse2, coeffs1, sums, pairing) = refs[:12], refs[12:]
    sx, sy, sz = ins[0].shape
    at_x = position(where_ref)[0]
    x1, y1 = sx // 2, sy // 2
    lane = lane_of((sx, sy, LANES))
    lanes = [slice(k * LANES, (k + 1) * LANES) for k in range(2)]
    mine = slice(HALO, HALO + sx)
    for a in range(6):
        to = arrays[2 * a]
        below, above = neighbours(counts[0], at_x, main_x[0][a], main_x[-1][a])
        to[:HALO, :sy] = below
        to[mine, :sy] = ins[a][...]
        to[HALO + sx:, :sy] = above
        arrays[2 * a + 1][mine, :sy] = unpacked(ins[6][...], a, lane)
    for n, (firsts, seconds) in enumerate(((BOTH, BOTH), (ODD, BOTH), (BOTH, ODD), (BOTH, BOTH))):
        for k in range(2):
            for i in range(x1):
                source = arrays[2 * (n + 2) + k]
                sums[n, i, :, lanes[k]] = rows_of(source, HALO + 2 * i, y1, firsts, seconds)
    pairs = pair_table(2 * LANES, LANES, False)
    odds = pair_table(2 * LANES, LANES, True)
    paired = to_level1(sums, 0, 3, pairs, 0.0625)
    mass1 = (2.0 * WEIGHT) * paired[0]
    faces1 = (paired[1], paired[2], to_level1(sums, 3, 1, odds, 0.0625)[0])
    diag1 = mass1 + faces1[0] + below_x(faces1[0])
    diag1 = diag1 + faces1[1] + faces1[2] + turn(faces1[2], 1, 2)
    for n, values in enumerate((mass1, diag1) + faces1):
        coeffs1[n] = values
    parts = (
        (mass1, False, False, False, 0.125),
        (faces1[0], True, False, False, 0.0625),
        (faces1[1], False, True, False, 0.0625),
        (faces1[2], False, False, True, 0.0625),
    )
    for n, (values, *odd_axes, factor) in enumerate(parts):
        pairing[n] = values
        coarse2[n] = level2_rows(pairing.at[n], odd_axes, factor, x1 // 2, y1 // 2, sz // 4)


def down_kernel(counts, where_ref, zpack, *refs):
    refs = refs[12:]
    n_x = 1 if counts[0] == 2 else 2
    halos_x = refs[:n_x]
    main_two, main_one, rest_two, rest_one, coeffs1 = refs[n_x:5 + n_x]
    flat, refs = refs[5 + n_x:17 + n_x], refs[17 + n_x:]
    arrays = tuple(zip(flat[::2], flat[1::2]))
    own1, refs = refs[0], refs[1:]
    sends, near_two, near_one, refs = refs[:n_x], refs[n_x], refs[n_x + 1], refs[n_x + 2:]
    sends_xy, refs = refs[:2 * n_x], refs[2 * n_x:]
    kept_m, kept_h, weight_m, weight_h = refs[:4]
    packs, half_m, half_h, diag_m, diag_h, sums, left = refs[4:]
    field, rhs, alpha, bx, by, bz = arrays
    sx, sy, sz = zpack.shape
    ex, ey = sx + 2 * HALO, sy + 2 * HALO
    at_x, at_y, _ = position(where_ref)

    rest = neighbours(counts[1], at_y, rest_one[...], rest_two[...])
    rest = jnp.concatenate(rest[::-1], axis=1)
    for a in range(7):
        if a < 6:
            to = arrays[a][0]
            rows = neighbours(counts[1], at_y, main_one[a], main_two[a])
            rows = jnp.concatenate(rows[::-1], axis=1)
        else:
            to = packs
            rows = rest[21:]
            below, above = neighbours(counts[0], at_x, halos_x[0][...], halos_x[-1][...])
            to[:HALO, :sy] = below
            to[HALO + sx:, :sy] = above
        to[HALO:HALO + sx, sy:] = rows
        low, high = corner_tiles(*(rest[3 * a + n] for n in range(3)))
        for n in range(HALO):
            to[n, sy:] = low[n]
            to[HALO + sx + n, sy:] = high[n]
    lane = lane_of((ey, LANES))
    lane_low = lane_of((2 * HALO, LANES))

    def unpack_rows(x):
        packed = packs[x, sy:]
        for a in range(6):
            arrays[a][1][x, sy:] = unpacked(packed, a, lane_low)

    def unpack(x):
        packed = packs[x]
        for a in range(6):
            arrays[a][1][x] = unpacked(packed, a, lane)

    each(0, HALO, unpack)
    each(HALO, HALO + sx, unpack_rows)
    each(HALO + sx, ex, unpack)
    halfway, weight, kept = (half_m, half_h), (weight_m, weight_h), (kept_m, kept_h)
    diag = (diag_m, diag_h)

    def first_sweep(x):
        faces = [half[x] for half in bz]
        downs = ring_down(faces[0], faces[1], lane)
        centre, near = pull_slab(field, bx, by, bz, x, lane)
        for k in range(2):
            face = by[k][x]
            mass = WEIGHT * alpha[k][x]
            d = mass + bx[k][x] + bx[k][x - 1] + face + turn(face, 1, 0) + faces[k] + downs[k]
            w = relaxer(mass, d)
            diag[k][x] = d
            weight[k][x] = w
            halfway[k][x] = KEEP * centre[k] + w * (rhs[k][x] + near[k])

    each(1, ex - 1, first_sweep)

    def second_sweep(x):
        centre, near = pull_slab(halfway, bx, by, bz, x, lane)
        for k in range(2):
            kept[k][x] = KEEP * centre[k] + weight[k][x] * (rhs[k][x] + near[k])

    each(2, ex - 2, second_sweep)

    def residual(x):
        centre, near = pull_slab(kept, bx, by, bz, x, lane)
        for k in range(2):
            halfway[k][x] = rhs[k][x] - diag[k][x] * centre[k] + near[k]

    each(HALO, ex - HALO, residual)

    x1, y1 = sx // 2, sy // 2
    for k in range(2):
        lanes = slice(k * LANES, (k + 1) * LANES)
        for i in range(x1):
            x = HALO + 2 * i
            sums[0, i, :, lanes] = rows_of(halfway[k], x, y1, BOTH, BOTH)
            left[...] = turn(by[k][x] + by[k][x + 1], 1, 0)
            sums[1, i, :, lanes] = left[pl.ds(0, y1, stride=2), :]
        sums[2, 0, :, lanes] = rows_of(bx[k], HALO - 1, y1, (0,), BOTH)
        sums[2, 1:, :, lanes] = jnp.zeros((x1 - 1, y1, LANES), F32)
    rhs1, low_y, low_x = to_level1(sums, 0, 3, pair_table(2 * LANES, LANES, False), 0.0625)
    weight1 = relaxer(coeffs1[0], coeffs1[1] + low_y + low_x)
    packed = pack_level1((2.0 * rhs1, weight1, coeffs1[2], coeffs1[3], coeffs1[4]))
    for n, values in enumerate(packed):
        own1[n] = values
        for send, face in zip(sends, faces_x(values[None], at_x % 2, n_x, NEAR)):
            send[n] = face[0]
        near_one[n], near_two[n] = faces_y(values, at_y % 2, NEAR)
        for send, tiles in zip(sends_xy, diagonal_sends(values, n_x, at_x % 2, at_y % 2)):
            for t in range(3):
                send[3 * n + t] = tiles[t]


def level2_rows(source, odd_axes, factor, x2, y2, z2):
    rows = []
    for i in range(x2):
        total = None
        for p in (1,) if odd_axes[0] else (0, 1):
            for q in (1,) if odd_axes[1] else (0, 1):
                term = source[2 * i + p, pl.ds(q, y2, stride=2), :]
                total = term if total is None else total + term
        rows.append(total)
    flat = jnp.concatenate(rows, axis=0)
    flat = factor * times_table(flat, pair_table(LANES, LANES, odd_axes[2]))
    lane = lane_of((y2, LANES))
    packed = jnp.zeros((y2, LANES), F32)
    for i in range(x2):
        mask = (lane >= i * z2) & (lane < (i + 1) * z2)
        packed = jnp.where(mask, turn(flat[i * y2:(i + 1) * y2], i * z2, 1), packed)
    return packed


def near_kernel(counts, devices, where_ref, ring, *refs):
    n_x = 1 if counts[0] == 2 else 2
    halos_x = refs[:n_x]
    main_two, main_one = refs[n_x:n_x + 2]
    diagonals, (coarse2, copies, level1, left) = refs[n_x + 2:3 * n_x + 2], refs[3 * n_x + 2:]
    n, bx1, by1, _ = ring.shape
    at_x, at_y, _ = position(where_ref)
    sides = [
        neighbours(counts[0], at_x, diagonals[k][...], diagonals[k - 2][...]) for k in range(2)
    ]
    rest = []
    for one, two in zip(*sides):
        rows = neighbours(counts[1], at_y, one, two)
        rest.append(jnp.concatenate(rows[::-1], axis=1))
    whole = []
    for a in range(n):
        below, above = neighbours(counts[0], at_x, halos_x[0][a], halos_x[-1][a])
        rows = neighbours(counts[1], at_y, main_one[a], main_two[a])
        rows = jnp.concatenate(rows[::-1], axis=1)
        low, high = (diagonal_tiles(*(side[3 * a + k] for k in range(3))) for side in rest)
        low = low[::-1]
        rows = jnp.concatenate(
            [tile[None] for tile in low] + [rows] + [tile[None] for tile in high], axis=0
        )
        block = jnp.concatenate([below, ring[a], above], axis=0)
        whole.append(jnp.concatenate([block, rows], axis=1))
    whole = unpack_level1(whole)
    rhs1, weight1 = whole[:2]
    faces1 = tuple(whole[2:])
    field1 = weight1 * rhs1
    field1 = sweep(field1, rhs1, weight1, faces1)
    for a, values in enumerate([field1] + whole):
        level1[a] = values
    mine = slice(NEAR, NEAR + bx1)
    inner = weight1[mine]
    diag1 = RELAX / jnp.where(inner > 0.0, inner, 1.0)
    remain = rhs1[mine] - diag1 * field1[mine] + pull(field1, faces1)[mine]
    left[...] = remain
    packed = level2_rows(left, (False,) * 3, 0.125, bx1 // 2, by1 // 2, LANES // 4)
    blocks = LANES // (LANES // 4)
    shift = position(where_ref)[2] % blocks * (LANES // blocks)
    slots = [pltpu.roll(values, shift, 1) for values in [packed] + [coarse2[a] for a in range(4)]]
    for d in range(devices):
        for a in range(5):
            copies[d, a] = slots[a]


def inner_sweep(values, rhs, weight, faces, first):
    part = slice(first, rhs.shape[0] - first)
    below = slice(first - 1, rhs.shape[0] - first - 1)
    bx, by, bz = faces
    centre = values[1:-1]
    near = bx[part] * values[2:] + bx[below] * values[:-2]
    near = near + (by[part] * turn(centre, -1, 1) + turn(by[part] * centre, 1, 1))
    near = near + (bz[part] * turn(centre, -1, 2) + turn(bz[part] * centre, 1, 2))
    return KEEP * centre + weight[part] * (rhs[part] + near)


def halve(values, odd_axis, step):
    half = values.shape[0] // 2
    even = [values[2 * i:2 * i + 1] for i in range(half)]
    odd = [values[2 * i + 1:2 * i + 2] for i in range(half)]
    if odd_axis != 0:
        odd = [a + b for a, b in zip(even, odd)]
    values = jnp.concatenate(odd, axis=0)
    for axis in (1, 2):
        next_one = turn(values, -step, axis)
        values = next_one if odd_axis == axis else values + next_one
    return values


def double(values, step):
    values = values + turn(values, step, 1)
    values = values + turn(values, step, 2)
    return jnp.concatenate([values[i // 2:i // 2 + 1] for i in range(2 * values.shape[0])], axis=0)


def coarse_levels(mass, faces, y, z):
    levels = []
    for level in range(2, LEVELS):
        step = 2 ** (level - 2)
        bx, by, bz = faces
        row = lax.broadcasted_iota(jnp.int32, by.shape, 1)
        lane = lane_of(bz.shape)
        upper = (
            bx,
            jnp.where(row == (y - 1) * step, 0.0, by),
            jnp.where(lane == (z - 1) * step, 0.0, bz),
        )
        lower = (below_x(bx), turn(upper[1], step, 1), turn(upper[2], step, 2))
        mass = jnp.where((row % step == 0) & (lane % step == 0), mass, 0.0)
        diag = mass + bx + lower[0] + by + lower[1] + bz + lower[2]
        levels.append((diag, relaxer(mass, diag), upper, lower))
        if level < LEVELS - 1:
            faces = tuple(0.0625 * halve(face, axis, step) for axis, face in enumerate(faces))
            mass = 0.125 * halve(mass, -1, step)
            y, z = y // 2, z // 2
    return levels


def coupled(values, upper, lower, step):
    ups = (above_x(values), turn(values, -step, 1), turn(values, -step, 2))
    downs = (below_x(values), turn(values, step, 1), turn(values, step, 2))
    x, y, z = (u * up + l * down for u, up, l, down in zip(upper, ups, lower, downs))
    return (y + z) + x if values.shape[0] > 1 else y + z


def coarse_cycle(level, rhs, levels):
    step = 2 ** (level - 2)
    diag, weight, upper, lower = levels[level - 2]
    scaled = tuple(tuple(weight * b for b in faces) for faces in (upper, lower))
    source = weight * rhs

    def relax(field):
        return (KEEP * field + source) + coupled(field, *scaled, step)

    field = source
    if level == LEVELS - 1:
        for _ in range(BOTTOM - 1):
            field = relax(field)
        return field
    for _ in range(SWEEPS - 1):
        field = relax(field)
    remain = (rhs - diag * field) + coupled(field, upper, lower, step)
    correction = coarse_cycle(level + 1, 0.125 * halve(remain, -1, step), levels)
    field = field + double(correction, step)
    for _ in range(SWEEPS):
        field = relax(field)
    return field


def spread_out(counts, slots, whole):
    gx, gy, gz = counts
    y2 = slots.shape[-2]
    x2 = whole.shape[0] // gx
    z2 = LANES // x2
    lane = lane_of((y2, LANES))
    for i in range(gx):
        for j in range(gy):
            for x in range(x2):
                for part in range(whole.shape[2] // LANES):
                    total = None
                    for k in range(LANES // z2):
                        column = part * (LANES // z2) + k
                        if column < gz:
                            block = slots[(i * gy + j) * gz + column]
                            at = (x + k) * z2 % LANES
                            mask = (lane >= at) & (lane < at + z2)
                            if total is None:
                                total = jnp.where(mask, block, 0.0)
                            total = jnp.where(mask, block, total)
                    if x:
                        total = turn(total, -x * z2, 1)
                    lanes = slice(part * LANES, (part + 1) * LANES)
                    whole[i * x2 + x, j * y2:(j + 1) * y2, lanes] = total


def up_kernel(counts, where_ref, gathered, level1, *refs):
    kept, weight, rhs, bx, by, bz = zip(refs[0:12:2], refs[1:12:2])
    out, whole, second, lift, spread_m, spread_h, field_m, field_h, half_m, half_h = refs[12:]
    gx, gy, gz = counts
    at_x, at_y, at_z = position(where_ref)
    sx, sy, sz = out.shape
    x1, y1 = sx // 2, sy // 2
    x2, y2, z2 = x1 // 2, y1 // 2, sz // 4
    columns = max(LANES, gz * z2)
    for a in range(5):
        spread_out(counts, gathered.at[:, a], whole.at[a])
    levels = coarse_levels(whole[1], (whole[2], whole[3], whole[4]), gy * y2, gz * z2)
    correction = coarse_cycle(2, whole[0], levels)

    wide = gx * x2
    half = NEAR // 2
    ex1, ey1 = x1 + 2 * NEAR, y1 + 2 * NEAR
    second[:half] = jnp.zeros((half,) + correction.shape[1:], F32)
    second[half:half + wide] = correction
    second[half + wide:] = jnp.zeros((half,) + correction.shape[1:], F32)
    window = second[pl.ds(at_x * x2, x2 + NEAR)]
    rows = correction.shape[1]
    row = iota2((columns, LANES), 0)
    col = iota2((columns, LANES), 1)
    place = jnp.where(col < LANES * 3 // 4, col, col - LANES)
    table_z = (row == at_z * z2 + lax.shift_right_arithmetic(place, 1)).astype(F32)
    flat = times_table(window.reshape((x2 + NEAR) * rows, columns), table_z)
    flat = flat.reshape(x2 + NEAR, rows, LANES)
    flat = pltpu.roll(flat, (rows - at_y * y2) % rows, 1)
    for i in range(x2 + NEAR):
        for q in range(2):
            lift[i, pl.ds(q, y2, stride=2), :] = flat[i, :y2]
            lift[i, pl.ds(y1 + q, half, stride=2), :] = flat[i, y2:y2 + half]
            lift[i, pl.ds(y1 + NEAR + q, half, stride=2), :] = flat[i, rows - half:]
    lifted = jnp.concatenate([lift[i // 2][None] for i in range(ex1)], axis=0)
    field1, rhs1, weight1 = level1[0], level1[1], level1[2]
    faces1 = (level1[3], level1[4], level1[5])
    field1 = (field1 + jnp.where(weight1 > 0.0, lifted, 0.0))[1:-1]
    for n in range(SWEEPS):
        field1 = inner_sweep(field1, rhs1, weight1, faces1, 2 + n)

    ex, ey = sx + 2 * HALO, sy + 2 * HALO
    near = field1.reshape((x1 + 2) * ey1, LANES)
    row = iota2((LANES, 2 * LANES), 0)
    col = iota2((LANES, 2 * LANES), 1)
    lifted = times_table(near, (col // 2 == row).astype(F32))
    quarter = NEAR // 2
    for k, spread in enumerate((spread_m, spread_h)):
        block = lifted[:, k * LANES:(k + 1) * LANES].reshape(x1 + 2, ey1, LANES)
        for i in range(x1 + 2):
            for q in range(2):
                spread[i, pl.ds(q, y1, stride=2), :] = block[i, :y1]
                spread[i, pl.ds(sy + q, quarter, stride=2), :] = block[i, y1:y1 + quarter]
                spread[i, pl.ds(sy + HALO + q, quarter, stride=2), :] = block[i, ey1 - quarter:]
    before, after = (field_m, field_h), (half_m, half_h)
    first = HALO - 2
    for x in range(first, ex - first):
        for k, spread in enumerate((spread_m, spread_h)):
            before[k][x] = kept[k][x] + spread[(x - first) // 2]

    lane = lane_of((ey, LANES))

    def sweep_out(x):
        centre, around = pull_slab(before, bx, by, bz, x, lane)
        for k in range(2):
            after[k][x] = KEEP * centre[k] + weight[k][x] * (rhs[k][x] + around[k])

    each(first + 1, ex - first - 1, sweep_out)

    def sweep_own(x):
        centre, around = pull_slab(after, bx, by, bz, x, lane)
        value = KEEP * centre[0] + weight[0][x] * (rhs[0][x] + around[0])
        out[x - HALO] = value[:sy]

    each(HALO, ex - HALO, sweep_own)


def run(kernel, outs, where, arrays, scratch=(), grant=16, micros=1, aliases={}):
    return pl.pallas_call(
        kernel,
        out_shape=tuple(jax.ShapeDtypeStruct(shape, F32) for shape in outs),
        in_specs=[SM] * len(where) + [VM] * len(arrays),
        out_specs=tuple(VM for _ in outs),
        input_output_aliases=aliases,
        scratch_shapes=[pltpu.VMEM(shape, F32) for shape in scratch],
        compiler_params=pltpu.CompilerParams(vmem_limit_bytes=grant * 1024 * 1024),
        cost_estimate=pl.CostEstimate(
            flops=0, bytes_accessed=int(micros * 3.6e6), transcendentals=0
        ),
    )(*where, *arrays)


def partners(count, k):
    partner = list(range(count))
    for low in range(k, count - 1, 2):
        partner[low], partner[low + 1] = low + 1, low
    return partner


def swaps(axis, sends, other=None):
    count = lax.axis_size(axis)
    got = []
    for k, block in enumerate(sends):
        partner = partners(count, k)
        if k == 1 and other is None:
            partner[0], partner[-1] = count - 1, 0
        if k == 0 or other is None:
            got.append(lax.ppermute(block, axis, list(enumerate(partner))))
            continue
        rows = lax.axis_size(other)
        pairs = []
        for row in range(rows):
            for i in range(count):
                ends = [(row, i), (min(row ^ 1, rows - 1) if partner[i] == i else row, partner[i])]
                if axis < other:
                    pairs.append(tuple(at * rows + line for line, at in ends))
                else:
                    pairs.append(tuple(line * count + at for line, at in ends))
        got.append(lax.ppermute(block, tuple(sorted((axis, other))), pairs))
    return got


def diagonal_swaps(sends):
    count_x, count_y = lax.axis_size("gx"), lax.axis_size("gy")
    got = []
    for n, block in enumerate(sends):
        xs, ys = partners(count_x, n // 2), partners(count_y, n % 2)
        pairs = [
            (x * count_y + y, xs[x] * count_y + ys[y])
            for x in range(count_x)
            for y in range(count_y)
        ]
        got.append(lax.ppermute(block, ("gx", "gy"), pairs))
    return got


def local(initial, right_side, alpha, beta_x, beta_y, beta_z):
    axes = ("gx", "gy", "gz")
    counts = tuple(lax.axis_size(axis) for axis in axes)
    devices = counts[0] * counts[1] * counts[2]
    where = (lax.axis_index("gx") * STRIDE + lax.axis_index("gy")) * STRIDE + lax.axis_index("gz")
    where = (where.astype(jnp.int32).reshape(1),)
    ins = (initial, right_side, alpha, beta_x, beta_y, beta_z)
    sx, sy, sz = initial.shape
    n_x = 1 if counts[0] == 2 else 2
    ex, ey = sx + 2 * HALO, sy + 2 * HALO
    fine = (ex, ey, LANES)

    *sends_x, two_y, one_y, first, second = run(
        functools.partial(faces_kernel, counts),
        [(6, HALO, sy, LANES)] * n_x
        + [(6, sx, HALO, LANES)] * 2
        + [(sx // 2, sy, LANES)] * 2,
        where,
        ins,
        grant=60,
    )
    main_x = tuple(swaps("gx", sends_x, "gy"))
    main_y = tuple(swaps("gy", (one_y, two_y))[::-1])
    got = swaps("gz", (first, second), "gy")
    zpack, *sends = run(
        functools.partial(halo_z_kernel, counts),
        [(sx, sy, LANES)] + [(HALO, sy, LANES)] * n_x,
        where,
        tuple(got),
    )
    halos_x = tuple(swaps("gx", sends, "gy"))
    x1, y1 = sx // 2, sy // 2
    *laid, coarse2, coeffs1 = run(
        functools.partial(coefficient_kernel, counts),
        [fine] * 12 + [(4, y1 // 2, LANES), (5, x1, y1, LANES)],
        where,
        ins + (zpack,) + main_x,
        [(4, x1, y1, 2 * LANES), (4, x1, y1, LANES)],
        micros=2,
    )
    two_y, one_y = run(
        functools.partial(corners_kernel, counts),
        [(21 + sx, HALO, LANES)] * 2,
        where,
        (zpack,) + main_x + halos_x + (coarse2,),
    )
    rest_y = tuple(swaps("gy", (one_y, two_y), "gz")[::-1])
    outs = run(
        functools.partial(down_kernel, counts),
        [fine] * 12
        + [(3, x1, y1, LANES)]
        + [(3, NEAR, y1, LANES)] * n_x
        + [(3, x1, NEAR, LANES)] * 2
        + [(9, NEAR, LANES)] * (2 * n_x)
        + [fine] * 4,
        where,
        (zpack,) + tuple(laid) + halos_x + main_y + rest_y + (coeffs1,),
        [fine] * 5 + [(3, x1, y1, 2 * LANES), (ey, LANES)],
        24,
        micros=4,
        aliases={n + 2: n for n in range(12)},
    )
    laid, own1, outs = outs[:12], outs[12], outs[13:]
    sends_x, (two_y, one_y), outs = outs[:n_x], outs[n_x:n_x + 2], outs[n_x + 2:]
    sends_xy, fine_arrays = outs[:2 * n_x], outs[2 * n_x:]
    fine_arrays = tuple(fine_arrays) + tuple(laid[2:4]) + tuple(laid[6:])

    near_x = tuple(swaps("gx", sends_x, "gy"))
    near_y = tuple(swaps("gy", (one_y, two_y), "gz")[::-1])
    near_xy = tuple(diagonal_swaps(sends_xy))
    copies, level1 = run(
        functools.partial(near_kernel, counts, devices),
        [(devices, 5, y1 // 2, LANES), (6, x1 + 2 * NEAR, y1 + 2 * NEAR, LANES)],
        where,
        (own1,) + near_x + near_y + near_xy + (coarse2,),
        [(x1, y1 + 2 * NEAR, LANES)],
    )

    gathered = lax.all_to_all(copies, axes, 0, 0, tiled=True)
    wide, rows = counts[0] * x1 // 2, counts[1] * y1 // 2
    columns = max(LANES, counts[2] * sz // 4)
    (result,) = run(
        functools.partial(up_kernel, counts),
        [(sx, sy, sz)],
        where,
        (gathered, level1) + tuple(fine_arrays),
        [(5, wide, rows, columns), (wide + NEAR, rows, columns)]
        + [(x1 // 2 + NEAR, y1 + 2 * NEAR, LANES)]
        + [(x1 + 2, ey, LANES)] * 2
        + [fine] * 4,
        24,
        micros=4,
    )
    return result


def solution(mesh):
    spec = P("gx", "gy", "gz")
    return jax.shard_map(
        local, mesh=mesh, in_specs=(spec,) * 6, out_specs=spec, check_vma=False
    )
```

```python
import functools

import jax
import jax.numpy as jnp
from jax import lax
from jax.experimental import pallas as pl
from jax.experimental.pallas import tpu as pltpu
from jax.sharding import PartitionSpec as P

LEVELS = 6
SWEEPS = 2
BOTTOM = 8
WEIGHT = 0.25 ** (LEVELS - 1)
RELAX = 2.0 / 3.0
KEEP = 1.0 / 3.0

HALO = 4
NEAR = 4
LANES = 128
PLACE = (0, 11, 21, 31, 41, 51)
DEPTH = (11, 10, 10, 10, 10, 11)
SIDE = LANES // 2
STRIDE = 256

VM = pl.BlockSpec(memory_space=pltpu.VMEM)
SM = pl.BlockSpec(memory_space=pltpu.SMEM)
F32 = jnp.float32


def position(where_ref):
    code = where_ref[0]
    return code // (STRIDE * STRIDE), code // STRIDE % STRIDE, code % STRIDE


def lane_of(shape):
    return lax.broadcasted_iota(jnp.int32, shape, len(shape) - 1)


def pick(flag, yes, no):
    return jnp.where(jnp.full(yes.shape, flag, jnp.int32) == 1, yes, no)


def neighbours(count, place, one, two):
    if count == 2:
        two = jnp.zeros_like(one)
    else:
        ends = jnp.full(two.shape, place, jnp.int32)
        two = jnp.where((ends == 0) | (ends == count - 1), 0.0, two)
    return pick(place % 2, one, two), pick(place % 2, two, one)


def turn(values, shift, axis):
    return pltpu.roll(values, shift % values.shape[axis], axis)


def parts_of(values):
    high = values.astype(jnp.bfloat16)
    return high, (values - high.astype(F32)).astype(jnp.bfloat16)


def times_table(values, table):
    table = table.astype(jnp.bfloat16)
    total = None
    for part in reversed(parts_of(values)):
        term = jnp.dot(part, table, preferred_element_type=F32)
        total = term if total is None else total + term
    return total


def iota2(shape, axis):
    return lax.broadcasted_iota(jnp.int32, shape, axis)


def pair_table(rows, cols, odd):
    row = iota2((rows, cols), 0)
    col = iota2((rows, cols), 1)
    hit = (row == 2 * col + 1) if odd else (row // 2 == col)
    return hit.astype(F32)


def below_x(values):
    if values.shape[0] == 1:
        return jnp.zeros_like(values)
    return jnp.concatenate([jnp.zeros_like(values[:1]), values[:-1]], axis=0)


def above_x(values):
    if values.shape[0] == 1:
        return jnp.zeros_like(values)
    return jnp.concatenate([values[1:], jnp.zeros_like(values[:1])], axis=0)


def pull(values, faces, step=1):
    bx, by, bz = faces
    total = bx * above_x(values) + below_x(bx * values)
    total = total + (by * turn(values, -step, 1) + turn(by * values, step, 1))
    return total + (bz * turn(values, -step, 2) + turn(bz * values, step, 2))


def diagonal(mass, faces, coupled, step=1):
    bx, by, bz = faces
    _, cy, cz = coupled
    return mass + bx + below_x(bx) + by + turn(cy, step, 1) + bz + turn(cz, step, 2)


def relaxer(mass, diag):
    inside = mass > 0.0
    return jnp.where(inside, RELAX / jnp.where(inside, diag, 1.0), 0.0)


def sweep(values, rhs, weight, faces, step=1):
    return KEEP * values + weight * (rhs + pull(values, faces, step))


def faces_x(values, odd, n_x, width):
    head, tail = values[:, :width], values[:, values.shape[1] - width:]
    return [pick(odd, head, tail), pick(odd, tail, head)][:n_x]


def faces_y(values, odd, width):
    head, tail = values[:, :width], values[:, values.shape[1] - width:]
    return pick(odd, head, tail), pick(odd, tail, head)


def corner_sends(below, above, odd):
    packs = []
    for rows, sign in ((slice(0, 8), 1), (slice(below.shape[1] - 8, below.shape[1]), -1)):
        low = [below[3 - i, rows] for i in range(3)]
        high = [above[i, rows] for i in range(3)]
        row = iota2(low[0].shape, 0)
        row = row if sign == 1 else 7 - row
        pack = (
            jnp.where(row < 3, low[0], turn(low[2], 3 * sign, 0)),
            jnp.where(row < 2, low[1], turn(high[1], 2 * sign, 0)),
            jnp.where(row < 3, high[0], turn(high[2], 3 * sign, 0)),
        )
        packs.append([p[:4] if sign == 1 else p[4:] for p in pack])
    return [(pick(odd, h, t), pick(odd, t, h)) for h, t in zip(*packs)]


def inner_rows(tile, by):
    upper = iota2(tile.shape, 0) < 4
    return jnp.where(upper, turn(tile, -by, 0), turn(tile, by, 0))


def corner_tiles(first, second, third):
    zero = jnp.zeros_like(first)
    low = (zero, inner_rows(first, 3), second, first)
    return low, (third, inner_rows(second, 2), inner_rows(third, 3), zero)


def diagonal_sends(values, n_x, odd_x, odd_y):
    corners = []
    for slabs in ([values[i] for i in range(4)], [values[values.shape[0] - 1 - i] for i in range(4)]):
        for sign in (1, -1):
            row = iota2(slabs[0].shape, 0)
            row = row if sign == 1 else 7 - row
            tiles = (slabs[0], jnp.where(row < 3, slabs[1], turn(slabs[3], 3 * sign, 0)), slabs[2])
            corners.append([t[:4] if sign == 1 else t[4:] for t in tiles])
    sends = []
    for k_x in range(n_x):
        for k_y in range(2):
            head_x = odd_x if k_x == 0 else 1 - odd_x
            head_y = odd_y if k_y == 0 else 1 - odd_y
            sends.append(
                [
                    pick(head_x, pick(head_y, hh, ht), pick(head_y, th, tt))
                    for hh, ht, th, tt in zip(*corners)
                ]
            )
    return sends


def diagonal_tiles(first, second, third):
    return [first, second, third, inner_rows(second, 3)]


def faces_kernel(counts, where_ref, *refs):
    ins, refs = refs[:6], refs[6:]
    n_x = 1 if counts[0] == 2 else 2
    sends_x, (two_y, one_y, first, second) = refs[:n_x], refs[n_x:]
    odd_x, odd_y, odd = (place % 2 for place in position(where_ref))
    sx, sy, sz = ins[0].shape
    half = sx // 2
    lane = lane_of((half, sy, LANES))
    head = jnp.zeros((half, sy, LANES), F32)
    tail = head
    for a, ref in enumerate(ins):
        for send, face in zip(sends_x, faces_x(ref[...][None], odd_x, n_x, HALO)):
            send[a] = face[0]
        one_y[a], two_y[a] = faces_y(ref[...], odd_y, HALO)
        for g in range(2):
            values = ref[g * half:(g + 1) * half]
            at = SIDE * g + PLACE[a]
            mask = (lane >= at) & (lane < at + DEPTH[a])
            head = jnp.where(mask, turn(values, at, 2), head)
            tail = jnp.where(mask, turn(values, at + DEPTH[a], 2), tail)
    first[...] = pick(odd, head, tail)
    second[...] = pick(odd, tail, head)


def halo_z_kernel(counts, where_ref, one_ref, two_ref, zpack, *sends):
    at_x, _, at_z = position(where_ref)
    half = one_ref.shape[0]
    below, above = neighbours(counts[2], at_z, one_ref[...], two_ref[...])
    lane = lane_of(below.shape)
    zpack[:half] = jnp.where(lane < SIDE, above, turn(below, SIDE, 2))
    zpack[half:] = jnp.where(lane < SIDE, turn(above, SIDE, 2), below)
    for send, face in zip(sends, faces_x(zpack[...][None], at_x % 2, len(sends), HALO)):
        send[...] = face[0]


def corners_kernel(counts, where_ref, zpack, *refs):
    n_x = 1 if counts[0] == 2 else 2
    main_x, halos_x, (two_y, one_y) = refs[:n_x], refs[n_x:2 * n_x], refs[2 * n_x + 1:]
    at_x, at_y, _ = position(where_ref)
    for a in range(7):
        if a < 6:
            below, above = neighbours(counts[0], at_x, main_x[0][a], main_x[-1][a])
        else:
            below, above = neighbours(counts[0], at_x, halos_x[0][...], halos_x[-1][...])
        for n, pair in enumerate(corner_sends(below, above, at_y % 2)):
            one_y[3 * a + n], two_y[3 * a + n] = pair
    one_y[21:], two_y[21:] = faces_y(zpack[...], at_y % 2, HALO)


def each(first, last, body):
    for x in range(first, last):
        body(x)


def ring_up(main, halo, lane):
    main_up, halo_up = turn(main, -1, 1), turn(halo, -1, 1)
    last = lane == LANES - 1
    return jnp.where(last, halo_up, main_up), jnp.where(last, main_up, halo_up)


def ring_down(main, halo, lane):
    main_down, halo_down = turn(main, 1, 1), turn(halo, 1, 1)
    zero = lane == 0
    return jnp.where(zero, halo_down, main_down), jnp.where(zero, main_down, halo_down)


def pull_slab(field, bx, by, bz, x, lane):
    centre = [half[x] for half in field]
    out = []
    for k in range(2):
        c, face = centre[k], by[k][x]
        t = bx[k][x] * field[k][x + 1] + bx[k][x - 1] * field[k][x - 1]
        out.append(t + (face * turn(c, -1, 0) + turn(face * c, 1, 0)))
    faces = [half[x] for half in bz]
    ups = ring_up(centre[0], centre[1], lane)
    downs = ring_down(faces[0] * centre[0], faces[1] * centre[1], lane)
    return centre, [out[k] + (faces[k] * ups[k] + downs[k]) for k in range(2)]


def unpacked(packed, a, lane):
    at, depth = PLACE[a], DEPTH[a]
    axis = packed.ndim - 1
    right, left = turn(packed, -at, axis), turn(packed, SIDE - depth - at, axis)
    return jnp.where(lane < depth, right, jnp.where(lane >= LANES - depth, left, 0.0))


def rows_of(source, x, count, firsts, seconds):
    total = None
    for p in firsts:
        for q in seconds:
            term = source[x + p, pl.ds(q, count, stride=2), :]
            total = term if total is None else total + term
    return total


BOTH, ODD = (0, 1), (1,)


def to_level1(sums, first, count, table, factor):
    _, x1, y1, _ = sums.shape
    flat = sums[first:first + count].reshape(count * x1 * y1, 2 * LANES)
    return factor * times_table(flat, table).reshape(count, x1, y1, LANES)


def coefficient_kernel(counts, where_ref, *refs):
    ins, refs = refs[:7], refs[7:]
    n_x = 1 if counts[0] == 2 else 2
    main_x, refs = refs[:n_x], refs[n_x:]
    arrays, (coarse2, coeffs1, sums, pairing) = refs[:12], refs[12:]
    sx, sy, sz = ins[0].shape
    at_x = position(where_ref)[0]
    x1, y1 = sx // 2, sy // 2
    lane = lane_of((sx, sy, LANES))
    lanes = [slice(k * LANES, (k + 1) * LANES) for k in range(2)]
    mine = slice(HALO, HALO + sx)
    for a in range(6):
        to = arrays[2 * a]
        below, above = neighbours(counts[0], at_x, main_x[0][a], main_x[-1][a])
        to[:HALO, :sy] = below
        to[mine, :sy] = ins[a][...]
        to[HALO + sx:, :sy] = above
        arrays[2 * a + 1][mine, :sy] = unpacked(ins[6][...], a, lane)
    for n, (firsts, seconds) in enumerate(((BOTH, BOTH), (ODD, BOTH), (BOTH, ODD), (BOTH, BOTH))):
        for k in range(2):
            for i in range(x1):
                source = arrays[2 * (n + 2) + k]
                sums[n, i, :, lanes[k]] = rows_of(source, HALO + 2 * i, y1, firsts, seconds)
    pairs = pair_table(2 * LANES, LANES, False)
    odds = pair_table(2 * LANES, LANES, True)
    paired = to_level1(sums, 0, 3, pairs, 0.0625)
    mass1 = (2.0 * WEIGHT) * paired[0]
    faces1 = (paired[1], paired[2], to_level1(sums, 3, 1, odds, 0.0625)[0])
    diag1 = mass1 + faces1[0] + below_x(faces1[0])
    diag1 = diag1 + faces1[1] + faces1[2] + turn(faces1[2], 1, 2)
    for n, values in enumerate((mass1, diag1) + faces1):
        coeffs1[n] = values
    parts = (
        (mass1, False, False, False, 0.125),
        (faces1[0], True, False, False, 0.0625),
        (faces1[1], False, True, False, 0.0625),
        (faces1[2], False, False, True, 0.0625),
    )
    for n, (values, *odd_axes, factor) in enumerate(parts):
        pairing[n] = values
        coarse2[n] = level2_rows(pairing.at[n], odd_axes, factor, x1 // 2, y1 // 2, sz // 4)


def down_kernel(counts, where_ref, zpack, *refs):
    refs = refs[12:]
    n_x = 1 if counts[0] == 2 else 2
    halos_x = refs[:n_x]
    main_two, main_one, rest_two, rest_one, coeffs1 = refs[n_x:5 + n_x]
    flat, refs = refs[5 + n_x:17 + n_x], refs[17 + n_x:]
    arrays = tuple(zip(flat[::2], flat[1::2]))
    own1, refs = refs[0], refs[1:]
    sends, near_two, near_one, refs = refs[:n_x], refs[n_x], refs[n_x + 1], refs[n_x + 2:]
    sends_xy, refs = refs[:2 * n_x], refs[2 * n_x:]
    kept_m, kept_h, weight_m, weight_h = refs[:4]
    packs, half_m, half_h, diag_m, diag_h, sums, left = refs[4:]
    field, rhs, alpha, bx, by, bz = arrays
    sx, sy, sz = zpack.shape
    ex, ey = sx + 2 * HALO, sy + 2 * HALO
    at_x, at_y, _ = position(where_ref)

    rest = neighbours(counts[1], at_y, rest_one[...], rest_two[...])
    rest = jnp.concatenate(rest[::-1], axis=1)
    for a in range(7):
        if a < 6:
            to = arrays[a][0]
            rows = neighbours(counts[1], at_y, main_one[a], main_two[a])
            rows = jnp.concatenate(rows[::-1], axis=1)
        else:
            to = packs
            rows = rest[21:]
            below, above = neighbours(counts[0], at_x, halos_x[0][...], halos_x[-1][...])
            to[:HALO, :sy] = below
            to[HALO + sx:, :sy] = above
        to[HALO:HALO + sx, sy:] = rows
        low, high = corner_tiles(*(rest[3 * a + n] for n in range(3)))
        for n in range(HALO):
            to[n, sy:] = low[n]
            to[HALO + sx + n, sy:] = high[n]
    lane = lane_of((ey, LANES))
    lane_low = lane_of((2 * HALO, LANES))

    def unpack_rows(x):
        packed = packs[x, sy:]
        for a in range(6):
            arrays[a][1][x, sy:] = unpacked(packed, a, lane_low)

    def unpack(x):
        packed = packs[x]
        for a in range(6):
            arrays[a][1][x] = unpacked(packed, a, lane)

    each(0, HALO, unpack)
    each(HALO, HALO + sx, unpack_rows)
    each(HALO + sx, ex, unpack)
    halfway, weight, kept = (half_m, half_h), (weight_m, weight_h), (kept_m, kept_h)
    diag = (diag_m, diag_h)

    def first_sweep(x):
        faces = [half[x] for half in bz]
        downs = ring_down(faces[0], faces[1], lane)
        centre, near = pull_slab(field, bx, by, bz, x, lane)
        for k in range(2):
            face = by[k][x]
            mass = WEIGHT * alpha[k][x]
            d = mass + bx[k][x] + bx[k][x - 1] + face + turn(face, 1, 0) + faces[k] + downs[k]
            w = relaxer(mass, d)
            diag[k][x] = d
            weight[k][x] = w
            halfway[k][x] = KEEP * centre[k] + w * (rhs[k][x] + near[k])

    each(1, ex - 1, first_sweep)

    def second_sweep(x):
        centre, near = pull_slab(halfway, bx, by, bz, x, lane)
        for k in range(2):
            kept[k][x] = KEEP * centre[k] + weight[k][x] * (rhs[k][x] + near[k])

    each(2, ex - 2, second_sweep)

    def residual(x):
        centre, near = pull_slab(kept, bx, by, bz, x, lane)
        for k in range(2):
            halfway[k][x] = rhs[k][x] - diag[k][x] * centre[k] + near[k]

    each(HALO, ex - HALO, residual)

    x1, y1 = sx // 2, sy // 2
    for k in range(2):
        lanes = slice(k * LANES, (k + 1) * LANES)
        for i in range(x1):
            x = HALO + 2 * i
            sums[0, i, :, lanes] = rows_of(halfway[k], x, y1, BOTH, BOTH)
            left[...] = turn(by[k][x] + by[k][x + 1], 1, 0)
            sums[1, i, :, lanes] = left[pl.ds(0, y1, stride=2), :]
        sums[2, 0, :, lanes] = rows_of(bx[k], HALO - 1, y1, (0,), BOTH)
        sums[2, 1:, :, lanes] = jnp.zeros((x1 - 1, y1, LANES), F32)
    rhs1, low_y, low_x = to_level1(sums, 0, 3, pair_table(2 * LANES, LANES, False), 0.0625)
    weight1 = relaxer(coeffs1[0], coeffs1[1] + low_y + low_x)
    for n, values in enumerate((2.0 * rhs1, weight1, coeffs1[2], coeffs1[3], coeffs1[4])):
        own1[n] = values
        for send, face in zip(sends, faces_x(values[None], at_x % 2, n_x, NEAR)):
            send[n] = face[0]
        near_one[n], near_two[n] = faces_y(values, at_y % 2, NEAR)
        for send, tiles in zip(sends_xy, diagonal_sends(values, n_x, at_x % 2, at_y % 2)):
            for t in range(3):
                send[3 * n + t] = tiles[t]


def level2_rows(source, odd_axes, factor, x2, y2, z2):
    rows = []
    for i in range(x2):
        total = None
        for p in (1,) if odd_axes[0] else (0, 1):
            for q in (1,) if odd_axes[1] else (0, 1):
                term = source[2 * i + p, pl.ds(q, y2, stride=2), :]
                total = term if total is None else total + term
        rows.append(total)
    flat = jnp.concatenate(rows, axis=0)
    flat = factor * times_table(flat, pair_table(LANES, LANES, odd_axes[2]))
    lane = lane_of((y2, LANES))
    packed = jnp.zeros((y2, LANES), F32)
    for i in range(x2):
        mask = (lane >= i * z2) & (lane < (i + 1) * z2)
        packed = jnp.where(mask, turn(flat[i * y2:(i + 1) * y2], i * z2, 1), packed)
    return packed


def near_kernel(counts, devices, where_ref, ring, *refs):
    n_x = 1 if counts[0] == 2 else 2
    halos_x = refs[:n_x]
    main_two, main_one = refs[n_x:n_x + 2]
    diagonals, (coarse2, copies, level1, left) = refs[n_x + 2:3 * n_x + 2], refs[3 * n_x + 2:]
    n, bx1, by1, _ = ring.shape
    at_x, at_y, _ = position(where_ref)
    sides = [
        neighbours(counts[0], at_x, diagonals[k][...], diagonals[k - 2][...]) for k in range(2)
    ]
    rest = []
    for one, two in zip(*sides):
        rows = neighbours(counts[1], at_y, one, two)
        rest.append(jnp.concatenate(rows[::-1], axis=1))
    whole = []
    for a in range(n):
        below, above = neighbours(counts[0], at_x, halos_x[0][a], halos_x[-1][a])
        rows = neighbours(counts[1], at_y, main_one[a], main_two[a])
        rows = jnp.concatenate(rows[::-1], axis=1)
        low, high = (diagonal_tiles(*(side[3 * a + k] for k in range(3))) for side in rest)
        low = low[::-1]
        rows = jnp.concatenate(
            [tile[None] for tile in low] + [rows] + [tile[None] for tile in high], axis=0
        )
        block = jnp.concatenate([below, ring[a], above], axis=0)
        whole.append(jnp.concatenate([block, rows], axis=1))
    rhs1, weight1 = whole[:2]
    faces1 = tuple(whole[2:])
    field1 = weight1 * rhs1
    field1 = sweep(field1, rhs1, weight1, faces1)
    for a, values in enumerate([field1] + whole):
        level1[a] = values
    mine = slice(NEAR, NEAR + bx1)
    inner = weight1[mine]
    diag1 = RELAX / jnp.where(inner > 0.0, inner, 1.0)
    remain = rhs1[mine] - diag1 * field1[mine] + pull(field1, faces1)[mine]
    left[...] = remain
    packed = level2_rows(left, (False,) * 3, 0.125, bx1 // 2, by1 // 2, LANES // 4)
    blocks = LANES // (LANES // 4)
    shift = position(where_ref)[2] % blocks * (LANES // blocks)
    slots = [pltpu.roll(values, shift, 1) for values in [packed] + [coarse2[a] for a in range(4)]]
    for d in range(devices):
        for a in range(n):
            copies[d, a] = slots[a]


def inner_sweep(values, rhs, weight, faces, first):
    part = slice(first, rhs.shape[0] - first)
    below = slice(first - 1, rhs.shape[0] - first - 1)
    bx, by, bz = faces
    centre = values[1:-1]
    near = bx[part] * values[2:] + bx[below] * values[:-2]
    near = near + (by[part] * turn(centre, -1, 1) + turn(by[part] * centre, 1, 1))
    near = near + (bz[part] * turn(centre, -1, 2) + turn(bz[part] * centre, 1, 2))
    return KEEP * centre + weight[part] * (rhs[part] + near)


def halve(values, odd_axis, step):
    half = values.shape[0] // 2
    even = [values[2 * i:2 * i + 1] for i in range(half)]
    odd = [values[2 * i + 1:2 * i + 2] for i in range(half)]
    if odd_axis != 0:
        odd = [a + b for a, b in zip(even, odd)]
    values = jnp.concatenate(odd, axis=0)
    for axis in (1, 2):
        next_one = turn(values, -step, axis)
        values = next_one if odd_axis == axis else values + next_one
    return values


def double(values, step):
    values = values + turn(values, step, 1)
    values = values + turn(values, step, 2)
    return jnp.concatenate([values[i // 2:i // 2 + 1] for i in range(2 * values.shape[0])], axis=0)


def coarse_levels(mass, faces, y, z):
    levels = []
    for level in range(2, LEVELS):
        step = 2 ** (level - 2)
        bx, by, bz = faces
        row = lax.broadcasted_iota(jnp.int32, by.shape, 1)
        lane = lane_of(bz.shape)
        upper = (
            bx,
            jnp.where(row == (y - 1) * step, 0.0, by),
            jnp.where(lane == (z - 1) * step, 0.0, bz),
        )
        lower = (below_x(bx), turn(upper[1], step, 1), turn(upper[2], step, 2))
        mass = jnp.where((row % step == 0) & (lane % step == 0), mass, 0.0)
        diag = mass + bx + lower[0] + by + lower[1] + bz + lower[2]
        levels.append((diag, relaxer(mass, diag), upper, lower))
        if level < LEVELS - 1:
            faces = tuple(0.0625 * halve(face, axis, step) for axis, face in enumerate(faces))
            mass = 0.125 * halve(mass, -1, step)
            y, z = y // 2, z // 2
    return levels


def coupled(values, upper, lower, step):
    ups = (above_x(values), turn(values, -step, 1), turn(values, -step, 2))
    downs = (below_x(values), turn(values, step, 1), turn(values, step, 2))
    x, y, z = (u * up + l * down for u, up, l, down in zip(upper, ups, lower, downs))
    return (y + z) + x if values.shape[0] > 1 else y + z


def coarse_cycle(level, rhs, levels):
    step = 2 ** (level - 2)
    diag, weight, upper, lower = levels[level - 2]
    scaled = tuple(tuple(weight * b for b in faces) for faces in (upper, lower))
    source = weight * rhs

    def relax(field):
        return (KEEP * field + source) + coupled(field, *scaled, step)

    field = source
    if level == LEVELS - 1:
        for _ in range(BOTTOM - 1):
            field = relax(field)
        return field
    for _ in range(SWEEPS - 1):
        field = relax(field)
    remain = (rhs - diag * field) + coupled(field, upper, lower, step)
    correction = coarse_cycle(level + 1, 0.125 * halve(remain, -1, step), levels)
    field = field + double(correction, step)
    for _ in range(SWEEPS):
        field = relax(field)
    return field


def spread_out(counts, slots, whole):
    gx, gy, gz = counts
    y2 = slots.shape[-2]
    x2 = whole.shape[0] // gx
    z2 = LANES // x2
    lane = lane_of((y2, LANES))
    for i in range(gx):
        for j in range(gy):
            for x in range(x2):
                for part in range(whole.shape[2] // LANES):
                    total = None
                    for k in range(LANES // z2):
                        column = part * (LANES // z2) + k
                        if column < gz:
                            block = slots[(i * gy + j) * gz + column]
                            at = (x + k) * z2 % LANES
                            mask = (lane >= at) & (lane < at + z2)
                            if total is None:
                                total = jnp.where(mask, block, 0.0)
                            total = jnp.where(mask, block, total)
                    if x:
                        total = turn(total, -x * z2, 1)
                    lanes = slice(part * LANES, (part + 1) * LANES)
                    whole[i * x2 + x, j * y2:(j + 1) * y2, lanes] = total


def up_kernel(counts, where_ref, gathered, level1, *refs):
    kept, weight, rhs, bx, by, bz = zip(refs[0:12:2], refs[1:12:2])
    out, whole, second, lift, spread_m, spread_h, field_m, field_h, half_m, half_h = refs[12:]
    gx, gy, gz = counts
    at_x, at_y, at_z = position(where_ref)
    sx, sy, sz = out.shape
    x1, y1 = sx // 2, sy // 2
    x2, y2, z2 = x1 // 2, y1 // 2, sz // 4
    columns = max(LANES, gz * z2)
    for a in range(5):
        spread_out(counts, gathered.at[:, a], whole.at[a])
    levels = coarse_levels(whole[1], (whole[2], whole[3], whole[4]), gy * y2, gz * z2)
    correction = coarse_cycle(2, whole[0], levels)

    wide = gx * x2
    half = NEAR // 2
    ex1, ey1 = x1 + 2 * NEAR, y1 + 2 * NEAR
    second[:half] = jnp.zeros((half,) + correction.shape[1:], F32)
    second[half:half + wide] = correction
    second[half + wide:] = jnp.zeros((half,) + correction.shape[1:], F32)
    window = second[pl.ds(at_x * x2, x2 + NEAR)]
    rows = correction.shape[1]
    row = iota2((columns, LANES), 0)
    col = iota2((columns, LANES), 1)
    place = jnp.where(col < LANES * 3 // 4, col, col - LANES)
    table_z = (row == at_z * z2 + lax.shift_right_arithmetic(place, 1)).astype(F32)
    flat = times_table(window.reshape((x2 + NEAR) * rows, columns), table_z)
    flat = flat.reshape(x2 + NEAR, rows, LANES)
    flat = pltpu.roll(flat, (rows - at_y * y2) % rows, 1)
    for i in range(x2 + NEAR):
        for q in range(2):
            lift[i, pl.ds(q, y2, stride=2), :] = flat[i, :y2]
            lift[i, pl.ds(y1 + q, half, stride=2), :] = flat[i, y2:y2 + half]
            lift[i, pl.ds(y1 + NEAR + q, half, stride=2), :] = flat[i, rows - half:]
    lifted = jnp.concatenate([lift[i // 2][None] for i in range(ex1)], axis=0)
    field1, rhs1, weight1 = level1[0], level1[1], level1[2]
    faces1 = (level1[3], level1[4], level1[5])
    field1 = (field1 + jnp.where(weight1 > 0.0, lifted, 0.0))[1:-1]
    for n in range(SWEEPS):
        field1 = inner_sweep(field1, rhs1, weight1, faces1, 2 + n)

    ex, ey = sx + 2 * HALO, sy + 2 * HALO
    near = field1.reshape((x1 + 2) * ey1, LANES)
    row = iota2((LANES, 2 * LANES), 0)
    col = iota2((LANES, 2 * LANES), 1)
    lifted = times_table(near, (col // 2 == row).astype(F32))
    quarter = NEAR // 2
    for k, spread in enumerate((spread_m, spread_h)):
        block = lifted[:, k * LANES:(k + 1) * LANES].reshape(x1 + 2, ey1, LANES)
        for i in range(x1 + 2):
            for q in range(2):
                spread[i, pl.ds(q, y1, stride=2), :] = block[i, :y1]
                spread[i, pl.ds(sy + q, quarter, stride=2), :] = block[i, y1:y1 + quarter]
                spread[i, pl.ds(sy + HALO + q, quarter, stride=2), :] = block[i, ey1 - quarter:]
    before, after = (field_m, field_h), (half_m, half_h)
    first = HALO - 2
    for x in range(first, ex - first):
        for k, spread in enumerate((spread_m, spread_h)):
            before[k][x] = kept[k][x] + spread[(x - first) // 2]

    lane = lane_of((ey, LANES))

    def sweep_out(x):
        centre, around = pull_slab(before, bx, by, bz, x, lane)
        for k in range(2):
            after[k][x] = KEEP * centre[k] + weight[k][x] * (rhs[k][x] + around[k])

    each(first + 1, ex - first - 1, sweep_out)

    def sweep_own(x):
        centre, around = pull_slab(after, bx, by, bz, x, lane)
        value = KEEP * centre[0] + weight[0][x] * (rhs[0][x] + around[0])
        out[x - HALO] = value[:sy]

    each(HALO, ex - HALO, sweep_own)


def run(kernel, outs, where, arrays, scratch=(), grant=16, micros=1, aliases={}):
    return pl.pallas_call(
        kernel,
        out_shape=tuple(jax.ShapeDtypeStruct(shape, F32) for shape in outs),
        in_specs=[SM] * len(where) + [VM] * len(arrays),
        out_specs=tuple(VM for _ in outs),
        input_output_aliases=aliases,
        scratch_shapes=[pltpu.VMEM(shape, F32) for shape in scratch],
        compiler_params=pltpu.CompilerParams(vmem_limit_bytes=grant * 1024 * 1024),
        cost_estimate=pl.CostEstimate(
            flops=0, bytes_accessed=int(micros * 3.6e6), transcendentals=0
        ),
    )(*where, *arrays)


def partners(count, k):
    partner = list(range(count))
    for low in range(k, count - 1, 2):
        partner[low], partner[low + 1] = low + 1, low
    return partner


def swaps(axis, sends, other=None):
    count = lax.axis_size(axis)
    got = []
    for k, block in enumerate(sends):
        partner = partners(count, k)
        if k == 1 and other is None:
            partner[0], partner[-1] = count - 1, 0
        if k == 0 or other is None:
            got.append(lax.ppermute(block, axis, list(enumerate(partner))))
            continue
        rows = lax.axis_size(other)
        pairs = []
        for row in range(rows):
            for i in range(count):
                ends = [(row, i), (min(row ^ 1, rows - 1) if partner[i] == i else row, partner[i])]
                if axis < other:
                    pairs.append(tuple(at * rows + line for line, at in ends))
                else:
                    pairs.append(tuple(line * count + at for line, at in ends))
        got.append(lax.ppermute(block, tuple(sorted((axis, other))), pairs))
    return got


def diagonal_swaps(sends):
    count_x, count_y = lax.axis_size("gx"), lax.axis_size("gy")
    got = []
    for n, block in enumerate(sends):
        xs, ys = partners(count_x, n // 2), partners(count_y, n % 2)
        pairs = [
            (x * count_y + y, xs[x] * count_y + ys[y])
            for x in range(count_x)
            for y in range(count_y)
        ]
        got.append(lax.ppermute(block, ("gx", "gy"), pairs))
    return got


def local(initial, right_side, alpha, beta_x, beta_y, beta_z):
    axes = ("gx", "gy", "gz")
    counts = tuple(lax.axis_size(axis) for axis in axes)
    devices = counts[0] * counts[1] * counts[2]
    where = (lax.axis_index("gx") * STRIDE + lax.axis_index("gy")) * STRIDE + lax.axis_index("gz")
    where = (where.astype(jnp.int32).reshape(1),)
    ins = (initial, right_side, alpha, beta_x, beta_y, beta_z)
    sx, sy, sz = initial.shape
    n_x = 1 if counts[0] == 2 else 2
    ex, ey = sx + 2 * HALO, sy + 2 * HALO
    fine = (ex, ey, LANES)

    *sends_x, two_y, one_y, first, second = run(
        functools.partial(faces_kernel, counts),
        [(6, HALO, sy, LANES)] * n_x
        + [(6, sx, HALO, LANES)] * 2
        + [(sx // 2, sy, LANES)] * 2,
        where,
        ins,
        grant=60,
    )
    main_x = tuple(swaps("gx", sends_x, "gy"))
    main_y = tuple(swaps("gy", (one_y, two_y))[::-1])
    got = swaps("gz", (first, second), "gy")
    zpack, *sends = run(
        functools.partial(halo_z_kernel, counts),
        [(sx, sy, LANES)] + [(HALO, sy, LANES)] * n_x,
        where,
        tuple(got),
    )
    halos_x = tuple(swaps("gx", sends, "gy"))
    x1, y1 = sx // 2, sy // 2
    *laid, coarse2, coeffs1 = run(
        functools.partial(coefficient_kernel, counts),
        [fine] * 12 + [(4, y1 // 2, LANES), (5, x1, y1, LANES)],
        where,
        ins + (zpack,) + main_x,
        [(4, x1, y1, 2 * LANES), (4, x1, y1, LANES)],
        micros=2,
    )
    two_y, one_y = run(
        functools.partial(corners_kernel, counts),
        [(21 + sx, HALO, LANES)] * 2,
        where,
        (zpack,) + main_x + halos_x + (coarse2,),
    )
    rest_y = tuple(swaps("gy", (one_y, two_y), "gx")[::-1])
    outs = run(
        functools.partial(down_kernel, counts),
        [fine] * 12
        + [(5, x1, y1, LANES)]
        + [(5, NEAR, y1, LANES)] * n_x
        + [(5, x1, NEAR, LANES)] * 2
        + [(15, NEAR, LANES)] * (2 * n_x)
        + [fine] * 4,
        where,
        (zpack,) + tuple(laid) + halos_x + main_y + rest_y + (coeffs1,),
        [fine] * 5 + [(3, x1, y1, 2 * LANES), (ey, LANES)],
        24,
        micros=4,
        aliases={n + 2: n for n in range(12)},
    )
    laid, own1, outs = outs[:12], outs[12], outs[13:]
    sends_x, (two_y, one_y), outs = outs[:n_x], outs[n_x:n_x + 2], outs[n_x + 2:]
    sends_xy, fine_arrays = outs[:2 * n_x], outs[2 * n_x:]
    fine_arrays = tuple(fine_arrays) + tuple(laid[2:4]) + tuple(laid[6:])

    near_x = tuple(swaps("gx", sends_x, "gy"))
    near_y = tuple(swaps("gy", (one_y, two_y))[::-1])
    near_xy = tuple(diagonal_swaps(sends_xy))
    copies, level1 = run(
        functools.partial(near_kernel, counts, devices),
        [(devices, 5, y1 // 2, LANES), (6, x1 + 2 * NEAR, y1 + 2 * NEAR, LANES)],
        where,
        (own1,) + near_x + near_y + near_xy + (coarse2,),
        [(x1, y1 + 2 * NEAR, LANES)],
    )

    gathered = lax.all_to_all(copies, axes, 0, 0, tiled=True)
    wide, rows = counts[0] * x1 // 2, counts[1] * y1 // 2
    columns = max(LANES, counts[2] * sz // 4)
    (result,) = run(
        functools.partial(up_kernel, counts),
        [(sx, sy, sz)],
        where,
        (gathered, level1) + tuple(fine_arrays),
        [(5, wide, rows, columns), (wide + NEAR, rows, columns)]
        + [(x1 // 2 + NEAR, y1 + 2 * NEAR, LANES)]
        + [(x1 + 2, ey, LANES)] * 2
        + [fine] * 4,
        24,
        micros=4,
    )
    return result


def solution(mesh):
    spec = P("gx", "gy", "gz")
    return jax.shard_map(
        local, mesh=mesh, in_specs=(spec,) * 6, out_specs=spec, check_vma=False
    )
```

```python
import functools

import jax
import jax.numpy as jnp
from jax import lax
from jax.experimental import pallas as pl
from jax.experimental.pallas import tpu as pltpu
from jax.sharding import PartitionSpec as P

LEVELS = 6
SWEEPS = 2
BOTTOM = 8
WEIGHT = 0.25 ** (LEVELS - 1)
RELAX = 2.0 / 3.0
KEEP = 1.0 / 3.0

HALO = 4
NEAR = 4
LANES = 128
PLACE = (0, 11, 21, 31, 41, 51)
DEPTH = (11, 10, 10, 10, 10, 11)
SIDE = LANES // 2
STRIDE = 256

VM = pl.BlockSpec(memory_space=pltpu.VMEM)
SM = pl.BlockSpec(memory_space=pltpu.SMEM)
F32 = jnp.float32


def position(where_ref):
    code = where_ref[0]
    return code // (STRIDE * STRIDE), code // STRIDE % STRIDE, code % STRIDE


def lane_of(shape):
    return lax.broadcasted_iota(jnp.int32, shape, len(shape) - 1)


def pick(flag, yes, no):
    return jnp.where(jnp.full(yes.shape, flag, jnp.int32) == 1, yes, no)


def neighbours(count, place, one, two):
    if count == 2:
        two = jnp.zeros_like(one)
    else:
        ends = jnp.full(two.shape, place, jnp.int32)
        two = jnp.where((ends == 0) | (ends == count - 1), 0.0, two)
    return pick(place % 2, one, two), pick(place % 2, two, one)


def turn(values, shift, axis):
    return pltpu.roll(values, shift % values.shape[axis], axis)


def parts_of(values):
    high = values.astype(jnp.bfloat16)
    return high, (values - high.astype(F32)).astype(jnp.bfloat16)


def times_table(values, table):
    table = table.astype(jnp.bfloat16)
    total = None
    for part in reversed(parts_of(values)):
        term = jnp.dot(part, table, preferred_element_type=F32)
        total = term if total is None else total + term
    return total


def iota2(shape, axis):
    return lax.broadcasted_iota(jnp.int32, shape, axis)


def pair_table(rows, cols, odd):
    row = iota2((rows, cols), 0)
    col = iota2((rows, cols), 1)
    hit = (row == 2 * col + 1) if odd else (row // 2 == col)
    return hit.astype(F32)


def below_x(values):
    if values.shape[0] == 1:
        return jnp.zeros_like(values)
    return jnp.concatenate([jnp.zeros_like(values[:1]), values[:-1]], axis=0)


def above_x(values):
    if values.shape[0] == 1:
        return jnp.zeros_like(values)
    return jnp.concatenate([values[1:], jnp.zeros_like(values[:1])], axis=0)


def pull(values, faces, step=1):
    bx, by, bz = faces
    total = bx * above_x(values) + below_x(bx * values)
    total = total + (by * turn(values, -step, 1) + turn(by * values, step, 1))
    return total + (bz * turn(values, -step, 2) + turn(bz * values, step, 2))


def diagonal(mass, faces, coupled, step=1):
    bx, by, bz = faces
    _, cy, cz = coupled
    return mass + bx + below_x(bx) + by + turn(cy, step, 1) + bz + turn(cz, step, 2)


def relaxer(mass, diag):
    inside = mass > 0.0
    return jnp.where(inside, RELAX / jnp.where(inside, diag, 1.0), 0.0)


def sweep(values, rhs, weight, faces, step=1):
    return KEEP * values + weight * (rhs + pull(values, faces, step))


def faces_x(values, odd, n_x, width):
    head, tail = values[:, :width], values[:, values.shape[1] - width:]
    return [pick(odd, head, tail), pick(odd, tail, head)][:n_x]


def faces_y(values, odd, width):
    head, tail = values[:, :width], values[:, values.shape[1] - width:]
    return pick(odd, head, tail), pick(odd, tail, head)


def corner_sends(below, above, odd):
    packs = []
    for rows, sign in ((slice(0, 8), 1), (slice(below.shape[1] - 8, below.shape[1]), -1)):
        low = [below[3 - i, rows] for i in range(3)]
        high = [above[i, rows] for i in range(3)]
        row = iota2(low[0].shape, 0)
        row = row if sign == 1 else 7 - row
        pack = (
            jnp.where(row < 3, low[0], turn(low[2], 3 * sign, 0)),
            jnp.where(row < 2, low[1], turn(high[1], 2 * sign, 0)),
            jnp.where(row < 3, high[0], turn(high[2], 3 * sign, 0)),
        )
        packs.append([p[:4] if sign == 1 else p[4:] for p in pack])
    return [(pick(odd, h, t), pick(odd, t, h)) for h, t in zip(*packs)]


def inner_rows(tile, by):
    upper = iota2(tile.shape, 0) < 4
    return jnp.where(upper, turn(tile, -by, 0), turn(tile, by, 0))


def corner_tiles(first, second, third):
    zero = jnp.zeros_like(first)
    low = (zero, inner_rows(first, 3), second, first)
    return low, (third, inner_rows(second, 2), inner_rows(third, 3), zero)


def diagonal_sends(values, n_x, odd_x, odd_y):
    corners = []
    for slabs in ([values[i] for i in range(4)], [values[values.shape[0] - 1 - i] for i in range(4)]):
        for sign in (1, -1):
            row = iota2(slabs[0].shape, 0)
            row = row if sign == 1 else 7 - row
            tiles = (slabs[0], jnp.where(row < 3, slabs[1], turn(slabs[3], 3 * sign, 0)), slabs[2])
            corners.append([t[:4] if sign == 1 else t[4:] for t in tiles])
    sends = []
    for k_x in range(n_x):
        for k_y in range(2):
            head_x = odd_x if k_x == 0 else 1 - odd_x
            head_y = odd_y if k_y == 0 else 1 - odd_y
            sends.append(
                [
                    pick(head_x, pick(head_y, hh, ht), pick(head_y, th, tt))
                    for hh, ht, th, tt in zip(*corners)
                ]
            )
    return sends


def diagonal_tiles(first, second, third):
    return [first, second, third, inner_rows(second, 3)]


def faces_kernel(counts, where_ref, *refs):
    ins, refs = refs[:6], refs[6:]
    n_x = 1 if counts[0] == 2 else 2
    sends_x, (two_y, one_y, first, second) = refs[:n_x], refs[n_x:]
    odd_x, odd_y, odd = (place % 2 for place in position(where_ref))
    sx, sy, sz = ins[0].shape
    half = sx // 2
    lane = lane_of((half, sy, LANES))
    head = jnp.zeros((half, sy, LANES), F32)
    tail = head
    for a, ref in enumerate(ins):
        for send, face in zip(sends_x, faces_x(ref[...][None], odd_x, n_x, HALO)):
            send[a] = face[0]
        one_y[a], two_y[a] = faces_y(ref[...], odd_y, HALO)
        for g in range(2):
            values = ref[g * half:(g + 1) * half]
            at = SIDE * g + PLACE[a]
            mask = (lane >= at) & (lane < at + DEPTH[a])
            head = jnp.where(mask, turn(values, at, 2), head)
            tail = jnp.where(mask, turn(values, at + DEPTH[a], 2), tail)
    first[...] = pick(odd, head, tail)
    second[...] = pick(odd, tail, head)


def halo_z_kernel(counts, where_ref, one_ref, two_ref, zpack, *sends):
    at_x, _, at_z = position(where_ref)
    half = one_ref.shape[0]
    below, above = neighbours(counts[2], at_z, one_ref[...], two_ref[...])
    lane = lane_of(below.shape)
    zpack[:half] = jnp.where(lane < SIDE, above, turn(below, SIDE, 2))
    zpack[half:] = jnp.where(lane < SIDE, turn(above, SIDE, 2), below)
    for send, face in zip(sends, faces_x(zpack[...][None], at_x % 2, len(sends), HALO)):
        send[...] = face[0]


def corners_kernel(counts, where_ref, zpack, *refs):
    n_x = 1 if counts[0] == 2 else 2
    main_x, halos_x, (two_y, one_y) = refs[:n_x], refs[n_x:2 * n_x], refs[2 * n_x + 1:]
    at_x, at_y, _ = position(where_ref)
    for a in range(7):
        if a < 6:
            below, above = neighbours(counts[0], at_x, main_x[0][a], main_x[-1][a])
        else:
            below, above = neighbours(counts[0], at_x, halos_x[0][...], halos_x[-1][...])
        for n, pair in enumerate(corner_sends(below, above, at_y % 2)):
            one_y[3 * a + n], two_y[3 * a + n] = pair
    one_y[21:], two_y[21:] = faces_y(zpack[...], at_y % 2, HALO)


def each(first, last, body):
    for x in range(first, last):
        body(x)


def ring_up(main, halo, lane):
    main_up, halo_up = turn(main, -1, 1), turn(halo, -1, 1)
    last = lane == LANES - 1
    return jnp.where(last, halo_up, main_up), jnp.where(last, main_up, halo_up)


def ring_down(main, halo, lane):
    main_down, halo_down = turn(main, 1, 1), turn(halo, 1, 1)
    zero = lane == 0
    return jnp.where(zero, halo_down, main_down), jnp.where(zero, main_down, halo_down)


def pull_slab(field, bx, by, bz, x, lane):
    centre = [half[x] for half in field]
    out = []
    for k in range(2):
        c, face = centre[k], by[k][x]
        t = bx[k][x] * field[k][x + 1] + bx[k][x - 1] * field[k][x - 1]
        out.append(t + (face * turn(c, -1, 0) + turn(face * c, 1, 0)))
    faces = [half[x] for half in bz]
    ups = ring_up(centre[0], centre[1], lane)
    downs = ring_down(faces[0] * centre[0], faces[1] * centre[1], lane)
    return centre, [out[k] + (faces[k] * ups[k] + downs[k]) for k in range(2)]


def unpacked(packed, a, lane):
    at, depth = PLACE[a], DEPTH[a]
    axis = packed.ndim - 1
    right, left = turn(packed, -at, axis), turn(packed, SIDE - depth - at, axis)
    return jnp.where(lane < depth, right, jnp.where(lane >= LANES - depth, left, 0.0))


def rows_of(source, x, count, firsts, seconds):
    total = None
    for p in firsts:
        for q in seconds:
            term = source[x + p, pl.ds(q, count, stride=2), :]
            total = term if total is None else total + term
    return total


BOTH, ODD = (0, 1), (1,)


def to_level1(sums, first, count, table, factor):
    _, x1, y1, _ = sums.shape
    flat = sums[first:first + count].reshape(count * x1 * y1, 2 * LANES)
    return factor * times_table(flat, table).reshape(count, x1, y1, LANES)


def coefficient_kernel(counts, where_ref, *refs):
    ins, refs = refs[:7], refs[7:]
    n_x = 1 if counts[0] == 2 else 2
    main_x, refs = refs[:n_x], refs[n_x:]
    arrays, (coarse2, coeffs1, sums, pairing) = refs[:12], refs[12:]
    sx, sy, sz = ins[0].shape
    at_x = position(where_ref)[0]
    x1, y1 = sx // 2, sy // 2
    lane = lane_of((sx, sy, LANES))
    lanes = [slice(k * LANES, (k + 1) * LANES) for k in range(2)]
    mine = slice(HALO, HALO + sx)
    for a in range(6):
        to = arrays[2 * a]
        below, above = neighbours(counts[0], at_x, main_x[0][a], main_x[-1][a])
        to[:HALO, :sy] = below
        to[mine, :sy] = ins[a][...]
        to[HALO + sx:, :sy] = above
        arrays[2 * a + 1][mine, :sy] = unpacked(ins[6][...], a, lane)
    for n, (firsts, seconds) in enumerate(((BOTH, BOTH), (ODD, BOTH), (BOTH, ODD), (BOTH, BOTH))):
        for k in range(2):
            for i in range(x1):
                source = arrays[2 * (n + 2) + k]
                sums[n, i, :, lanes[k]] = rows_of(source, HALO + 2 * i, y1, firsts, seconds)
    pairs = pair_table(2 * LANES, LANES, False)
    odds = pair_table(2 * LANES, LANES, True)
    paired = to_level1(sums, 0, 3, pairs, 0.0625)
    mass1 = (2.0 * WEIGHT) * paired[0]
    faces1 = (paired[1], paired[2], to_level1(sums, 3, 1, odds, 0.0625)[0])
    diag1 = mass1 + faces1[0] + below_x(faces1[0])
    diag1 = diag1 + faces1[1] + faces1[2] + turn(faces1[2], 1, 2)
    for n, values in enumerate((mass1, diag1) + faces1):
        coeffs1[n] = values
    parts = (
        (mass1, False, False, False, 0.125),
        (faces1[0], True, False, False, 0.0625),
        (faces1[1], False, True, False, 0.0625),
        (faces1[2], False, False, True, 0.0625),
    )
    for n, (values, *odd_axes, factor) in enumerate(parts):
        pairing[n] = values
        coarse2[n] = level2_rows(pairing.at[n], odd_axes, factor, x1 // 2, y1 // 2, sz // 4)


def down_kernel(counts, where_ref, zpack, *refs):
    refs = refs[12:]
    n_x = 1 if counts[0] == 2 else 2
    halos_x = refs[:n_x]
    main_two, main_one, rest_two, rest_one, coeffs1 = refs[n_x:5 + n_x]
    flat, refs = refs[5 + n_x:17 + n_x], refs[17 + n_x:]
    arrays = tuple(zip(flat[::2], flat[1::2]))
    own1, refs = refs[0], refs[1:]
    sends, near_two, near_one, refs = refs[:n_x], refs[n_x], refs[n_x + 1], refs[n_x + 2:]
    sends_xy, refs = refs[:2 * n_x], refs[2 * n_x:]
    kept_m, kept_h, weight_m, weight_h = refs[:4]
    packs, half_m, half_h, diag_m, diag_h, sums, left = refs[4:]
    field, rhs, alpha, bx, by, bz = arrays
    sx, sy, sz = zpack.shape
    ex, ey = sx + 2 * HALO, sy + 2 * HALO
    at_x, at_y, _ = position(where_ref)

    rest = neighbours(counts[1], at_y, rest_one[...], rest_two[...])
    rest = jnp.concatenate(rest[::-1], axis=1)
    for a in range(7):
        if a < 6:
            to = arrays[a][0]
            rows = neighbours(counts[1], at_y, main_one[a], main_two[a])
            rows = jnp.concatenate(rows[::-1], axis=1)
        else:
            to = packs
            rows = rest[21:]
            below, above = neighbours(counts[0], at_x, halos_x[0][...], halos_x[-1][...])
            to[:HALO, :sy] = below
            to[HALO + sx:, :sy] = above
        to[HALO:HALO + sx, sy:] = rows
        low, high = corner_tiles(*(rest[3 * a + n] for n in range(3)))
        for n in range(HALO):
            to[n, sy:] = low[n]
            to[HALO + sx + n, sy:] = high[n]
    lane = lane_of((ey, LANES))
    lane_low = lane_of((2 * HALO, LANES))

    def unpack_rows(x):
        packed = packs[x, sy:]
        for a in range(6):
            arrays[a][1][x, sy:] = unpacked(packed, a, lane_low)

    def unpack(x):
        packed = packs[x]
        for a in range(6):
            arrays[a][1][x] = unpacked(packed, a, lane)

    each(0, HALO, unpack)
    each(HALO, HALO + sx, unpack_rows)
    each(HALO + sx, ex, unpack)
    halfway, weight, kept = (half_m, half_h), (weight_m, weight_h), (kept_m, kept_h)
    diag = (diag_m, diag_h)

    def first_sweep(x):
        faces = [half[x] for half in bz]
        downs = ring_down(faces[0], faces[1], lane)
        centre, near = pull_slab(field, bx, by, bz, x, lane)
        for k in range(2):
            face = by[k][x]
            mass = WEIGHT * alpha[k][x]
            d = mass + bx[k][x] + bx[k][x - 1] + face + turn(face, 1, 0) + faces[k] + downs[k]
            w = relaxer(mass, d)
            diag[k][x] = d
            weight[k][x] = w
            halfway[k][x] = KEEP * centre[k] + w * (rhs[k][x] + near[k])

    each(1, ex - 1, first_sweep)

    def second_sweep(x):
        centre, near = pull_slab(halfway, bx, by, bz, x, lane)
        for k in range(2):
            kept[k][x] = KEEP * centre[k] + weight[k][x] * (rhs[k][x] + near[k])

    each(2, ex - 2, second_sweep)

    def residual(x):
        centre, near = pull_slab(kept, bx, by, bz, x, lane)
        for k in range(2):
            halfway[k][x] = rhs[k][x] - diag[k][x] * centre[k] + near[k]

    each(HALO, ex - HALO, residual)

    x1, y1 = sx // 2, sy // 2
    for k in range(2):
        lanes = slice(k * LANES, (k + 1) * LANES)
        for i in range(x1):
            x = HALO + 2 * i
            sums[0, i, :, lanes] = rows_of(halfway[k], x, y1, BOTH, BOTH)
            left[...] = turn(by[k][x] + by[k][x + 1], 1, 0)
            sums[1, i, :, lanes] = left[pl.ds(0, y1, stride=2), :]
        sums[2, 0, :, lanes] = rows_of(bx[k], HALO - 1, y1, (0,), BOTH)
        sums[2, 1:, :, lanes] = jnp.zeros((x1 - 1, y1, LANES), F32)
    rhs1, low_y, low_x = to_level1(sums, 0, 3, pair_table(2 * LANES, LANES, False), 0.0625)
    weight1 = relaxer(coeffs1[0], coeffs1[1] + low_y + low_x)
    for n, values in enumerate((2.0 * rhs1, weight1, coeffs1[2], coeffs1[3], coeffs1[4])):
        own1[n] = values
        for send, face in zip(sends, faces_x(values[None], at_x % 2, n_x, NEAR)):
            send[n] = face[0]
        near_one[n], near_two[n] = faces_y(values, at_y % 2, NEAR)
        for send, tiles in zip(sends_xy, diagonal_sends(values, n_x, at_x % 2, at_y % 2)):
            for t in range(3):
                send[3 * n + t] = tiles[t]


def level2_rows(source, odd_axes, factor, x2, y2, z2):
    rows = []
    for i in range(x2):
        total = None
        for p in (1,) if odd_axes[0] else (0, 1):
            for q in (1,) if odd_axes[1] else (0, 1):
                term = source[2 * i + p, pl.ds(q, y2, stride=2), :]
                total = term if total is None else total + term
        rows.append(total)
    flat = jnp.concatenate(rows, axis=0)
    flat = factor * times_table(flat, pair_table(LANES, LANES, odd_axes[2]))
    lane = lane_of((y2, LANES))
    packed = jnp.zeros((y2, LANES), F32)
    for i in range(x2):
        mask = (lane >= i * z2) & (lane < (i + 1) * z2)
        packed = jnp.where(mask, turn(flat[i * y2:(i + 1) * y2], i * z2, 1), packed)
    return packed


def near_kernel(counts, devices, where_ref, ring, *refs):
    n_x = 1 if counts[0] == 2 else 2
    halos_x = refs[:n_x]
    main_two, main_one = refs[n_x:n_x + 2]
    diagonals, (coarse2, copies, level1, left) = refs[n_x + 2:3 * n_x + 2], refs[3 * n_x + 2:]
    n, bx1, by1, _ = ring.shape
    at_x, at_y, _ = position(where_ref)
    sides = [
        neighbours(counts[0], at_x, diagonals[k][...], diagonals[k - 2][...]) for k in range(2)
    ]
    rest = []
    for one, two in zip(*sides):
        rows = neighbours(counts[1], at_y, one, two)
        rest.append(jnp.concatenate(rows[::-1], axis=1))
    whole = []
    for a in range(n):
        below, above = neighbours(counts[0], at_x, halos_x[0][a], halos_x[-1][a])
        rows = neighbours(counts[1], at_y, main_one[a], main_two[a])
        rows = jnp.concatenate(rows[::-1], axis=1)
        low, high = (diagonal_tiles(*(side[3 * a + k] for k in range(3))) for side in rest)
        low = low[::-1]
        rows = jnp.concatenate(
            [tile[None] for tile in low] + [rows] + [tile[None] for tile in high], axis=0
        )
        block = jnp.concatenate([below, ring[a], above], axis=0)
        whole.append(jnp.concatenate([block, rows], axis=1))
    rhs1, weight1 = whole[:2]
    faces1 = tuple(whole[2:])
    field1 = weight1 * rhs1
    field1 = sweep(field1, rhs1, weight1, faces1)
    for a, values in enumerate([field1] + whole):
        level1[a] = values
    mine = slice(NEAR, NEAR + bx1)
    near = slice(NEAR - 1, NEAR + bx1 + 1)
    inner = weight1[mine]
    diag1 = RELAX / jnp.where(inner > 0.0, inner, 1.0)
    remain = rhs1[mine] - diag1 * field1[mine] + pull(field1[near], [face[near] for face in faces1])[1:-1]
    left[...] = remain
    packed = level2_rows(left, (False,) * 3, 0.125, bx1 // 2, by1 // 2, LANES // 4)
    blocks = LANES // (LANES // 4)
    shift = position(where_ref)[2] % blocks * (LANES // blocks)
    slots = [pltpu.roll(values, shift, 1) for values in [packed] + [coarse2[a] for a in range(4)]]
    for d in range(devices):
        for a in range(n):
            copies[d, a] = slots[a]


def inner_sweep(values, rhs, weight, faces, first):
    part = slice(first, rhs.shape[0] - first)
    below = slice(first - 1, rhs.shape[0] - first - 1)
    bx, by, bz = faces
    centre = values[1:-1]
    near = bx[part] * values[2:] + bx[below] * values[:-2]
    near = near + (by[part] * turn(centre, -1, 1) + turn(by[part] * centre, 1, 1))
    near = near + (bz[part] * turn(centre, -1, 2) + turn(bz[part] * centre, 1, 2))
    return KEEP * centre + weight[part] * (rhs[part] + near)


def halve(values, odd_axis, step):
    half = values.shape[0] // 2
    even = [values[2 * i:2 * i + 1] for i in range(half)]
    odd = [values[2 * i + 1:2 * i + 2] for i in range(half)]
    if odd_axis != 0:
        odd = [a + b for a, b in zip(even, odd)]
    values = jnp.concatenate(odd, axis=0)
    for axis in (1, 2):
        next_one = turn(values, -step, axis)
        values = next_one if odd_axis == axis else values + next_one
    return values


def double(values, step):
    values = values + turn(values, step, 1)
    values = values + turn(values, step, 2)
    return jnp.concatenate([values[i // 2:i // 2 + 1] for i in range(2 * values.shape[0])], axis=0)


def coarse_levels(mass, faces, y, z):
    levels = []
    for level in range(2, LEVELS):
        step = 2 ** (level - 2)
        bx, by, bz = faces
        row = lax.broadcasted_iota(jnp.int32, by.shape, 1)
        lane = lane_of(bz.shape)
        upper = (
            bx,
            jnp.where(row == (y - 1) * step, 0.0, by),
            jnp.where(lane == (z - 1) * step, 0.0, bz),
        )
        lower = (below_x(bx), turn(upper[1], step, 1), turn(upper[2], step, 2))
        mass = jnp.where((row % step == 0) & (lane % step == 0), mass, 0.0)
        diag = mass + bx + lower[0] + by + lower[1] + bz + lower[2]
        levels.append((diag, relaxer(mass, diag), upper, lower))
        if level < LEVELS - 1:
            faces = tuple(0.0625 * halve(face, axis, step) for axis, face in enumerate(faces))
            mass = 0.125 * halve(mass, -1, step)
            y, z = y // 2, z // 2
    return levels


def coupled(values, upper, lower, step):
    ups = (above_x(values), turn(values, -step, 1), turn(values, -step, 2))
    downs = (below_x(values), turn(values, step, 1), turn(values, step, 2))
    x, y, z = (u * up + l * down for u, up, l, down in zip(upper, ups, lower, downs))
    return (y + z) + x if values.shape[0] > 1 else y + z


def coarse_cycle(level, rhs, levels):
    step = 2 ** (level - 2)
    diag, weight, upper, lower = levels[level - 2]
    scaled = tuple(tuple(weight * b for b in faces) for faces in (upper, lower))
    source = weight * rhs

    def relax(field):
        return (KEEP * field + source) + coupled(field, *scaled, step)

    field = source
    if level == LEVELS - 1:
        for _ in range(BOTTOM - 1):
            field = relax(field)
        return field
    for _ in range(SWEEPS - 1):
        field = relax(field)
    remain = (rhs - diag * field) + coupled(field, upper, lower, step)
    correction = coarse_cycle(level + 1, 0.125 * halve(remain, -1, step), levels)
    field = field + double(correction, step)
    for _ in range(SWEEPS):
        field = relax(field)
    return field


def spread_out(counts, slots, whole):
    gx, gy, gz = counts
    y2 = slots.shape[-2]
    x2 = whole.shape[0] // gx
    z2 = LANES // x2
    lane = lane_of((y2, LANES))
    for i in range(gx):
        for j in range(gy):
            for x in range(x2):
                for part in range(whole.shape[2] // LANES):
                    total = None
                    for k in range(LANES // z2):
                        column = part * (LANES // z2) + k
                        if column < gz:
                            block = slots[(i * gy + j) * gz + column]
                            at = (x + k) * z2 % LANES
                            mask = (lane >= at) & (lane < at + z2)
                            if total is None:
                                total = jnp.where(mask, block, 0.0)
                            total = jnp.where(mask, block, total)
                    if x:
                        total = turn(total, -x * z2, 1)
                    lanes = slice(part * LANES, (part + 1) * LANES)
                    whole[i * x2 + x, j * y2:(j + 1) * y2, lanes] = total


def up_kernel(counts, where_ref, gathered, level1, *refs):
    kept, weight, rhs, bx, by, bz = zip(refs[0:12:2], refs[1:12:2])
    out, whole, second, lift, spread_m, spread_h, field_m, field_h, half_m, half_h = refs[12:]
    gx, gy, gz = counts
    at_x, at_y, at_z = position(where_ref)
    sx, sy, sz = out.shape
    x1, y1 = sx // 2, sy // 2
    x2, y2, z2 = x1 // 2, y1 // 2, sz // 4
    columns = max(LANES, gz * z2)
    for a in range(5):
        spread_out(counts, gathered.at[:, a], whole.at[a])
    levels = coarse_levels(whole[1], (whole[2], whole[3], whole[4]), gy * y2, gz * z2)
    correction = coarse_cycle(2, whole[0], levels)

    wide = gx * x2
    half = NEAR // 2
    ex1, ey1 = x1 + 2 * NEAR, y1 + 2 * NEAR
    second[:half] = jnp.zeros((half,) + correction.shape[1:], F32)
    second[half:half + wide] = correction
    second[half + wide:] = jnp.zeros((half,) + correction.shape[1:], F32)
    window = second[pl.ds(at_x * x2, x2 + NEAR)]
    rows = correction.shape[1]
    row = iota2((columns, LANES), 0)
    col = iota2((columns, LANES), 1)
    place = jnp.where(col < LANES * 3 // 4, col, col - LANES)
    table_z = (row == at_z * z2 + lax.shift_right_arithmetic(place, 1)).astype(F32)
    flat = times_table(window.reshape((x2 + NEAR) * rows, columns), table_z)
    flat = flat.reshape(x2 + NEAR, rows, LANES)
    flat = pltpu.roll(flat, (rows - at_y * y2) % rows, 1)
    for i in range(x2 + NEAR):
        for q in range(2):
            lift[i, pl.ds(q, y2, stride=2), :] = flat[i, :y2]
            lift[i, pl.ds(y1 + q, half, stride=2), :] = flat[i, y2:y2 + half]
            lift[i, pl.ds(y1 + NEAR + q, half, stride=2), :] = flat[i, rows - half:]
    lifted = jnp.concatenate([lift[i // 2][None] for i in range(ex1)], axis=0)
    field1, rhs1, weight1 = level1[0], level1[1], level1[2]
    faces1 = (level1[3], level1[4], level1[5])
    field1 = (field1 + jnp.where(weight1 > 0.0, lifted, 0.0))[1:-1]
    for n in range(SWEEPS):
        field1 = inner_sweep(field1, rhs1, weight1, faces1, 2 + n)

    ex, ey = sx + 2 * HALO, sy + 2 * HALO
    near = field1.reshape((x1 + 2) * ey1, LANES)
    row = iota2((LANES, 2 * LANES), 0)
    col = iota2((LANES, 2 * LANES), 1)
    lifted = times_table(near, (col // 2 == row).astype(F32))
    quarter = NEAR // 2
    for k, spread in enumerate((spread_m, spread_h)):
        block = lifted[:, k * LANES:(k + 1) * LANES].reshape(x1 + 2, ey1, LANES)
        for i in range(x1 + 2):
            for q in range(2):
                spread[i, pl.ds(q, y1, stride=2), :] = block[i, :y1]
                spread[i, pl.ds(sy + q, quarter, stride=2), :] = block[i, y1:y1 + quarter]
                spread[i, pl.ds(sy + HALO + q, quarter, stride=2), :] = block[i, ey1 - quarter:]
    before, after = (field_m, field_h), (half_m, half_h)
    first = HALO - 2
    for x in range(first, ex - first):
        for k, spread in enumerate((spread_m, spread_h)):
            before[k][x] = kept[k][x] + spread[(x - first) // 2]

    lane = lane_of((ey, LANES))

    def sweep_out(x):
        centre, around = pull_slab(before, bx, by, bz, x, lane)
        for k in range(2):
            after[k][x] = KEEP * centre[k] + weight[k][x] * (rhs[k][x] + around[k])

    each(first + 1, ex - first - 1, sweep_out)

    def sweep_own(x):
        centre, around = pull_slab(after, bx, by, bz, x, lane)
        value = KEEP * centre[0] + weight[0][x] * (rhs[0][x] + around[0])
        out[x - HALO] = value[:sy]

    each(HALO, ex - HALO, sweep_own)


def run(kernel, outs, where, arrays, scratch=(), grant=16, micros=1, aliases={}):
    return pl.pallas_call(
        kernel,
        out_shape=tuple(jax.ShapeDtypeStruct(shape, F32) for shape in outs),
        in_specs=[SM] * len(where) + [VM] * len(arrays),
        out_specs=tuple(VM for _ in outs),
        input_output_aliases=aliases,
        scratch_shapes=[pltpu.VMEM(shape, F32) for shape in scratch],
        compiler_params=pltpu.CompilerParams(vmem_limit_bytes=grant * 1024 * 1024),
        cost_estimate=pl.CostEstimate(
            flops=0, bytes_accessed=int(micros * 3.6e6), transcendentals=0
        ),
    )(*where, *arrays)


def partners(count, k):
    partner = list(range(count))
    for low in range(k, count - 1, 2):
        partner[low], partner[low + 1] = low + 1, low
    return partner


def swaps(axis, sends, other=None):
    count = lax.axis_size(axis)
    got = []
    for k, block in enumerate(sends):
        partner = partners(count, k)
        if k == 1 and other is None:
            partner[0], partner[-1] = count - 1, 0
        if k == 0 or other is None:
            got.append(lax.ppermute(block, axis, list(enumerate(partner))))
            continue
        rows = lax.axis_size(other)
        pairs = []
        for row in range(rows):
            for i in range(count):
                ends = [(row, i), (min(row ^ 1, rows - 1) if partner[i] == i else row, partner[i])]
                if axis < other:
                    pairs.append(tuple(at * rows + line for line, at in ends))
                else:
                    pairs.append(tuple(line * count + at for line, at in ends))
        got.append(lax.ppermute(block, tuple(sorted((axis, other))), pairs))
    return got


def diagonal_swaps(sends):
    count_x, count_y = lax.axis_size("gx"), lax.axis_size("gy")
    got = []
    for n, block in enumerate(sends):
        xs, ys = partners(count_x, n // 2), partners(count_y, n % 2)
        pairs = [
            (x * count_y + y, xs[x] * count_y + ys[y])
            for x in range(count_x)
            for y in range(count_y)
        ]
        got.append(lax.ppermute(block, ("gx", "gy"), pairs))
    return got


def local(initial, right_side, alpha, beta_x, beta_y, beta_z):
    axes = ("gx", "gy", "gz")
    counts = tuple(lax.axis_size(axis) for axis in axes)
    devices = counts[0] * counts[1] * counts[2]
    where = (lax.axis_index("gx") * STRIDE + lax.axis_index("gy")) * STRIDE + lax.axis_index("gz")
    where = (where.astype(jnp.int32).reshape(1),)
    ins = (initial, right_side, alpha, beta_x, beta_y, beta_z)
    sx, sy, sz = initial.shape
    n_x = 1 if counts[0] == 2 else 2
    ex, ey = sx + 2 * HALO, sy + 2 * HALO
    fine = (ex, ey, LANES)

    *sends_x, two_y, one_y, first, second = run(
        functools.partial(faces_kernel, counts),
        [(6, HALO, sy, LANES)] * n_x
        + [(6, sx, HALO, LANES)] * 2
        + [(sx // 2, sy, LANES)] * 2,
        where,
        ins,
        grant=60,
    )
    main_x = tuple(swaps("gx", sends_x, "gy"))
    main_y = tuple(swaps("gy", (one_y, two_y))[::-1])
    got = swaps("gz", (first, second), "gy")
    zpack, *sends = run(
        functools.partial(halo_z_kernel, counts),
        [(sx, sy, LANES)] + [(HALO, sy, LANES)] * n_x,
        where,
        tuple(got),
    )
    halos_x = tuple(swaps("gx", sends, "gy"))
    x1, y1 = sx // 2, sy // 2
    *laid, coarse2, coeffs1 = run(
        functools.partial(coefficient_kernel, counts),
        [fine] * 12 + [(4, y1 // 2, LANES), (5, x1, y1, LANES)],
        where,
        ins + (zpack,) + main_x,
        [(4, x1, y1, 2 * LANES), (4, x1, y1, LANES)],
        micros=2,
    )
    two_y, one_y = run(
        functools.partial(corners_kernel, counts),
        [(21 + sx, HALO, LANES)] * 2,
        where,
        (zpack,) + main_x + halos_x + (coarse2,),
    )
    rest_y = tuple(swaps("gy", (one_y, two_y), "gx")[::-1])
    outs = run(
        functools.partial(down_kernel, counts),
        [fine] * 12
        + [(5, x1, y1, LANES)]
        + [(5, NEAR, y1, LANES)] * n_x
        + [(5, x1, NEAR, LANES)] * 2
        + [(15, NEAR, LANES)] * (2 * n_x)
        + [fine] * 4,
        where,
        (zpack,) + tuple(laid) + halos_x + main_y + rest_y + (coeffs1,),
        [fine] * 5 + [(3, x1, y1, 2 * LANES), (ey, LANES)],
        24,
        micros=4,
        aliases={n + 2: n for n in range(12)},
    )
    laid, own1, outs = outs[:12], outs[12], outs[13:]
    sends_x, (two_y, one_y), outs = outs[:n_x], outs[n_x:n_x + 2], outs[n_x + 2:]
    sends_xy, fine_arrays = outs[:2 * n_x], outs[2 * n_x:]
    fine_arrays = tuple(fine_arrays) + tuple(laid[2:4]) + tuple(laid[6:])

    near_x = tuple(swaps("gx", sends_x, "gy"))
    near_y = tuple(swaps("gy", (one_y, two_y), "gz")[::-1])
    near_xy = tuple(diagonal_swaps(sends_xy))
    copies, level1 = run(
        functools.partial(near_kernel, counts, devices),
        [(devices, 5, y1 // 2, LANES), (6, x1 + 2 * NEAR, y1 + 2 * NEAR, LANES)],
        where,
        (own1,) + near_x + near_y + near_xy + (coarse2,),
        [(x1, y1 + 2 * NEAR, LANES)],
    )

    gathered = lax.all_to_all(copies, axes, 0, 0, tiled=True)
    wide, rows = counts[0] * x1 // 2, counts[1] * y1 // 2
    columns = max(LANES, counts[2] * sz // 4)
    (result,) = run(
        functools.partial(up_kernel, counts),
        [(sx, sy, sz)],
        where,
        (gathered, level1) + tuple(fine_arrays),
        [(5, wide, rows, columns), (wide + NEAR, rows, columns)]
        + [(x1 // 2 + NEAR, y1 + 2 * NEAR, LANES)]
        + [(x1 + 2, ey, LANES)] * 2
        + [fine] * 4,
        24,
        micros=4,
    )
    return result


def solution(mesh):
    spec = P("gx", "gy", "gz")
    return jax.shard_map(
        local, mesh=mesh, in_specs=(spec,) * 6, out_specs=spec, check_vma=False
    )
```

```python
import functools

import jax
import jax.numpy as jnp
from jax import lax
from jax.experimental import pallas as pl
from jax.experimental.pallas import tpu as pltpu
from jax.sharding import PartitionSpec as P

LEVELS = 6
SWEEPS = 2
BOTTOM = 8
WEIGHT = 0.25 ** (LEVELS - 1)
RELAX = 2.0 / 3.0
KEEP = 1.0 / 3.0

HALO = 4
NEAR = 4
LANES = 128
PLACE = (0, 11, 21, 31, 41, 51)
DEPTH = (11, 10, 10, 10, 10, 11)
SIDE = LANES // 2
STRIDE = 256

VM = pl.BlockSpec(memory_space=pltpu.VMEM)
SM = pl.BlockSpec(memory_space=pltpu.SMEM)
F32 = jnp.float32


def position(where_ref):
    code = where_ref[0]
    return code // (STRIDE * STRIDE), code // STRIDE % STRIDE, code % STRIDE


def lane_of(shape):
    return lax.broadcasted_iota(jnp.int32, shape, len(shape) - 1)


def pick(flag, yes, no):
    return jnp.where(jnp.full(yes.shape, flag, jnp.int32) == 1, yes, no)


def neighbours(count, place, one, two):
    if count == 2:
        two = jnp.zeros_like(one)
    else:
        ends = jnp.full(two.shape, place, jnp.int32)
        two = jnp.where((ends == 0) | (ends == count - 1), 0.0, two)
    return pick(place % 2, one, two), pick(place % 2, two, one)


def turn(values, shift, axis):
    return pltpu.roll(values, shift % values.shape[axis], axis)


def parts_of(values):
    high = values.astype(jnp.bfloat16)
    return high, (values - high.astype(F32)).astype(jnp.bfloat16)


def times_table(values, table):
    table = table.astype(jnp.bfloat16)
    total = None
    for part in reversed(parts_of(values)):
        term = jnp.dot(part, table, preferred_element_type=F32)
        total = term if total is None else total + term
    return total


def iota2(shape, axis):
    return lax.broadcasted_iota(jnp.int32, shape, axis)


def pair_table(rows, cols, odd):
    row = iota2((rows, cols), 0)
    col = iota2((rows, cols), 1)
    hit = (row == 2 * col + 1) if odd else (row // 2 == col)
    return hit.astype(F32)


def below_x(values):
    if values.shape[0] == 1:
        return jnp.zeros_like(values)
    return jnp.concatenate([jnp.zeros_like(values[:1]), values[:-1]], axis=0)


def above_x(values):
    if values.shape[0] == 1:
        return jnp.zeros_like(values)
    return jnp.concatenate([values[1:], jnp.zeros_like(values[:1])], axis=0)


def pull(values, faces, step=1):
    bx, by, bz = faces
    total = bx * above_x(values) + below_x(bx * values)
    total = total + (by * turn(values, -step, 1) + turn(by * values, step, 1))
    return total + (bz * turn(values, -step, 2) + turn(bz * values, step, 2))


def diagonal(mass, faces, coupled, step=1):
    bx, by, bz = faces
    _, cy, cz = coupled
    return mass + bx + below_x(bx) + by + turn(cy, step, 1) + bz + turn(cz, step, 2)


def relaxer(mass, diag):
    inside = mass > 0.0
    return jnp.where(inside, RELAX / jnp.where(inside, diag, 1.0), 0.0)


def sweep(values, rhs, weight, faces, step=1):
    return KEEP * values + weight * (rhs + pull(values, faces, step))


def faces_x(values, odd, n_x, width):
    head, tail = values[:, :width], values[:, values.shape[1] - width:]
    return [pick(odd, head, tail), pick(odd, tail, head)][:n_x]


def faces_y(values, odd, width):
    head, tail = values[:, :width], values[:, values.shape[1] - width:]
    return pick(odd, head, tail), pick(odd, tail, head)


def corner_sends(below, above, odd):
    packs = []
    for rows, sign in ((slice(0, 8), 1), (slice(below.shape[1] - 8, below.shape[1]), -1)):
        low = [below[3 - i, rows] for i in range(3)]
        high = [above[i, rows] for i in range(3)]
        row = iota2(low[0].shape, 0)
        row = row if sign == 1 else 7 - row
        pack = (
            jnp.where(row < 3, low[0], turn(low[2], 3 * sign, 0)),
            jnp.where(row < 2, low[1], turn(high[1], 2 * sign, 0)),
            jnp.where(row < 3, high[0], turn(high[2], 3 * sign, 0)),
        )
        packs.append([p[:4] if sign == 1 else p[4:] for p in pack])
    return [(pick(odd, h, t), pick(odd, t, h)) for h, t in zip(*packs)]


def inner_rows(tile, by):
    upper = iota2(tile.shape, 0) < 4
    return jnp.where(upper, turn(tile, -by, 0), turn(tile, by, 0))


def corner_tiles(first, second, third):
    zero = jnp.zeros_like(first)
    low = (zero, inner_rows(first, 3), second, first)
    return low, (third, inner_rows(second, 2), inner_rows(third, 3), zero)


def diagonal_sends(values, n_x, odd_x, odd_y):
    corners = []
    for slabs in ([values[i] for i in range(4)], [values[values.shape[0] - 1 - i] for i in range(4)]):
        for sign in (1, -1):
            row = iota2(slabs[0].shape, 0)
            row = row if sign == 1 else 7 - row
            tiles = (slabs[0], jnp.where(row < 3, slabs[1], turn(slabs[3], 3 * sign, 0)), slabs[2])
            corners.append([t[:4] if sign == 1 else t[4:] for t in tiles])
    sends = []
    for k_x in range(n_x):
        for k_y in range(2):
            head_x = odd_x if k_x == 0 else 1 - odd_x
            head_y = odd_y if k_y == 0 else 1 - odd_y
            sends.append(
                [
                    pick(head_x, pick(head_y, hh, ht), pick(head_y, th, tt))
                    for hh, ht, th, tt in zip(*corners)
                ]
            )
    return sends


def diagonal_tiles(first, second, third):
    return [first, second, third, inner_rows(second, 3)]


def faces_kernel(counts, where_ref, *refs):
    ins, refs = refs[:6], refs[6:]
    n_x = 1 if counts[0] == 2 else 2
    sends_x, (two_y, one_y, first, second) = refs[:n_x], refs[n_x:]
    odd_x, odd_y, odd = (place % 2 for place in position(where_ref))
    sx, sy, sz = ins[0].shape
    half = sx // 2
    lane = lane_of((half, sy, LANES))
    head = jnp.zeros((half, sy, LANES), F32)
    tail = head
    for a, ref in enumerate(ins):
        for send, face in zip(sends_x, faces_x(ref[...][None], odd_x, n_x, HALO)):
            send[a] = face[0]
        one_y[a], two_y[a] = faces_y(ref[...], odd_y, HALO)
        for g in range(2):
            values = ref[g * half:(g + 1) * half]
            at = SIDE * g + PLACE[a]
            mask = (lane >= at) & (lane < at + DEPTH[a])
            head = jnp.where(mask, turn(values, at, 2), head)
            tail = jnp.where(mask, turn(values, at + DEPTH[a], 2), tail)
    first[...] = pick(odd, head, tail)
    second[...] = pick(odd, tail, head)


def halo_z_kernel(counts, where_ref, one_ref, two_ref, zpack, *sends):
    at_x, _, at_z = position(where_ref)
    half = one_ref.shape[0]
    below, above = neighbours(counts[2], at_z, one_ref[...], two_ref[...])
    lane = lane_of(below.shape)
    zpack[:half] = jnp.where(lane < SIDE, above, turn(below, SIDE, 2))
    zpack[half:] = jnp.where(lane < SIDE, turn(above, SIDE, 2), below)
    for send, face in zip(sends, faces_x(zpack[...][None], at_x % 2, len(sends), HALO)):
        send[...] = face[0]


def corners_kernel(counts, where_ref, zpack, *refs):
    n_x = 1 if counts[0] == 2 else 2
    main_x, halos_x, (two_y, one_y) = refs[:n_x], refs[n_x:2 * n_x], refs[2 * n_x + 1:]
    at_x, at_y, _ = position(where_ref)
    for a in range(7):
        if a < 6:
            below, above = neighbours(counts[0], at_x, main_x[0][a], main_x[-1][a])
        else:
            below, above = neighbours(counts[0], at_x, halos_x[0][...], halos_x[-1][...])
        for n, pair in enumerate(corner_sends(below, above, at_y % 2)):
            one_y[3 * a + n], two_y[3 * a + n] = pair
    one_y[21:], two_y[21:] = faces_y(zpack[...], at_y % 2, HALO)


def each(first, last, body):
    for x in range(first, last):
        body(x)


def ring_up(main, halo, lane):
    main_up, halo_up = turn(main, -1, 1), turn(halo, -1, 1)
    last = lane == LANES - 1
    return jnp.where(last, halo_up, main_up), jnp.where(last, main_up, halo_up)


def ring_down(main, halo, lane):
    main_down, halo_down = turn(main, 1, 1), turn(halo, 1, 1)
    zero = lane == 0
    return jnp.where(zero, halo_down, main_down), jnp.where(zero, main_down, halo_down)


def pull_slab(field, bx, by, bz, x, lane):
    centre = [half[x] for half in field]
    out = []
    for k in range(2):
        c, face = centre[k], by[k][x]
        t = bx[k][x] * field[k][x + 1] + bx[k][x - 1] * field[k][x - 1]
        out.append(t + (face * turn(c, -1, 0) + turn(face * c, 1, 0)))
    faces = [half[x] for half in bz]
    ups = ring_up(centre[0], centre[1], lane)
    downs = ring_down(faces[0] * centre[0], faces[1] * centre[1], lane)
    return centre, [out[k] + (faces[k] * ups[k] + downs[k]) for k in range(2)]


def unpacked(packed, a, lane):
    at, depth = PLACE[a], DEPTH[a]
    axis = packed.ndim - 1
    right, left = turn(packed, -at, axis), turn(packed, SIDE - depth - at, axis)
    return jnp.where(lane < depth, right, jnp.where(lane >= LANES - depth, left, 0.0))


def rows_of(source, x, count, firsts, seconds):
    total = None
    for p in firsts:
        for q in seconds:
            term = source[x + p, pl.ds(q, count, stride=2), :]
            total = term if total is None else total + term
    return total


BOTH, ODD = (0, 1), (1,)


def to_level1(sums, first, count, table, factor):
    _, x1, y1, _ = sums.shape
    flat = sums[first:first + count].reshape(count * x1 * y1, 2 * LANES)
    return factor * times_table(flat, table).reshape(count, x1, y1, LANES)


def coefficient_kernel(counts, where_ref, *refs):
    ins, refs = refs[:7], refs[7:]
    n_x = 1 if counts[0] == 2 else 2
    main_x, refs = refs[:n_x], refs[n_x:]
    arrays, (coarse2, coeffs1, sums, pairing) = refs[:12], refs[12:]
    sx, sy, sz = ins[0].shape
    at_x = position(where_ref)[0]
    x1, y1 = sx // 2, sy // 2
    lane = lane_of((sx, sy, LANES))
    lanes = [slice(k * LANES, (k + 1) * LANES) for k in range(2)]
    mine = slice(HALO, HALO + sx)
    for a in range(6):
        to = arrays[2 * a]
        below, above = neighbours(counts[0], at_x, main_x[0][a], main_x[-1][a])
        to[:HALO, :sy] = below
        to[mine, :sy] = ins[a][...]
        to[HALO + sx:, :sy] = above
        arrays[2 * a + 1][mine, :sy] = unpacked(ins[6][...], a, lane)
    for n, (firsts, seconds) in enumerate(((BOTH, BOTH), (ODD, BOTH), (BOTH, ODD), (BOTH, BOTH))):
        for k in range(2):
            for i in range(x1):
                source = arrays[2 * (n + 2) + k]
                sums[n, i, :, lanes[k]] = rows_of(source, HALO + 2 * i, y1, firsts, seconds)
    pairs = pair_table(2 * LANES, LANES, False)
    odds = pair_table(2 * LANES, LANES, True)
    paired = to_level1(sums, 0, 3, pairs, 0.0625)
    mass1 = (2.0 * WEIGHT) * paired[0]
    faces1 = (paired[1], paired[2], to_level1(sums, 3, 1, odds, 0.0625)[0])
    diag1 = mass1 + faces1[0] + below_x(faces1[0])
    diag1 = diag1 + faces1[1] + faces1[2] + turn(faces1[2], 1, 2)
    for n, values in enumerate((mass1, diag1) + faces1):
        coeffs1[n] = values
    parts = (
        (mass1, False, False, False, 0.125),
        (faces1[0], True, False, False, 0.0625),
        (faces1[1], False, True, False, 0.0625),
        (faces1[2], False, False, True, 0.0625),
    )
    for n, (values, *odd_axes, factor) in enumerate(parts):
        pairing[n] = values
        coarse2[n] = level2_rows(pairing.at[n], odd_axes, factor, x1 // 2, y1 // 2, sz // 4)


def down_kernel(counts, where_ref, zpack, *refs):
    refs = refs[12:]
    n_x = 1 if counts[0] == 2 else 2
    halos_x = refs[:n_x]
    main_two, main_one, rest_two, rest_one, coeffs1 = refs[n_x:5 + n_x]
    flat, refs = refs[5 + n_x:17 + n_x], refs[17 + n_x:]
    arrays = tuple(zip(flat[::2], flat[1::2]))
    own1, refs = refs[0], refs[1:]
    sends, near_two, near_one, refs = refs[:n_x], refs[n_x], refs[n_x + 1], refs[n_x + 2:]
    sends_xy, refs = refs[:2 * n_x], refs[2 * n_x:]
    kept_m, kept_h, weight_m, weight_h = refs[:4]
    packs, half_m, half_h, diag_m, diag_h, sums, left = refs[4:]
    field, rhs, alpha, bx, by, bz = arrays
    sx, sy, sz = zpack.shape
    ex, ey = sx + 2 * HALO, sy + 2 * HALO
    at_x, at_y, _ = position(where_ref)

    rest = neighbours(counts[1], at_y, rest_one[...], rest_two[...])
    rest = jnp.concatenate(rest[::-1], axis=1)
    for a in range(7):
        if a < 6:
            to = arrays[a][0]
            rows = neighbours(counts[1], at_y, main_one[a], main_two[a])
            rows = jnp.concatenate(rows[::-1], axis=1)
        else:
            to = packs
            rows = rest[21:]
            below, above = neighbours(counts[0], at_x, halos_x[0][...], halos_x[-1][...])
            to[:HALO, :sy] = below
            to[HALO + sx:, :sy] = above
        to[HALO:HALO + sx, sy:] = rows
        low, high = corner_tiles(*(rest[3 * a + n] for n in range(3)))
        for n in range(HALO):
            to[n, sy:] = low[n]
            to[HALO + sx + n, sy:] = high[n]
    lane = lane_of((ey, LANES))
    lane_low = lane_of((2 * HALO, LANES))

    def unpack_rows(x):
        packed = packs[x, sy:]
        for a in range(6):
            arrays[a][1][x, sy:] = unpacked(packed, a, lane_low)

    def unpack(x):
        packed = packs[x]
        for a in range(6):
            arrays[a][1][x] = unpacked(packed, a, lane)

    each(0, HALO, unpack)
    each(HALO, HALO + sx, unpack_rows)
    each(HALO + sx, ex, unpack)
    halfway, weight, kept = (half_m, half_h), (weight_m, weight_h), (kept_m, kept_h)
    diag = (diag_m, diag_h)

    def first_sweep(x):
        faces = [half[x] for half in bz]
        downs = ring_down(faces[0], faces[1], lane)
        centre, near = pull_slab(field, bx, by, bz, x, lane)
        for k in range(2):
            face = by[k][x]
            mass = WEIGHT * alpha[k][x]
            d = mass + bx[k][x] + bx[k][x - 1] + face + turn(face, 1, 0) + faces[k] + downs[k]
            w = relaxer(mass, d)
            diag[k][x] = d
            weight[k][x] = w
            halfway[k][x] = KEEP * centre[k] + w * (rhs[k][x] + near[k])

    each(1, ex - 1, first_sweep)

    def second_sweep(x):
        centre, near = pull_slab(halfway, bx, by, bz, x, lane)
        for k in range(2):
            kept[k][x] = KEEP * centre[k] + weight[k][x] * (rhs[k][x] + near[k])

    each(2, ex - 2, second_sweep)

    def residual(x):
        centre, near = pull_slab(kept, bx, by, bz, x, lane)
        for k in range(2):
            halfway[k][x] = rhs[k][x] - diag[k][x] * centre[k] + near[k]

    each(HALO, ex - HALO, residual)

    x1, y1 = sx // 2, sy // 2
    for k in range(2):
        lanes = slice(k * LANES, (k + 1) * LANES)
        for i in range(x1):
            x = HALO + 2 * i
            sums[0, i, :, lanes] = rows_of(halfway[k], x, y1, BOTH, BOTH)
            left[...] = turn(by[k][x] + by[k][x + 1], 1, 0)
            sums[1, i, :, lanes] = left[pl.ds(0, y1, stride=2), :]
        sums[2, 0, :, lanes] = rows_of(bx[k], HALO - 1, y1, (0,), BOTH)
        sums[2, 1:, :, lanes] = jnp.zeros((x1 - 1, y1, LANES), F32)
    rhs1, low_y, low_x = to_level1(sums, 0, 3, pair_table(2 * LANES, LANES, False), 0.0625)
    weight1 = relaxer(coeffs1[0], coeffs1[1] + low_y + low_x)
    for n, values in enumerate((2.0 * rhs1, weight1, coeffs1[2], coeffs1[3], coeffs1[4])):
        own1[n] = values
        for send, face in zip(sends, faces_x(values[None], at_x % 2, n_x, NEAR)):
            send[n] = face[0]
        near_one[n], near_two[n] = faces_y(values, at_y % 2, NEAR)
        for send, tiles in zip(sends_xy, diagonal_sends(values, n_x, at_x % 2, at_y % 2)):
            for t in range(3):
                send[3 * n + t] = tiles[t]


def level2_rows(source, odd_axes, factor, x2, y2, z2):
    rows = []
    for i in range(x2):
        total = None
        for p in (1,) if odd_axes[0] else (0, 1):
            for q in (1,) if odd_axes[1] else (0, 1):
                term = source[2 * i + p, pl.ds(q, y2, stride=2), :]
                total = term if total is None else total + term
        rows.append(total)
    flat = jnp.concatenate(rows, axis=0)
    flat = factor * times_table(flat, pair_table(LANES, LANES, odd_axes[2]))
    lane = lane_of((y2, LANES))
    packed = jnp.zeros((y2, LANES), F32)
    for i in range(x2):
        mask = (lane >= i * z2) & (lane < (i + 1) * z2)
        packed = jnp.where(mask, turn(flat[i * y2:(i + 1) * y2], i * z2, 1), packed)
    return packed


def near_kernel(counts, devices, where_ref, ring, *refs):
    n_x = 1 if counts[0] == 2 else 2
    halos_x = refs[:n_x]
    main_two, main_one = refs[n_x:n_x + 2]
    diagonals, (coarse2, copies, level1, left) = refs[n_x + 2:3 * n_x + 2], refs[3 * n_x + 2:]
    n, bx1, by1, _ = ring.shape
    at_x, at_y, _ = position(where_ref)
    sides = [
        neighbours(counts[0], at_x, diagonals[k][...], diagonals[k - 2][...]) for k in range(2)
    ]
    rest = []
    for one, two in zip(*sides):
        rows = neighbours(counts[1], at_y, one, two)
        rest.append(jnp.concatenate(rows[::-1], axis=1))
    whole = []
    for a in range(n):
        below, above = neighbours(counts[0], at_x, halos_x[0][a], halos_x[-1][a])
        rows = neighbours(counts[1], at_y, main_one[a], main_two[a])
        rows = jnp.concatenate(rows[::-1], axis=1)
        low, high = (diagonal_tiles(*(side[3 * a + k] for k in range(3))) for side in rest)
        low = low[::-1]
        rows = jnp.concatenate(
            [tile[None] for tile in low] + [rows] + [tile[None] for tile in high], axis=0
        )
        block = jnp.concatenate([below, ring[a], above], axis=0)
        whole.append(jnp.concatenate([block, rows], axis=1))
    rhs1, weight1 = whole[:2]
    faces1 = tuple(whole[2:])
    field1 = weight1 * rhs1
    field1 = sweep(field1, rhs1, weight1, faces1)
    for a, values in enumerate([field1] + whole):
        level1[a] = values
    mine = slice(NEAR, NEAR + bx1)
    near = slice(NEAR - 1, NEAR + bx1 + 1)
    inner = weight1[mine]
    diag1 = RELAX / jnp.where(inner > 0.0, inner, 1.0)
    remain = rhs1[mine] - diag1 * field1[mine] + pull(field1[near], [face[near] for face in faces1])[1:-1]
    left[...] = remain
    packed = level2_rows(left, (False,) * 3, 0.125, bx1 // 2, by1 // 2, LANES // 4)
    blocks = LANES // (LANES // 4)
    shift = position(where_ref)[2] % blocks * (LANES // blocks)
    slots = [pltpu.roll(values, shift, 1) for values in [packed] + [coarse2[a] for a in range(4)]]
    for d in range(devices):
        for a in range(n):
            copies[d, a] = slots[a]


def inner_sweep(values, rhs, weight, faces, first):
    part = slice(first, rhs.shape[0] - first)
    below = slice(first - 1, rhs.shape[0] - first - 1)
    bx, by, bz = faces
    centre = values[1:-1]
    near = bx[part] * values[2:] + bx[below] * values[:-2]
    near = near + (by[part] * turn(centre, -1, 1) + turn(by[part] * centre, 1, 1))
    near = near + (bz[part] * turn(centre, -1, 2) + turn(bz[part] * centre, 1, 2))
    return KEEP * centre + weight[part] * (rhs[part] + near)


def halve(values, odd_axis, step):
    half = values.shape[0] // 2
    even = [values[2 * i:2 * i + 1] for i in range(half)]
    odd = [values[2 * i + 1:2 * i + 2] for i in range(half)]
    if odd_axis != 0:
        odd = [a + b for a, b in zip(even, odd)]
    values = jnp.concatenate(odd, axis=0)
    for axis in (1, 2):
        next_one = turn(values, -step, axis)
        values = next_one if odd_axis == axis else values + next_one
    return values


def double(values, step):
    values = values + turn(values, step, 1)
    values = values + turn(values, step, 2)
    return jnp.concatenate([values[i // 2:i // 2 + 1] for i in range(2 * values.shape[0])], axis=0)


def coarse_levels(mass, faces, y, z):
    levels = []
    for level in range(2, LEVELS):
        step = 2 ** (level - 2)
        bx, by, bz = faces
        row = lax.broadcasted_iota(jnp.int32, by.shape, 1)
        lane = lane_of(bz.shape)
        upper = (
            bx,
            jnp.where(row == (y - 1) * step, 0.0, by),
            jnp.where(lane == (z - 1) * step, 0.0, bz),
        )
        lower = (below_x(bx), turn(upper[1], step, 1), turn(upper[2], step, 2))
        mass = jnp.where((row % step == 0) & (lane % step == 0), mass, 0.0)
        diag = mass + bx + lower[0] + by + lower[1] + bz + lower[2]
        levels.append((diag, relaxer(mass, diag), upper, lower))
        if level < LEVELS - 1:
            faces = tuple(0.0625 * halve(face, axis, step) for axis, face in enumerate(faces))
            mass = 0.125 * halve(mass, -1, step)
            y, z = y // 2, z // 2
    return levels


def coupled(values, upper, lower, step):
    ups = (above_x(values), turn(values, -step, 1), turn(values, -step, 2))
    downs = (below_x(values), turn(values, step, 1), turn(values, step, 2))
    x, y, z = (u * up + l * down for u, up, l, down in zip(upper, ups, lower, downs))
    return (y + z) + x if values.shape[0] > 1 else y + z


def coarse_cycle(level, rhs, levels):
    step = 2 ** (level - 2)
    diag, weight, upper, lower = levels[level - 2]
    scaled = tuple(tuple(weight * b for b in faces) for faces in (upper, lower))
    source = weight * rhs

    def relax(field):
        return (KEEP * field + source) + coupled(field, *scaled, step)

    field = source
    if level == LEVELS - 1:
        for _ in range(BOTTOM - 1):
            field = relax(field)
        return field
    for _ in range(SWEEPS - 1):
        field = relax(field)
    remain = (rhs - diag * field) + coupled(field, upper, lower, step)
    correction = coarse_cycle(level + 1, 0.125 * halve(remain, -1, step), levels)
    field = field + double(correction, step)
    for _ in range(SWEEPS):
        field = relax(field)
    return field


def spread_out(counts, slots, whole):
    gx, gy, gz = counts
    y2 = slots.shape[-2]
    x2 = whole.shape[0] // gx
    z2 = LANES // x2
    lane = lane_of((y2, LANES))
    for i in range(gx):
        for j in range(gy):
            for x in range(x2):
                for part in range(whole.shape[2] // LANES):
                    total = None
                    for k in range(LANES // z2):
                        column = part * (LANES // z2) + k
                        if column < gz:
                            block = slots[(i * gy + j) * gz + column]
                            at = (x + k) * z2 % LANES
                            mask = (lane >= at) & (lane < at + z2)
                            if total is None:
                                total = jnp.where(mask, block, 0.0)
                            total = jnp.where(mask, block, total)
                    if x:
                        total = turn(total, -x * z2, 1)
                    lanes = slice(part * LANES, (part + 1) * LANES)
                    whole[i * x2 + x, j * y2:(j + 1) * y2, lanes] = total


def up_kernel(counts, where_ref, gathered, level1, *refs):
    kept, weight, rhs, bx, by, bz = zip(refs[0:12:2], refs[1:12:2])
    out, whole, second, lift, spread_m, spread_h, field_m, field_h, half_m, half_h = refs[12:]
    gx, gy, gz = counts
    at_x, at_y, at_z = position(where_ref)
    sx, sy, sz = out.shape
    x1, y1 = sx // 2, sy // 2
    x2, y2, z2 = x1 // 2, y1 // 2, sz // 4
    columns = max(LANES, gz * z2)
    for a in range(5):
        spread_out(counts, gathered.at[:, a], whole.at[a])
    levels = coarse_levels(whole[1], (whole[2], whole[3], whole[4]), gy * y2, gz * z2)
    correction = coarse_cycle(2, whole[0], levels)

    wide = gx * x2
    half = NEAR // 2
    ex1, ey1 = x1 + 2 * NEAR, y1 + 2 * NEAR
    second[:half] = jnp.zeros((half,) + correction.shape[1:], F32)
    second[half:half + wide] = correction
    second[half + wide:] = jnp.zeros((half,) + correction.shape[1:], F32)
    window = second[pl.ds(at_x * x2, x2 + NEAR)]
    rows = correction.shape[1]
    row = iota2((columns, LANES), 0)
    col = iota2((columns, LANES), 1)
    place = jnp.where(col < LANES * 3 // 4, col, col - LANES)
    table_z = (row == at_z * z2 + lax.shift_right_arithmetic(place, 1)).astype(F32)
    flat = times_table(window.reshape((x2 + NEAR) * rows, columns), table_z)
    flat = flat.reshape(x2 + NEAR, rows, LANES)
    flat = pltpu.roll(flat, (rows - at_y * y2) % rows, 1)
    for i in range(x2 + NEAR):
        for q in range(2):
            lift[i, pl.ds(q, y2, stride=2), :] = flat[i, :y2]
            lift[i, pl.ds(y1 + q, half, stride=2), :] = flat[i, y2:y2 + half]
            lift[i, pl.ds(y1 + NEAR + q, half, stride=2), :] = flat[i, rows - half:]
    lifted = jnp.concatenate([lift[i // 2][None] for i in range(ex1)], axis=0)
    field1, rhs1, weight1 = level1[0], level1[1], level1[2]
    faces1 = (level1[3], level1[4], level1[5])
    field1 = (field1 + jnp.where(weight1 > 0.0, lifted, 0.0))[1:-1]
    for n in range(SWEEPS):
        field1 = inner_sweep(field1, rhs1, weight1, faces1, 2 + n)

    ex, ey = sx + 2 * HALO, sy + 2 * HALO
    near = field1.reshape((x1 + 2) * ey1, LANES)
    row = iota2((LANES, 2 * LANES), 0)
    col = iota2((LANES, 2 * LANES), 1)
    lifted = times_table(near, (col // 2 == row).astype(F32))
    quarter = NEAR // 2
    for k, spread in enumerate((spread_m, spread_h)):
        block = lifted[:, k * LANES:(k + 1) * LANES].reshape(x1 + 2, ey1, LANES)
        for i in range(x1 + 2):
            for q in range(2):
                spread[i, pl.ds(q, y1, stride=2), :] = block[i, :y1]
                spread[i, pl.ds(sy + q, quarter, stride=2), :] = block[i, y1:y1 + quarter]
                spread[i, pl.ds(sy + HALO + q, quarter, stride=2), :] = block[i, ey1 - quarter:]
    before, after = (field_m, field_h), (half_m, half_h)
    first = HALO - 2
    for x in range(first, ex - first):
        for k, spread in enumerate((spread_m, spread_h)):
            before[k][x] = kept[k][x] + spread[(x - first) // 2]

    lane = lane_of((ey, LANES))

    def sweep_out(x):
        centre, around = pull_slab(before, bx, by, bz, x, lane)
        for k in range(2):
            after[k][x] = KEEP * centre[k] + weight[k][x] * (rhs[k][x] + around[k])

    each(first + 1, ex - first - 1, sweep_out)

    def sweep_own(x):
        centre, around = pull_slab(after, bx, by, bz, x, lane)
        value = KEEP * centre[0] + weight[0][x] * (rhs[0][x] + around[0])
        out[x - HALO] = value[:sy]

    each(HALO, ex - HALO, sweep_own)


def run(kernel, outs, where, arrays, scratch=(), grant=16, micros=1, aliases={}):
    return pl.pallas_call(
        kernel,
        out_shape=tuple(jax.ShapeDtypeStruct(shape, F32) for shape in outs),
        in_specs=[SM] * len(where) + [VM] * len(arrays),
        out_specs=tuple(VM for _ in outs),
        input_output_aliases=aliases,
        scratch_shapes=[pltpu.VMEM(shape, F32) for shape in scratch],
        compiler_params=pltpu.CompilerParams(vmem_limit_bytes=grant * 1024 * 1024),
        cost_estimate=pl.CostEstimate(
            flops=0, bytes_accessed=int(micros * 3.6e6), transcendentals=0
        ),
    )(*where, *arrays)


def partners(count, k):
    partner = list(range(count))
    for low in range(k, count - 1, 2):
        partner[low], partner[low + 1] = low + 1, low
    return partner


def swaps(axis, sends, other=None):
    count = lax.axis_size(axis)
    got = []
    for k, block in enumerate(sends):
        partner = partners(count, k)
        if k == 1 and other is None:
            partner[0], partner[-1] = count - 1, 0
        if k == 0 or other is None:
            got.append(lax.ppermute(block, axis, list(enumerate(partner))))
            continue
        rows = lax.axis_size(other)
        pairs = []
        for row in range(rows):
            for i in range(count):
                ends = [(row, i), (min(row ^ 1, rows - 1) if partner[i] == i else row, partner[i])]
                if axis < other:
                    pairs.append(tuple(at * rows + line for line, at in ends))
                else:
                    pairs.append(tuple(line * count + at for line, at in ends))
        got.append(lax.ppermute(block, tuple(sorted((axis, other))), pairs))
    return got


def diagonal_swaps(sends):
    count_x, count_y = lax.axis_size("gx"), lax.axis_size("gy")
    got = []
    for n, block in enumerate(sends):
        xs, ys = partners(count_x, n // 2), partners(count_y, n % 2)
        pairs = [
            (x * count_y + y, xs[x] * count_y + ys[y])
            for x in range(count_x)
            for y in range(count_y)
        ]
        got.append(lax.ppermute(block, ("gx", "gy"), pairs))
    return got


def local(initial, right_side, alpha, beta_x, beta_y, beta_z):
    axes = ("gx", "gy", "gz")
    counts = tuple(lax.axis_size(axis) for axis in axes)
    devices = counts[0] * counts[1] * counts[2]
    where = (lax.axis_index("gx") * STRIDE + lax.axis_index("gy")) * STRIDE + lax.axis_index("gz")
    where = (where.astype(jnp.int32).reshape(1),)
    ins = (initial, right_side, alpha, beta_x, beta_y, beta_z)
    sx, sy, sz = initial.shape
    n_x = 1 if counts[0] == 2 else 2
    ex, ey = sx + 2 * HALO, sy + 2 * HALO
    fine = (ex, ey, LANES)

    *sends_x, two_y, one_y, first, second = run(
        functools.partial(faces_kernel, counts),
        [(6, HALO, sy, LANES)] * n_x
        + [(6, sx, HALO, LANES)] * 2
        + [(sx // 2, sy, LANES)] * 2,
        where,
        ins,
        grant=60,
    )
    main_x = tuple(swaps("gx", sends_x, "gy"))
    main_y = tuple(swaps("gy", (one_y, two_y))[::-1])
    got = swaps("gz", (first, second), "gy")
    zpack, *sends = run(
        functools.partial(halo_z_kernel, counts),
        [(sx, sy, LANES)] + [(HALO, sy, LANES)] * n_x,
        where,
        tuple(got),
    )
    halos_x = tuple(swaps("gx", sends, "gy"))
    x1, y1 = sx // 2, sy // 2
    *laid, coarse2, coeffs1 = run(
        functools.partial(coefficient_kernel, counts),
        [fine] * 12 + [(4, y1 // 2, LANES), (5, x1, y1, LANES)],
        where,
        ins + (zpack,) + main_x,
        [(4, x1, y1, 2 * LANES), (4, x1, y1, LANES)],
        micros=2,
    )
    two_y, one_y = run(
        functools.partial(corners_kernel, counts),
        [(21 + sx, HALO, LANES)] * 2,
        where,
        (zpack,) + main_x + halos_x + (coarse2,),
    )
    rest_y = tuple(swaps("gy", (one_y, two_y), "gx")[::-1])
    outs = run(
        functools.partial(down_kernel, counts),
        [fine] * 12
        + [(5, x1, y1, LANES)]
        + [(5, NEAR, y1, LANES)] * n_x
        + [(5, x1, NEAR, LANES)] * 2
        + [(15, NEAR, LANES)] * (2 * n_x)
        + [fine] * 4,
        where,
        (zpack,) + tuple(laid) + halos_x + main_y + rest_y + (coeffs1,),
        [fine] * 5 + [(3, x1, y1, 2 * LANES), (ey, LANES)],
        24,
        micros=4,
        aliases={n + 2: n for n in range(12)},
    )
    laid, own1, outs = outs[:12], outs[12], outs[13:]
    sends_x, (two_y, one_y), outs = outs[:n_x], outs[n_x:n_x + 2], outs[n_x + 2:]
    sends_xy, fine_arrays = outs[:2 * n_x], outs[2 * n_x:]
    fine_arrays = tuple(fine_arrays) + tuple(laid[2:4]) + tuple(laid[6:])

    near_x = tuple(swaps("gx", sends_x, "gy"))
    near_y = tuple(swaps("gy", (one_y, two_y))[::-1])
    near_xy = tuple(diagonal_swaps(sends_xy))
    copies, level1 = run(
        functools.partial(near_kernel, counts, devices),
        [(devices, 5, y1 // 2, LANES), (6, x1 + 2 * NEAR, y1 + 2 * NEAR, LANES)],
        where,
        (own1,) + near_x + near_y + near_xy + (coarse2,),
        [(x1, y1 + 2 * NEAR, LANES)],
    )

    gathered = lax.all_to_all(copies, axes, 0, 0, tiled=True)
    wide, rows = counts[0] * x1 // 2, counts[1] * y1 // 2
    columns = max(LANES, counts[2] * sz // 4)
    (result,) = run(
        functools.partial(up_kernel, counts),
        [(sx, sy, sz)],
        where,
        (gathered, level1) + tuple(fine_arrays),
        [(5, wide, rows, columns), (wide + NEAR, rows, columns)]
        + [(x1 // 2 + NEAR, y1 + 2 * NEAR, LANES)]
        + [(x1 + 2, ey, LANES)] * 2
        + [fine] * 4,
        24,
        micros=4,
    )
    return result


def solution(mesh):
    spec = P("gx", "gy", "gz")
    return jax.shard_map(
        local, mesh=mesh, in_specs=(spec,) * 6, out_specs=spec, check_vma=False
    )
```
